32 devices in a mesh: dp: 4 (over y, x), expert: 8 (over z, core).
Axes of the slice: x: 2, y: 2, z: 4, core: 2. Of those that a mesh axis runs over, the one named last changes fastest.
Arguments:
- cell_table: bfloat16 [65536, 256], P(('dp', 'expert')), may hold values from -6 to 6
- sample_index: int32 [32768], P(('dp', 'expert')), may hold values from 0 to 2047
- region: int32 [32768, 1], P(('dp', 'expert')), may hold values from 0 to 7; in each aligned block of 1024 rows (0 to 1023, 1024 to 2047, ...) at most 256 rows name the same one
- targets: bfloat16 [32768, 256], P(('dp', 'expert')), may hold values from -6 to 6
- trunk_weight: bfloat16 [256, 256], replicated, may hold values from -0.375 to 0.375
- expert_params: float32 [8, 2, 256, 2048], P('expert', None, None, 'dp'), may hold values from -0.375 to 0.375
- first_moment: float32 [8, 2, 256, 2048], P('expert', None, None, 'dp'), may hold values from -4 to 4
- second_moment: float32 [8, 2, 256, 2048], P('expert', None, None, 'dp'), may hold values from 0.05 to 1
Outputs:
- trunk_grad: float32 [256, 256], replicated
- row_loss: float32 [32768], P(('dp', 'expert'))
- new_params: float32 [8, 2, 256, 2048], P('expert', None, None, 'dp')
- new_first: float32 [8, 2, 256, 2048], P('expert', None, None, 'dp')
- new_second: float32 [8, 2, 256, 2048], P('expert', None, None, 'dp')
The draws below stay inside these ranges and needn't reach their ends.
Inputs may be any that keep to these rules, and one draw needn't show every extreme that they name: In the 1024 rows of one device no region is named more than 256 times; some region exactly 256 times. `sample_index`: indexes the rows of the same device's block of cell_table.
All inputs are finite; a program needn't handle non-finite values.
Results may differ from the reference program's by a relative error of at most 0.0044.
Values may be sent and summed in bfloat16 or wider, within the bound.
No kernel may reach another device: no remote copies, remote signals or barrier semaphores. Data moves between devices by JAX's collectives and lax.ppermute only.
A program may use at most 128 MiB of HBM per device.

```python
import math
import jax
import jax.numpy as jnp
import numpy as np
from jax import lax

D = 256
HID = 2048
ROWS_DEV = 1024
CELLS_DEV = 2048
EXPERTS = 8
CAP = 256
TOKENS = 32768
CELLS = 65536
N_DP = 4
N_EXPERT = 8


def with_ends(result, key, low, largest):
    dims = result.shape
    spot = [jax.random.randint(jax.random.fold_in(key, axis), (), 0, dims[axis]) for axis in range(len(dims))]
    result = result.at[tuple(spot)].set(low)
    longest = dims.index(max(dims))
    spot[longest] = (spot[longest] + 1) % dims[longest]
    return result.at[tuple(spot)].set(largest)


def level_of(stream_key, extent, shards, low, top_value):
    loudness, own = 1.0, jax.random.fold_in(stream_key, 6)
    for position, blocks in shards:
        steps = jnp.exp(jax.random.uniform(jax.random.fold_in(own, position), (blocks,), jnp.float32, low / len(shards), top_value / len(shards)))
        loudness = loudness * jnp.repeat(steps, extent[position] // blocks).reshape([-1 if axis == position else 1 for axis in range(len(extent))])
    return loudness


def assign_block(stream_key, own, number, rows, count, top, bound, lean):
    order = jax.random.permutation(stream_key, count)
    heavy_load, usual = shares(count, rows * top, bound, lean, True), shares(count, rows * top, bound, lean, False)
    places = jnp.arange(count)

    def named(lengths, offset_by):
        used = int((lengths > 0).sum())
        fixed = max(1, used // 4)
        shifted = fixed + (places - fixed + offset_by * (used - fixed)) % max(1, count - fixed)
        return jnp.zeros((count,), jnp.int32).at[order[jnp.where(places < fixed, places, shifted)]].set(jnp.asarray(lengths, jnp.int32))

    lengths = jnp.where(number % 4 == 0, named(heavy_load, number // 4), named(usual, number - number // 4 - 1))
    mixed = jax.random.permutation(jax.random.fold_in(own, 3), count)
    source_of, sink = mixed[0:count // 2 * 2:2], mixed[1:count // 2 * 2:2]
    margin = jnp.minimum(lengths[source_of] - 1, bound - lengths[sink]) // 2
    margin = jnp.where((source_of == order[0]) | (sink == order[0]) | (lengths[sink] == 0), 0, jnp.maximum(margin, 0))
    shifted = jax.random.randint(jax.random.fold_in(own, 4), (count // 2,), 0, 1 << 20) % (margin + 1)
    lengths = lengths.at[source_of].add(-shifted).at[sink].add(shifted)
    labels = jnp.searchsorted(jnp.cumsum(lengths), jnp.arange(rows * top), side="right").astype(jnp.int32)
    grid = labels.reshape(top, rows).T
    grid = grid[jax.random.permutation(jax.random.fold_in(own, 1), rows)]
    offset_by = jax.random.randint(jax.random.fold_in(own, 2), (rows, 1), 0, top)
    return jnp.take_along_axis(grid, (jnp.arange(top)[None, :] + offset_by) % top, axis=1)


def shares(amount, total, most, slope, full):
    portions = [(1 << 20) // math.isqrt(standing ** slope) + 1 for standing in range(1, amount + 1)]
    largest = most if full else min(most, max(-(-total // amount), total * portions[0] // sum(portions)))
    least = 1 if total - largest >= amount - 1 else 0
    given, rest = [largest] + [least] * (amount - 1), total - largest - least * (amount - 1)
    while rest > 0:
        movable = [i for i in range(1, amount) if given[i] < largest] or [i for i in range(1, amount) if given[i] < most]
        whole, budget = sum([portions[i] for i in movable]), rest
        for i in movable:
            more = min(most - given[i], max(1, budget * portions[i] // whole), rest)
            given[i] = given[i] + more
            rest = rest - more
    return np.array(given)


def centred(key, shape, width, bound, pieces=(), held_as=jnp.bfloat16):
    gain = level_of(key, shape, pieces, -0.22, 0.18) if pieces else 1.0
    entries = jax.random.normal(key, shape, jnp.float32) * width * gain
    return jnp.minimum(jnp.maximum(entries, -bound), bound).astype(held_as)


def setup_inputs(seed: int = 0) -> dict:
    arg_keys = jax.random.split(jax.random.key(seed), 9)
    cell_table = centred(arg_keys[0], (CELLS, D), 1.0, 6.0, ((0, 32),))
    sample_index = with_ends(jax.random.randint(arg_keys[1], (TOKENS,), 0, CELLS_DEV), jax.random.fold_in(arg_keys[1], 1), 0, CELLS_DEV - 1).astype(jnp.int32)
    region_keys = jax.random.split(jax.random.fold_in(arg_keys[2], 1), TOKENS // ROWS_DEV)
    region_turns = jax.random.permutation(jax.random.fold_in(arg_keys[2], 3), TOKENS // ROWS_DEV)
    region = jax.vmap(lambda own, number: assign_block(jax.random.fold_in(arg_keys[2], 2), own, number, ROWS_DEV, EXPERTS, 1, CAP, 2))(region_keys, region_turns).reshape((TOKENS, 1))
    targets = centred(arg_keys[3], (TOKENS, D), 1.0, 6.0, ((0, 32),))
    trunk_weight = centred(arg_keys[4], (D, D), D ** -0.5, 0.375)
    expert_params = centred(arg_keys[5], (EXPERTS, 2, D, HID), D ** -0.5, 0.375, ((0, 8), (3, 4)), jnp.float32)
    first_moment = centred(arg_keys[6], (EXPERTS, 2, D, HID), 0.3, 4.0, ((0, 8), (3, 4)), jnp.float32)
    second_moment = jnp.clip(jnp.exp(math.log(1.0) - 2.9957323 * jax.random.uniform(arg_keys[7], (EXPERTS, 2, D, HID), jnp.float32) ** level_of(arg_keys[7], (EXPERTS, 2, D, HID), ((0, 8), (3, 4)), -0.2, 0.2)), 0.05, 1.0)
    return {"cell_table": cell_table, "sample_index": sample_index, "region": region, "targets": targets, "trunk_weight": trunk_weight, "expert_params": expert_params, "first_moment": first_moment, "second_moment": second_moment}


loss_scale = 1.0 / 32.0
beta_one = 0.9
beta_two = 0.999
learn_rate = 0.05
adam_eps = 1e-08
adam_step = 10

def silu_slope(values):
    sigma = jax.nn.sigmoid(values)
    return sigma * (1.0 + values * (1.0 - sigma))

def expert_forward(arrived, w_up, w_down):
    up_pre = jnp.dot(arrived, w_up, preferred_element_type=jnp.float32)
    hidden = jax.nn.silu(up_pre).astype(jnp.bfloat16)
    predicted = lax.dot_general(hidden, w_down, (((1,), (1,)), ((), ())), preferred_element_type=jnp.float32)
    return (up_pre, hidden, predicted)

def expert_backward(arrived, up_pre, hidden, scaled_error, w_up, w_down):
    grad_down = lax.dot_general(scaled_error, hidden, (((0,), (0,)), ((), ())), preferred_element_type=jnp.float32)
    hidden_grad = jnp.dot(scaled_error, w_down, preferred_element_type=jnp.float32)
    pre_grad = (hidden_grad * silu_slope(up_pre)).astype(jnp.bfloat16)
    grad_up = lax.dot_general(arrived, pre_grad, (((0,), (0,)), ((), ())), preferred_element_type=jnp.float32)
    input_grad = lax.dot_general(pre_grad, w_up, (((1,), (1,)), ((), ())), preferred_element_type=jnp.float32).astype(jnp.bfloat16)
    return (grad_up, grad_down, input_grad)

def error_terms(predicted, target):
    errors = predicted - target.astype(jnp.float32)
    losses = lax.optimization_barrier(jnp.sum(errors * errors, axis=1)) * (0.5 * loss_scale)
    return (losses, (errors * loss_scale).astype(jnp.bfloat16))

def adam_update(params, first, second, grads):
    first_new = beta_one * first + (1.0 - beta_one) * grads
    second_new = beta_two * second + (1.0 - beta_two) * grads * grads
    first_hat = first_new / (1.0 - beta_one ** adam_step)
    second_hat = second_new / (1.0 - beta_two ** adam_step)
    return (params - learn_rate * first_hat / (jnp.sqrt(second_hat) + adam_eps), first_new, second_new)

def reference(cell_table, sample_index, region, targets, trunk_weight, expert_params, first_moment, second_moment):
    devices_all = N_DP * N_EXPERT
    experts = N_EXPERT
    table = cell_table.reshape(devices_all, CELLS_DEV, D)
    picks = sample_index.reshape(devices_all, ROWS_DEV)
    features = jax.vmap(lambda shard_rows, picked: jnp.take(shard_rows, picked, axis=0))(table, picks).reshape(-1, D)
    trunk_pre = jnp.dot(features, trunk_weight, preferred_element_type=jnp.float32)
    trunk_out = (features.astype(jnp.float32) + jax.nn.silu(trunk_pre)).astype(jnp.bfloat16)
    routed = region[:, 0].reshape(devices_all, ROWS_DEV)
    onehot = (routed[:, :, None] == jnp.arange(experts, dtype=jnp.int32)[None, None, :]).astype(jnp.int32)
    slots = lax.optimization_barrier(jnp.sum(jnp.cumsum(onehot, axis=1) * onehot, axis=2)) - 1
    device_ids = jnp.arange(devices_all, dtype=jnp.int32)[:, None]
    group_ids = device_ids // N_EXPERT
    source_ids = device_ids % N_EXPERT
    places = (((routed * N_DP + group_ids) * N_EXPERT + source_ids) * CAP + slots).reshape(-1).astype(jnp.int32)
    total = experts * N_DP * N_EXPERT * CAP
    inputs_buffer = jnp.zeros((total, D), jnp.bfloat16).at[places].set(trunk_out).reshape(experts, N_DP, N_EXPERT * CAP, D)
    target_buffer = jnp.zeros((total, D), jnp.bfloat16).at[places].set(targets).reshape(experts, N_DP, N_EXPERT * CAP, D)
    weights = expert_params.astype(jnp.bfloat16)

    def per_expert(operands):
        arrived_all, target_all, weight_pair = operands
        grad_up = jnp.zeros((D, HID), jnp.float32)
        grad_down = jnp.zeros((D, HID), jnp.float32)
        losses = []
        inputs_grads = []
        for group in range(N_DP):
            up_pre, hidden, predicted = expert_forward(arrived_all[group], weight_pair[0], weight_pair[1])
            slot_loss, scaled_error = error_terms(predicted, target_all[group])
            part_up, part_down, input_grad = expert_backward(arrived_all[group], up_pre, hidden, scaled_error, weight_pair[0], weight_pair[1])
            grad_up = grad_up + part_up
            grad_down = grad_down + part_down
            losses.append(slot_loss)
            inputs_grads.append(input_grad)
        return (jnp.stack(losses), jnp.stack(inputs_grads), jnp.stack([grad_up, grad_down]))
    slot_losses, input_grads, grads = lax.map(per_expert, (inputs_buffer, target_buffer, weights))
    row_grad = input_grads.reshape(-1, D)[places]
    row_loss = slot_losses.reshape(-1)[places]
    trunk_slope = (row_grad.astype(jnp.float32) * silu_slope(trunk_pre)).astype(jnp.bfloat16)
    trunk_grad = lax.dot_general(features, trunk_slope, (((0,), (0,)), ((), ())), preferred_element_type=jnp.float32)
    new_params, new_first, new_second = adam_update(expert_params, first_moment, second_moment, grads)
    return (trunk_grad, row_loss, new_params, new_first, new_second)
```

```python
import functools

import jax
import jax.numpy as jnp
from jax import lax
from jax.experimental import pallas as pl
from jax.experimental.pallas import tpu as pltpu
from jax.sharding import PartitionSpec as P

loss_scale = 1.0 / 32.0
beta_one = 0.9
beta_two = 0.999
learn_rate = 0.05
adam_eps = 1e-08
adam_step = 10

LANES = 128
F32 = jnp.float32
BF16 = jnp.bfloat16
MIB = 1 << 20


def iota(shape, dim):
    return lax.broadcasted_iota(jnp.int32, shape, dim)


def dot(a, b, ca=1, cb=0):
    return lax.dot_general(a, b, (((ca,), (cb,)), ((), ())), preferred_element_type=F32)


def whole(memory_space=pltpu.VMEM):
    return pl.BlockSpec(memory_space=memory_space)


def pack_kernel(experts, capacity, me_ref, index_ref, region_ref, table_ref, target_ref, *refs):
    blocks, place_ref, rows_ref = refs[:experts], refs[experts], refs[experts + 1]
    me = me_ref[0]
    groups = index_ref.shape[0]
    cells, width = table_ref.shape
    expert_id = iota((experts, LANES), 0)
    starts = ((expert_id ^ me) * capacity).astype(F32)
    ahead = jnp.where(iota((LANES, LANES), 0) <= iota((LANES, LANES), 1), 1.0, 0.0).astype(BF16)
    counted = jnp.zeros((experts, LANES), F32)
    places = []
    for g in range(groups):
        hot = jnp.where(region_ref[g : g + 1, :] == expert_id, 1.0, 0.0)
        upto = dot(hot.astype(BF16), ahead)
        places.append(jnp.sum(hot * (upto - 1.0 + counted + starts), axis=0, keepdims=True))
        counted = counted + jnp.broadcast_to(upto[:, LANES - 1 :], (experts, LANES))
    for g in range(groups):
        place_ref[g : g + 1, :] = places[g].astype(jnp.int32)
    place = jnp.concatenate(places, axis=1)

    step = 2
    cell_id = iota((LANES * step, LANES), 1).astype(F32)
    for g in range(0, groups, step):
        column = jnp.concatenate(
            [
                jnp.broadcast_to(index_ref[h : h + 1, :].astype(F32), (LANES, LANES)).T
                for h in range(g, g + step)
            ],
            axis=0,
        )
        picks = jnp.concatenate(
            [
                jnp.where(column == cell_id + float(LANES * t), 1.0, 0.0).astype(BF16)
                for t in range(cells // LANES)
            ],
            axis=1,
        )
        at = slice(g * LANES, (g + step) * LANES)
        rows_ref[at, :width] = dot(picks, table_ref[...]).astype(BF16)
        rows_ref[at, width:] = target_ref[at, :]

    slot_id = iota((capacity, place.shape[1]), 0).astype(F32)
    for s in range(experts):
        spread = jnp.where(place == slot_id + float(s * capacity), 1.0, 0.0).astype(BF16)
        blocks[s][...] = dot(spread, rows_ref[...]).astype(BF16)


def pack(me, index, region, table, targets, experts, capacity):
    rows, width = targets.shape
    groups = rows // LANES
    return pl.pallas_call(
        functools.partial(pack_kernel, experts, capacity),
        out_shape=[jax.ShapeDtypeStruct((capacity, 2 * width), BF16)] * experts
        + [jax.ShapeDtypeStruct((groups, LANES), jnp.int32)],
        in_specs=[whole(pltpu.SMEM)] + [whole()] * 4,
        out_specs=[whole()] * (experts + 1),
        scratch_shapes=[pltpu.VMEM((rows, 2 * width), BF16)],
        compiler_params=pltpu.CompilerParams(vmem_limit_bytes=32 * MIB),
        cost_estimate=pl.CostEstimate(
            flops=2 * rows * width * (table.shape[0] + 2 * experts * capacity),
            bytes_accessed=6 * MIB,
            transcendentals=0,
        ),
        name="pack_rows",
    )(me, index.reshape(groups, LANES), region.reshape(groups, LANES), table, targets)


def sigmoid(v):
    return 0.5 * jnp.tanh(0.5 * v) + 0.5


def expert_kernel(counts, first, last, *refs):
    blocks, shares, experts, steps, step_rows = counts
    refs = list(refs)

    def take(n):
        got = refs[:n]
        del refs[:n]
        return got

    xs = take(blocks)
    (trunk_ref,) = take(1)
    weights = take(shares)
    if not first:
        prior_ref, prior_trunk_ref = take(2)
    if last:
        loss_refs = take(last - 1)
        (me_ref,) = take(1)
        (own_ref,) = take(1)
        sent = take(shares - 1)
        notes = take(experts)
        part = trunk_part_rows(trunk_ref.shape[0], experts)
        if not part:
            (all_trunk_ref,) = take(1)
    else:
        acc_ref, acc_trunk_ref, loss_ref = take(3)
    x_ref, hid_ref, slope_ref = take(3)
    if last:
        acc_ref, acc_trunk_ref, loss_ref = take(3)

    width = trunk_ref.shape[0]
    share = weights[0].shape[2]
    block_rows = xs[0].shape[0]
    for i, ref in enumerate(xs):
        x_ref[i * block_rows : (i + 1) * block_rows, :] = ref[...]
    if first:
        acc_ref[...] = jnp.zeros(acc_ref.shape, F32)
        acc_trunk_ref[...] = jnp.zeros(acc_trunk_ref.shape, F32)
    else:
        acc_ref[...] = prior_ref[...]
        acc_trunk_ref[...] = prior_trunk_ref[...]

    def step(i, carry):
        at = pl.ds(pl.multiple_of(i * step_rows, step_rows), step_rows)
        feats = x_ref[at, :width]
        feats_f = feats.astype(F32)
        trunk_pre = dot(feats, trunk_ref[...])
        gate = sigmoid(trunk_pre)
        act = trunk_pre * gate
        trunk_slope = gate + act * (1.0 - gate)
        out_f = feats_f + act
        out = out_f.astype(BF16)
        predicted = jnp.zeros((step_rows, width), F32)
        for j in range(shares):
            up = dot(out, weights[j][0])
            s = sigmoid(up)
            h = up * s
            slope_ref[:, j * share : (j + 1) * share] = s + h * (1.0 - s)
            h = h.astype(BF16)
            hid_ref[:, j * share : (j + 1) * share] = h
            predicted = predicted + dot(h, weights[j][1], 1, 1)
        errors = predicted - x_ref[at, width:].astype(F32)
        squares = errors * errors
        half = squares[:, :LANES]
        for k in range(1, width // LANES):
            half = half + squares[:, k * LANES : (k + 1) * LANES]
        loss_ref[pl.ds(i, 1), :] = jnp.sum(half.T, axis=0, keepdims=True) * (0.5 * loss_scale)
        scaled_f = errors * loss_scale
        scaled = scaled_f.astype(BF16)
        scaled_t = scaled_f.T.astype(BF16)
        out_t = out_f.T.astype(BF16)
        row_grad = jnp.zeros((step_rows, width), F32)
        for j in range(shares):
            part = slice(j * share, (j + 1) * share)
            acc_ref[j, 1] += dot(scaled_t, hid_ref[:, part])
            pre = (dot(scaled, weights[j][1]) * slope_ref[:, part]).astype(BF16)
            acc_ref[j, 0] += dot(out_t, pre)
            row_grad = row_grad + dot(pre, weights[j][0], 1, 1)
        slope = (row_grad.astype(BF16).astype(F32) * trunk_slope).astype(BF16)
        acc_trunk_ref[...] += dot(feats_f.T.astype(BF16), slope)
        return carry

    if steps == 1:
        step(0, 0)
    else:
        lax.fori_loop(0, steps, step, 0)
    if last:
        own_ref[...] = acc_ref[0]
        for j in range(1, shares):
            sent[j - 1][...] = acc_ref[j].astype(BF16)
        me = me_ref[0]
        if not part:
            all_trunk_ref[...] = acc_trunk_ref[...]
        for s in range(experts):
            if part:
                mine = pl.ds(pl.multiple_of((me ^ s) * part, part), part)
                notes[s][:part, :] = acc_trunk_ref[mine, :]
            row = loss_row(list(loss_refs) + [loss_ref], s * block_rows // step_rows)
            start = s * block_rows % step_rows
            notes[s][part:, :] = jnp.zeros((8, width), F32)
            notes[s][part:, :block_rows] = jnp.broadcast_to(
                row[:, start : start + block_rows], (8, block_rows)
            )


def loss_row(refs, row):
    for ref in refs:
        if row < ref.shape[0]:
            return ref[row : row + 1, :]
        row -= ref.shape[0]


def expert_call(xs, trunk_weight, weights, prior, losses, me, experts, last):
    block_rows = xs[0].shape[0]
    width = trunk_weight.shape[0]
    shares = len(weights)
    share = weights[0].shape[2]
    rows = block_rows * len(xs)
    step_rows = min(256, rows)
    steps = rows // step_rows
    first = prior is None
    acc = jax.ShapeDtypeStruct((shares, 2, width, share), F32)
    acc_trunk = jax.ShapeDtypeStruct((width, width), F32)
    loss = jax.ShapeDtypeStruct((steps, step_rows), F32)
    args = list(xs) + [trunk_weight] + list(weights)
    if not first:
        args += list(prior)
    in_specs = [whole()] * len(args)
    scratch = [
        pltpu.VMEM((rows, 2 * width), BF16),
        pltpu.VMEM((step_rows, shares * share), BF16),
        pltpu.VMEM((step_rows, shares * share), F32),
    ]
    if last:
        args += list(losses) + [me]
        in_specs += [whole()] * len(losses) + [whole(pltpu.SMEM)]
        outs = [jax.ShapeDtypeStruct((2, width, share), F32)]
        outs += [jax.ShapeDtypeStruct((2, width, share), BF16)] * (shares - 1)
        part = trunk_part_rows(width, experts)
        outs += [jax.ShapeDtypeStruct((part + 8, width), F32)] * experts
        if not part:
            outs += [acc_trunk]
        scratch += [pltpu.VMEM(a.shape, a.dtype) for a in (acc, acc_trunk, loss)]
    else:
        outs = [acc, acc_trunk, loss]
    counts = (len(xs), shares, experts, steps, step_rows)
    return pl.pallas_call(
        functools.partial(expert_kernel, counts, first, len(losses) + 1 if last else 0),
        out_shape=outs,
        in_specs=in_specs,
        out_specs=[whole()] * len(outs),
        scratch_shapes=scratch,
        compiler_params=pltpu.CompilerParams(vmem_limit_bytes=40 * MIB),
        cost_estimate=pl.CostEstimate(
            flops=12 * rows * width * shares * share,
            bytes_accessed=10 * MIB,
            transcendentals=rows * shares * share,
        ),
        name="expert_rows",
    )(*args)


def finish_kernel(experts, me_ref, place_ref, loss_ref, *refs):
    *parts, row_loss_ref, trunk_ref = refs
    me = me_ref[0]
    part = parts[0].shape[0]
    if len(parts) == 1:
        trunk_ref[...] = parts[0][...]
    for s in range(len(parts) if len(parts) > 1 else 0):
        trunk_ref[pl.ds(pl.multiple_of((me ^ s) * part, part), part), :] = parts[s][...]
    capacity = loss_ref.shape[1]
    loss = loss_ref[...]
    for g in range(place_ref.shape[0]):
        place = place_ref[g : g + 1, :]
        block = place // capacity
        slot = place - block * capacity
        picks = jnp.where(iota((capacity, LANES), 0) == slot, 1.0, 0.0)
        found = lax.dot_general(
            loss,
            picks,
            (((1,), (0,)), ((), ())),
            precision=lax.Precision.HIGHEST,
            preferred_element_type=F32,
        )
        mine = jnp.where(iota((experts, LANES), 0) == block, found, 0.0)
        row_loss_ref[g : g + 1, :] = jnp.sum(mine, axis=0, keepdims=True)


def finish(me, place, loss, parts):
    experts = loss.shape[0]
    part, width = parts[0].shape
    return pl.pallas_call(
        functools.partial(finish_kernel, experts),
        out_shape=[
            jax.ShapeDtypeStruct(place.shape, F32),
            jax.ShapeDtypeStruct((len(parts) * part, width), F32),
        ],
        in_specs=[whole(pltpu.SMEM)] + [whole()] * (len(parts) + 2),
        out_specs=[whole()] * 2,
        compiler_params=pltpu.CompilerParams(vmem_limit_bytes=16 * MIB),
        name="finish_rows",
    )(me, place, loss, *parts)


def adam_update(params, first, second, grads):
    first_new = beta_one * first + (1.0 - beta_one) * grads
    second_new = beta_two * second + (1.0 - beta_two) * grads * grads
    first_hat = first_new / (1.0 - beta_one**adam_step)
    second_hat = second_new / (1.0 - beta_two**adam_step)
    return (
        params - learn_rate * first_hat / (jnp.sqrt(second_hat) + adam_eps),
        first_new,
        second_new,
    )


def trunk_part_rows(width, experts):
    return 0 if width % (8 * experts) else width // experts


def swap(value, axis, s):
    if s == 0:
        return value
    return lax.ppermute(value, axis, [(i, i ^ s) for i in range(lax.axis_size(axis))])


def on_device(
    cell_table,
    sample_index,
    region,
    targets,
    trunk_weight,
    expert_params,
    first_moment,
    second_moment,
):
    rows = sample_index.shape[0]
    width = cell_table.shape[1]
    experts = lax.axis_size("expert")
    replicas = lax.axis_size("dp")
    capacity = 2 * rows // experts
    me = lax.axis_index("expert").astype(jnp.int32).reshape(1)

    rounded = expert_params[0].astype(BF16)
    weights = [swap(rounded, "dp", j) for j in range(replicas)]
    *blocks, place = pack(me, sample_index, region[:, 0], cell_table, targets, experts, capacity)
    arrived = [swap(blocks[s], "expert", s) for s in range(experts)]

    cuts = [0, experts // 2, 3 * experts // 4, 7 * experts // 8, experts]
    prior, losses = None, []
    for k in range(len(cuts) - 1):
        xs = arrived[cuts[k] : cuts[k + 1]]
        last = k == len(cuts) - 2
        outs = expert_call(xs, trunk_weight, weights, prior, losses, me, experts, last)
        if not last:
            prior = outs[:2]
            losses.append(outs[2])
    grads = outs[0]
    sent = outs[1:replicas]
    notes = outs[replicas : replicas + experts]

    back = [swap(notes[s], "expert", s) for s in range(experts)]
    part = trunk_part_rows(width, experts)
    if part:
        trunk_part = sum(note[:part] for note in back)
        trunk_part = sum(swap(trunk_part, "dp", j) for j in range(replicas))
        parts = [swap(trunk_part, "expert", s) for s in range(experts)]
    else:
        parts = [lax.psum(outs[-1], ("dp", "expert"))]
    loss = jnp.concatenate([note[part : part + 1, :capacity] for note in back], axis=0)
    row_loss, trunk_grad = finish(me, place, loss, parts)

    for j in range(1, replicas):
        grads = grads + swap(sent[j - 1], "dp", j).astype(F32)
    new_params, new_first, new_second = adam_update(
        expert_params, first_moment, second_moment, grads[None]
    )
    return (trunk_grad, row_loss.reshape(rows), new_params, new_first, new_second)


def solution(mesh):
    placed = (
        P(("dp", "expert"), None),
        P(("dp", "expert")),
        P(("dp", "expert"), None),
        P(("dp", "expert"), None),
        P(),
        P("expert", None, None, "dp"),
        P("expert", None, None, "dp"),
        P("expert", None, None, "dp"),
    )
    return jax.shard_map(
        on_device,
        mesh=mesh,
        in_specs=placed,
        out_specs=(
            P(),
            P(("dp", "expert")),
            P("expert", None, None, "dp"),
            P("expert", None, None, "dp"),
            P("expert", None, None, "dp"),
        ),
        check_vma=False,
    )
```

```python
import functools

import jax
import jax.numpy as jnp
from jax import lax
from jax.experimental import pallas as pl
from jax.experimental.pallas import tpu as pltpu
from jax.sharding import PartitionSpec as P

loss_scale = 1.0 / 32.0
beta_one = 0.9
beta_two = 0.999
learn_rate = 0.05
adam_eps = 1e-08
adam_step = 10

LANES = 128
F32 = jnp.float32
BF16 = jnp.bfloat16
MIB = 1 << 20


def iota(shape, dim):
    return lax.broadcasted_iota(jnp.int32, shape, dim)


def dot(a, b, ca=1, cb=0):
    return lax.dot_general(a, b, (((ca,), (cb,)), ((), ())), preferred_element_type=F32)


def whole(memory_space=pltpu.VMEM):
    return pl.BlockSpec(memory_space=memory_space)


def pack_kernel(experts, capacity, me_ref, *refs):
    sources, blocks, place_ref = refs[:4], refs[4 : 4 + experts], refs[4 + experts]
    rows_ref, index_ref, region_ref, table_ref, target_ref, sems = refs[5 + experts :]
    loads = [
        pltpu.make_async_copy(source, held, sems.at[i])
        for i, (source, held) in enumerate(
            zip(sources, (index_ref, region_ref, table_ref, target_ref))
        )
    ]
    for load in loads:
        load.start()
    me = me_ref[0]
    groups = index_ref.shape[0]
    cells, width = table_ref.shape
    loads[1].wait()
    expert_id = iota((experts, LANES), 0)
    starts = ((expert_id ^ me) * capacity).astype(F32)
    ahead = jnp.where(iota((LANES, LANES), 0) <= iota((LANES, LANES), 1), 1.0, 0.0).astype(BF16)
    counted = jnp.zeros((experts, LANES), F32)
    places = []
    for g in range(groups):
        hot = jnp.where(region_ref[g : g + 1, :] == expert_id, 1.0, 0.0)
        upto = dot(hot.astype(BF16), ahead)
        places.append(jnp.sum(hot * (upto - 1.0 + counted + starts), axis=0, keepdims=True))
        counted = counted + jnp.broadcast_to(upto[:, LANES - 1 :], (experts, LANES))
    for g in range(groups):
        place_ref[g : g + 1, :] = places[g].astype(jnp.int32)
    place = jnp.concatenate(places, axis=1)

    loads[0].wait()
    loads[2].wait()
    loads[3].wait()
    step = 2
    cell_id = iota((LANES * step, LANES), 1).astype(F32)
    for g in range(0, groups, step):
        column = jnp.concatenate(
            [
                jnp.broadcast_to(index_ref[h : h + 1, :].astype(F32), (LANES, LANES)).T
                for h in range(g, g + step)
            ],
            axis=0,
        )
        picks = jnp.concatenate(
            [
                jnp.where(column == cell_id + float(LANES * t), 1.0, 0.0).astype(BF16)
                for t in range(cells // LANES)
            ],
            axis=1,
        )
        at = slice(g * LANES, (g + step) * LANES)
        rows_ref[at, :width] = dot(picks, table_ref[...]).astype(BF16)
        rows_ref[at, width:] = target_ref[at, :]

    slot_id = iota((capacity, place.shape[1]), 0).astype(F32)
    for s in range(experts):
        spread = jnp.where(place == slot_id + float(s * capacity), 1.0, 0.0).astype(BF16)
        blocks[s][...] = dot(spread, rows_ref[...]).astype(BF16)


def pack(me, index, region, table, targets, experts, capacity):
    rows, width = targets.shape
    groups = rows // LANES
    return pl.pallas_call(
        functools.partial(pack_kernel, experts, capacity),
        out_shape=[jax.ShapeDtypeStruct((capacity, 2 * width), BF16)] * experts
        + [jax.ShapeDtypeStruct((groups, LANES), jnp.int32)],
        in_specs=[whole(pltpu.SMEM)] + [whole(pltpu.HBM)] * 4,
        out_specs=[whole()] * (experts + 1),
        scratch_shapes=[
            pltpu.VMEM((rows, 2 * width), BF16),
            pltpu.VMEM((groups, LANES), jnp.int32),
            pltpu.VMEM((groups, LANES), jnp.int32),
            pltpu.VMEM(table.shape, BF16),
            pltpu.VMEM(targets.shape, BF16),
            pltpu.SemaphoreType.DMA((4,)),
        ],
        compiler_params=pltpu.CompilerParams(vmem_limit_bytes=58 * MIB),
        cost_estimate=pl.CostEstimate(
            flops=2 * rows * width * (table.shape[0] + 2 * experts * capacity),
            bytes_accessed=6 * MIB,
            transcendentals=0,
        ),
        name="pack_rows",
    )(me, index.reshape(groups, LANES), region.reshape(groups, LANES), table, targets)


def sigmoid(v):
    return 0.5 * jnp.tanh(0.5 * v) + 0.5


def expert_kernel(counts, order, first, last, *refs):
    blocks, shares, experts, steps, step_rows = counts
    refs = list(refs)

    def take(n):
        got = refs[:n]
        del refs[:n]
        return got

    xs = take(blocks)
    (trunk_ref,) = take(1)
    weights = take(shares)
    if not first:
        prior_ref, prior_trunk_ref = take(2)
    if last:
        loss_refs = take(last - 1)
        (me_ref,) = take(1)
        (own_ref,) = take(1)
        sent_up, sent_down = take(shares - 1), take(shares - 1)
        kept_ref, note_ref = take(2)
    else:
        acc_ref, acc_trunk_ref, loss_ref = take(3)
    x_ref, hid_ref, slope_ref = take(3)
    if last:
        acc_ref, acc_trunk_ref, loss_ref = take(3)

    width = trunk_ref.shape[0]
    share = weights[0].shape[2]
    block_rows = xs[0].shape[0]
    for i, ref in enumerate(xs):
        x_ref[i * block_rows : (i + 1) * block_rows, :] = ref[...]
    if first:
        acc_ref[...] = jnp.zeros(acc_ref.shape, F32)
        acc_trunk_ref[...] = jnp.zeros(acc_trunk_ref.shape, F32)
    else:
        acc_ref[...] = prior_ref[...]
        acc_trunk_ref[...] = prior_trunk_ref[...]

    def step(i, carry):
        at = pl.ds(pl.multiple_of(i * step_rows, step_rows), step_rows)
        feats = x_ref[at, :width]
        feats_f = feats.astype(F32)
        trunk_pre = dot(feats, trunk_ref[...])
        gate = sigmoid(trunk_pre)
        act = trunk_pre * gate
        trunk_slope = gate + act * (1.0 - gate)
        out_f = feats_f + act
        out = out_f.astype(BF16)
        predicted = jnp.zeros((step_rows, width), F32)
        for j in range(shares):
            up = dot(out, weights[j][0])
            s = sigmoid(up)
            h = up * s
            slope_ref[:, j * share : (j + 1) * share] = s + h * (1.0 - s)
            h = h.astype(BF16)
            hid_ref[:, j * share : (j + 1) * share] = h
            predicted = predicted + dot(h, weights[j][1], 1, 1)
        errors = predicted - x_ref[at, width:].astype(F32)
        squares = errors * errors
        half = squares[:, :LANES]
        for k in range(1, width // LANES):
            half = half + squares[:, k * LANES : (k + 1) * LANES]
        loss_ref[pl.ds(i, 1), :] = jnp.sum(half.T, axis=0, keepdims=True) * (0.5 * loss_scale)
        scaled_f = errors * loss_scale
        scaled = scaled_f.astype(BF16)
        scaled_t = scaled_f.T.astype(BF16)
        out_t = out_f.T.astype(BF16)
        row_grad = jnp.zeros((step_rows, width), F32)
        for j in range(shares):
            part = slice(j * share, (j + 1) * share)
            acc_ref[j, 1] += dot(scaled_t, hid_ref[:, part])
            pre = (dot(scaled, weights[j][1]) * slope_ref[:, part]).astype(BF16)
            acc_ref[j, 0] += dot(out_t, pre)
            row_grad = row_grad + dot(pre, weights[j][0], 1, 1)
        slope = (row_grad.astype(BF16).astype(F32) * trunk_slope).astype(BF16)
        acc_trunk_ref[...] += dot(feats_f.T.astype(BF16), slope)
        return carry

    if steps == 1:
        step(0, 0)
    else:
        lax.fori_loop(0, steps, step, 0)
    if last:
        own_ref[...] = acc_ref[0]
        for j in range(1, shares):
            sent_up[j - 1][...] = acc_ref[j, 0].astype(BF16)
            sent_down[j - 1][...] = acc_ref[j, 1].astype(BF16)
        all_losses = list(loss_refs) + [loss_ref]
        if not in_turns(experts):
            kept_ref[...] = acc_trunk_ref[...]
            for row in range(note_ref.shape[0]):
                note_ref[row : row + 1, :] = loss_row(all_losses, row)
            return
        me = me_ref[0]
        part = width // experts
        kept_ref[experts // 2 * part :, :] = jnp.zeros((8, width), F32)
        note_ref[experts // 2 * part :, :] = jnp.zeros((8, width), F32)
        for s in range(experts):
            ref = note_ref if s % 2 else kept_ref
            mine = pl.ds(pl.multiple_of((me ^ s) * part, part), part)
            ref[s // 2 * part : (s // 2 + 1) * part, :] = acc_trunk_ref[mine, :]
            at = experts // 2 * part + s // 2
            ref[at : at + 1, :] = loss_row(all_losses, order.index(s))


def in_turns(experts):
    return experts == 8


def loss_row(refs, row):
    for ref in refs:
        if row < ref.shape[0]:
            return ref[row : row + 1, :]
        row -= ref.shape[0]


def expert_call(xs, trunk_weight, weights, prior, losses, me, order, last):
    experts = len(order)
    block_rows = xs[0].shape[0]
    width = trunk_weight.shape[0]
    shares = len(weights)
    share = weights[0].shape[2]
    rows = block_rows * len(xs)
    step_rows = min(256, rows)
    steps = rows // step_rows
    first = prior is None
    acc = jax.ShapeDtypeStruct((shares, 2, width, share), F32)
    acc_trunk = jax.ShapeDtypeStruct((width, width), F32)
    loss = jax.ShapeDtypeStruct((steps, step_rows), F32)
    args = list(xs) + [trunk_weight] + list(weights)
    if not first:
        args += list(prior)
    in_specs = [whole()] * len(args)
    scratch = [
        pltpu.VMEM((rows, 2 * width), BF16),
        pltpu.VMEM((step_rows, shares * share), BF16),
        pltpu.VMEM((step_rows, shares * share), F32),
    ]
    if last:
        args += list(losses) + [me]
        in_specs += [whole()] * len(losses) + [whole(pltpu.SMEM)]
        outs = [jax.ShapeDtypeStruct((2, width, share), F32)]
        outs += [jax.ShapeDtypeStruct((width, share), BF16)] * (2 * (shares - 1))
        if in_turns(experts):
            outs += [jax.ShapeDtypeStruct((width // 2 + 8, width), F32)] * 2
        else:
            outs += [
                acc_trunk,
                jax.ShapeDtypeStruct((experts * block_rows // step_rows, step_rows), F32),
            ]
        scratch += [pltpu.VMEM(a.shape, a.dtype) for a in (acc, acc_trunk, loss)]
    else:
        outs = [acc, acc_trunk, loss]
    counts = (len(xs), shares, experts, steps, step_rows)
    return pl.pallas_call(
        functools.partial(expert_kernel, counts, order, first, len(losses) + 1 if last else 0),
        out_shape=outs,
        in_specs=in_specs,
        out_specs=[whole()] * len(outs),
        scratch_shapes=scratch,
        compiler_params=pltpu.CompilerParams(vmem_limit_bytes=40 * MIB),
        cost_estimate=pl.CostEstimate(
            flops=12 * rows * width * shares * share,
            bytes_accessed=10 * MIB,
            transcendentals=rows * shares * share,
        ),
        name="expert_rows",
    )(*args)


def turn_one_kernel(part, kept_ref, got_ref, next_ref, note_ref):
    for s in range(4):
        ref, k = (note_ref, s // 2) if s % 2 else (next_ref, s // 2)
        at = slice(s * part, (s + 1) * part)
        ref[k * part : (k + 1) * part, :] = kept_ref[at, :] + got_ref[at, :]
    lost = kept_ref[4 * part :, :]
    found = got_ref[4 * part :, :]
    for ref, first in ((next_ref, 0), (note_ref, 1)):
        ref[2 * part :, :] = jnp.concatenate(
            [
                lost[first : first + 1],
                found[first : first + 1],
                lost[first + 2 : first + 3],
                found[first + 2 : first + 3],
                jnp.zeros((4, lost.shape[1]), F32),
            ],
            axis=0,
        )


def turn_two_kernel(part, kept_ref, got_ref, next_ref, note_ref):
    next_ref[:part, :] = kept_ref[:part, :] + got_ref[:part, :]
    note_ref[:part, :] = kept_ref[part : 2 * part, :] + got_ref[part : 2 * part, :]
    lost = kept_ref[2 * part :, :]
    found = got_ref[2 * part :, :]
    for ref, first in ((next_ref, 0), (note_ref, 2)):
        ref[part:, :] = jnp.concatenate(
            [
                lost[first : first + 2],
                found[first : first + 2],
                jnp.zeros((4, lost.shape[1]), F32),
            ],
            axis=0,
        )


def turn_three_kernel(part, kept_ref, got_ref, sum_ref, loss_ref):
    sum_ref[...] = kept_ref[:part, :] + got_ref[:part, :]
    loss_ref[...] = jnp.concatenate([kept_ref[part : part + 4, :], got_ref[part : part + 4, :]], axis=0)


def turn(kernel, kept, got, part, shapes, name):
    return pl.pallas_call(
        functools.partial(kernel, part),
        out_shape=[jax.ShapeDtypeStruct((rows, kept.shape[1]), F32) for rows in shapes],
        in_specs=[whole()] * 2,
        out_specs=[whole()] * 2,
        compiler_params=pltpu.CompilerParams(vmem_limit_bytes=4 * MIB),
        name=name,
    )(kept, got)


def row_loss_kernel(place_ref, loss_ref, row_loss_ref):
    experts, capacity = loss_ref.shape
    loss = loss_ref[...]
    for g in range(place_ref.shape[0]):
        place = place_ref[g : g + 1, :]
        block = place // capacity
        slot = place - block * capacity
        picks = jnp.where(iota((capacity, LANES), 0) == slot, 1.0, 0.0)
        found = lax.dot_general(
            loss,
            picks,
            (((1,), (0,)), ((), ())),
            precision=lax.Precision.HIGHEST,
            preferred_element_type=F32,
        )
        mine = jnp.where(iota((experts, LANES), 0) == block, found, 0.0)
        row_loss_ref[g : g + 1, :] = jnp.sum(mine, axis=0, keepdims=True)


def loss_by_row(place, loss):
    return pl.pallas_call(
        row_loss_kernel,
        out_shape=jax.ShapeDtypeStruct(place.shape, F32),
        in_specs=[whole()] * 2,
        out_specs=whole(),
        compiler_params=pltpu.CompilerParams(vmem_limit_bytes=16 * MIB),
        name="row_loss",
    )(place, loss)


def assemble_kernel(part, me_ref, *refs):
    *held, trunk_ref = refs
    me = me_ref[0]
    order = iter((0, 4, 2, 6, 1, 5, 3, 7))
    for ref in held:
        for k in range(ref.shape[0] // part):
            at = pl.ds(pl.multiple_of((me ^ next(order)) * part, part), part)
            trunk_ref[at, :] = ref[k * part : (k + 1) * part, :]


def assemble(me, held, part):
    width = held[0].shape[1]
    return pl.pallas_call(
        functools.partial(assemble_kernel, part),
        out_shape=jax.ShapeDtypeStruct((8 * part, width), F32),
        in_specs=[whole(pltpu.SMEM)] + [whole()] * len(held),
        out_specs=whole(),
        compiler_params=pltpu.CompilerParams(vmem_limit_bytes=4 * MIB),
        name="assemble_trunk",
    )(me, *held)


def after(value, *others):
    return pl.pallas_call(
        lambda *refs: None,
        out_shape=jax.ShapeDtypeStruct(value.shape, value.dtype),
        in_specs=[whole(pl.ANY)] * (1 + len(others)),
        out_specs=whole(pl.ANY),
        input_output_aliases={0: 0},
        name="in_order",
    )(value, *others)


def adam_update(params, first, second, grads):
    first_new = beta_one * first + (1.0 - beta_one) * grads
    second_new = beta_two * second + (1.0 - beta_two) * grads * grads
    first_hat = first_new / (1.0 - beta_one**adam_step)
    second_hat = second_new / (1.0 - beta_two**adam_step)
    return (
        params - learn_rate * first_hat / (jnp.sqrt(second_hat) + adam_eps),
        first_new,
        second_new,
    )


def swap(value, axis, s):
    if s == 0:
        return value
    return lax.ppermute(value, axis, [(i, i ^ s) for i in range(lax.axis_size(axis))])


def on_device(
    cell_table,
    sample_index,
    region,
    targets,
    trunk_weight,
    expert_params,
    first_moment,
    second_moment,
):
    rows = sample_index.shape[0]
    width = cell_table.shape[1]
    experts = lax.axis_size("expert")
    replicas = lax.axis_size("dp")
    capacity = 2 * rows // experts
    me = lax.axis_index("expert").astype(jnp.int32).reshape(1)

    rounded = expert_params[0].astype(BF16)
    weights = [swap(rounded, "dp", j) for j in range(replicas)]
    *blocks, place = pack(me, sample_index, region[:, 0], cell_table, targets, experts, capacity)
    arrived = list(blocks)
    if in_turns(experts) and replicas == 4:
        for s in (4, 6):
            arrived[s] = swap(blocks[s], "expert", s)
        for s, ahead in (
            (5, weights[1]),
            (7, weights[2]),
            (2, weights[3]),
            (3, arrived[4]),
            (1, arrived[6]),
        ):
            arrived[s] = swap(after(blocks[s], ahead), "expert", s)
        batches = ((0, 4, 6), (1, 2, 3), (5,), (7,))
    else:
        arrived = [swap(blocks[s], "expert", s) for s in range(experts)]
        batches = (range(experts // 2), range(experts // 2, experts))

    order = [s for batch in batches for s in batch]
    prior, losses = None, []
    for k, batch in enumerate(batches):
        last = k == len(batches) - 1
        outs = expert_call(
            [arrived[s] for s in batch], trunk_weight, weights, prior, losses, me, order, last
        )
        if not last:
            prior = outs[:2]
            losses.append(outs[2])
    grads, sent_up, sent_down = outs[0], outs[1:replicas], outs[replicas : 2 * replicas - 1]
    kept, note = outs[-2:]

    part = width // experts
    downs = [swap(sent_down[j - 1], "dp", j) for j in range(1, replicas)]
    if in_turns(experts):
        kept, note = turn(
            turn_one_kernel, kept, swap(note, "expert", 1), part, (2 * part + 8,) * 2, "turn_one"
        )
        kept, note = turn(
            turn_two_kernel, kept, swap(note, "expert", 2), part, (part + 8,) * 2, "turn_two"
        )
        total, loss = turn(
            turn_three_kernel, kept, swap(note, "expert", 4), part, (part, experts), "turn_three"
        )
        others = [swap(total, "dp", j) for j in range(1, replicas)]
        sent_up = [after(value, *others) for value in sent_up]
        if replicas == 4:
            total = (total + others[0]) + (others[1] + others[2])
        else:
            total = total + sum(others)
        held = [total]
        for s in (4, 2, 1):
            message = held[0] if len(held) == 1 else jnp.concatenate(held, axis=0)
            held.append(swap(message, "expert", s))
        trunk_grad = assemble(me, held, part)
    else:
        trunk_grad = lax.psum(kept, ("dp", "expert"))
        mine = jnp.arange(experts, dtype=jnp.int32) ^ me
        note = note.reshape(experts, capacity)
        loss = lax.all_to_all(note[mine], "expert", split_axis=0, concat_axis=0, tiled=True)[mine]
    row_loss = loss_by_row(place, loss)
    ups = [swap(sent_up[j - 1], "dp", j) for j in range(1, replicas)]

    grads = grads + sum(jnp.stack([u, d]).astype(F32) for u, d in zip(ups, downs))
    new_params, new_first, new_second = adam_update(
        expert_params, first_moment, second_moment, grads[None]
    )
    return (trunk_grad, row_loss.reshape(rows), new_params, new_first, new_second)


def solution(mesh):
    placed = (
        P(("dp", "expert"), None),
        P(("dp", "expert")),
        P(("dp", "expert"), None),
        P(("dp", "expert"), None),
        P(),
        P("expert", None, None, "dp"),
        P("expert", None, None, "dp"),
        P("expert", None, None, "dp"),
    )
    return jax.shard_map(
        on_device,
        mesh=mesh,
        in_specs=placed,
        out_specs=(
            P(),
            P(("dp", "expert")),
            P("expert", None, None, "dp"),
            P("expert", None, None, "dp"),
            P("expert", None, None, "dp"),
        ),
        check_vma=False,
    )
```

```python
import functools

import jax
import jax.numpy as jnp
from jax import lax
from jax.experimental import pallas as pl
from jax.experimental.pallas import tpu as pltpu
from jax.sharding import PartitionSpec as P

loss_scale = 1.0 / 32.0
beta_one = 0.9
beta_two = 0.999
learn_rate = 0.05
adam_eps = 1e-08
adam_step = 10

LANES = 128
F32 = jnp.float32
BF16 = jnp.bfloat16
MIB = 1 << 20


def iota(shape, dim):
    return lax.broadcasted_iota(jnp.int32, shape, dim)


def dot(a, b, ca=1, cb=0):
    return lax.dot_general(a, b, (((ca,), (cb,)), ((), ())), preferred_element_type=F32)


def whole(memory_space=pltpu.VMEM):
    return pl.BlockSpec(memory_space=memory_space)


def pack_kernel(experts, capacity, me_ref, index_ref, region_ref, table_ref, target_ref, *refs):
    blocks, place_ref, rows_ref = refs[:experts], refs[experts], refs[experts + 1]
    me = me_ref[0]
    groups = index_ref.shape[0]
    cells, width = table_ref.shape
    expert_id = iota((experts, LANES), 0)
    starts = ((expert_id ^ me) * capacity).astype(F32)
    ahead = jnp.where(iota((LANES, LANES), 0) <= iota((LANES, LANES), 1), 1.0, 0.0).astype(BF16)
    counted = jnp.zeros((experts, LANES), F32)
    places = []
    for g in range(groups):
        hot = jnp.where(region_ref[g : g + 1, :] == expert_id, 1.0, 0.0)
        upto = dot(hot.astype(BF16), ahead)
        places.append(jnp.sum(hot * (upto - 1.0 + counted + starts), axis=0, keepdims=True))
        counted = counted + jnp.broadcast_to(upto[:, LANES - 1 :], (experts, LANES))
    for g in range(groups):
        place_ref[g : g + 1, :] = places[g].astype(jnp.int32)
    place = jnp.concatenate(places, axis=1)

    step = 2
    cell_id = iota((LANES * step, LANES), 1).astype(F32)
    for g in range(0, groups, step):
        column = jnp.concatenate(
            [
                jnp.broadcast_to(index_ref[h : h + 1, :].astype(F32), (LANES, LANES)).T
                for h in range(g, g + step)
            ],
            axis=0,
        )
        picks = jnp.concatenate(
            [
                jnp.where(column == cell_id + float(LANES * t), 1.0, 0.0).astype(BF16)
                for t in range(cells // LANES)
            ],
            axis=1,
        )
        at = slice(g * LANES, (g + step) * LANES)
        rows_ref[at, :width] = dot(picks, table_ref[...]).astype(BF16)
        rows_ref[at, width:] = target_ref[at, :]

    slot_id = iota((capacity, place.shape[1]), 0).astype(F32)
    for s in range(experts):
        spread = jnp.where(place == slot_id + float(s * capacity), 1.0, 0.0).astype(BF16)
        blocks[s][...] = dot(spread, rows_ref[...]).astype(BF16)


def pack(me, index, region, table, targets, experts, capacity):
    rows, width = targets.shape
    groups = rows // LANES
    return pl.pallas_call(
        functools.partial(pack_kernel, experts, capacity),
        out_shape=[jax.ShapeDtypeStruct((capacity, 2 * width), BF16)] * experts
        + [jax.ShapeDtypeStruct((groups, LANES), jnp.int32)],
        in_specs=[whole(pltpu.SMEM)] + [whole()] * 4,
        out_specs=[whole()] * (experts + 1),
        scratch_shapes=[pltpu.VMEM((rows, 2 * width), BF16)],
        compiler_params=pltpu.CompilerParams(vmem_limit_bytes=32 * MIB),
        cost_estimate=pl.CostEstimate(
            flops=2 * rows * width * (table.shape[0] + 2 * experts * capacity),
            bytes_accessed=6 * MIB,
            transcendentals=0,
        ),
        name="pack_rows",
    )(me, index.reshape(groups, LANES), region.reshape(groups, LANES), table, targets)


def sigmoid(v):
    return 0.5 * jnp.tanh(0.5 * v) + 0.5


def expert_kernel(counts, order, first, last, *refs):
    blocks, shares, experts, steps, step_rows = counts
    refs = list(refs)

    def take(n):
        got = refs[:n]
        del refs[:n]
        return got

    xs = take(blocks)
    (trunk_ref,) = take(1)
    weights = take(shares)
    if not first:
        prior_ref, prior_trunk_ref = take(2)
    if last:
        loss_refs = take(last - 1)
        (me_ref,) = take(1)
        own_ref, next_up_ref, next_down_ref, sent_up_ref, sent_down_ref = take(5)
        kept_ref, note_ref = take(2)
    else:
        acc_ref, acc_trunk_ref, loss_ref = take(3)
    x_ref, hid_ref, slope_ref = take(3)
    if last:
        acc_ref, acc_trunk_ref, loss_ref = take(3)

    width = trunk_ref.shape[0]
    share = weights[0].shape[2]
    block_rows = xs[0].shape[0]
    for i, ref in enumerate(xs):
        x_ref[i * block_rows : (i + 1) * block_rows, :] = ref[...]
    looped = steps > 3
    if looped and first:
        acc_ref[...] = jnp.zeros(acc_ref.shape, F32)
        acc_trunk_ref[...] = jnp.zeros(acc_trunk_ref.shape, F32)
    elif looped:
        acc_ref[...] = prior_ref[...]
        acc_trunk_ref[...] = prior_trunk_ref[...]

    def add(i, ref, source, at, value):
        if looped or i > 0:
            ref[at] += value
        elif first:
            ref[at] = value
        else:
            ref[at] = source[at] + value

    prior = None if first else prior_ref
    prior_trunk = None if first else prior_trunk_ref

    def step(i, carry):
        if looped:
            at = pl.ds(pl.multiple_of(i * step_rows, step_rows), step_rows)
        else:
            at = slice(i * step_rows, (i + 1) * step_rows)
        feats = x_ref[at, :width]
        feats_f = feats.astype(F32)
        trunk_pre = dot(feats, trunk_ref[...])
        gate = sigmoid(trunk_pre)
        act = trunk_pre * gate
        trunk_slope = gate + act * (1.0 - gate)
        out_f = feats_f + act
        out = out_f.astype(BF16)
        predicted = jnp.zeros((step_rows, width), F32)
        for j in range(shares):
            up = dot(out, weights[j][0])
            s = sigmoid(up)
            h = up * s
            slope_ref[:, j * share : (j + 1) * share] = s + h * (1.0 - s)
            h = h.astype(BF16)
            hid_ref[:, j * share : (j + 1) * share] = h
            predicted = predicted + dot(h, weights[j][1], 1, 1)
        errors = predicted - x_ref[at, width:].astype(F32)
        squares = errors * errors
        half = squares[:, :LANES]
        for k in range(1, width // LANES):
            half = half + squares[:, k * LANES : (k + 1) * LANES]
        loss_ref[pl.ds(i, 1), :] = jnp.sum(half.T, axis=0, keepdims=True) * (0.5 * loss_scale)
        scaled_f = errors * loss_scale
        scaled = scaled_f.astype(BF16)
        scaled_t = scaled_f.T.astype(BF16)
        out_t = out_f.T.astype(BF16)
        row_grad = jnp.zeros((step_rows, width), F32)
        for j in range(shares):
            part = slice(j * share, (j + 1) * share)
            add(i, acc_ref, prior, (j, 1), dot(scaled_t, hid_ref[:, part]))
            pre = (dot(scaled, weights[j][1]) * slope_ref[:, part]).astype(BF16)
            add(i, acc_ref, prior, (j, 0), dot(out_t, pre))
            row_grad = row_grad + dot(pre, weights[j][0], 1, 1)
        slope = (row_grad.astype(BF16).astype(F32) * trunk_slope).astype(BF16)
        add(i, acc_trunk_ref, prior_trunk, ..., dot(feats_f.T.astype(BF16), slope))
        return carry

    if looped:
        lax.fori_loop(0, steps, step, 0)
    else:
        for i in range(steps):
            step(i, 0)
    if last:
        own_ref[...] = acc_ref[0]
        next_up_ref[...] = acc_ref[2, 0]
        next_down_ref[...] = acc_ref[1, 1]
        for k, j in enumerate((1, 3)):
            sent_up_ref[k] = acc_ref[j, 0].astype(BF16)
        for k, j in enumerate((2, 3)):
            sent_down_ref[k] = acc_ref[j, 1].astype(BF16)
        all_losses = list(loss_refs) + [loss_ref]
        if not in_turns(experts):
            kept_ref[...] = acc_trunk_ref[...]
            for row in range(note_ref.shape[0]):
                note_ref[row : row + 1, :] = loss_row(all_losses, row)
            return
        me = me_ref[0]
        part = width // experts
        kept_ref[experts // 2 * part :, :] = jnp.zeros((8, width), F32)
        note_ref[experts // 2 * part :, :] = jnp.zeros((8, width), F32)
        for s in range(experts):
            ref = note_ref if s % 2 else kept_ref
            mine = pl.ds(pl.multiple_of((me ^ s) * part, part), part)
            ref[s // 2 * part : (s // 2 + 1) * part, :] = acc_trunk_ref[mine, :]
            at = experts // 2 * part + s // 2
            ref[at : at + 1, :] = loss_row(all_losses, order.index(s))


def in_turns(experts):
    return experts == 8


def loss_row(refs, row):
    for ref in refs:
        if row < ref.shape[0]:
            return ref[row : row + 1, :]
        row -= ref.shape[0]


def expert_call(xs, trunk_weight, weights, prior, losses, me, order, last):
    experts = len(order)
    block_rows = xs[0].shape[0]
    width = trunk_weight.shape[0]
    shares = len(weights)
    share = weights[0].shape[2]
    rows = block_rows * len(xs)
    step_rows = min(256, rows)
    steps = rows // step_rows
    first = prior is None
    acc = jax.ShapeDtypeStruct((shares, 2, width, share), F32)
    acc_trunk = jax.ShapeDtypeStruct((width, width), F32)
    loss = jax.ShapeDtypeStruct((steps, step_rows), F32)
    args = list(xs) + [trunk_weight] + list(weights)
    if not first:
        args += list(prior)
    in_specs = [whole()] * len(args)
    scratch = [
        pltpu.VMEM((rows, 2 * width), BF16),
        pltpu.VMEM((step_rows, shares * share), BF16),
        pltpu.VMEM((step_rows, shares * share), F32),
    ]
    if last:
        args += list(losses) + [me]
        in_specs += [whole()] * len(losses) + [whole(pltpu.SMEM)]
        outs = [jax.ShapeDtypeStruct((2, width, share), F32)]
        outs += [jax.ShapeDtypeStruct((width, share), F32)] * 2
        outs += [jax.ShapeDtypeStruct((2, width, share), BF16)] * 2
        if in_turns(experts):
            outs += [jax.ShapeDtypeStruct((width // 2 + 8, width), F32)] * 2
        else:
            outs += [
                acc_trunk,
                jax.ShapeDtypeStruct((experts * block_rows // step_rows, step_rows), F32),
            ]
        scratch += [pltpu.VMEM(a.shape, a.dtype) for a in (acc, acc_trunk, loss)]
    else:
        outs = [acc, acc_trunk, loss]
    counts = (len(xs), shares, experts, steps, step_rows)
    return pl.pallas_call(
        functools.partial(expert_kernel, counts, order, first, len(losses) + 1 if last else 0),
        out_shape=outs,
        in_specs=in_specs,
        out_specs=[whole()] * len(outs),
        scratch_shapes=scratch,
        compiler_params=pltpu.CompilerParams(vmem_limit_bytes=40 * MIB),
        cost_estimate=pl.CostEstimate(
            flops=12 * rows * width * shares * share,
            bytes_accessed=10 * MIB,
            transcendentals=rows * shares * share,
        ),
        name="expert_rows",
    )(*args)


def turn_one_kernel(part, kept_ref, got_ref, next_ref, note_ref):
    for s in range(4):
        ref, k = (note_ref, s // 2) if s % 2 else (next_ref, s // 2)
        at = slice(s * part, (s + 1) * part)
        ref[k * part : (k + 1) * part, :] = kept_ref[at, :] + got_ref[at, :]
    lost = kept_ref[4 * part :, :]
    found = got_ref[4 * part :, :]
    for ref, first in ((next_ref, 0), (note_ref, 1)):
        ref[2 * part :, :] = jnp.concatenate(
            [
                lost[first : first + 1],
                found[first : first + 1],
                lost[first + 2 : first + 3],
                found[first + 2 : first + 3],
                jnp.zeros((4, lost.shape[1]), F32),
            ],
            axis=0,
        )


def turn_two_kernel(part, kept_ref, got_ref, both_ref):
    both_ref[: 2 * part, :] = kept_ref[: 2 * part, :] + got_ref[: 2 * part, :]
    lost = kept_ref[2 * part :, :]
    found = got_ref[2 * part :, :]
    both_ref[2 * part :, :] = jnp.concatenate(
        [lost[0:2], found[0:2], lost[2:4], found[2:4]], axis=0
    )


def turn_three_kernel(part, both_ref, got_ref, sum_ref, loss_ref):
    sum_ref[:part, :] = both_ref[:part, :] + got_ref[part : 2 * part, :]
    sum_ref[part:, :] = both_ref[part : 2 * part, :] + got_ref[:part, :]
    loss_ref[...] = jnp.concatenate(
        [both_ref[2 * part : 2 * part + 4, :], got_ref[2 * part + 4 :, :]], axis=0
    )


def add_kernel(part, one_ref, other_ref, *refs):
    refs[-1][...] = one_ref[...] + other_ref[...]


def turn(kernel, kept, got, part, shapes, name, ahead=()):
    return pl.pallas_call(
        functools.partial(kernel, part),
        out_shape=[jax.ShapeDtypeStruct((rows, kept.shape[1]), F32) for rows in shapes],
        in_specs=[whole()] * 2 + [whole(pl.ANY)] * len(ahead),
        out_specs=[whole()] * len(shapes),
        compiler_params=pltpu.CompilerParams(vmem_limit_bytes=4 * MIB),
        name=name,
    )(kept, got, *ahead)


def pass_on_kernel(next_up_ref, got_up_ref, next_down_ref, got_down_ref, *refs):
    up_ref, down_ref = refs[-2:]
    up_ref[...] = (next_up_ref[...] + got_up_ref[1].astype(F32)).astype(BF16)
    down_ref[...] = (next_down_ref[...] + got_down_ref[1].astype(F32)).astype(BF16)


def pass_on(next_up, got_up, next_down, got_down, ahead=()):
    up, down = pl.pallas_call(
        pass_on_kernel,
        out_shape=[jax.ShapeDtypeStruct(next_up.shape, BF16)] * 2,
        in_specs=[whole()] * 4 + [whole(pl.ANY)] * len(ahead),
        out_specs=[whole()] * 2,
        compiler_params=pltpu.CompilerParams(vmem_limit_bytes=8 * MIB),
        name="pass_on",
    )(next_up, got_up, next_down, got_down, *ahead)
    return swap(up, "dp", 2), swap(down, "dp", 1)


def row_loss_kernel(place_ref, loss_ref, row_loss_ref):
    experts, capacity = loss_ref.shape
    loss = loss_ref[...]
    for g in range(place_ref.shape[0]):
        place = place_ref[g : g + 1, :]
        block = place // capacity
        slot = place - block * capacity
        picks = jnp.where(iota((capacity, LANES), 0) == slot, 1.0, 0.0)
        found = lax.dot_general(
            loss,
            picks,
            (((1,), (0,)), ((), ())),
            precision=lax.Precision.HIGHEST,
            preferred_element_type=F32,
        )
        mine = jnp.where(iota((experts, LANES), 0) == block, found, 0.0)
        row_loss_ref[g : g + 1, :] = jnp.sum(mine, axis=0, keepdims=True)


def loss_by_row(place, loss):
    return pl.pallas_call(
        row_loss_kernel,
        out_shape=jax.ShapeDtypeStruct(place.shape, F32),
        in_specs=[whole()] * 2,
        out_specs=whole(),
        compiler_params=pltpu.CompilerParams(vmem_limit_bytes=16 * MIB),
        name="row_loss",
    )(place, loss)


def assemble_kernel(part, me_ref, *refs):
    *held, trunk_ref = refs
    me = me_ref[0]
    order = iter((0, 4, 2, 6, 1, 5, 3, 7))
    for ref in held:
        for k in range(ref.shape[0] // part):
            at = pl.ds(pl.multiple_of((me ^ next(order)) * part, part), part)
            trunk_ref[at, :] = ref[k * part : (k + 1) * part, :]


def assemble(me, held, part):
    width = held[0].shape[1]
    return pl.pallas_call(
        functools.partial(assemble_kernel, part),
        out_shape=jax.ShapeDtypeStruct((8 * part, width), F32),
        in_specs=[whole(pltpu.SMEM)] + [whole()] * len(held),
        out_specs=whole(),
        compiler_params=pltpu.CompilerParams(vmem_limit_bytes=4 * MIB),
        name="assemble_trunk",
    )(me, *held)


def adam_update(params, first, second, grads):
    first_new = beta_one * first + (1.0 - beta_one) * grads
    second_new = beta_two * second + (1.0 - beta_two) * grads * grads
    first_hat = first_new / (1.0 - beta_one**adam_step)
    second_hat = second_new / (1.0 - beta_two**adam_step)
    return (
        params - learn_rate * first_hat / (jnp.sqrt(second_hat) + adam_eps),
        first_new,
        second_new,
    )


def swap(value, axis, s):
    if s == 0:
        return value
    return lax.ppermute(value, axis, [(i, i ^ s) for i in range(lax.axis_size(axis))])


def on_device(
    cell_table,
    sample_index,
    region,
    targets,
    trunk_weight,
    expert_params,
    first_moment,
    second_moment,
):
    rows = sample_index.shape[0]
    width = cell_table.shape[1]
    experts = lax.axis_size("expert")
    replicas = lax.axis_size("dp")
    capacity = 2 * rows // experts
    me = lax.axis_index("expert").astype(jnp.int32).reshape(1)

    rounded = expert_params[0].astype(BF16)
    weights = [swap(rounded, "dp", j) for j in range(replicas)]
    *blocks, place = pack(me, sample_index, region[:, 0], cell_table, targets, experts, capacity)
    arrived = [swap(blocks[s], "expert", s) for s in range(experts)]
    if in_turns(experts):
        batches = ((0,), (4, 6), (1, 2, 3), (5,), (7,))
    else:
        batches = (range(experts // 2), range(experts // 2, experts))

    order = [s for batch in batches for s in batch]
    prior, losses = None, []
    for k, batch in enumerate(batches):
        last = k == len(batches) - 1
        outs = expert_call(
            [arrived[s] for s in batch], trunk_weight, weights, prior, losses, me, order, last
        )
        if not last:
            prior = outs[:2]
            losses.append(outs[2])
    own, next_up, next_down, sent_up, sent_down, kept, note = outs

    got_up = swap(sent_up, "dp", 1)
    got_down = swap(sent_down, "dp", 2)
    part = width // experts
    if in_turns(experts):
        kept, note = turn(
            turn_one_kernel, kept, swap(note, "expert", 1), part, (2 * part + 8,) * 2, "turn_one"
        )
        (both,) = turn(
            turn_two_kernel, kept, swap(note, "expert", 2), part, (2 * part + 8,), "turn_two"
        )
        total, loss = turn(
            turn_three_kernel,
            both,
            swap(both, "expert", 4),
            part,
            (2 * part, experts),
            "turn_three",
        )
        more_up, more_down = pass_on(next_up, got_up, next_down, got_down, (total,))
        (total,) = turn(
            add_kernel, total, swap(total, "dp", 1), part, (2 * part,), "turn_four", (got_up, got_down)
        )
        (total,) = turn(
            add_kernel, total, swap(total, "dp", 2), part, (2 * part,), "turn_five", (more_up, more_down)
        )
        other = swap(total, "expert", 2)
        rest = swap(jnp.concatenate([total, other], axis=0), "expert", 1)
        trunk_grad = assemble(me, [total, other, rest], part)
    else:
        more_up, more_down = pass_on(next_up, got_up, next_down, got_down)
        trunk_grad = lax.psum(kept, ("dp", "expert"))
        mine = jnp.arange(experts, dtype=jnp.int32) ^ me
        note = note.reshape(experts, capacity)
        loss = lax.all_to_all(note[mine], "expert", split_axis=0, concat_axis=0, tiled=True)[mine]
    row_loss = loss_by_row(place, loss)

    grads = jnp.stack(
        [
            own[0] + got_up[0].astype(F32) + more_up.astype(F32),
            own[1] + got_down[0].astype(F32) + more_down.astype(F32),
        ]
    )
    new_params, new_first, new_second = adam_update(
        expert_params, first_moment, second_moment, grads[None]
    )
    return (trunk_grad, row_loss.reshape(rows), new_params, new_first, new_second)


def solution(mesh):
    placed = (
        P(("dp", "expert"), None),
        P(("dp", "expert")),
        P(("dp", "expert"), None),
        P(("dp", "expert"), None),
        P(),
        P("expert", None, None, "dp"),
        P("expert", None, None, "dp"),
        P("expert", None, None, "dp"),
    )
    return jax.shard_map(
        on_device,
        mesh=mesh,
        in_specs=placed,
        out_specs=(
            P(),
            P(("dp", "expert")),
            P("expert", None, None, "dp"),
            P("expert", None, None, "dp"),
            P("expert", None, None, "dp"),
        ),
        check_vma=False,
    )
```

```python
import functools

import jax
import jax.numpy as jnp
from jax import lax
from jax.experimental import pallas as pl
from jax.experimental.pallas import tpu as pltpu
from jax.sharding import PartitionSpec as P

loss_scale = 1.0 / 32.0
beta_one = 0.9
beta_two = 0.999
learn_rate = 0.05
adam_eps = 1e-08
adam_step = 10

LANES = 128
F32 = jnp.float32
BF16 = jnp.bfloat16
MIB = 1 << 20


def iota(shape, dim):
    return lax.broadcasted_iota(jnp.int32, shape, dim)


def dot(a, b, ca=1, cb=0):
    return lax.dot_general(a, b, (((ca,), (cb,)), ((), ())), preferred_element_type=F32)


def whole(memory_space=pltpu.VMEM):
    return pl.BlockSpec(memory_space=memory_space)


def pack_kernel(experts, capacity, me_ref, index_ref, region_ref, table_ref, target_ref, *refs):
    blocks, place_ref, rows_ref = refs[:experts], refs[experts], refs[experts + 1]
    me = me_ref[0]
    groups = index_ref.shape[0]
    cells, width = table_ref.shape
    expert_id = iota((experts, LANES), 0)
    starts = ((expert_id ^ me) * capacity).astype(F32)
    ahead = jnp.where(iota((LANES, LANES), 0) <= iota((LANES, LANES), 1), 1.0, 0.0).astype(BF16)
    counted = jnp.zeros((experts, LANES), F32)
    places = []
    for g in range(groups):
        hot = jnp.where(region_ref[g : g + 1, :] == expert_id, 1.0, 0.0)
        upto = dot(hot.astype(BF16), ahead)
        places.append(jnp.sum(hot * (upto - 1.0 + counted + starts), axis=0, keepdims=True))
        counted = counted + jnp.broadcast_to(upto[:, LANES - 1 :], (experts, LANES))
    for g in range(groups):
        place_ref[g : g + 1, :] = places[g].astype(jnp.int32)
    place = jnp.concatenate(places, axis=1)

    step = 2
    cell_id = iota((LANES * step, LANES), 1).astype(F32)
    for g in range(0, groups, step):
        column = jnp.concatenate(
            [
                jnp.broadcast_to(index_ref[h : h + 1, :].astype(F32), (LANES, LANES)).T
                for h in range(g, g + step)
            ],
            axis=0,
        )
        picks = jnp.concatenate(
            [
                jnp.where(column == cell_id + float(LANES * t), 1.0, 0.0).astype(BF16)
                for t in range(cells // LANES)
            ],
            axis=1,
        )
        at = slice(g * LANES, (g + step) * LANES)
        rows_ref[at, :width] = dot(picks, table_ref[...]).astype(BF16)
        rows_ref[at, width:] = target_ref[at, :]

    slot_id = iota((capacity, place.shape[1]), 0).astype(F32)
    for s in range(experts):
        spread = jnp.where(place == slot_id + float(s * capacity), 1.0, 0.0).astype(BF16)
        blocks[s][...] = dot(spread, rows_ref[...]).astype(BF16)


def pack(me, index, region, table, targets, experts, capacity):
    rows, width = targets.shape
    groups = rows // LANES
    return pl.pallas_call(
        functools.partial(pack_kernel, experts, capacity),
        out_shape=[jax.ShapeDtypeStruct((capacity, 2 * width), BF16)] * experts
        + [jax.ShapeDtypeStruct((groups, LANES), jnp.int32)],
        in_specs=[whole(pltpu.SMEM)] + [whole()] * 4,
        out_specs=[whole()] * (experts + 1),
        scratch_shapes=[pltpu.VMEM((rows, 2 * width), BF16)],
        compiler_params=pltpu.CompilerParams(vmem_limit_bytes=32 * MIB),
        cost_estimate=pl.CostEstimate(
            flops=2 * rows * width * (table.shape[0] + 2 * experts * capacity),
            bytes_accessed=6 * MIB,
            transcendentals=0,
        ),
        name="pack_rows",
    )(me, index.reshape(groups, LANES), region.reshape(groups, LANES), table, targets)


def pair_kernel(one_ref, other_ref, ahead_ref, both_ref):
    both_ref[0] = one_ref[...]
    both_ref[1] = other_ref[...]


def pair(one, other, ahead):
    return pl.pallas_call(
        pair_kernel,
        out_shape=jax.ShapeDtypeStruct((2, *one.shape), one.dtype),
        in_specs=[whole()] * 2 + [whole(pl.ANY)],
        out_specs=whole(),
        compiler_params=pltpu.CompilerParams(vmem_limit_bytes=4 * MIB),
        name="pair",
    )(one, other, ahead)


def sigmoid(v):
    return 0.5 * jnp.tanh(0.5 * v) + 0.5


def expert_kernel(counts, order, first, last, *refs):
    blocks, shares, experts, steps, step_rows = counts
    refs = list(refs)

    def take(n):
        got = refs[:n]
        del refs[:n]
        return got

    xs = take(blocks)
    trunk_ref, ups_near, ups_far, downs_near, downs_far = take(5)
    ups = (ups_near.at[0], ups_near.at[1], ups_far.at[0], ups_far.at[1])
    downs = (downs_near.at[0], downs_far.at[0], downs_near.at[1], downs_far.at[1])
    if not first:
        prior_ref, prior_trunk_ref = take(2)
    if last:
        loss_refs = take(last - 1)
        (me_ref,) = take(1)
        own_ref, next_up_ref, next_down_ref, sent_up_ref, sent_down_ref = take(5)
        kept_ref, note_ref = take(2)
    else:
        acc_ref, acc_trunk_ref, loss_ref = take(3)
    x_ref, hid_ref, slope_ref = take(3)
    if last:
        acc_ref, acc_trunk_ref, loss_ref = take(3)

    width = trunk_ref.shape[0]
    share = ups_near.shape[2]
    block_rows = xs[0].shape[0]
    for i, ref in enumerate(xs):
        x_ref[i * block_rows : (i + 1) * block_rows, :] = ref[...]
    looped = steps > 3
    if looped and first:
        acc_ref[...] = jnp.zeros(acc_ref.shape, F32)
        acc_trunk_ref[...] = jnp.zeros(acc_trunk_ref.shape, F32)
    elif looped:
        acc_ref[...] = prior_ref[...]
        acc_trunk_ref[...] = prior_trunk_ref[...]

    def add(i, ref, source, at, value):
        if looped or i > 0:
            ref[at] += value
        elif first:
            ref[at] = value
        else:
            ref[at] = source[at] + value

    prior = None if first else prior_ref
    prior_trunk = None if first else prior_trunk_ref

    def step(i, carry):
        if looped:
            at = pl.ds(pl.multiple_of(i * step_rows, step_rows), step_rows)
        else:
            at = slice(i * step_rows, (i + 1) * step_rows)
        feats = x_ref[at, :width]
        feats_f = feats.astype(F32)
        trunk_pre = dot(feats, trunk_ref[...])
        gate = sigmoid(trunk_pre)
        act = trunk_pre * gate
        trunk_slope = gate + act * (1.0 - gate)
        out_f = feats_f + act
        out = out_f.astype(BF16)
        predicted = jnp.zeros((step_rows, width), F32)
        for j in range(shares):
            up = dot(out, ups[j][...])
            s = sigmoid(up)
            h = up * s
            slope_ref[:, j * share : (j + 1) * share] = s + h * (1.0 - s)
            h = h.astype(BF16)
            hid_ref[:, j * share : (j + 1) * share] = h
            predicted = predicted + dot(h, downs[j][...], 1, 1)
        errors = predicted - x_ref[at, width:].astype(F32)
        squares = errors * errors
        half = squares[:, :LANES]
        for k in range(1, width // LANES):
            half = half + squares[:, k * LANES : (k + 1) * LANES]
        loss_ref[pl.ds(i, 1), :] = jnp.sum(half.T, axis=0, keepdims=True) * (0.5 * loss_scale)
        scaled_f = errors * loss_scale
        scaled = scaled_f.astype(BF16)
        scaled_t = scaled_f.T.astype(BF16)
        out_t = out_f.T.astype(BF16)
        row_grad = jnp.zeros((step_rows, width), F32)
        for j in range(shares):
            part = slice(j * share, (j + 1) * share)
            add(i, acc_ref, prior, (j, 1), dot(scaled_t, hid_ref[:, part]))
            pre = (dot(scaled, downs[j][...]) * slope_ref[:, part]).astype(BF16)
            add(i, acc_ref, prior, (j, 0), dot(out_t, pre))
            row_grad = row_grad + dot(pre, ups[j][...], 1, 1)
        slope = (row_grad.astype(BF16).astype(F32) * trunk_slope).astype(BF16)
        add(i, acc_trunk_ref, prior_trunk, ..., dot(feats_f.T.astype(BF16), slope))
        return carry

    if looped:
        lax.fori_loop(0, steps, step, 0)
    else:
        for i in range(steps):
            step(i, 0)
    if last:
        own_ref[...] = acc_ref[0]
        next_up_ref[...] = acc_ref[2, 0]
        next_down_ref[...] = acc_ref[1, 1]
        for k, j in enumerate((1, 3)):
            sent_up_ref[k] = acc_ref[j, 0].astype(BF16)
        for k, j in enumerate((2, 3)):
            sent_down_ref[k] = acc_ref[j, 1].astype(BF16)
        all_losses = list(loss_refs) + [loss_ref]
        if not in_turns(experts):
            kept_ref[...] = acc_trunk_ref[...]
            for row in range(note_ref.shape[0]):
                note_ref[row : row + 1, :] = loss_row(all_losses, row)
            return
        me = me_ref[0]
        part = width // experts
        kept_ref[experts // 2 * part :, :] = jnp.zeros((8, width), F32)
        note_ref[experts // 2 * part :, :] = jnp.zeros((8, width), F32)
        for s in range(experts):
            ref = note_ref if s % 2 else kept_ref
            mine = pl.ds(pl.multiple_of((me ^ s) * part, part), part)
            ref[s // 2 * part : (s // 2 + 1) * part, :] = acc_trunk_ref[mine, :]
            at = experts // 2 * part + s // 2
            ref[at : at + 1, :] = loss_row(all_losses, order.index(s))


def in_turns(experts):
    return experts == 8


def loss_row(refs, row):
    for ref in refs:
        if row < ref.shape[0]:
            return ref[row : row + 1, :]
        row -= ref.shape[0]


def expert_call(xs, trunk_weight, weights, prior, losses, me, order, last):
    experts = len(order)
    block_rows = xs[0].shape[0]
    width = trunk_weight.shape[0]
    shares, share = len(weights), weights[0].shape[2]
    rows = block_rows * len(xs)
    step_rows = min(256, rows)
    steps = rows // step_rows
    first = prior is None
    acc = jax.ShapeDtypeStruct((shares, 2, width, share), F32)
    acc_trunk = jax.ShapeDtypeStruct((width, width), F32)
    loss = jax.ShapeDtypeStruct((steps, step_rows), F32)
    args = list(xs) + [trunk_weight, *weights]
    if not first:
        args += list(prior)
    in_specs = [whole()] * len(args)
    scratch = [
        pltpu.VMEM((rows, 2 * width), BF16),
        pltpu.VMEM((step_rows, shares * share), BF16),
        pltpu.VMEM((step_rows, shares * share), F32),
    ]
    if last:
        args += list(losses) + [me]
        in_specs += [whole()] * len(losses) + [whole(pltpu.SMEM)]
        outs = [jax.ShapeDtypeStruct((2, width, share), F32)]
        outs += [jax.ShapeDtypeStruct((width, share), F32)] * 2
        outs += [jax.ShapeDtypeStruct((2, width, share), BF16)] * 2
        if in_turns(experts):
            outs += [jax.ShapeDtypeStruct((width // 2 + 8, width), F32)] * 2
        else:
            outs += [
                acc_trunk,
                jax.ShapeDtypeStruct((experts * block_rows // step_rows, step_rows), F32),
            ]
        scratch += [pltpu.VMEM(a.shape, a.dtype) for a in (acc, acc_trunk, loss)]
    else:
        outs = [acc, acc_trunk, loss]
    counts = (len(xs), shares, experts, steps, step_rows)
    return pl.pallas_call(
        functools.partial(expert_kernel, counts, order, first, len(losses) + 1 if last else 0),
        out_shape=outs,
        in_specs=in_specs,
        out_specs=[whole()] * len(outs),
        scratch_shapes=scratch,
        compiler_params=pltpu.CompilerParams(vmem_limit_bytes=40 * MIB),
        cost_estimate=pl.CostEstimate(
            flops=12 * rows * width * shares * share,
            bytes_accessed=10 * MIB,
            transcendentals=rows * shares * share,
        ),
        name="expert_rows",
    )(*args)


def turn_one_kernel(part, kept_ref, got_ref, *outs):
    lost = kept_ref[4 * part :, :]
    found = got_ref[4 * part :, :]
    for k, ref in enumerate(outs):
        at = slice(k * part, (k + 1) * part)
        ref[:part, :] = kept_ref[at, :] + got_ref[at, :]
        ref[part:, :] = jnp.concatenate(
            [lost[k : k + 1], found[k : k + 1], jnp.zeros((6, lost.shape[1]), F32)], axis=0
        )


def turn_two_kernel(part, *refs):
    *notes, sum_ref, loss_ref = refs
    held = [ref[:part, :] for ref in notes]
    sum_ref[...] = (held[0] + held[1]) + (held[2] + held[3])
    loss_ref[...] = jnp.concatenate([ref[part : part + 2, :] for ref in notes], axis=0)


def turn_three_kernel(part, *refs):
    held = [ref[...] for ref in refs[:4]]
    refs[-1][...] = (held[0] + held[1]) + (held[2] + held[3])


def turn(kernel, held, part, shapes, name, ahead=()):
    return pl.pallas_call(
        functools.partial(kernel, part),
        out_shape=[jax.ShapeDtypeStruct((rows, held[0].shape[1]), F32) for rows in shapes],
        in_specs=[whole()] * len(held) + [whole(pl.ANY)] * len(ahead),
        out_specs=[whole()] * len(shapes),
        compiler_params=pltpu.CompilerParams(vmem_limit_bytes=4 * MIB),
        name=name,
    )(*held, *ahead)


def pass_on_kernel(next_up_ref, got_up_ref, next_down_ref, got_down_ref, *refs):
    up_ref, down_ref = refs[-2:]
    up_ref[...] = (next_up_ref[...] + got_up_ref[1].astype(F32)).astype(BF16)
    down_ref[...] = (next_down_ref[...] + got_down_ref[1].astype(F32)).astype(BF16)


def pass_on(next_up, got_up, next_down, got_down, ahead=()):
    up, down = pl.pallas_call(
        pass_on_kernel,
        out_shape=[jax.ShapeDtypeStruct(next_up.shape, BF16)] * 2,
        in_specs=[whole()] * 4 + [whole(pl.ANY)] * len(ahead),
        out_specs=[whole()] * 2,
        compiler_params=pltpu.CompilerParams(vmem_limit_bytes=8 * MIB),
        name="pass_on",
    )(next_up, got_up, next_down, got_down, *ahead)
    return swap(up, "dp", 2), swap(down, "dp", 1)


def row_loss_kernel(place_ref, loss_ref, row_loss_ref):
    experts, capacity = loss_ref.shape
    loss = loss_ref[...]
    for g in range(place_ref.shape[0]):
        place = place_ref[g : g + 1, :]
        block = place // capacity
        slot = place - block * capacity
        picks = jnp.where(iota((capacity, LANES), 0) == slot, 1.0, 0.0)
        found = lax.dot_general(
            loss,
            picks,
            (((1,), (0,)), ((), ())),
            precision=lax.Precision.HIGHEST,
            preferred_element_type=F32,
        )
        mine = jnp.where(iota((experts, LANES), 0) == block, found, 0.0)
        row_loss_ref[g : g + 1, :] = jnp.sum(mine, axis=0, keepdims=True)


def loss_by_row(place, loss):
    return pl.pallas_call(
        row_loss_kernel,
        out_shape=jax.ShapeDtypeStruct(place.shape, F32),
        in_specs=[whole()] * 2,
        out_specs=whole(),
        compiler_params=pltpu.CompilerParams(vmem_limit_bytes=16 * MIB),
        name="row_loss",
    )(place, loss)


def assemble_kernel(part, me_ref, *refs):
    *held, trunk_ref = refs
    me = me_ref[0]
    order = iter(range(8))
    for ref in held:
        for k in range(ref.shape[0] // part):
            at = pl.ds(pl.multiple_of((me ^ next(order)) * part, part), part)
            trunk_ref[at, :] = ref[k * part : (k + 1) * part, :]


def assemble(me, held, part):
    width = held[0].shape[1]
    return pl.pallas_call(
        functools.partial(assemble_kernel, part),
        out_shape=jax.ShapeDtypeStruct((8 * part, width), F32),
        in_specs=[whole(pltpu.SMEM)] + [whole()] * len(held),
        out_specs=whole(),
        compiler_params=pltpu.CompilerParams(vmem_limit_bytes=4 * MIB),
        name="assemble_trunk",
    )(me, *held)


def adam_update(params, first, second, grads):
    first_new = beta_one * first + (1.0 - beta_one) * grads
    second_new = beta_two * second + (1.0 - beta_two) * grads * grads
    first_hat = first_new / (1.0 - beta_one**adam_step)
    second_hat = second_new / (1.0 - beta_two**adam_step)
    return (
        params - learn_rate * first_hat / (jnp.sqrt(second_hat) + adam_eps),
        first_new,
        second_new,
    )


def swap(value, axis, s):
    if s == 0:
        return value
    return lax.ppermute(value, axis, [(i, i ^ s) for i in range(lax.axis_size(axis))])


def on_device(
    cell_table,
    sample_index,
    region,
    targets,
    trunk_weight,
    expert_params,
    first_moment,
    second_moment,
):
    rows = sample_index.shape[0]
    width = cell_table.shape[1]
    experts = lax.axis_size("expert")
    replicas = lax.axis_size("dp")
    capacity = 2 * rows // experts
    me = lax.axis_index("expert").astype(jnp.int32).reshape(1)

    up, down = expert_params[0, 0].astype(BF16), expert_params[0, 1].astype(BF16)
    near_up, near_down = swap(up, "dp", 1), swap(down, "dp", 2)
    *blocks, place = pack(me, sample_index, region[:, 0], cell_table, targets, experts, capacity)
    ups, downs = pair(up, near_up, place), pair(down, near_down, place)
    weights = [ups, swap(ups, "dp", 2), downs, swap(downs, "dp", 1)]
    arrived = [swap(blocks[s], "expert", s) for s in range(experts)]
    if in_turns(experts):
        batches = ((0,), (4, 5), (2, 3, 1), (6,), (7,))
    else:
        batches = (range(experts // 2), range(experts // 2, experts))

    order = [s for batch in batches for s in batch]
    prior, losses = None, []
    for k, batch in enumerate(batches):
        last = k == len(batches) - 1
        outs = expert_call(
            [arrived[s] for s in batch], trunk_weight, weights, prior, losses, me, order, last
        )
        if not last:
            prior = outs[:2]
            losses.append(outs[2])
    own, next_up, next_down, sent_up, sent_down, kept, note = outs

    got_up = swap(sent_up, "dp", 1)
    got_down = swap(sent_down, "dp", 2)
    part = width // experts
    if in_turns(experts):
        ours, *notes = turn(
            turn_one_kernel, [kept, swap(note, "expert", 1)], part, (part + 8,) * 4, "turn_one"
        )
        notes = [swap(note, "expert", s) for note, s in zip(notes, (2, 4, 6))]
        total, loss = turn(turn_two_kernel, [ours] + notes, part, (part, experts), "turn_two")
        (total,) = turn(
            turn_three_kernel,
            [total] + [swap(total, "dp", j) for j in range(1, replicas)],
            part,
            (part,),
            "turn_three",
            (got_up, got_down),
        )
        more_up, more_down = pass_on(next_up, got_up, next_down, got_down, (total,))
        chip = jnp.concatenate([total, swap(total, "expert", 1)], axis=0)
        trunk_grad = assemble(me, [chip] + [swap(chip, "expert", s) for s in (2, 4, 6)], part)
    else:
        more_up, more_down = pass_on(next_up, got_up, next_down, got_down)
        trunk_grad = lax.psum(kept, ("dp", "expert"))
        places = jnp.arange(experts, dtype=jnp.int32) ^ me
        note = note.reshape(experts, capacity)[places]
        loss = lax.all_to_all(note, "expert", split_axis=0, concat_axis=0, tiled=True)[places]
    row_loss = loss_by_row(place, loss)

    grads = jnp.stack(
        [
            own[0] + got_up[0].astype(F32) + more_up.astype(F32),
            own[1] + got_down[0].astype(F32) + more_down.astype(F32),
        ]
    )
    new_params, new_first, new_second = adam_update(
        expert_params, first_moment, second_moment, grads[None]
    )
    return (trunk_grad, row_loss.reshape(rows), new_params, new_first, new_second)


def solution(mesh):
    placed = (
        P(("dp", "expert"), None),
        P(("dp", "expert")),
        P(("dp", "expert"), None),
        P(("dp", "expert"), None),
        P(),
        P("expert", None, None, "dp"),
        P("expert", None, None, "dp"),
        P("expert", None, None, "dp"),
    )
    return jax.shard_map(
        on_device,
        mesh=mesh,
        in_specs=placed,
        out_specs=(
            P(),
            P(("dp", "expert")),
            P("expert", None, None, "dp"),
            P("expert", None, None, "dp"),
            P("expert", None, None, "dp"),
        ),
        check_vma=False,
    )
```

```python
import functools

import jax
import jax.numpy as jnp
from jax import lax
from jax.experimental import pallas as pl
from jax.experimental.pallas import tpu as pltpu
from jax.sharding import PartitionSpec as P

loss_scale = 1.0 / 32.0
beta_one = 0.9
beta_two = 0.999
learn_rate = 0.05
adam_eps = 1e-08
adam_step = 10

LANES = 128
F32 = jnp.float32
BF16 = jnp.bfloat16
MIB = 1 << 20


def iota(shape, dim):
    return lax.broadcasted_iota(jnp.int32, shape, dim)


def dot(a, b, ca=1, cb=0):
    return lax.dot_general(a, b, (((ca,), (cb,)), ((), ())), preferred_element_type=F32)


def whole(memory_space=pltpu.VMEM):
    return pl.BlockSpec(memory_space=memory_space)


def pack_kernel(experts, capacity, me_ref, index_ref, region_ref, table_ref, target_ref, *refs):
    blocks, place_ref, rows_ref = refs[:experts], refs[experts], refs[experts + 1]
    me = me_ref[0]
    groups = index_ref.shape[0]
    cells, width = table_ref.shape
    expert_id = iota((experts, LANES), 0)
    starts = ((expert_id ^ me) * capacity).astype(F32)
    ahead = jnp.where(iota((LANES, LANES), 0) <= iota((LANES, LANES), 1), 1.0, 0.0).astype(BF16)
    counted = jnp.zeros((experts, LANES), F32)
    places = []
    for g in range(groups):
        hot = jnp.where(region_ref[g : g + 1, :] == expert_id, 1.0, 0.0)
        upto = dot(hot.astype(BF16), ahead)
        places.append(jnp.sum(hot * (upto - 1.0 + counted + starts), axis=0, keepdims=True))
        counted = counted + jnp.broadcast_to(upto[:, LANES - 1 :], (experts, LANES))
    for g in range(groups):
        place_ref[g : g + 1, :] = places[g].astype(jnp.int32)
    place = jnp.concatenate(places, axis=1)

    step = 2
    cell_id = iota((LANES * step, LANES), 1).astype(F32)
    for g in range(0, groups, step):
        column = jnp.concatenate(
            [
                jnp.broadcast_to(index_ref[h : h + 1, :].astype(F32), (LANES, LANES)).T
                for h in range(g, g + step)
            ],
            axis=0,
        )
        picks = jnp.concatenate(
            [
                jnp.where(column == cell_id + float(LANES * t), 1.0, 0.0).astype(BF16)
                for t in range(cells // LANES)
            ],
            axis=1,
        )
        at = slice(g * LANES, (g + step) * LANES)
        rows_ref[at, :width] = dot(picks, table_ref[...]).astype(BF16)
        rows_ref[at, width:] = target_ref[at, :]

    slot_id = iota((capacity, place.shape[1]), 0).astype(F32)
    for s in range(experts):
        spread = jnp.where(place == slot_id + float(s * capacity), 1.0, 0.0).astype(BF16)
        blocks[s][...] = dot(spread, rows_ref[...]).astype(BF16)


def pack(me, index, region, table, targets, experts, capacity):
    rows, width = targets.shape
    groups = rows // LANES
    return pl.pallas_call(
        functools.partial(pack_kernel, experts, capacity),
        out_shape=[jax.ShapeDtypeStruct((capacity, 2 * width), BF16)] * experts
        + [jax.ShapeDtypeStruct((groups, LANES), jnp.int32)],
        in_specs=[whole(pltpu.SMEM)] + [whole()] * 4,
        out_specs=[whole()] * (experts + 1),
        scratch_shapes=[pltpu.VMEM((rows, 2 * width), BF16)],
        compiler_params=pltpu.CompilerParams(vmem_limit_bytes=32 * MIB),
        cost_estimate=pl.CostEstimate(
            flops=2 * rows * width * (table.shape[0] + 2 * experts * capacity),
            bytes_accessed=6 * MIB,
            transcendentals=0,
        ),
        name="pack_rows",
    )(me, index.reshape(groups, LANES), region.reshape(groups, LANES), table, targets)


def pair_kernel(one_ref, other_ref, ahead_ref, both_ref):
    both_ref[0] = one_ref[...]
    both_ref[1] = other_ref[...]


def pair(one, other, ahead):
    return pl.pallas_call(
        pair_kernel,
        out_shape=jax.ShapeDtypeStruct((2, *one.shape), one.dtype),
        in_specs=[whole()] * 2 + [whole(pl.ANY)],
        out_specs=whole(),
        compiler_params=pltpu.CompilerParams(vmem_limit_bytes=4 * MIB),
        name="pair",
    )(one, other, ahead)


def sigmoid(v):
    return 0.5 * jnp.tanh(0.5 * v) + 0.5


def expert_kernel(counts, order, first, last, *refs):
    blocks, shares, experts, steps, step_rows, relays = counts
    refs = list(refs)

    def take(n):
        got = refs[:n]
        del refs[:n]
        return got

    xs = take(blocks)
    trunk_ref, ups_near, ups_far, downs_near, downs_far = take(5)
    ups = (ups_near.at[0], ups_near.at[1], ups_far.at[0], ups_far.at[1])
    downs = (downs_near.at[0], downs_far.at[0], downs_near.at[1], downs_far.at[1])
    if not first:
        prior_ref, prior_trunk_ref = take(2)
    held = take(relays)
    if last:
        loss_refs = take(last - 1)
        (me_ref,) = take(1)
        own_ref, next_up_ref, next_down_ref, sent_up_ref, sent_down_ref = take(5)
        kept_ref, note_ref = take(2)
    else:
        acc_ref, acc_trunk_ref, loss_ref = take(3)
        for source, copy in zip(held, take(relays)):
            copy[...] = source[...]
    x_ref, hid_ref, slope_ref = take(3)
    if last:
        acc_ref, acc_trunk_ref, loss_ref = take(3)

    width = trunk_ref.shape[0]
    share = ups_near.shape[2]
    block_rows = xs[0].shape[0]
    for i, ref in enumerate(xs):
        x_ref[i * block_rows : (i + 1) * block_rows, :] = ref[...]
    looped = steps > 3
    if looped and first:
        acc_ref[...] = jnp.zeros(acc_ref.shape, F32)
        acc_trunk_ref[...] = jnp.zeros(acc_trunk_ref.shape, F32)
    elif looped:
        acc_ref[...] = prior_ref[...]
        acc_trunk_ref[...] = prior_trunk_ref[...]

    def add(i, ref, source, at, value):
        if looped or i > 0:
            ref[at] += value
        elif first:
            ref[at] = value
        else:
            ref[at] = source[at] + value

    prior = None if first else prior_ref
    prior_trunk = None if first else prior_trunk_ref

    def step(i, carry):
        if looped:
            at = pl.ds(pl.multiple_of(i * step_rows, step_rows), step_rows)
        else:
            at = slice(i * step_rows, (i + 1) * step_rows)
        feats = x_ref[at, :width]
        feats_f = feats.astype(F32)
        trunk_pre = dot(feats, trunk_ref[...])
        gate = sigmoid(trunk_pre)
        act = trunk_pre * gate
        trunk_slope = gate + act * (1.0 - gate)
        out_f = feats_f + act
        out = out_f.astype(BF16)
        predicted = jnp.zeros((step_rows, width), F32)
        for j in range(shares):
            up = dot(out, ups[j][...])
            s = sigmoid(up)
            h = up * s
            slope_ref[:, j * share : (j + 1) * share] = s + h * (1.0 - s)
            h = h.astype(BF16)
            hid_ref[:, j * share : (j + 1) * share] = h
            predicted = predicted + dot(h, downs[j][...], 1, 1)
        errors = predicted - x_ref[at, width:].astype(F32)
        squares = errors * errors
        half = squares[:, :LANES]
        for k in range(1, width // LANES):
            half = half + squares[:, k * LANES : (k + 1) * LANES]
        loss_ref[pl.ds(i, 1), :] = jnp.sum(half.T, axis=0, keepdims=True) * (0.5 * loss_scale)
        scaled_f = errors * loss_scale
        scaled = scaled_f.astype(BF16)
        scaled_t = scaled_f.T.astype(BF16)
        out_t = out_f.T.astype(BF16)
        row_grad = jnp.zeros((step_rows, width), F32)
        for j in range(shares):
            part = slice(j * share, (j + 1) * share)
            add(i, acc_ref, prior, (j, 1), dot(scaled_t, hid_ref[:, part]))
            pre = (dot(scaled, downs[j][...]) * slope_ref[:, part]).astype(BF16)
            add(i, acc_ref, prior, (j, 0), dot(out_t, pre))
            row_grad = row_grad + dot(pre, ups[j][...], 1, 1)
        slope = (row_grad.astype(BF16).astype(F32) * trunk_slope).astype(BF16)
        add(i, acc_trunk_ref, prior_trunk, ..., dot(feats_f.T.astype(BF16), slope))
        return carry

    if looped:
        lax.fori_loop(0, steps, step, 0)
    else:
        for i in range(steps):
            step(i, 0)
    if last:
        own_ref[...] = acc_ref[0]
        next_up_ref[...] = acc_ref[2, 0]
        next_down_ref[...] = acc_ref[1, 1]
        for k, j in enumerate((1, 3)):
            sent_up_ref[k] = acc_ref[j, 0].astype(BF16)
        for k, j in enumerate((2, 3)):
            sent_down_ref[k] = acc_ref[j, 1].astype(BF16)
        all_losses = list(loss_refs) + [loss_ref]
        if not in_turns(experts):
            kept_ref[...] = acc_trunk_ref[...]
            for row in range(note_ref.shape[0]):
                note_ref[row : row + 1, :] = loss_row(all_losses, row)
            return
        me = me_ref[0]
        part = width // experts
        kept_ref[experts // 2 * part :, :] = jnp.zeros((8, width), F32)
        note_ref[experts // 2 * part :, :] = jnp.zeros((8, width), F32)
        for s in range(experts):
            ref = note_ref if s % 2 else kept_ref
            mine = pl.ds(pl.multiple_of((me ^ s) * part, part), part)
            ref[s // 2 * part : (s // 2 + 1) * part, :] = acc_trunk_ref[mine, :]
            at = experts // 2 * part + s // 2
            ref[at : at + 1, :] = loss_row(all_losses, order.index(s))


def in_turns(experts):
    return experts == 8


def loss_row(refs, row):
    for ref in refs:
        if row < ref.shape[0]:
            return ref[row : row + 1, :]
        row -= ref.shape[0]


def expert_call(xs, trunk_weight, weights, prior, losses, me, order, last, relays=()):
    experts = len(order)
    block_rows = xs[0].shape[0]
    width = trunk_weight.shape[0]
    shares, share = len(weights), weights[0].shape[2]
    rows = block_rows * len(xs)
    step_rows = min(256, rows)
    steps = rows // step_rows
    first = prior is None
    acc = jax.ShapeDtypeStruct((shares, 2, width, share), F32)
    acc_trunk = jax.ShapeDtypeStruct((width, width), F32)
    loss = jax.ShapeDtypeStruct((steps, step_rows), F32)
    args = list(xs) + [trunk_weight, *weights]
    if not first:
        args += list(prior)
    args += relays
    in_specs = [whole()] * len(args)
    scratch = [
        pltpu.VMEM((rows, 2 * width), BF16),
        pltpu.VMEM((step_rows, shares * share), BF16),
        pltpu.VMEM((step_rows, shares * share), F32),
    ]
    if last:
        args += list(losses) + [me]
        in_specs += [whole()] * len(losses) + [whole(pltpu.SMEM)]
        outs = [jax.ShapeDtypeStruct((2, width, share), F32)]
        outs += [jax.ShapeDtypeStruct((width, share), F32)] * 2
        outs += [jax.ShapeDtypeStruct((2, width, share), BF16)] * 2
        if in_turns(experts):
            outs += [jax.ShapeDtypeStruct((width // 2 + 8, width), F32)] * 2
        else:
            outs += [
                acc_trunk,
                jax.ShapeDtypeStruct((experts * block_rows // step_rows, step_rows), F32),
            ]
        scratch += [pltpu.VMEM(a.shape, a.dtype) for a in (acc, acc_trunk, loss)]
    else:
        outs = [acc, acc_trunk, loss]
        outs += [jax.ShapeDtypeStruct(relay.shape, relay.dtype) for relay in relays]
    counts = (len(xs), shares, experts, steps, step_rows, len(relays))
    return pl.pallas_call(
        functools.partial(expert_kernel, counts, order, first, len(losses) + 1 if last else 0),
        out_shape=outs,
        in_specs=in_specs,
        out_specs=[whole()] * len(outs),
        scratch_shapes=scratch,
        compiler_params=pltpu.CompilerParams(vmem_limit_bytes=40 * MIB),
        cost_estimate=pl.CostEstimate(
            flops=12 * rows * width * shares * share,
            bytes_accessed=10 * MIB,
            transcendentals=rows * shares * share,
        ),
        name="expert_rows",
    )(*args)


def turn_one_kernel(part, kept_ref, got_ref, *outs):
    lost = kept_ref[4 * part :, :]
    found = got_ref[4 * part :, :]
    for k, ref in enumerate(outs):
        at = slice(k * part, (k + 1) * part)
        ref[:part, :] = kept_ref[at, :] + got_ref[at, :]
        ref[part:, :] = jnp.concatenate(
            [lost[k : k + 1], found[k : k + 1], jnp.zeros((6, lost.shape[1]), F32)], axis=0
        )


def turn_two_kernel(part, *refs):
    *notes, sum_ref, loss_ref = refs
    held = [ref[:part, :] for ref in notes]
    sum_ref[...] = (held[0] + held[1]) + (held[2] + held[3])
    loss_ref[...] = jnp.concatenate([ref[part : part + 2, :] for ref in notes], axis=0)


def turn_three_kernel(part, *refs):
    held = [ref[...] for ref in refs[:4]]
    refs[-1][...] = (held[0] + held[1]) + (held[2] + held[3])


def turn_four_kernel(part, *refs):
    for k in range(4):
        refs[-1][k * part : (k + 1) * part, :] = refs[k][...]


def turn(kernel, held, part, shapes, name, ahead=()):
    return pl.pallas_call(
        functools.partial(kernel, part),
        out_shape=[jax.ShapeDtypeStruct((rows, held[0].shape[1]), F32) for rows in shapes],
        in_specs=[whole()] * len(held) + [whole(pl.ANY)] * len(ahead),
        out_specs=[whole()] * len(shapes),
        compiler_params=pltpu.CompilerParams(vmem_limit_bytes=4 * MIB),
        name=name,
    )(*held, *ahead)


def pass_on_kernel(next_up_ref, got_up_ref, next_down_ref, got_down_ref, *refs):
    up_ref, down_ref = refs[-2:]
    up_ref[...] = (next_up_ref[...] + got_up_ref[1].astype(F32)).astype(BF16)
    down_ref[...] = (next_down_ref[...] + got_down_ref[1].astype(F32)).astype(BF16)


def pass_on(next_up, got_up, next_down, got_down, ahead=()):
    up, down = pl.pallas_call(
        pass_on_kernel,
        out_shape=[jax.ShapeDtypeStruct(next_up.shape, BF16)] * 2,
        in_specs=[whole()] * 4 + [whole(pl.ANY)] * len(ahead),
        out_specs=[whole()] * 2,
        compiler_params=pltpu.CompilerParams(vmem_limit_bytes=8 * MIB),
        name="pass_on",
    )(next_up, got_up, next_down, got_down, *ahead)
    return swap(up, "dp", 2), swap(down, "dp", 1)


def row_loss_kernel(place_ref, loss_ref, row_loss_ref):
    experts, capacity = loss_ref.shape
    loss = loss_ref[...]
    for g in range(place_ref.shape[0]):
        place = place_ref[g : g + 1, :]
        block = place // capacity
        slot = place - block * capacity
        picks = jnp.where(iota((capacity, LANES), 0) == slot, 1.0, 0.0)
        found = lax.dot_general(
            loss,
            picks,
            (((1,), (0,)), ((), ())),
            precision=lax.Precision.HIGHEST,
            preferred_element_type=F32,
        )
        mine = jnp.where(iota((experts, LANES), 0) == block, found, 0.0)
        row_loss_ref[g : g + 1, :] = jnp.sum(mine, axis=0, keepdims=True)


def loss_by_row(place, loss):
    return pl.pallas_call(
        row_loss_kernel,
        out_shape=jax.ShapeDtypeStruct(place.shape, F32),
        in_specs=[whole()] * 2,
        out_specs=whole(),
        compiler_params=pltpu.CompilerParams(vmem_limit_bytes=16 * MIB),
        name="row_loss",
    )(place, loss)


def assemble_kernel(part, me_ref, *refs):
    *held, trunk_ref = refs
    me = me_ref[0]
    order = iter((0, 2, 4, 6, 1, 3, 5, 7))
    for ref in held:
        for k in range(ref.shape[0] // part):
            at = pl.ds(pl.multiple_of((me ^ next(order)) * part, part), part)
            trunk_ref[at, :] = ref[k * part : (k + 1) * part, :]


def assemble(me, held, part):
    width = held[0].shape[1]
    return pl.pallas_call(
        functools.partial(assemble_kernel, part),
        out_shape=jax.ShapeDtypeStruct((8 * part, width), F32),
        in_specs=[whole(pltpu.SMEM)] + [whole()] * len(held),
        out_specs=whole(),
        compiler_params=pltpu.CompilerParams(vmem_limit_bytes=4 * MIB),
        name="assemble_trunk",
    )(me, *held)


def adam_update(params, first, second, grads):
    first_new = beta_one * first + (1.0 - beta_one) * grads
    second_new = beta_two * second + (1.0 - beta_two) * grads * grads
    first_hat = first_new / (1.0 - beta_one**adam_step)
    second_hat = second_new / (1.0 - beta_two**adam_step)
    return (
        params - learn_rate * first_hat / (jnp.sqrt(second_hat) + adam_eps),
        first_new,
        second_new,
    )


def swap(value, axis, s):
    if s == 0:
        return value
    return lax.ppermute(value, axis, [(i, i ^ s) for i in range(lax.axis_size(axis))])


def on_device(
    cell_table,
    sample_index,
    region,
    targets,
    trunk_weight,
    expert_params,
    first_moment,
    second_moment,
):
    rows = sample_index.shape[0]
    width = cell_table.shape[1]
    experts = lax.axis_size("expert")
    replicas = lax.axis_size("dp")
    capacity = 2 * rows // experts
    me = lax.axis_index("expert").astype(jnp.int32).reshape(1)

    up, down = expert_params[0, 0].astype(BF16), expert_params[0, 1].astype(BF16)
    near_up, near_down = swap(up, "dp", 1), swap(down, "dp", 2)
    *blocks, place = pack(me, sample_index, region[:, 0], cell_table, targets, experts, capacity)
    ups, downs = pair(up, near_up, place), pair(down, near_down, place)
    weights = [ups, swap(ups, "dp", 2), downs, swap(downs, "dp", 1)]
    if in_turns(experts):
        batches, later = ((0,), (4, 5), (2, 3, 1), (6,), (7,)), (6, 7)
    else:
        batches, later = (range(experts // 2), range(experts // 2, experts)), ()
    order = [s for batch in batches for s in batch]
    arrived = {s: swap(blocks[s], "expert", s) for s in order if s not in later}
    prior, losses = None, []
    for k, batch in enumerate(batches):
        last = k == len(batches) - 1
        relays = [blocks[s] for s in later] if k == 0 else []
        outs = expert_call(
            [arrived[s] for s in batch], trunk_weight, weights, prior, losses, me, order, last, relays
        )
        if not last:
            prior = outs[:2]
            losses.append(outs[2])
            for s, block in zip(later, outs[3:]):
                arrived[s] = swap(block, "expert", s)
    own, next_up, next_down, sent_up, sent_down, kept, note = outs

    got_up = swap(sent_up, "dp", 1)
    got_down = swap(sent_down, "dp", 2)
    part = width // experts
    if in_turns(experts):
        ours, *notes = turn(
            turn_one_kernel, [kept, swap(note, "expert", 1)], part, (part + 8,) * 4, "turn_one"
        )
        notes = [swap(note, "expert", s) for note, s in zip(notes, (2, 4, 6))]
        total, loss = turn(turn_two_kernel, [ours] + notes, part, (part, experts), "turn_two")
        (total,) = turn(
            turn_three_kernel,
            [total] + [swap(total, "dp", j) for j in range(1, replicas)],
            part,
            (part,),
            "turn_three",
            (got_up, got_down),
        )
        more_up, more_down = pass_on(next_up, got_up, next_down, got_down, (total,))
        column = [total] + [swap(total, "expert", s) for s in (2, 4, 6)]
        (column,) = turn(
            turn_four_kernel, column, part, (4 * part,), "turn_four", (more_up, more_down)
        )
        trunk_grad = assemble(me, [column, swap(column, "expert", 1)], part)
    else:
        more_up, more_down = pass_on(next_up, got_up, next_down, got_down)
        trunk_grad = lax.psum(kept, ("dp", "expert"))
        places = jnp.arange(experts, dtype=jnp.int32) ^ me
        note = note.reshape(experts, capacity)[places]
        loss = lax.all_to_all(note, "expert", split_axis=0, concat_axis=0, tiled=True)[places]
    row_loss = loss_by_row(place, loss)

    grads = jnp.stack(
        [
            own[0] + got_up[0].astype(F32) + more_up.astype(F32),
            own[1] + got_down[0].astype(F32) + more_down.astype(F32),
        ]
    )
    new_params, new_first, new_second = adam_update(
        expert_params, first_moment, second_moment, grads[None]
    )
    return (trunk_grad, row_loss.reshape(rows), new_params, new_first, new_second)


def solution(mesh):
    placed = (
        P(("dp", "expert"), None),
        P(("dp", "expert")),
        P(("dp", "expert"), None),
        P(("dp", "expert"), None),
        P(),
        P("expert", None, None, "dp"),
        P("expert", None, None, "dp"),
        P("expert", None, None, "dp"),
    )
    return jax.shard_map(
        on_device,
        mesh=mesh,
        in_specs=placed,
        out_specs=(
            P(),
            P(("dp", "expert")),
            P("expert", None, None, "dp"),
            P("expert", None, None, "dp"),
            P("expert", None, None, "dp"),
        ),
        check_vma=False,
    )
```

```python
import functools

import jax
import jax.numpy as jnp
from jax import lax
from jax.experimental import pallas as pl
from jax.experimental.pallas import tpu as pltpu
from jax.sharding import PartitionSpec as P

loss_scale = 1.0 / 32.0
beta_one = 0.9
beta_two = 0.999
learn_rate = 0.05
adam_eps = 1e-08
adam_step = 10

LANES = 128
F32 = jnp.float32
BF16 = jnp.bfloat16
MIB = 1 << 20
NEAR = 4


def iota(shape, dim):
    return lax.broadcasted_iota(jnp.int32, shape, dim)


def dot(a, b, ca=1, cb=0):
    return lax.dot_general(a, b, (((ca,), (cb,)), ((), ())), preferred_element_type=F32)


def whole(memory_space=pltpu.VMEM):
    return pl.BlockSpec(memory_space=memory_space)


def pack_kernel(experts, capacity, me_ref, index_ref, region_ref, table_ref, target_ref, *refs):
    *blocks, place_ref, rows_ref = refs
    if in_turns(experts):
        blocks = [blocks[0].at[s] for s in range(NEAR)] + blocks[1:]
    me = me_ref[0]
    groups = index_ref.shape[0]
    cells, width = table_ref.shape
    expert_id = iota((experts, LANES), 0)
    block_id = expert_id ^ me
    if in_turns(experts):
        block_id = jnp.where(block_id < NEAR, expert_id & (NEAR - 1), block_id)
    starts = (block_id * capacity).astype(F32)
    ahead = jnp.where(iota((LANES, LANES), 0) <= iota((LANES, LANES), 1), 1.0, 0.0).astype(BF16)
    counted = jnp.zeros((experts, LANES), F32)
    places = []
    for g in range(groups):
        hot = jnp.where(region_ref[g : g + 1, :] == expert_id, 1.0, 0.0)
        upto = dot(hot.astype(BF16), ahead)
        places.append(jnp.sum(hot * (upto - 1.0 + counted + starts), axis=0, keepdims=True))
        counted = counted + jnp.broadcast_to(upto[:, LANES - 1 :], (experts, LANES))
    for g in range(groups):
        place_ref[g : g + 1, :] = places[g].astype(jnp.int32)
    place = jnp.concatenate(places, axis=1)

    step = 2
    cell_id = iota((LANES * step, LANES), 1).astype(F32)
    for g in range(0, groups, step):
        column = jnp.concatenate(
            [
                jnp.broadcast_to(index_ref[h : h + 1, :].astype(F32), (LANES, LANES)).T
                for h in range(g, g + step)
            ],
            axis=0,
        )
        picks = jnp.concatenate(
            [
                jnp.where(column == cell_id + float(LANES * t), 1.0, 0.0).astype(BF16)
                for t in range(cells // LANES)
            ],
            axis=1,
        )
        at = slice(g * LANES, (g + step) * LANES)
        rows_ref[at, :width] = dot(picks, table_ref[...]).astype(BF16)
        rows_ref[at, width:] = target_ref[at, :]

    slot_id = iota((capacity, place.shape[1]), 0).astype(F32)
    for s in range(experts):
        spread = jnp.where(place == slot_id + float(s * capacity), 1.0, 0.0).astype(BF16)
        blocks[s][...] = dot(spread, rows_ref[...]).astype(BF16)


def pack(me, index, region, table, targets, experts, capacity):
    rows, width = targets.shape
    groups = rows // LANES
    shapes = [(capacity, 2 * width)] * experts
    if in_turns(experts):
        shapes = [(NEAR, *shapes[0])] + shapes[NEAR:]
    return pl.pallas_call(
        functools.partial(pack_kernel, experts, capacity),
        out_shape=[jax.ShapeDtypeStruct(shape, BF16) for shape in shapes]
        + [jax.ShapeDtypeStruct((groups, LANES), jnp.int32)],
        in_specs=[whole(pltpu.SMEM)] + [whole()] * 4,
        out_specs=[whole()] * (len(shapes) + 1),
        scratch_shapes=[pltpu.VMEM((rows, 2 * width), BF16)],
        compiler_params=pltpu.CompilerParams(vmem_limit_bytes=32 * MIB),
        cost_estimate=pl.CostEstimate(
            flops=2 * rows * width * (table.shape[0] + 2 * experts * capacity),
            bytes_accessed=6 * MIB,
            transcendentals=0,
        ),
        name="pack_rows",
    )(me, index.reshape(groups, LANES), region.reshape(groups, LANES), table, targets)


def pair_kernel(one_ref, other_ref, ahead_ref, both_ref):
    both_ref[0] = one_ref[...]
    both_ref[1] = other_ref[...]


def pair(one, other, ahead):
    return pl.pallas_call(
        pair_kernel,
        out_shape=jax.ShapeDtypeStruct((2, *one.shape), one.dtype),
        in_specs=[whole()] * 2 + [whole(pl.ANY)],
        out_specs=whole(),
        compiler_params=pltpu.CompilerParams(vmem_limit_bytes=4 * MIB),
        name="pair",
    )(one, other, ahead)


def sigmoid(v):
    return 0.5 * jnp.tanh(0.5 * v) + 0.5


def expert_kernel(counts, first, last, *refs):
    blocks, shares, experts, steps, step_rows, relays = counts
    refs = list(refs)

    def take(n):
        got = refs[:n]
        del refs[:n]
        return got

    xs = take(blocks)
    trunk_ref, ups_near, ups_far, downs_near, downs_far = take(5)
    ups = (ups_near.at[0], ups_near.at[1], ups_far.at[0], ups_far.at[1])
    downs = (downs_near.at[0], downs_far.at[0], downs_near.at[1], downs_far.at[1])
    if not first:
        prior_ref, prior_trunk_ref = take(2)
    held = take(relays)
    if last:
        loss_refs = take(last - 1)
        (me_ref,) = take(1)
        own_ref, next_up_ref, next_down_ref, sent_up_ref, sent_down_ref = take(5)
        kept_ref, note_ref = take(2)
    else:
        acc_ref, acc_trunk_ref, loss_ref = take(3)
        for source, copy in zip(held, take(relays)):
            copy[...] = source[...]
    x_ref, hid_ref, slope_ref = take(3)
    if last:
        acc_ref, acc_trunk_ref, loss_ref = take(3)

    width = trunk_ref.shape[0]
    share = ups_near.shape[2]
    block_rows = xs[-1].shape[0]
    if len(xs) == 1:
        x_ref = xs[0]
    else:
        for i, ref in enumerate(xs):
            x_ref[i * block_rows : (i + 1) * block_rows, :] = ref[...]
    looped = steps > 3
    if looped and first:
        acc_ref[...] = jnp.zeros(acc_ref.shape, F32)
        acc_trunk_ref[...] = jnp.zeros(acc_trunk_ref.shape, F32)
    elif looped:
        acc_ref[...] = prior_ref[...]
        acc_trunk_ref[...] = prior_trunk_ref[...]

    def add(i, ref, source, at, value):
        if looped or i > 0:
            ref[at] += value
        elif first:
            ref[at] = value
        else:
            ref[at] = source[at] + value

    prior = None if first else prior_ref
    prior_trunk = None if first else prior_trunk_ref

    def step(i, carry):
        if looped:
            at = pl.ds(pl.multiple_of(i * step_rows, step_rows), step_rows)
        else:
            at = slice(i * step_rows, (i + 1) * step_rows)
        feats = x_ref[at, :width]
        feats_f = feats.astype(F32)
        trunk_pre = dot(feats, trunk_ref[...])
        gate = sigmoid(trunk_pre)
        act = trunk_pre * gate
        trunk_slope = gate + act * (1.0 - gate)
        out_f = feats_f + act
        out = out_f.astype(BF16)
        predicted = jnp.zeros((step_rows, width), F32)
        for j in range(shares):
            up = dot(out, ups[j][...])
            s = sigmoid(up)
            h = up * s
            slope_ref[:, j * share : (j + 1) * share] = s + h * (1.0 - s)
            h = h.astype(BF16)
            hid_ref[:, j * share : (j + 1) * share] = h
            predicted = predicted + dot(h, downs[j][...], 1, 1)
        errors = predicted - x_ref[at, width:].astype(F32)
        squares = errors * errors
        half = squares[:, :LANES]
        for k in range(1, width // LANES):
            half = half + squares[:, k * LANES : (k + 1) * LANES]
        loss_ref[pl.ds(i, 1), :] = jnp.sum(half.T, axis=0, keepdims=True) * (0.5 * loss_scale)
        scaled_f = errors * loss_scale
        scaled = scaled_f.astype(BF16)
        scaled_t = scaled_f.T.astype(BF16)
        out_t = out_f.T.astype(BF16)
        row_grad = jnp.zeros((step_rows, width), F32)
        for j in range(shares):
            part = slice(j * share, (j + 1) * share)
            add(i, acc_ref, prior, (j, 1), dot(scaled_t, hid_ref[:, part]))
            pre = (dot(scaled, downs[j][...]) * slope_ref[:, part]).astype(BF16)
            add(i, acc_ref, prior, (j, 0), dot(out_t, pre))
            row_grad = row_grad + dot(pre, ups[j][...], 1, 1)
        slope = (row_grad.astype(BF16).astype(F32) * trunk_slope).astype(BF16)
        add(i, acc_trunk_ref, prior_trunk, ..., dot(feats_f.T.astype(BF16), slope))
        return carry

    if looped:
        lax.fori_loop(0, steps, step, 0)
    else:
        for i in range(steps):
            step(i, 0)
    if last:
        own_ref[...] = acc_ref[0]
        next_up_ref[...] = acc_ref[2, 0]
        next_down_ref[...] = acc_ref[1, 1]
        for k, j in enumerate((1, 3)):
            sent_up_ref[k] = acc_ref[j, 0].astype(BF16)
        for k, j in enumerate((2, 3)):
            sent_down_ref[k] = acc_ref[j, 1].astype(BF16)
        all_losses = list(loss_refs) + [loss_ref]
        if not in_turns(experts):
            kept_ref[...] = acc_trunk_ref[...]
            for row in range(note_ref.shape[0]):
                note_ref[row : row + 1, :] = loss_row(all_losses, row)
            return
        me = me_ref[0]
        part = width // experts
        kept_ref[experts // 2 * part :, :] = jnp.zeros((8, width), F32)
        note_ref[experts // 2 * part :, :] = jnp.zeros((8, width), F32)
        for s in range(experts):
            ref = note_ref if s % 2 else kept_ref
            mine = pl.ds(pl.multiple_of((me ^ s) * part, part), part)
            ref[s // 2 * part : (s // 2 + 1) * part, :] = acc_trunk_ref[mine, :]
            at = experts // 2 * part + s // 2
            if s < NEAR:
                ref[at : at + 1, :] = all_losses[0][pl.ds((me & (NEAR - 1)) ^ s, 1), :]
            else:
                ref[at : at + 1, :] = loss_row(all_losses, s)


def in_turns(experts):
    return experts == 8


def loss_row(refs, row):
    for ref in refs:
        if row < ref.shape[0]:
            return ref[row : row + 1, :]
        row -= ref.shape[0]


def expert_call(xs, trunk_weight, weights, prior, losses, me, experts, last, relays=()):
    rows = sum(x.shape[0] for x in xs)
    width = trunk_weight.shape[0]
    shares, share = len(weights), weights[0].shape[2]
    step_rows = min(256, rows)
    block_rows = 8 * step_rows // experts
    steps = rows // step_rows
    first = prior is None
    acc = jax.ShapeDtypeStruct((shares, 2, width, share), F32)
    acc_trunk = jax.ShapeDtypeStruct((width, width), F32)
    loss = jax.ShapeDtypeStruct((steps, step_rows), F32)
    args = list(xs) + [trunk_weight, *weights]
    if not first:
        args += list(prior)
    args += relays
    in_specs = [whole()] * len(args)
    scratch = [
        pltpu.VMEM((rows if len(xs) > 1 else 16, 2 * width), BF16),
        pltpu.VMEM((step_rows, shares * share), BF16),
        pltpu.VMEM((step_rows, shares * share), F32),
    ]
    if last:
        args += list(losses) + [me]
        in_specs += [whole()] * len(losses) + [whole(pltpu.SMEM)]
        outs = [jax.ShapeDtypeStruct((2, width, share), F32)]
        outs += [jax.ShapeDtypeStruct((width, share), F32)] * 2
        outs += [jax.ShapeDtypeStruct((2, width, share), BF16)] * 2
        if in_turns(experts):
            outs += [jax.ShapeDtypeStruct((width // 2 + 8, width), F32)] * 2
        else:
            outs += [
                acc_trunk,
                jax.ShapeDtypeStruct((experts * block_rows // step_rows, step_rows), F32),
            ]
        scratch += [pltpu.VMEM(a.shape, a.dtype) for a in (acc, acc_trunk, loss)]
    else:
        outs = [acc, acc_trunk, loss]
        outs += [jax.ShapeDtypeStruct(relay.shape, relay.dtype) for relay in relays]
    counts = (len(xs), shares, experts, steps, step_rows, len(relays))
    return pl.pallas_call(
        functools.partial(expert_kernel, counts, first, len(losses) + 1 if last else 0),
        out_shape=outs,
        in_specs=in_specs,
        out_specs=[whole()] * len(outs),
        scratch_shapes=scratch,
        compiler_params=pltpu.CompilerParams(vmem_limit_bytes=40 * MIB),
        cost_estimate=pl.CostEstimate(
            flops=12 * rows * width * shares * share,
            bytes_accessed=10 * MIB,
            transcendentals=rows * shares * share,
        ),
        name="expert_rows",
    )(*args)


def turn_one_kernel(part, kept_ref, got_ref, *outs):
    lost = kept_ref[4 * part :, :]
    found = got_ref[4 * part :, :]
    for k, ref in enumerate(outs):
        at = slice(k * part, (k + 1) * part)
        ref[:part, :] = kept_ref[at, :] + got_ref[at, :]
        ref[part:, :] = jnp.concatenate(
            [lost[k : k + 1], found[k : k + 1], jnp.zeros((6, lost.shape[1]), F32)], axis=0
        )


def turn_two_kernel(part, *refs):
    *notes, sum_ref, loss_ref = refs
    held = [ref[:part, :] for ref in notes]
    sum_ref[...] = (held[0] + held[1]) + (held[2] + held[3])
    loss_ref[...] = jnp.concatenate([ref[part : part + 2, :] for ref in notes], axis=0)


def turn_three_kernel(part, *refs):
    held = [ref[...] for ref in refs[:4]]
    refs[-1][...] = (held[0] + held[1]) + (held[2] + held[3])


def turn_four_kernel(part, *refs):
    for k in range(4):
        refs[-1][k * part : (k + 1) * part, :] = refs[k][...]


def turn(kernel, held, part, shapes, name, ahead=()):
    return pl.pallas_call(
        functools.partial(kernel, part),
        out_shape=[jax.ShapeDtypeStruct((rows, held[0].shape[1]), F32) for rows in shapes],
        in_specs=[whole()] * len(held) + [whole(pl.ANY)] * len(ahead),
        out_specs=[whole()] * len(shapes),
        compiler_params=pltpu.CompilerParams(vmem_limit_bytes=4 * MIB),
        name=name,
    )(*held, *ahead)


def pass_on_kernel(next_up_ref, got_up_ref, next_down_ref, got_down_ref, *refs):
    up_ref, down_ref = refs[-2:]
    up_ref[...] = (next_up_ref[...] + got_up_ref[1].astype(F32)).astype(BF16)
    down_ref[...] = (next_down_ref[...] + got_down_ref[1].astype(F32)).astype(BF16)


def pass_on(next_up, got_up, next_down, got_down, ahead=()):
    up, down = pl.pallas_call(
        pass_on_kernel,
        out_shape=[jax.ShapeDtypeStruct(next_up.shape, BF16)] * 2,
        in_specs=[whole()] * 4 + [whole(pl.ANY)] * len(ahead),
        out_specs=[whole()] * 2,
        compiler_params=pltpu.CompilerParams(vmem_limit_bytes=8 * MIB),
        name="pass_on",
    )(next_up, got_up, next_down, got_down, *ahead)
    return swap(up, "dp", 2), swap(down, "dp", 1)


def row_loss_kernel(me_ref, place_ref, loss_ref, row_loss_ref):
    experts, capacity = loss_ref.shape
    me = me_ref[0]
    loss = loss_ref[...]
    for g in range(place_ref.shape[0]):
        place = place_ref[g : g + 1, :]
        block = place // capacity
        slot = place - block * capacity
        if in_turns(experts):
            block = jnp.where(block < NEAR, block ^ (me & (NEAR - 1)), block)
        picks = jnp.where(iota((capacity, LANES), 0) == slot, 1.0, 0.0)
        found = lax.dot_general(
            loss,
            picks,
            (((1,), (0,)), ((), ())),
            precision=lax.Precision.HIGHEST,
            preferred_element_type=F32,
        )
        mine = jnp.where(iota((experts, LANES), 0) == block, found, 0.0)
        row_loss_ref[g : g + 1, :] = jnp.sum(mine, axis=0, keepdims=True)


def loss_by_row(me, place, loss):
    return pl.pallas_call(
        row_loss_kernel,
        out_shape=jax.ShapeDtypeStruct(place.shape, F32),
        in_specs=[whole(pltpu.SMEM)] + [whole()] * 2,
        out_specs=whole(),
        compiler_params=pltpu.CompilerParams(vmem_limit_bytes=16 * MIB),
        name="row_loss",
    )(me, place, loss)


def assemble_kernel(part, me_ref, *refs):
    *held, trunk_ref = refs
    me = me_ref[0]
    order = iter((0, 2, 4, 6, 1, 3, 5, 7))
    for ref in held:
        for k in range(ref.shape[0] // part):
            at = pl.ds(pl.multiple_of((me ^ next(order)) * part, part), part)
            trunk_ref[at, :] = ref[k * part : (k + 1) * part, :]


def assemble(me, held, part):
    width = held[0].shape[1]
    return pl.pallas_call(
        functools.partial(assemble_kernel, part),
        out_shape=jax.ShapeDtypeStruct((8 * part, width), F32),
        in_specs=[whole(pltpu.SMEM)] + [whole()] * len(held),
        out_specs=whole(),
        compiler_params=pltpu.CompilerParams(vmem_limit_bytes=4 * MIB),
        name="assemble_trunk",
    )(me, *held)


def adam_update(params, first, second, grads):
    first_new = beta_one * first + (1.0 - beta_one) * grads
    second_new = beta_two * second + (1.0 - beta_two) * grads * grads
    first_hat = first_new / (1.0 - beta_one**adam_step)
    second_hat = second_new / (1.0 - beta_two**adam_step)
    return (
        params - learn_rate * first_hat / (jnp.sqrt(second_hat) + adam_eps),
        first_new,
        second_new,
    )


def swap(value, axis, s):
    if s == 0:
        return value
    return lax.ppermute(value, axis, [(i, i ^ s) for i in range(lax.axis_size(axis))])


def on_device(
    cell_table,
    sample_index,
    region,
    targets,
    trunk_weight,
    expert_params,
    first_moment,
    second_moment,
):
    rows = sample_index.shape[0]
    width = cell_table.shape[1]
    experts = lax.axis_size("expert")
    replicas = lax.axis_size("dp")
    capacity = 2 * rows // experts
    me = lax.axis_index("expert").astype(jnp.int32).reshape(1)

    up, down = expert_params[0, 0].astype(BF16), expert_params[0, 1].astype(BF16)
    near_up, near_down = swap(up, "dp", 1), swap(down, "dp", 2)
    *blocks, place = pack(me, sample_index, region[:, 0], cell_table, targets, experts, capacity)
    ups, downs = pair(up, near_up, place), pair(down, near_down, place)
    weights = [ups, swap(ups, "dp", 2), downs, swap(downs, "dp", 1)]
    if in_turns(experts):
        near = lax.all_to_all(
            blocks[0],
            "expert",
            split_axis=0,
            concat_axis=0,
            tiled=True,
            axis_index_groups=[list(range(g, g + NEAR)) for g in range(0, experts, NEAR)],
        )
        far = [swap(block, "expert", s) for s, block in enumerate(blocks[1:-1], NEAR)]
        batches, relays = [[near.reshape(-1, 2 * width)], far[:2], far[2:], []], blocks[-1:]
    else:
        arrived = [swap(blocks[s], "expert", s) for s in range(experts)]
        batches, relays = [arrived[: experts // 2], arrived[experts // 2 :]], []
    prior, losses = None, []
    for k, xs in enumerate(batches):
        last = k == len(batches) - 1
        outs = expert_call(xs, trunk_weight, weights, prior, losses, me, experts, last, relays)
        if relays:
            batches[-1].append(swap(outs[-1], "expert", experts - 1))
            relays = []
        if not last:
            prior = outs[:2]
            losses.append(outs[2])
    own, next_up, next_down, sent_up, sent_down, kept, note = outs

    got_up = swap(sent_up, "dp", 1)
    got_down = swap(sent_down, "dp", 2)
    part = width // experts
    if in_turns(experts):
        ours, *notes = turn(
            turn_one_kernel, [kept, swap(note, "expert", 1)], part, (part + 8,) * 4, "turn_one"
        )
        notes = [swap(note, "expert", s) for note, s in zip(notes, (2, 4, 6))]
        total, loss = turn(turn_two_kernel, [ours] + notes, part, (part, experts), "turn_two")
        (total,) = turn(
            turn_three_kernel,
            [total] + [swap(total, "dp", j) for j in range(1, replicas)],
            part,
            (part,),
            "turn_three",
            (got_up, got_down),
        )
        more_up, more_down = pass_on(next_up, got_up, next_down, got_down, (total,))
        column = [total] + [swap(total, "expert", s) for s in (2, 4, 6)]
        (column,) = turn(
            turn_four_kernel, column, part, (4 * part,), "turn_four", (more_up, more_down)
        )
        trunk_grad = assemble(me, [column, swap(column, "expert", 1)], part)
    else:
        more_up, more_down = pass_on(next_up, got_up, next_down, got_down)
        trunk_grad = lax.psum(kept, ("dp", "expert"))
        places = jnp.arange(experts, dtype=jnp.int32) ^ me
        note = note.reshape(experts, capacity)[places]
        loss = lax.all_to_all(note, "expert", split_axis=0, concat_axis=0, tiled=True)[places]
    row_loss = loss_by_row(me, place, loss)

    grads = jnp.stack(
        [
            own[0] + got_up[0].astype(F32) + more_up.astype(F32),
            own[1] + got_down[0].astype(F32) + more_down.astype(F32),
        ]
    )
    new_params, new_first, new_second = adam_update(
        expert_params, first_moment, second_moment, grads[None]
    )
    return (trunk_grad, row_loss.reshape(rows), new_params, new_first, new_second)


def solution(mesh):
    placed = (
        P(("dp", "expert"), None),
        P(("dp", "expert")),
        P(("dp", "expert"), None),
        P(("dp", "expert"), None),
        P(),
        P("expert", None, None, "dp"),
        P("expert", None, None, "dp"),
        P("expert", None, None, "dp"),
    )
    return jax.shard_map(
        on_device,
        mesh=mesh,
        in_specs=placed,
        out_specs=(
            P(),
            P(("dp", "expert")),
            P("expert", None, None, "dp"),
            P("expert", None, None, "dp"),
            P("expert", None, None, "dp"),
        ),
        check_vma=False,
    )
```

```python
import functools

import jax
import jax.numpy as jnp
from jax import lax
from jax.experimental import pallas as pl
from jax.experimental.pallas import tpu as pltpu
from jax.sharding import PartitionSpec as P

loss_scale = 1.0 / 32.0
beta_one = 0.9
beta_two = 0.999
learn_rate = 0.05
adam_eps = 1e-08
adam_step = 10

LANES = 128
F32 = jnp.float32
BF16 = jnp.bfloat16
MIB = 1 << 20


def iota(shape, dim):
    return lax.broadcasted_iota(jnp.int32, shape, dim)


def dot(a, b, ca=1, cb=0):
    return lax.dot_general(a, b, (((ca,), (cb,)), ((), ())), preferred_element_type=F32)


def whole(memory_space=pltpu.VMEM):
    return pl.BlockSpec(memory_space=memory_space)


def pack_kernel(experts, capacity, me_ref, index_ref, region_ref, table_ref, target_ref, *refs):
    blocks, place_ref, rows_ref = refs[:experts], refs[experts], refs[experts + 1]
    me = me_ref[0]
    groups = index_ref.shape[0]
    cells, width = table_ref.shape
    expert_id = iota((experts, LANES), 0)
    starts = ((expert_id ^ me) * capacity).astype(F32)
    ahead = jnp.where(iota((LANES, LANES), 0) <= iota((LANES, LANES), 1), 1.0, 0.0).astype(BF16)
    counted = jnp.zeros((experts, LANES), F32)
    places = []
    for g in range(groups):
        hot = jnp.where(region_ref[g : g + 1, :] == expert_id, 1.0, 0.0)
        upto = dot(hot.astype(BF16), ahead)
        places.append(jnp.sum(hot * (upto - 1.0 + counted + starts), axis=0, keepdims=True))
        counted = counted + jnp.broadcast_to(upto[:, LANES - 1 :], (experts, LANES))
    for g in range(groups):
        place_ref[g : g + 1, :] = places[g].astype(jnp.int32)
    place = jnp.concatenate(places, axis=1)

    step = 2
    cell_id = iota((LANES * step, LANES), 1).astype(F32)
    for g in range(0, groups, step):
        column = jnp.concatenate(
            [
                jnp.broadcast_to(index_ref[h : h + 1, :].astype(F32), (LANES, LANES)).T
                for h in range(g, g + step)
            ],
            axis=0,
        )
        picks = jnp.concatenate(
            [
                jnp.where(column == cell_id + float(LANES * t), 1.0, 0.0).astype(BF16)
                for t in range(cells // LANES)
            ],
            axis=1,
        )
        at = slice(g * LANES, (g + step) * LANES)
        rows_ref[at, :width] = dot(picks, table_ref[...]).astype(BF16)
        rows_ref[at, width:] = target_ref[at, :]

    slot_id = iota((capacity, place.shape[1]), 0).astype(F32)
    for s in range(experts):
        spread = jnp.where(place == slot_id + float(s * capacity), 1.0, 0.0).astype(BF16)
        blocks[s][...] = dot(spread, rows_ref[...]).astype(BF16)


def pack(me, index, region, table, targets, experts, capacity):
    rows, width = targets.shape
    groups = rows // LANES
    return pl.pallas_call(
        functools.partial(pack_kernel, experts, capacity),
        out_shape=[jax.ShapeDtypeStruct((capacity, 2 * width), BF16)] * experts
        + [jax.ShapeDtypeStruct((groups, LANES), jnp.int32)],
        in_specs=[whole(pltpu.SMEM)] + [whole()] * 4,
        out_specs=[whole()] * (experts + 1),
        scratch_shapes=[pltpu.VMEM((rows, 2 * width), BF16)],
        compiler_params=pltpu.CompilerParams(vmem_limit_bytes=32 * MIB),
        cost_estimate=pl.CostEstimate(
            flops=2 * rows * width * (table.shape[0] + 2 * experts * capacity),
            bytes_accessed=6 * MIB,
            transcendentals=0,
        ),
        name="pack_rows",
    )(me, index.reshape(groups, LANES), region.reshape(groups, LANES), table, targets)


def pair_kernel(one_ref, other_ref, ahead_ref, both_ref):
    both_ref[0] = one_ref[...]
    both_ref[1] = other_ref[...]


def pair(one, other, ahead):
    return pl.pallas_call(
        pair_kernel,
        out_shape=jax.ShapeDtypeStruct((2, *one.shape), one.dtype),
        in_specs=[whole()] * 2 + [whole(pl.ANY)],
        out_specs=whole(),
        compiler_params=pltpu.CompilerParams(vmem_limit_bytes=4 * MIB),
        name="pair",
    )(one, other, ahead)


def sigmoid(v):
    return 0.5 * jnp.tanh(0.5 * v) + 0.5


def expert_kernel(counts, order, first, last, *refs):
    blocks, shares, experts, steps, step_rows, relays = counts
    refs = list(refs)

    def take(n):
        got = refs[:n]
        del refs[:n]
        return got

    xs = take(blocks)
    trunk_ref, ups_near, ups_far, downs_near, downs_far = take(5)
    ups = (ups_near.at[0], ups_near.at[1], ups_far.at[0], ups_far.at[1])
    downs = (downs_near.at[0], downs_far.at[0], downs_near.at[1], downs_far.at[1])
    if not first:
        prior_ref, prior_trunk_ref = take(2)
    held = take(relays)
    if last:
        loss_refs = take(last - 1)
        (me_ref,) = take(1)
        own_ref, next_up_ref, next_down_ref, sent_up_ref, sent_down_ref = take(5)
        kept_ref, note_ref = take(2)
    else:
        acc_ref, acc_trunk_ref, loss_ref = take(3)
        for source, copy in zip(held, take(relays)):
            copy[...] = source[...]
    x_ref, hid_ref, slope_ref = take(3)
    if last:
        acc_ref, acc_trunk_ref, loss_ref = take(3)

    width = trunk_ref.shape[0]
    share = ups_near.shape[2]
    block_rows = xs[0].shape[0]
    for i, ref in enumerate(xs):
        x_ref[i * block_rows : (i + 1) * block_rows, :] = ref[...]
    looped = steps > 3
    if looped and first:
        acc_ref[...] = jnp.zeros(acc_ref.shape, F32)
        acc_trunk_ref[...] = jnp.zeros(acc_trunk_ref.shape, F32)
    elif looped:
        acc_ref[...] = prior_ref[...]
        acc_trunk_ref[...] = prior_trunk_ref[...]

    def add(i, ref, source, at, value):
        if looped or i > 0:
            ref[at] += value
        elif first:
            ref[at] = value
        else:
            ref[at] = source[at] + value

    prior = None if first else prior_ref
    prior_trunk = None if first else prior_trunk_ref

    def step(i, carry):
        if looped:
            at = pl.ds(pl.multiple_of(i * step_rows, step_rows), step_rows)
        else:
            at = slice(i * step_rows, (i + 1) * step_rows)
        feats = x_ref[at, :width]
        feats_f = feats.astype(F32)
        trunk_pre = dot(feats, trunk_ref[...])
        gate = sigmoid(trunk_pre)
        act = trunk_pre * gate
        trunk_slope = gate + act * (1.0 - gate)
        out_f = feats_f + act
        out = out_f.astype(BF16)
        predicted = jnp.zeros((step_rows, width), F32)
        for j in range(shares):
            up = dot(out, ups[j][...])
            s = sigmoid(up)
            h = up * s
            slope_ref[:, j * share : (j + 1) * share] = s + h * (1.0 - s)
            h = h.astype(BF16)
            hid_ref[:, j * share : (j + 1) * share] = h
            predicted = predicted + dot(h, downs[j][...], 1, 1)
        errors = predicted - x_ref[at, width:].astype(F32)
        squares = errors * errors
        half = squares[:, :LANES]
        for k in range(1, width // LANES):
            half = half + squares[:, k * LANES : (k + 1) * LANES]
        loss_ref[pl.ds(i, 1), :] = jnp.sum(half.T, axis=0, keepdims=True) * (0.5 * loss_scale)
        scaled_f = errors * loss_scale
        scaled = scaled_f.astype(BF16)
        scaled_t = scaled_f.T.astype(BF16)
        out_t = out_f.T.astype(BF16)
        row_grad = jnp.zeros((step_rows, width), F32)
        for j in range(shares):
            part = slice(j * share, (j + 1) * share)
            add(i, acc_ref, prior, (j, 1), dot(scaled_t, hid_ref[:, part]))
            pre = (dot(scaled, downs[j][...]) * slope_ref[:, part]).astype(BF16)
            add(i, acc_ref, prior, (j, 0), dot(out_t, pre))
            row_grad = row_grad + dot(pre, ups[j][...], 1, 1)
        slope = (row_grad.astype(BF16).astype(F32) * trunk_slope).astype(BF16)
        add(i, acc_trunk_ref, prior_trunk, ..., dot(feats_f.T.astype(BF16), slope))
        return carry

    if looped:
        lax.fori_loop(0, steps, step, 0)
    else:
        for i in range(steps):
            step(i, 0)
    if last:
        own_ref[...] = acc_ref[0]
        next_up_ref[...] = acc_ref[2, 0]
        next_down_ref[...] = acc_ref[1, 1]
        for k, j in enumerate((1, 3)):
            sent_up_ref[k] = acc_ref[j, 0].astype(BF16)
        for k, j in enumerate((2, 3)):
            sent_down_ref[k] = acc_ref[j, 1].astype(BF16)
        all_losses = list(loss_refs) + [loss_ref]
        if not in_turns(experts):
            kept_ref[...] = acc_trunk_ref[...]
            for row in range(note_ref.shape[0]):
                note_ref[row : row + 1, :] = loss_row(all_losses, row)
            return
        me = me_ref[0]
        part = width // experts
        kept_ref[experts // 2 * part :, :] = jnp.zeros((8, width), F32)
        note_ref[experts // 2 * part :, :] = jnp.zeros((8, width), F32)
        for s in range(experts):
            ref = note_ref if s % 2 else kept_ref
            mine = pl.ds(pl.multiple_of((me ^ s) * part, part), part)
            ref[s // 2 * part : (s // 2 + 1) * part, :] = acc_trunk_ref[mine, :]
            at = experts // 2 * part + s // 2
            ref[at : at + 1, :] = loss_row(all_losses, order.index(s))


def in_turns(experts):
    return experts == 8


def loss_row(refs, row):
    for ref in refs:
        if row < ref.shape[0]:
            return ref[row : row + 1, :]
        row -= ref.shape[0]


def expert_call(xs, trunk_weight, weights, prior, losses, me, order, last, relays=()):
    experts = len(order)
    block_rows = xs[0].shape[0]
    width = trunk_weight.shape[0]
    shares, share = len(weights), weights[0].shape[2]
    rows = block_rows * len(xs)
    step_rows = min(256, rows)
    steps = rows // step_rows
    first = prior is None
    acc = jax.ShapeDtypeStruct((shares, 2, width, share), F32)
    acc_trunk = jax.ShapeDtypeStruct((width, width), F32)
    loss = jax.ShapeDtypeStruct((steps, step_rows), F32)
    args = list(xs) + [trunk_weight, *weights]
    if not first:
        args += list(prior)
    args += relays
    in_specs = [whole()] * len(args)
    scratch = [
        pltpu.VMEM((rows, 2 * width), BF16),
        pltpu.VMEM((step_rows, shares * share), BF16),
        pltpu.VMEM((step_rows, shares * share), F32),
    ]
    if last:
        args += list(losses) + [me]
        in_specs += [whole()] * len(losses) + [whole(pltpu.SMEM)]
        outs = [jax.ShapeDtypeStruct((2, width, share), F32)]
        outs += [jax.ShapeDtypeStruct((width, share), F32)] * 2
        outs += [jax.ShapeDtypeStruct((2, width, share), BF16)] * 2
        if in_turns(experts):
            outs += [jax.ShapeDtypeStruct((width // 2 + 8, width), F32)] * 2
        else:
            outs += [
                acc_trunk,
                jax.ShapeDtypeStruct((experts * block_rows // step_rows, step_rows), F32),
            ]
        scratch += [pltpu.VMEM(a.shape, a.dtype) for a in (acc, acc_trunk, loss)]
    else:
        outs = [acc, acc_trunk, loss]
        outs += [jax.ShapeDtypeStruct(relay.shape, relay.dtype) for relay in relays]
    counts = (len(xs), shares, experts, steps, step_rows, len(relays))
    return pl.pallas_call(
        functools.partial(expert_kernel, counts, order, first, len(losses) + 1 if last else 0),
        out_shape=outs,
        in_specs=in_specs,
        out_specs=[whole()] * len(outs),
        scratch_shapes=scratch,
        compiler_params=pltpu.CompilerParams(vmem_limit_bytes=40 * MIB),
        cost_estimate=pl.CostEstimate(
            flops=12 * rows * width,
            bytes_accessed=rows * width,
            transcendentals=0,
        ),
        name="expert_rows",
    )(*args)


def turn_one_kernel(part, kept_ref, got_ref, *outs):
    lost = kept_ref[4 * part :, :]
    found = got_ref[4 * part :, :]
    for k, ref in enumerate(outs):
        at = slice(k * part, (k + 1) * part)
        ref[:part, :] = kept_ref[at, :] + got_ref[at, :]
        ref[part:, :] = jnp.concatenate(
            [lost[k : k + 1], found[k : k + 1], jnp.zeros((6, lost.shape[1]), F32)], axis=0
        )


def turn_two_kernel(part, *refs):
    *notes, sum_ref, loss_ref = refs
    held = [ref[:part, :] for ref in notes]
    sum_ref[...] = (held[0] + held[1]) + (held[2] + held[3])
    loss_ref[...] = jnp.concatenate([ref[part : part + 2, :] for ref in notes], axis=0)


def turn_three_kernel(part, *refs):
    held = [ref[...] for ref in refs[:4]]
    refs[-1][...] = (held[0] + held[1]) + (held[2] + held[3])


def turn_four_kernel(part, *refs):
    for k in range(4):
        refs[-1][k * part : (k + 1) * part, :] = refs[k][...]


def turn(kernel, held, part, shapes, name, ahead=()):
    return pl.pallas_call(
        functools.partial(kernel, part),
        out_shape=[jax.ShapeDtypeStruct((rows, held[0].shape[1]), F32) for rows in shapes],
        in_specs=[whole()] * len(held) + [whole(pl.ANY)] * len(ahead),
        out_specs=[whole()] * len(shapes),
        compiler_params=pltpu.CompilerParams(vmem_limit_bytes=4 * MIB),
        name=name,
    )(*held, *ahead)


def pass_on_kernel(next_up_ref, got_up_ref, next_down_ref, got_down_ref, *refs):
    up_ref, down_ref = refs[-2:]
    up_ref[...] = (next_up_ref[...] + got_up_ref[1].astype(F32)).astype(BF16)
    down_ref[...] = (next_down_ref[...] + got_down_ref[1].astype(F32)).astype(BF16)


def pass_on(next_up, got_up, next_down, got_down, ahead=()):
    up, down = pl.pallas_call(
        pass_on_kernel,
        out_shape=[jax.ShapeDtypeStruct(next_up.shape, BF16)] * 2,
        in_specs=[whole()] * 4 + [whole(pl.ANY)] * len(ahead),
        out_specs=[whole()] * 2,
        compiler_params=pltpu.CompilerParams(vmem_limit_bytes=8 * MIB),
        name="pass_on",
    )(next_up, got_up, next_down, got_down, *ahead)
    return swap(up, "dp", 2), swap(down, "dp", 1)


def row_loss_kernel(place_ref, loss_ref, row_loss_ref):
    experts, capacity = loss_ref.shape
    loss = loss_ref[...]
    for g in range(place_ref.shape[0]):
        place = place_ref[g : g + 1, :]
        block = place // capacity
        slot = place - block * capacity
        picks = jnp.where(iota((capacity, LANES), 0) == slot, 1.0, 0.0)
        found = lax.dot_general(
            loss,
            picks,
            (((1,), (0,)), ((), ())),
            precision=lax.Precision.HIGHEST,
            preferred_element_type=F32,
        )
        mine = jnp.where(iota((experts, LANES), 0) == block, found, 0.0)
        row_loss_ref[g : g + 1, :] = jnp.sum(mine, axis=0, keepdims=True)


def loss_by_row(place, loss):
    return pl.pallas_call(
        row_loss_kernel,
        out_shape=jax.ShapeDtypeStruct(place.shape, F32),
        in_specs=[whole()] * 2,
        out_specs=whole(),
        compiler_params=pltpu.CompilerParams(vmem_limit_bytes=16 * MIB),
        name="row_loss",
    )(place, loss)


def assemble_kernel(part, me_ref, *refs):
    *held, trunk_ref = refs
    me = me_ref[0]
    order = iter((0, 2, 4, 6, 1, 3, 5, 7))
    for ref in held:
        for k in range(ref.shape[0] // part):
            at = pl.ds(pl.multiple_of((me ^ next(order)) * part, part), part)
            trunk_ref[at, :] = ref[k * part : (k + 1) * part, :]


def assemble(me, held, part):
    width = held[0].shape[1]
    return pl.pallas_call(
        functools.partial(assemble_kernel, part),
        out_shape=jax.ShapeDtypeStruct((8 * part, width), F32),
        in_specs=[whole(pltpu.SMEM)] + [whole()] * len(held),
        out_specs=whole(),
        compiler_params=pltpu.CompilerParams(vmem_limit_bytes=4 * MIB),
        name="assemble_trunk",
    )(me, *held)


def adam_update(params, first, second, grads):
    first_new = beta_one * first + (1.0 - beta_one) * grads
    second_new = beta_two * second + (1.0 - beta_two) * grads * grads
    first_hat = first_new / (1.0 - beta_one**adam_step)
    second_hat = second_new / (1.0 - beta_two**adam_step)
    return (
        params - learn_rate * first_hat / (jnp.sqrt(second_hat) + adam_eps),
        first_new,
        second_new,
    )


def swap(value, axis, s):
    if s == 0:
        return value
    return lax.ppermute(value, axis, [(i, i ^ s) for i in range(lax.axis_size(axis))])


def on_device(
    cell_table,
    sample_index,
    region,
    targets,
    trunk_weight,
    expert_params,
    first_moment,
    second_moment,
):
    rows = sample_index.shape[0]
    width = cell_table.shape[1]
    experts = lax.axis_size("expert")
    replicas = lax.axis_size("dp")
    capacity = 2 * rows // experts
    me = lax.axis_index("expert").astype(jnp.int32).reshape(1)

    up, down = expert_params[0, 0].astype(BF16), expert_params[0, 1].astype(BF16)
    near_up, near_down = swap(up, "dp", 1), swap(down, "dp", 2)
    *blocks, place = pack(me, sample_index, region[:, 0], cell_table, targets, experts, capacity)
    ups, downs = pair(up, near_up, place), pair(down, near_down, place)
    weights = [ups, swap(ups, "dp", 2), downs, swap(downs, "dp", 1)]
    if in_turns(experts):
        batches, later = ((0, 1), (4, 5), (2, 3), (6,), (7,)), (7,)
    else:
        batches, later = (range(experts // 2), range(experts // 2, experts)), ()
    order = [s for batch in batches for s in batch]
    arrived = {s: swap(blocks[s], "expert", s) for s in order if s not in later}
    prior, losses = None, []
    for k, batch in enumerate(batches):
        last = k == len(batches) - 1
        relays = [blocks[s] for s in later] if k == 0 else []
        outs = expert_call(
            [arrived[s] for s in batch], trunk_weight, weights, prior, losses, me, order, last, relays
        )
        if not last:
            prior = outs[:2]
            losses.append(outs[2])
            for s, block in zip(later, outs[3:]):
                arrived[s] = swap(block, "expert", s)
    own, next_up, next_down, sent_up, sent_down, kept, note = outs

    got_up = swap(sent_up, "dp", 1)
    got_down = swap(sent_down, "dp", 2)
    part = width // experts
    if in_turns(experts):
        ours, *notes = turn(
            turn_one_kernel, [kept, swap(note, "expert", 1)], part, (part + 8,) * 4, "turn_one"
        )
        notes = [swap(note, "expert", s) for note, s in zip(notes, (2, 4, 6))]
        total, loss = turn(turn_two_kernel, [ours] + notes, part, (part, experts), "turn_two")
        (total,) = turn(
            turn_three_kernel,
            [total] + [swap(total, "dp", j) for j in range(1, replicas)],
            part,
            (part,),
            "turn_three",
            (got_up, got_down),
        )
        more_up, more_down = pass_on(next_up, got_up, next_down, got_down, (total,))
        column = [total] + [swap(total, "expert", s) for s in (2, 4, 6)]
        (column,) = turn(
            turn_four_kernel, column, part, (4 * part,), "turn_four", (more_up, more_down)
        )
        trunk_grad = assemble(me, [column, swap(column, "expert", 1)], part)
    else:
        more_up, more_down = pass_on(next_up, got_up, next_down, got_down)
        trunk_grad = lax.psum(kept, ("dp", "expert"))
        places = jnp.arange(experts, dtype=jnp.int32) ^ me
        note = note.reshape(experts, capacity)[places]
        loss = lax.all_to_all(note, "expert", split_axis=0, concat_axis=0, tiled=True)[places]
    row_loss = loss_by_row(place, loss)

    grads = jnp.stack(
        [
            own[0] + got_up[0].astype(F32) + more_up.astype(F32),
            own[1] + got_down[0].astype(F32) + more_down.astype(F32),
        ]
    )
    new_params, new_first, new_second = adam_update(
        expert_params, first_moment, second_moment, grads[None]
    )
    return (trunk_grad, row_loss.reshape(rows), new_params, new_first, new_second)


def solution(mesh):
    placed = (
        P(("dp", "expert"), None),
        P(("dp", "expert")),
        P(("dp", "expert"), None),
        P(("dp", "expert"), None),
        P(),
        P("expert", None, None, "dp"),
        P("expert", None, None, "dp"),
        P("expert", None, None, "dp"),
    )
    return jax.shard_map(
        on_device,
        mesh=mesh,
        in_specs=placed,
        out_specs=(
            P(),
            P(("dp", "expert")),
            P("expert", None, None, "dp"),
            P("expert", None, None, "dp"),
            P("expert", None, None, "dp"),
        ),
        check_vma=False,
    )
```

```python
import functools

import jax
import jax.numpy as jnp
from jax import lax
from jax.experimental import pallas as pl
from jax.experimental.pallas import tpu as pltpu
from jax.sharding import PartitionSpec as P

loss_scale = 1.0 / 32.0
beta_one = 0.9
beta_two = 0.999
learn_rate = 0.05
adam_eps = 1e-08
adam_step = 10

LANES = 128
F32 = jnp.float32
BF16 = jnp.bfloat16
MIB = 1 << 20


def iota(shape, dim):
    return lax.broadcasted_iota(jnp.int32, shape, dim)


def dot(a, b, ca=1, cb=0):
    return lax.dot_general(a, b, (((ca,), (cb,)), ((), ())), preferred_element_type=F32)


def whole(memory_space=pltpu.VMEM):
    return pl.BlockSpec(memory_space=memory_space)


def pack_kernel(experts, capacity, me_ref, index_ref, region_ref, table_ref, target_ref, *refs):
    blocks, place_ref, rows_ref = refs[:experts], refs[experts], refs[experts + 1]
    me = me_ref[0]
    groups = index_ref.shape[0]
    cells, width = table_ref.shape
    expert_id = iota((experts, LANES), 0)
    starts = ((expert_id ^ me) * capacity).astype(F32)
    ahead = jnp.where(iota((LANES, LANES), 0) <= iota((LANES, LANES), 1), 1.0, 0.0).astype(BF16)
    counted = jnp.zeros((experts, LANES), F32)
    places = []
    for g in range(groups):
        hot = jnp.where(region_ref[g : g + 1, :] == expert_id, 1.0, 0.0)
        upto = dot(hot.astype(BF16), ahead)
        places.append(jnp.sum(hot * (upto - 1.0 + counted + starts), axis=0, keepdims=True))
        counted = counted + jnp.broadcast_to(upto[:, LANES - 1 :], (experts, LANES))
    for g in range(groups):
        place_ref[g : g + 1, :] = places[g].astype(jnp.int32)
    place = jnp.concatenate(places, axis=1)

    step = 2
    cell_id = iota((LANES * step, LANES), 1).astype(F32)
    for g in range(0, groups, step):
        column = jnp.concatenate(
            [
                jnp.broadcast_to(index_ref[h : h + 1, :].astype(F32), (LANES, LANES)).T
                for h in range(g, g + step)
            ],
            axis=0,
        )
        picks = jnp.concatenate(
            [
                jnp.where(column == cell_id + float(LANES * t), 1.0, 0.0).astype(BF16)
                for t in range(cells // LANES)
            ],
            axis=1,
        )
        at = slice(g * LANES, (g + step) * LANES)
        rows_ref[at, :width] = dot(picks, table_ref[...]).astype(BF16)
        rows_ref[at, width:] = target_ref[at, :]

    slot_id = iota((capacity, place.shape[1]), 0).astype(F32)
    for s in range(experts):
        spread = jnp.where(place == slot_id + float(s * capacity), 1.0, 0.0).astype(BF16)
        blocks[s][...] = dot(spread, rows_ref[...]).astype(BF16)


def pack(me, index, region, table, targets, experts, capacity):
    rows, width = targets.shape
    groups = rows // LANES
    return pl.pallas_call(
        functools.partial(pack_kernel, experts, capacity),
        out_shape=[jax.ShapeDtypeStruct((capacity, 2 * width), BF16)] * experts
        + [jax.ShapeDtypeStruct((groups, LANES), jnp.int32)],
        in_specs=[whole(pltpu.SMEM)] + [whole()] * 4,
        out_specs=[whole()] * (experts + 1),
        scratch_shapes=[pltpu.VMEM((rows, 2 * width), BF16)],
        compiler_params=pltpu.CompilerParams(vmem_limit_bytes=32 * MIB),
        cost_estimate=pl.CostEstimate(
            flops=2 * rows * width * (table.shape[0] + 2 * experts * capacity),
            bytes_accessed=6 * MIB,
            transcendentals=0,
        ),
        name="pack_rows",
    )(me, index.reshape(groups, LANES), region.reshape(groups, LANES), table, targets)


def pair_kernel(one_ref, other_ref, ahead_ref, both_ref):
    both_ref[0] = one_ref[...]
    both_ref[1] = other_ref[...]


def pair(one, other, ahead):
    return pl.pallas_call(
        pair_kernel,
        out_shape=jax.ShapeDtypeStruct((2, *one.shape), one.dtype),
        in_specs=[whole()] * 2 + [whole(pl.ANY)],
        out_specs=whole(),
        compiler_params=pltpu.CompilerParams(vmem_limit_bytes=4 * MIB),
        name="pair",
    )(one, other, ahead)


def sigmoid(v):
    return 0.5 * jnp.tanh(0.5 * v) + 0.5


def expert_kernel(counts, order, first, last, *refs):
    blocks, shares, experts, steps, step_rows, relays = counts
    refs = list(refs)

    def take(n):
        got = refs[:n]
        del refs[:n]
        return got

    xs = take(blocks)
    trunk_ref, ups_near, ups_far, downs_near, downs_far = take(5)
    ups = (ups_near.at[0], ups_near.at[1], ups_far.at[0], ups_far.at[1])
    downs = (downs_near.at[0], downs_far.at[0], downs_near.at[1], downs_far.at[1])
    if not first:
        prior_ref, prior_trunk_ref = take(2)
    held = take(relays)
    if last:
        loss_refs = take(last - 1)
        (ids_ref,) = take(1)
        (acc_ref,) = take(1)
        trunk_parts = take(shares if in_turns(experts) else 1)
        (all_loss_ref,) = take(1)
    else:
        acc_ref, acc_trunk_ref, loss_ref = take(3)
        for source, copy in zip(held, take(relays)):
            copy[...] = source[...]
    x_ref, hid_ref, slope_ref = take(3)
    if last:
        acc_trunk_ref, loss_ref = take(2)

    width = trunk_ref.shape[0]
    share = ups_near.shape[2]
    block_rows = xs[0].shape[0]
    for i, ref in enumerate(xs):
        x_ref[i * block_rows : (i + 1) * block_rows, :] = ref[...]
    looped = steps > 3
    if looped and first:
        acc_ref[...] = jnp.zeros(acc_ref.shape, F32)
        acc_trunk_ref[...] = jnp.zeros(acc_trunk_ref.shape, F32)
    elif looped:
        acc_ref[...] = prior_ref[...]
        acc_trunk_ref[...] = prior_trunk_ref[...]

    def add(i, ref, source, at, value):
        if looped or i > 0:
            ref[at] += value
        elif first:
            ref[at] = value
        else:
            ref[at] = source[at] + value

    prior = None if first else prior_ref
    prior_trunk = None if first else prior_trunk_ref

    def step(i, carry):
        if looped:
            at = pl.ds(pl.multiple_of(i * step_rows, step_rows), step_rows)
        else:
            at = slice(i * step_rows, (i + 1) * step_rows)
        feats = x_ref[at, :width]
        feats_f = feats.astype(F32)
        trunk_pre = dot(feats, trunk_ref[...])
        gate = sigmoid(trunk_pre)
        act = trunk_pre * gate
        trunk_slope = gate + act * (1.0 - gate)
        out_f = feats_f + act
        out = out_f.astype(BF16)
        predicted = jnp.zeros((step_rows, width), F32)
        for j in range(shares):
            up = dot(out, ups[j][...])
            s = sigmoid(up)
            h = up * s
            slope_ref[:, j * share : (j + 1) * share] = s + h * (1.0 - s)
            h = h.astype(BF16)
            hid_ref[:, j * share : (j + 1) * share] = h
            predicted = predicted + dot(h, downs[j][...], 1, 1)
        errors = predicted - x_ref[at, width:].astype(F32)
        squares = errors * errors
        half = squares[:, :LANES]
        for k in range(1, width // LANES):
            half = half + squares[:, k * LANES : (k + 1) * LANES]
        loss_ref[pl.ds(i, 1), :] = jnp.sum(half.T, axis=0, keepdims=True) * (0.5 * loss_scale)
        scaled_f = errors * loss_scale
        scaled = scaled_f.astype(BF16)
        scaled_t = scaled_f.T.astype(BF16)
        out_t = out_f.T.astype(BF16)
        row_grad = jnp.zeros((step_rows, width), F32)
        for j in range(shares):
            part = slice(j * share, (j + 1) * share)
            add(i, acc_ref, prior, (j, 1), dot(scaled_t, hid_ref[:, part]))
            pre = (dot(scaled, downs[j][...]) * slope_ref[:, part]).astype(BF16)
            add(i, acc_ref, prior, (j, 0), dot(out_t, pre))
            row_grad = row_grad + dot(pre, ups[j][...], 1, 1)
        slope = (row_grad.astype(BF16).astype(F32) * trunk_slope).astype(BF16)
        add(i, acc_trunk_ref, prior_trunk, ..., dot(feats_f.T.astype(BF16), slope))
        return carry

    if looped:
        lax.fori_loop(0, steps, step, 0)
    else:
        for i in range(steps):
            step(i, 0)
    if last:
        all_losses = list(loss_refs) + [loss_ref]
        if not in_turns(experts):
            trunk_parts[0][...] = acc_trunk_ref[...]
            for row in range(all_loss_ref.shape[0]):
                all_loss_ref[row : row + 1, :] = loss_row(all_losses, row)
            return
        quarter = width // shares
        for j, ref in enumerate(trunk_parts):
            at = pl.multiple_of((ids_ref[1] ^ j) * quarter, quarter)
            ref[...] = acc_trunk_ref[pl.ds(at, quarter), :]
        for s in range(experts):
            all_loss_ref[s : s + 1, :] = loss_row(all_losses, order.index(s))


def in_turns(experts):
    return experts == 8


def loss_row(refs, row):
    for ref in refs:
        if row < ref.shape[0]:
            return ref[row : row + 1, :]
        row -= ref.shape[0]


def expert_call(xs, trunk_weight, weights, prior, losses, ids, order, last, relays=()):
    experts = len(order)
    block_rows = xs[0].shape[0]
    width = trunk_weight.shape[0]
    shares, share = len(weights), weights[0].shape[2]
    rows = block_rows * len(xs)
    step_rows = min(256, rows)
    steps = rows // step_rows
    first = prior is None
    acc = jax.ShapeDtypeStruct((shares, 2, width, share), F32)
    acc_trunk = jax.ShapeDtypeStruct((width, width), F32)
    loss = jax.ShapeDtypeStruct((steps, step_rows), F32)
    args = list(xs) + [trunk_weight, *weights]
    if not first:
        args += list(prior)
    args += relays
    in_specs = [whole()] * len(args)
    scratch = [
        pltpu.VMEM((rows, 2 * width), BF16),
        pltpu.VMEM((step_rows, shares * share), BF16),
        pltpu.VMEM((step_rows, shares * share), F32),
    ]
    if last:
        args += list(losses) + [ids]
        in_specs += [whole()] * len(losses) + [whole(pltpu.SMEM)]
        outs = [acc]
        if in_turns(experts):
            outs += [jax.ShapeDtypeStruct((width // shares, width), F32)] * shares
        else:
            outs += [acc_trunk]
        outs += [jax.ShapeDtypeStruct((experts * block_rows // step_rows, step_rows), F32)]
        scratch += [pltpu.VMEM(a.shape, a.dtype) for a in (acc_trunk, loss)]
    else:
        outs = [acc, acc_trunk, loss]
        outs += [jax.ShapeDtypeStruct(relay.shape, relay.dtype) for relay in relays]
    counts = (len(xs), shares, experts, steps, step_rows, len(relays))
    return pl.pallas_call(
        functools.partial(expert_kernel, counts, order, first, len(losses) + 1 if last else 0),
        out_shape=outs,
        in_specs=in_specs,
        out_specs=[whole()] * len(outs),
        scratch_shapes=scratch,
        compiler_params=pltpu.CompilerParams(vmem_limit_bytes=40 * MIB),
        cost_estimate=pl.CostEstimate(
            flops=12 * rows * width,
            bytes_accessed=rows * width,
            transcendentals=0,
        ),
        name="expert_rows",
    )(*args)


def four(refs):
    return (refs[0][...] + refs[1][...]) + (refs[2][...] + refs[3][...])


def dp_turn_kernel(q0, q1, q2, q3, loss_ref, total_ref, note_ref):
    total = four((q0, q1, q2, q3))
    total_ref[...] = total
    rows = total.shape[0]
    note_ref[:rows, :] = total
    for k in range(4):
        note_ref[rows + k : rows + k + 1, :] = loss_ref[2 * k + 1 : 2 * k + 2, :]
    note_ref[rows + 4 :, :] = jnp.zeros((4, total.shape[1]), F32)


def pair_turn_kernel(ids_ref, total_ref, got_ref, loss_ref, *outs):
    rows, width = total_ref.shape
    half = rows // 2
    at = pl.ds(pl.multiple_of((ids_ref[0] & 1) * half, half), half)
    for k, ref in enumerate(outs):
        ref[:half, :] = total_ref[at, :] + got_ref[at, :]
        ref[half : half + 1, :] = loss_ref[2 * k : 2 * k + 1, :]
        ref[half + 1 : half + 2, :] = got_ref[rows + k : rows + k + 1, :]
        ref[half + 2 :, :] = jnp.zeros((6, width), F32)


def z_turn_kernel(*refs):
    *notes, total_ref, loss_ref = refs
    half = total_ref.shape[0]
    total_ref[...] = four([note.at[:half, :] for note in notes])
    for k, note in enumerate(notes):
        loss_ref[2 * k : 2 * k + 2, :] = note[half : half + 2, :]


def join_kernel(ids_ref, own_ref, other_ref, both_ref):
    half = own_ref.shape[0]
    core = ids_ref[0] & 1
    both_ref[pl.ds(pl.multiple_of(core * half, half), half), :] = own_ref[...]
    both_ref[pl.ds(pl.multiple_of((1 - core) * half, half), half), :] = other_ref[...]


def assemble_kernel(ids_ref, *refs):
    *held, _, trunk_ref = refs
    for j, ref in enumerate(held):
        rows = ref.shape[0]
        at = pl.multiple_of((ids_ref[1] ^ j) * rows, rows)
        trunk_ref[pl.ds(at, rows), :] = ref[...]


def turn(kernel, held, shapes, name, ids=None):
    first = [] if ids is None else [ids]
    width = held[0].shape[1]
    return pl.pallas_call(
        kernel,
        out_shape=[jax.ShapeDtypeStruct((rows, width), F32) for rows in shapes],
        in_specs=[whole(pltpu.SMEM)] * len(first) + [whole()] * len(held),
        out_specs=[whole()] * len(shapes),
        compiler_params=pltpu.CompilerParams(vmem_limit_bytes=4 * MIB),
        name=name,
    )(*first, *held)


def send_kernel(acc_ref, ahead_ref, up_ref, down_ref):
    for k in range(2):
        up_ref[k] = acc_ref[2 * k + 1, 0].astype(BF16)
        down_ref[k] = acc_ref[k + 2, 1].astype(BF16)


def pass_on_kernel(acc_ref, got_up_ref, got_down_ref, ahead_ref, up_ref, down_ref):
    up_ref[...] = (acc_ref[2, 0] + got_up_ref[1].astype(F32)).astype(BF16)
    down_ref[...] = (acc_ref[1, 1] + got_down_ref[1].astype(F32)).astype(BF16)


def messages(kernel, held, ahead, shape, name):
    return pl.pallas_call(
        kernel,
        out_shape=[jax.ShapeDtypeStruct(shape, BF16)] * 2,
        in_specs=[whole()] * len(held) + [whole(pl.ANY)],
        out_specs=[whole()] * 2,
        compiler_params=pltpu.CompilerParams(vmem_limit_bytes=16 * MIB),
        name=name,
    )(*held, ahead)


def row_loss_kernel(place_ref, loss_ref, row_loss_ref):
    experts, capacity = loss_ref.shape
    loss = loss_ref[...]
    for g in range(place_ref.shape[0]):
        place = place_ref[g : g + 1, :]
        block = place // capacity
        slot = place - block * capacity
        picks = jnp.where(iota((capacity, LANES), 0) == slot, 1.0, 0.0)
        found = lax.dot_general(
            loss,
            picks,
            (((1,), (0,)), ((), ())),
            precision=lax.Precision.HIGHEST,
            preferred_element_type=F32,
        )
        mine = jnp.where(iota((experts, LANES), 0) == block, found, 0.0)
        row_loss_ref[g : g + 1, :] = jnp.sum(mine, axis=0, keepdims=True)


def loss_by_row(place, loss):
    return pl.pallas_call(
        row_loss_kernel,
        out_shape=jax.ShapeDtypeStruct(place.shape, F32),
        in_specs=[whole()] * 2,
        out_specs=whole(),
        compiler_params=pltpu.CompilerParams(vmem_limit_bytes=16 * MIB),
        name="row_loss",
    )(place, loss)


def adam_update(params, first, second, grads):
    first_new = beta_one * first + (1.0 - beta_one) * grads
    second_new = beta_two * second + (1.0 - beta_two) * grads * grads
    first_hat = first_new / (1.0 - beta_one**adam_step)
    second_hat = second_new / (1.0 - beta_two**adam_step)
    return (
        params - learn_rate * first_hat / (jnp.sqrt(second_hat) + adam_eps),
        first_new,
        second_new,
    )


def adam_kernel(*refs):
    params_ref, first_ref, second_ref, acc_ref, *got = refs[:8]
    *outs, done_ref = refs[8:]
    for k in range(2):
        grads = acc_ref[0, k] + got[k][0].astype(F32) + got[2 + k][...].astype(F32)
        news = adam_update(params_ref[0, k], first_ref[0, k], second_ref[0, k], grads)
        for ref, new in zip(outs, news):
            ref[0, k] = new
    done_ref[...] = jnp.zeros(done_ref.shape, F32)


def adam(params, first, second, acc, got):
    shape = jax.ShapeDtypeStruct(params.shape, F32)
    return pl.pallas_call(
        adam_kernel,
        out_shape=[shape] * 3 + [jax.ShapeDtypeStruct((8, LANES), F32)],
        in_specs=[whole()] * 8,
        out_specs=[whole()] * 4,
        compiler_params=pltpu.CompilerParams(vmem_limit_bytes=24 * MIB),
        cost_estimate=pl.CostEstimate(
            flops=20 * params.size, bytes_accessed=8 * params.size, transcendentals=params.size
        ),
        name="adam",
    )(params, first, second, acc, *got)


def swap(value, axis, s):
    if s == 0:
        return value
    return lax.ppermute(value, axis, [(i, i ^ s) for i in range(lax.axis_size(axis))])


def on_device(
    cell_table,
    sample_index,
    region,
    targets,
    trunk_weight,
    expert_params,
    first_moment,
    second_moment,
):
    rows = sample_index.shape[0]
    width = cell_table.shape[1]
    experts = lax.axis_size("expert")
    replicas = lax.axis_size("dp")
    capacity = 2 * rows // experts
    me = lax.axis_index("expert").astype(jnp.int32).reshape(1)
    ids = jnp.concatenate([me, lax.axis_index("dp").astype(jnp.int32).reshape(1)])

    up, down = expert_params[0, 0].astype(BF16), expert_params[0, 1].astype(BF16)
    near_up, near_down = swap(up, "dp", 1), swap(down, "dp", 2)
    *blocks, place = pack(me, sample_index, region[:, 0], cell_table, targets, experts, capacity)
    ups, downs = pair(up, near_up, place), pair(down, near_down, place)
    weights = [ups, swap(ups, "dp", 2), downs, swap(downs, "dp", 1)]
    if in_turns(experts):
        batches, later = ((0, 1), (4, 5), (2,), (3,), (6,), (7,)), (7,)
    else:
        batches, later = (range(experts // 2), range(experts // 2, experts)), ()
    order = [s for batch in batches for s in batch]
    arrived = {s: swap(blocks[s], "expert", s) for s in order if s not in later}
    prior, losses = None, []
    for k, batch in enumerate(batches):
        last = k == len(batches) - 1
        relays = [blocks[s] for s in later] if k == 0 else []
        outs = expert_call(
            [arrived[s] for s in batch], trunk_weight, weights, prior, losses, ids, order, last, relays
        )
        if not last:
            prior = outs[:2]
            losses.append(outs[2])
            for s, block in zip(later, outs[3:]):
                arrived[s] = swap(block, "expert", s)
    acc, *parts, losses = outs

    def send(ahead):
        up, down = messages(send_kernel, [acc], ahead, (2, *acc.shape[2:]), "send")
        return swap(up, "dp", 1), swap(down, "dp", 2)

    def pass_on(got, ahead):
        up, down = messages(pass_on_kernel, [acc, *got], ahead, acc.shape[2:], "pass_on")
        return swap(up, "dp", 2), swap(down, "dp", 1)

    if in_turns(experts):
        quarter = width // replicas
        parts = [swap(part, "dp", j) for j, part in enumerate(parts)]
        total, note = turn(dp_turn_kernel, parts + [losses], (quarter, quarter + 8), "dp_turn")
        got = send(total)
        notes = turn(
            pair_turn_kernel,
            [total, swap(note, "expert", 1), losses],
            (quarter // 2 + 8,) * 4,
            "pair_turn",
            ids,
        )
        notes = [swap(note, "expert", 2 * k) for k, note in enumerate(notes)]
        total, loss = turn(z_turn_kernel, notes, (quarter // 2, experts), "z_turn")
        more_up, more_down = pass_on(got, total)
        (total,) = turn(join_kernel, [total, swap(total, "expert", 1)], (quarter,), "join", ids)
        parts = [swap(total, "dp", j) for j in range(replicas)]
        *news, done = adam(
            expert_params, first_moment, second_moment, acc, [*got, more_up, more_down]
        )
        (trunk_grad,) = turn(assemble_kernel, parts + [done], (width,), "assemble_trunk", ids)
    else:
        got = send(losses)
        more_up, more_down = pass_on(got, losses)
        *news, _ = adam(
            expert_params, first_moment, second_moment, acc, [*got, more_up, more_down]
        )
        trunk_grad = lax.psum(parts[0], ("dp", "expert"))
        places = jnp.arange(experts, dtype=jnp.int32) ^ me
        losses = losses.reshape(experts, capacity)[places]
        loss = lax.all_to_all(losses, "expert", split_axis=0, concat_axis=0, tiled=True)[places]
    row_loss = loss_by_row(place, loss)

    return (trunk_grad, row_loss.reshape(rows), *news)


def solution(mesh):
    placed = (
        P(("dp", "expert"), None),
        P(("dp", "expert")),
        P(("dp", "expert"), None),
        P(("dp", "expert"), None),
        P(),
        P("expert", None, None, "dp"),
        P("expert", None, None, "dp"),
        P("expert", None, None, "dp"),
    )
    return jax.shard_map(
        on_device,
        mesh=mesh,
        in_specs=placed,
        out_specs=(
            P(),
            P(("dp", "expert")),
            P("expert", None, None, "dp"),
            P("expert", None, None, "dp"),
            P("expert", None, None, "dp"),
        ),
        check_vma=False,
    )
```

```python
import functools

import jax
import jax.numpy as jnp
from jax import lax
from jax.experimental import pallas as pl
from jax.experimental.pallas import tpu as pltpu
from jax.sharding import PartitionSpec as P

loss_scale = 1.0 / 32.0
beta_one = 0.9
beta_two = 0.999
learn_rate = 0.05
adam_eps = 1e-08
adam_step = 10

LANES = 128
F32 = jnp.float32
BF16 = jnp.bfloat16
MIB = 1 << 20


def iota(shape, dim):
    return lax.broadcasted_iota(jnp.int32, shape, dim)


def dot(a, b, ca=1, cb=0):
    return lax.dot_general(a, b, (((ca,), (cb,)), ((), ())), preferred_element_type=F32)


def whole(memory_space=pltpu.VMEM):
    return pl.BlockSpec(memory_space=memory_space)


def pack_kernel(experts, capacity, me_ref, index_ref, region_ref, table_ref, target_ref, *refs):
    blocks, place_ref, rows_ref = refs[:experts], refs[experts], refs[experts + 1]
    me = me_ref[0]
    groups = index_ref.shape[0]
    cells, width = table_ref.shape
    expert_id = iota((experts, LANES), 0)
    starts = ((expert_id ^ me) * capacity).astype(F32)
    ahead = jnp.where(iota((LANES, LANES), 0) <= iota((LANES, LANES), 1), 1.0, 0.0).astype(BF16)
    counted = jnp.zeros((experts, LANES), F32)
    places = []
    for g in range(groups):
        hot = jnp.where(region_ref[g : g + 1, :] == expert_id, 1.0, 0.0)
        upto = dot(hot.astype(BF16), ahead)
        places.append(jnp.sum(hot * (upto - 1.0 + counted + starts), axis=0, keepdims=True))
        counted = counted + jnp.broadcast_to(upto[:, LANES - 1 :], (experts, LANES))
    for g in range(groups):
        place_ref[g : g + 1, :] = places[g].astype(jnp.int32)
    place = jnp.concatenate(places, axis=1)

    step = 2
    cell_id = iota((LANES * step, LANES), 1).astype(F32)
    for g in range(0, groups, step):
        column = jnp.concatenate(
            [
                jnp.broadcast_to(index_ref[h : h + 1, :].astype(F32), (LANES, LANES)).T
                for h in range(g, g + step)
            ],
            axis=0,
        )
        picks = jnp.concatenate(
            [
                jnp.where(column == cell_id + float(LANES * t), 1.0, 0.0).astype(BF16)
                for t in range(cells // LANES)
            ],
            axis=1,
        )
        at = slice(g * LANES, (g + step) * LANES)
        rows_ref[at, :width] = dot(picks, table_ref[...]).astype(BF16)
        rows_ref[at, width:] = target_ref[at, :]

    slot_id = iota((capacity, place.shape[1]), 0).astype(F32)
    for s in range(experts):
        spread = jnp.where(place == slot_id + float(s * capacity), 1.0, 0.0).astype(BF16)
        blocks[s][...] = dot(spread, rows_ref[...]).astype(BF16)


def pack(me, index, region, table, targets, experts, capacity):
    rows, width = targets.shape
    groups = rows // LANES
    return pl.pallas_call(
        functools.partial(pack_kernel, experts, capacity),
        out_shape=[jax.ShapeDtypeStruct((capacity, 2 * width), BF16)] * experts
        + [jax.ShapeDtypeStruct((groups, LANES), jnp.int32)],
        in_specs=[whole(pltpu.SMEM)] + [whole()] * 4,
        out_specs=[whole()] * (experts + 1),
        scratch_shapes=[pltpu.VMEM((rows, 2 * width), BF16)],
        compiler_params=pltpu.CompilerParams(vmem_limit_bytes=20 * MIB),
        cost_estimate=pl.CostEstimate(
            flops=2 * rows * width * (table.shape[0] + 2 * experts * capacity),
            bytes_accessed=6 * MIB,
            transcendentals=0,
        ),
        name="pack_rows",
    )(me, index.reshape(groups, LANES), region.reshape(groups, LANES), table, targets)


def pair_kernel(one_ref, other_ref, ahead_ref, both_ref):
    both_ref[0] = one_ref[...]
    both_ref[1] = other_ref[...]


def pair(one, other, ahead):
    return pl.pallas_call(
        pair_kernel,
        out_shape=jax.ShapeDtypeStruct((2, *one.shape), one.dtype),
        in_specs=[whole()] * 2 + [whole(pl.ANY)],
        out_specs=whole(),
        compiler_params=pltpu.CompilerParams(vmem_limit_bytes=4 * MIB),
        name="pair",
    )(one, other, ahead)


def sigmoid(v):
    return 0.5 * jnp.tanh(0.5 * v) + 0.5


def expert_kernel(counts, order, first, last, *refs):
    blocks, shares, experts, steps, step_rows, relays = counts
    refs = list(refs)

    def take(n):
        got = refs[:n]
        del refs[:n]
        return got

    xs = take(blocks)
    trunk_ref, ups_near, ups_far, downs_near, downs_far = take(5)
    ups = (ups_near.at[0], ups_near.at[1], ups_far.at[0], ups_far.at[1])
    downs = (downs_near.at[0], downs_far.at[0], downs_near.at[1], downs_far.at[1])
    if not first:
        prior_ref, prior_trunk_ref = take(2)
    held = take(relays)
    if last:
        loss_refs = take(last - 1)
        (ids_ref,) = take(1)
        (acc_ref,) = take(1)
        trunk_parts = take(shares if in_turns(experts) else 1)
        (all_loss_ref,) = take(1)
    else:
        acc_ref, acc_trunk_ref, loss_ref = take(3)
        for source, copy in zip(held, take(relays)):
            copy[...] = source[...]
    x_ref, hid_ref, slope_ref = take(3)
    if last:
        acc_trunk_ref, loss_ref = take(2)

    width = trunk_ref.shape[0]
    share = ups_near.shape[2]
    block_rows = xs[0].shape[0]
    for i, ref in enumerate(xs):
        x_ref[i * block_rows : (i + 1) * block_rows, :] = ref[...]
    looped = steps > 3
    if looped and first:
        acc_ref[...] = jnp.zeros(acc_ref.shape, F32)
        acc_trunk_ref[...] = jnp.zeros(acc_trunk_ref.shape, F32)
    elif looped:
        acc_ref[...] = prior_ref[...]
        acc_trunk_ref[...] = prior_trunk_ref[...]

    def add(i, ref, source, at, value):
        if looped or i > 0:
            ref[at] += value
        elif first:
            ref[at] = value
        else:
            ref[at] = source[at] + value

    prior = None if first else prior_ref
    prior_trunk = None if first else prior_trunk_ref

    def step(i, carry):
        if looped:
            at = pl.ds(pl.multiple_of(i * step_rows, step_rows), step_rows)
        else:
            at = slice(i * step_rows, (i + 1) * step_rows)
        feats = x_ref[at, :width]
        feats_f = feats.astype(F32)
        trunk_pre = dot(feats, trunk_ref[...])
        gate = sigmoid(trunk_pre)
        act = trunk_pre * gate
        trunk_slope = gate + act * (1.0 - gate)
        out_f = feats_f + act
        out = out_f.astype(BF16)
        predicted = jnp.zeros((step_rows, width), F32)
        for j in range(shares):
            up = dot(out, ups[j][...])
            s = sigmoid(up)
            h = up * s
            slope_ref[:, j * share : (j + 1) * share] = s + h * (1.0 - s)
            h = h.astype(BF16)
            hid_ref[:, j * share : (j + 1) * share] = h
            predicted = predicted + dot(h, downs[j][...], 1, 1)
        errors = predicted - x_ref[at, width:].astype(F32)
        squares = errors * errors
        half = squares[:, :LANES]
        for k in range(1, width // LANES):
            half = half + squares[:, k * LANES : (k + 1) * LANES]
        loss_ref[pl.ds(i, 1), :] = jnp.sum(half.T, axis=0, keepdims=True) * (0.5 * loss_scale)
        scaled_f = errors * loss_scale
        scaled = scaled_f.astype(BF16)
        scaled_t = scaled_f.T.astype(BF16)
        out_t = out_f.T.astype(BF16)
        row_grad = jnp.zeros((step_rows, width), F32)
        for j in range(shares):
            part = slice(j * share, (j + 1) * share)
            add(i, acc_ref, prior, (j, 1), dot(scaled_t, hid_ref[:, part]))
            pre = (dot(scaled, downs[j][...]) * slope_ref[:, part]).astype(BF16)
            add(i, acc_ref, prior, (j, 0), dot(out_t, pre))
            row_grad = row_grad + dot(pre, ups[j][...], 1, 1)
        slope = (row_grad.astype(BF16).astype(F32) * trunk_slope).astype(BF16)
        add(i, acc_trunk_ref, prior_trunk, ..., dot(feats_f.T.astype(BF16), slope))
        return carry

    if looped:
        lax.fori_loop(0, steps, step, 0)
    else:
        for i in range(steps):
            step(i, 0)
    if last:
        all_losses = list(loss_refs) + [loss_ref]
        if not in_turns(experts):
            trunk_parts[0][...] = acc_trunk_ref[...]
            for row in range(all_loss_ref.shape[0]):
                all_loss_ref[row : row + 1, :] = loss_row(all_losses, row)
            return
        quarter = width // shares
        for j, ref in enumerate(trunk_parts):
            at = pl.multiple_of((ids_ref[1] ^ j) * quarter, quarter)
            ref[...] = acc_trunk_ref[pl.ds(at, quarter), :]
        for s in range(experts):
            all_loss_ref[s : s + 1, :] = loss_row(all_losses, order.index(s))


def in_turns(experts):
    return experts == 8


def loss_row(refs, row):
    for ref in refs:
        if row < ref.shape[0]:
            return ref[row : row + 1, :]
        row -= ref.shape[0]


def expert_call(xs, trunk_weight, weights, prior, losses, ids, order, last, relays=()):
    experts = len(order)
    block_rows = xs[0].shape[0]
    width = trunk_weight.shape[0]
    shares, share = len(weights), weights[0].shape[2]
    rows = block_rows * len(xs)
    step_rows = min(256, rows)
    steps = rows // step_rows
    first = prior is None
    acc = jax.ShapeDtypeStruct((shares, 2, width, share), F32)
    acc_trunk = jax.ShapeDtypeStruct((width, width), F32)
    loss = jax.ShapeDtypeStruct((steps, step_rows), F32)
    args = list(xs) + [trunk_weight, *weights]
    if not first:
        args += list(prior)
    args += relays
    in_specs = [whole()] * len(args)
    scratch = [
        pltpu.VMEM((rows, 2 * width), BF16),
        pltpu.VMEM((step_rows, shares * share), BF16),
        pltpu.VMEM((step_rows, shares * share), F32),
    ]
    if last:
        args += list(losses) + [ids]
        in_specs += [whole()] * len(losses) + [whole(pltpu.SMEM)]
        outs = [acc]
        if in_turns(experts):
            outs += [jax.ShapeDtypeStruct((width // shares, width), F32)] * shares
        else:
            outs += [acc_trunk]
        outs += [jax.ShapeDtypeStruct((experts * block_rows // step_rows, step_rows), F32)]
        scratch += [pltpu.VMEM(a.shape, a.dtype) for a in (acc_trunk, loss)]
    else:
        outs = [acc, acc_trunk, loss]
        outs += [jax.ShapeDtypeStruct(relay.shape, relay.dtype) for relay in relays]
    counts = (len(xs), shares, experts, steps, step_rows, len(relays))
    return pl.pallas_call(
        functools.partial(expert_kernel, counts, order, first, len(losses) + 1 if last else 0),
        out_shape=outs,
        in_specs=in_specs,
        out_specs=[whole()] * len(outs),
        scratch_shapes=scratch,
        compiler_params=pltpu.CompilerParams(vmem_limit_bytes=24 * MIB),
        cost_estimate=pl.CostEstimate(
            flops=12 * rows * width,
            bytes_accessed=rows * width,
            transcendentals=0,
        ),
        name="expert_rows",
    )(*args)


def four(refs):
    return (refs[0][...] + refs[1][...]) + (refs[2][...] + refs[3][...])


def dp_turn_kernel(q0, q1, q2, q3, loss_ref, total_ref, note_ref):
    total = four((q0, q1, q2, q3))
    total_ref[...] = total
    rows = total.shape[0]
    note_ref[:rows, :] = total
    for k in range(4):
        note_ref[rows + k : rows + k + 1, :] = loss_ref[2 * k + 1 : 2 * k + 2, :]
    note_ref[rows + 4 :, :] = jnp.zeros((4, total.shape[1]), F32)


def pair_turn_kernel(total_ref, got_ref, loss_ref, *outs):
    rows, width = total_ref.shape
    total = total_ref[...] + got_ref[:rows, :]
    for k, ref in enumerate(outs):
        ref[:rows, :] = total
        ref[rows : rows + 1, :] = loss_ref[2 * k : 2 * k + 1, :]
        ref[rows + 1 : rows + 2, :] = got_ref[rows + k : rows + k + 1, :]
        ref[rows + 2 :, :] = jnp.zeros((6, width), F32)


def z_turn_kernel(*refs):
    *notes, total_ref, loss_ref = refs
    rows = total_ref.shape[0]
    total_ref[...] = four([note.at[:rows, :] for note in notes])
    for k, note in enumerate(notes):
        loss_ref[2 * k : 2 * k + 2, :] = note[rows : rows + 2, :]


def assemble_kernel(ids_ref, *refs):
    *held, _, trunk_ref = refs
    for j, ref in enumerate(held):
        rows = ref.shape[0]
        at = pl.multiple_of((ids_ref[1] ^ j) * rows, rows)
        trunk_ref[pl.ds(at, rows), :] = ref[...]


def turn(kernel, held, shapes, name, ids=None):
    first = [] if ids is None else [ids]
    width = held[0].shape[1]
    return pl.pallas_call(
        kernel,
        out_shape=[jax.ShapeDtypeStruct((rows, width), F32) for rows in shapes],
        in_specs=[whole(pltpu.SMEM)] * len(first) + [whole()] * len(held),
        out_specs=[whole()] * len(shapes),
        compiler_params=pltpu.CompilerParams(vmem_limit_bytes=4 * MIB),
        name=name,
    )(*first, *held)


def send_kernel(acc_ref, ahead_ref, up_ref, down_ref):
    for k in range(2):
        up_ref[k] = acc_ref[2 * k + 1, 0].astype(BF16)
        down_ref[k] = acc_ref[k + 2, 1].astype(BF16)


def pass_on_kernel(acc_ref, got_up_ref, got_down_ref, ahead_ref, up_ref, down_ref):
    up_ref[...] = (acc_ref[2, 0] + got_up_ref[1].astype(F32)).astype(BF16)
    down_ref[...] = (acc_ref[1, 1] + got_down_ref[1].astype(F32)).astype(BF16)


def messages(kernel, held, ahead, shape, name):
    return pl.pallas_call(
        kernel,
        out_shape=[jax.ShapeDtypeStruct(shape, BF16)] * 2,
        in_specs=[whole()] * len(held) + [whole(pl.ANY)],
        out_specs=[whole()] * 2,
        compiler_params=pltpu.CompilerParams(vmem_limit_bytes=16 * MIB),
        name=name,
    )(*held, ahead)


def row_loss_kernel(place_ref, loss_ref, row_loss_ref):
    experts, capacity = loss_ref.shape
    loss = loss_ref[...]
    for g in range(place_ref.shape[0]):
        place = place_ref[g : g + 1, :]
        block = place // capacity
        slot = place - block * capacity
        picks = jnp.where(iota((capacity, LANES), 0) == slot, 1.0, 0.0)
        found = lax.dot_general(
            loss,
            picks,
            (((1,), (0,)), ((), ())),
            precision=lax.Precision.HIGHEST,
            preferred_element_type=F32,
        )
        mine = jnp.where(iota((experts, LANES), 0) == block, found, 0.0)
        row_loss_ref[g : g + 1, :] = jnp.sum(mine, axis=0, keepdims=True)


def loss_by_row(place, loss):
    return pl.pallas_call(
        row_loss_kernel,
        out_shape=jax.ShapeDtypeStruct(place.shape, F32),
        in_specs=[whole()] * 2,
        out_specs=whole(),
        compiler_params=pltpu.CompilerParams(vmem_limit_bytes=16 * MIB),
        name="row_loss",
    )(place, loss)


def adam_update(params, first, second, grads):
    first_new = beta_one * first + (1.0 - beta_one) * grads
    second_new = beta_two * second + (1.0 - beta_two) * grads * grads
    first_hat = first_new / (1.0 - beta_one**adam_step)
    second_hat = second_new / (1.0 - beta_two**adam_step)
    return (
        params - learn_rate * first_hat / (jnp.sqrt(second_hat) + adam_eps),
        first_new,
        second_new,
    )


def adam_kernel(*refs):
    params_ref, first_ref, second_ref, acc_ref, *got = refs[:8]
    *outs, done_ref = refs[8:]
    for k in range(2):
        grads = acc_ref[0, k] + got[k][0].astype(F32) + got[2 + k][...].astype(F32)
        news = adam_update(params_ref[0, k], first_ref[0, k], second_ref[0, k], grads)
        for ref, new in zip(outs, news):
            ref[0, k] = new
    done_ref[...] = jnp.zeros(done_ref.shape, F32)


def adam(params, first, second, acc, got):
    shape = jax.ShapeDtypeStruct(params.shape, F32)
    return pl.pallas_call(
        adam_kernel,
        out_shape=[shape] * 3 + [jax.ShapeDtypeStruct((8, LANES), F32)],
        in_specs=[whole()] * 8,
        out_specs=[whole()] * 4,
        compiler_params=pltpu.CompilerParams(vmem_limit_bytes=24 * MIB),
        cost_estimate=pl.CostEstimate(
            flops=20 * params.size, bytes_accessed=8 * params.size, transcendentals=params.size
        ),
        name="adam",
    )(params, first, second, acc, *got)


def swap(value, axis, s):
    if s == 0:
        return value
    return lax.ppermute(value, axis, [(i, i ^ s) for i in range(lax.axis_size(axis))])


def on_device(
    cell_table,
    sample_index,
    region,
    targets,
    trunk_weight,
    expert_params,
    first_moment,
    second_moment,
):
    rows = sample_index.shape[0]
    width = cell_table.shape[1]
    experts = lax.axis_size("expert")
    replicas = lax.axis_size("dp")
    capacity = 2 * rows // experts
    me = lax.axis_index("expert").astype(jnp.int32).reshape(1)
    ids = jnp.concatenate([me, lax.axis_index("dp").astype(jnp.int32).reshape(1)])

    up, down = expert_params[0, 0].astype(BF16), expert_params[0, 1].astype(BF16)
    near_up, near_down = swap(up, "dp", 1), swap(down, "dp", 2)
    *blocks, place = pack(me, sample_index, region[:, 0], cell_table, targets, experts, capacity)
    ups, downs = pair(up, near_up, place), pair(down, near_down, place)
    weights = [ups, swap(ups, "dp", 2), downs, swap(downs, "dp", 1)]
    if in_turns(experts):
        batches, later = ((0, 1), (4, 5), (2,), (3,), (6,), (7,)), (6, 7)
    else:
        batches, later = (range(experts // 2), range(experts // 2, experts)), ()
    order = [s for batch in batches for s in batch]
    arrived = {s: swap(blocks[s], "expert", s) for s in order if s not in later}
    prior, losses = None, []
    for k, batch in enumerate(batches):
        last = k == len(batches) - 1
        relays = [blocks[s] for s in later] if k == 0 else []
        outs = expert_call(
            [arrived[s] for s in batch], trunk_weight, weights, prior, losses, ids, order, last, relays
        )
        if not last:
            prior = outs[:2]
            losses.append(outs[2])
            for s, block in zip(later, outs[3:]):
                arrived[s] = swap(block, "expert", s)
    acc, *parts, losses = outs

    def send(ahead):
        up, down = messages(send_kernel, [acc], ahead, (2, *acc.shape[2:]), "send")
        return swap(up, "dp", 1), swap(down, "dp", 2)

    def pass_on(got, ahead):
        up, down = messages(pass_on_kernel, [acc, *got], ahead, acc.shape[2:], "pass_on")
        return swap(up, "dp", 2), swap(down, "dp", 1)

    if in_turns(experts):
        quarter = width // replicas
        parts = [swap(part, "dp", j) for j, part in enumerate(parts)]
        total, note = turn(dp_turn_kernel, parts + [losses], (quarter, quarter + 8), "dp_turn")
        got = send(total)
        notes = turn(
            pair_turn_kernel,
            [total, swap(note, "expert", 1), losses],
            (quarter + 8,) * 4,
            "pair_turn",
        )
        notes = [swap(note, "expert", 2 * k) for k, note in enumerate(notes)]
        total, loss = turn(z_turn_kernel, notes, (quarter, experts), "z_turn")
        more_up, more_down = pass_on(got, total)
        parts = [swap(total, "dp", j) for j in range(replicas)]
        *news, done = adam(
            expert_params, first_moment, second_moment, acc, [*got, more_up, more_down]
        )
        (trunk_grad,) = turn(assemble_kernel, parts + [done], (width,), "assemble_trunk", ids)
    else:
        got = send(losses)
        more_up, more_down = pass_on(got, losses)
        *news, _ = adam(
            expert_params, first_moment, second_moment, acc, [*got, more_up, more_down]
        )
        trunk_grad = lax.psum(parts[0], ("dp", "expert"))
        places = jnp.arange(experts, dtype=jnp.int32) ^ me
        losses = losses.reshape(experts, capacity)[places]
        loss = lax.all_to_all(losses, "expert", split_axis=0, concat_axis=0, tiled=True)[places]
    row_loss = loss_by_row(place, loss)

    return (trunk_grad, row_loss.reshape(rows), *news)


def solution(mesh):
    placed = (
        P(("dp", "expert"), None),
        P(("dp", "expert")),
        P(("dp", "expert"), None),
        P(("dp", "expert"), None),
        P(),
        P("expert", None, None, "dp"),
        P("expert", None, None, "dp"),
        P("expert", None, None, "dp"),
    )
    return jax.shard_map(
        on_device,
        mesh=mesh,
        in_specs=placed,
        out_specs=(
            P(),
            P(("dp", "expert")),
            P("expert", None, None, "dp"),
            P("expert", None, None, "dp"),
            P("expert", None, None, "dp"),
        ),
        check_vma=False,
    )
```

```python
import functools

import jax
import jax.numpy as jnp
from jax import lax
from jax.experimental import pallas as pl
from jax.experimental.pallas import tpu as pltpu
from jax.sharding import PartitionSpec as P

loss_scale = 1.0 / 32.0
beta_one = 0.9
beta_two = 0.999
learn_rate = 0.05
adam_eps = 1e-08
adam_step = 10

LANES = 128
F32 = jnp.float32
BF16 = jnp.bfloat16
MIB = 1 << 20
LOSSES = 256


def iota(shape, dim):
    return lax.broadcasted_iota(jnp.int32, shape, dim)


def dot(a, b, ca=1, cb=0):
    return lax.dot_general(a, b, (((ca,), (cb,)), ((), ())), preferred_element_type=F32)


def whole(memory_space=pltpu.VMEM):
    return pl.BlockSpec(memory_space=memory_space)


def pack_kernel(experts, capacity, me_ref, index_ref, region_ref, table_ref, target_ref, *refs):
    blocks, place_ref, rows_ref = refs[:experts], refs[experts], refs[experts + 1]
    me = me_ref[0]
    groups = index_ref.shape[0]
    cells, width = table_ref.shape
    expert_id = iota((experts, LANES), 0)
    starts = ((expert_id ^ me) * capacity).astype(F32)
    ahead = jnp.where(iota((LANES, LANES), 0) <= iota((LANES, LANES), 1), 1.0, 0.0).astype(BF16)
    counted = jnp.zeros((experts, LANES), F32)
    places = []
    for g in range(groups):
        hot = jnp.where(region_ref[g : g + 1, :] == expert_id, 1.0, 0.0)
        upto = dot(hot.astype(BF16), ahead)
        places.append(jnp.sum(hot * (upto - 1.0 + counted + starts), axis=0, keepdims=True))
        counted = counted + jnp.broadcast_to(upto[:, LANES - 1 :], (experts, LANES))
    for g in range(groups):
        place_ref[g : g + 1, :] = places[g].astype(jnp.int32)
    place = jnp.concatenate(places, axis=1)

    step = 2
    cell_id = iota((LANES * step, LANES), 1).astype(F32)
    for g in range(0, groups, step):
        column = jnp.concatenate(
            [
                jnp.broadcast_to(index_ref[h : h + 1, :].astype(F32), (LANES, LANES)).T
                for h in range(g, g + step)
            ],
            axis=0,
        )
        picks = jnp.concatenate(
            [
                jnp.where(column == cell_id + float(LANES * t), 1.0, 0.0).astype(BF16)
                for t in range(cells // LANES)
            ],
            axis=1,
        )
        at = slice(g * LANES, (g + step) * LANES)
        rows_ref[at, :width] = dot(picks, table_ref[...]).astype(BF16)
        rows_ref[at, width:] = target_ref[at, :]

    slot_id = iota((capacity, place.shape[1]), 0).astype(F32)
    for s in range(experts):
        spread = jnp.where(place == slot_id + float(s * capacity), 1.0, 0.0).astype(BF16)
        blocks[s][...] = dot(spread, rows_ref[...]).astype(BF16)


def pack(me, index, region, table, targets, experts, capacity):
    rows, width = targets.shape
    groups = rows // LANES
    return pl.pallas_call(
        functools.partial(pack_kernel, experts, capacity),
        out_shape=[jax.ShapeDtypeStruct((capacity, 2 * width), BF16)] * experts
        + [jax.ShapeDtypeStruct((groups, LANES), jnp.int32)],
        in_specs=[whole(pltpu.SMEM)] + [whole()] * 4,
        out_specs=[whole()] * (experts + 1),
        scratch_shapes=[pltpu.VMEM((rows, 2 * width), BF16)],
        compiler_params=pltpu.CompilerParams(vmem_limit_bytes=24 * MIB),
        cost_estimate=pl.CostEstimate(
            flops=2 * rows * width * (table.shape[0] + 2 * experts * capacity),
            bytes_accessed=6 * MIB,
            transcendentals=0,
        ),
        name="pack_rows",
    )(me, index.reshape(groups, LANES), region.reshape(groups, LANES), table, targets)


def pair_kernel(one_ref, other_ref, ahead_ref, both_ref):
    both_ref[0] = one_ref[...]
    both_ref[1] = other_ref[...]


def pair(one, other, ahead):
    return pl.pallas_call(
        pair_kernel,
        out_shape=jax.ShapeDtypeStruct((2, *one.shape), one.dtype),
        in_specs=[whole()] * 2 + [whole(pl.ANY)],
        out_specs=whole(),
        compiler_params=pltpu.CompilerParams(vmem_limit_bytes=4 * MIB),
        name="pair",
    )(one, other, ahead)


def sigmoid(v):
    return 0.5 * jnp.tanh(0.5 * v) + 0.5


def expert_kernel(counts, order, first, last, *refs):
    blocks, shares, experts, steps, step_rows, relays = counts
    refs = list(refs)

    def take(n):
        got = refs[:n]
        del refs[:n]
        return got

    xs = take(blocks)
    trunk_ref, ups_near, ups_far, downs_near, downs_far = take(5)
    ups = (ups_near.at[0], ups_near.at[1], ups_far.at[0], ups_far.at[1])
    downs = (downs_near.at[0], downs_far.at[0], downs_near.at[1], downs_far.at[1])
    if not first:
        prior_ref, prior_trunk_ref = take(2)
    held = take(relays)
    if last:
        loss_refs = take(last - 1)
        (mine_ref,) = take(1)
        (acc_ref,) = take(1)
        trunk_parts = take(shares if in_turns(experts) else 1)
        (all_loss_ref,) = take(1)
    else:
        acc_ref, acc_trunk_ref, loss_ref = take(3)
        for source, copy in zip(held, take(relays)):
            copy[...] = source[...]
    x_ref, hid_ref, slope_ref = take(3)
    if last:
        acc_trunk_ref, loss_ref = take(2)

    width = trunk_ref.shape[0]
    share = ups_near.shape[2]
    block_rows = xs[0].shape[0]
    for i, ref in enumerate(xs):
        x_ref[i * block_rows : (i + 1) * block_rows, :] = ref[...]
    looped = steps > 3
    if looped and first:
        acc_ref[...] = jnp.zeros(acc_ref.shape, F32)
        acc_trunk_ref[...] = jnp.zeros(acc_trunk_ref.shape, F32)
    elif looped:
        acc_ref[...] = prior_ref[...]
        acc_trunk_ref[...] = prior_trunk_ref[...]

    def add(i, ref, source, at, value):
        if looped or i > 0:
            ref[at] += value
        elif first:
            ref[at] = value
        else:
            ref[at] = source[at] + value

    prior = None if first else prior_ref
    prior_trunk = None if first else prior_trunk_ref

    def step(i, carry):
        if looped:
            at = pl.ds(pl.multiple_of(i * step_rows, step_rows), step_rows)
        else:
            at = slice(i * step_rows, (i + 1) * step_rows)
        feats = x_ref[at, :width]
        feats_f = feats.astype(F32)
        trunk_pre = dot(feats, trunk_ref[...])
        gate = sigmoid(trunk_pre)
        act = trunk_pre * gate
        trunk_slope = gate + act * (1.0 - gate)
        out_f = feats_f + act
        out = out_f.astype(BF16)
        predicted = jnp.zeros((step_rows, width), F32)
        for j in range(shares):
            up = dot(out, ups[j][...])
            s = sigmoid(up)
            h = up * s
            slope_ref[:, j * share : (j + 1) * share] = s + h * (1.0 - s)
            h = h.astype(BF16)
            hid_ref[:, j * share : (j + 1) * share] = h
            predicted = predicted + dot(h, downs[j][...], 1, 1)
        errors = predicted - x_ref[at, width:].astype(F32)
        squares = errors * errors
        half = squares[:, :LANES]
        for k in range(1, width // LANES):
            half = half + squares[:, k * LANES : (k + 1) * LANES]
        lost = jnp.sum(half.T, axis=0, keepdims=True) * (0.5 * loss_scale)
        for k in range(step_rows // LOSSES):
            row = pl.ds(i * (step_rows // LOSSES) + k, 1)
            loss_ref[row, :] = lost[:, k * LOSSES : (k + 1) * LOSSES]
        scaled_f = errors * loss_scale
        scaled = scaled_f.astype(BF16)
        scaled_t = scaled_f.T.astype(BF16)
        out_t = out_f.T.astype(BF16)
        row_grad = jnp.zeros((step_rows, width), F32)
        for j in range(shares):
            part = slice(j * share, (j + 1) * share)
            add(i, acc_ref, prior, (j, 1), dot(scaled_t, hid_ref[:, part]))
            pre = (dot(scaled, downs[j][...]) * slope_ref[:, part]).astype(BF16)
            add(i, acc_ref, prior, (j, 0), dot(out_t, pre))
            row_grad = row_grad + dot(pre, ups[j][...], 1, 1)
        slope = (row_grad.astype(BF16).astype(F32) * trunk_slope).astype(BF16)
        add(i, acc_trunk_ref, prior_trunk, ..., dot(feats_f.T.astype(BF16), slope))
        return carry

    if looped:
        lax.fori_loop(0, steps, step, 0)
    else:
        for i in range(steps):
            step(i, 0)
    if last:
        all_losses = list(loss_refs) + [loss_ref]
        if not in_turns(experts):
            trunk_parts[0][...] = acc_trunk_ref[...]
            for row in range(all_loss_ref.shape[0]):
                all_loss_ref[row : row + 1, :] = loss_row(all_losses, row)
            return
        quarter = width // shares
        for j, ref in enumerate(trunk_parts):
            at = pl.multiple_of((mine_ref[0] ^ j) * quarter, quarter)
            ref[...] = acc_trunk_ref[pl.ds(at, quarter), :]
        for s in range(experts):
            all_loss_ref[s : s + 1, :] = loss_row(all_losses, order.index(s))


def in_turns(experts):
    return experts == 8


def loss_row(refs, row):
    for ref in refs:
        if row < ref.shape[0]:
            return ref[row : row + 1, :]
        row -= ref.shape[0]


def expert_call(xs, trunk_weight, weights, prior, losses, mine, order, last, relays=()):
    experts = len(order)
    block_rows = xs[0].shape[0]
    width = trunk_weight.shape[0]
    shares, share = len(weights), weights[0].shape[2]
    rows = block_rows * len(xs)
    step_rows = min(512, rows)
    steps = rows // step_rows
    first = prior is None
    acc = jax.ShapeDtypeStruct((shares, 2, width, share), F32)
    acc_trunk = jax.ShapeDtypeStruct((width, width), F32)
    loss = jax.ShapeDtypeStruct((rows // LOSSES, LOSSES), F32)
    args = list(xs) + [trunk_weight, *weights]
    if not first:
        args += list(prior)
    args += relays
    in_specs = [whole()] * len(args)
    scratch = [
        pltpu.VMEM((rows, 2 * width), BF16),
        pltpu.VMEM((step_rows, shares * share), BF16),
        pltpu.VMEM((step_rows, shares * share), F32),
    ]
    if last:
        args += list(losses) + [mine]
        in_specs += [whole()] * len(losses) + [whole(pltpu.SMEM)]
        outs = [acc]
        if in_turns(experts):
            outs += [jax.ShapeDtypeStruct((width // shares, width), F32)] * shares
        else:
            outs += [acc_trunk]
        outs += [jax.ShapeDtypeStruct((experts * block_rows // LOSSES, LOSSES), F32)]
        scratch += [pltpu.VMEM(a.shape, a.dtype) for a in (acc_trunk, loss)]
    else:
        outs = [acc, acc_trunk, loss]
        outs += [jax.ShapeDtypeStruct(relay.shape, relay.dtype) for relay in relays]
    counts = (len(xs), shares, experts, steps, step_rows, len(relays))
    return pl.pallas_call(
        functools.partial(expert_kernel, counts, order, first, len(losses) + 1 if last else 0),
        out_shape=outs,
        in_specs=in_specs,
        out_specs=[whole()] * len(outs),
        scratch_shapes=scratch,
        compiler_params=pltpu.CompilerParams(vmem_limit_bytes=28 * MIB),
        cost_estimate=pl.CostEstimate(
            flops=12 * rows * width,
            bytes_accessed=rows * width,
            transcendentals=0,
        ),
        name="expert_rows",
    )(*args)


def four(refs):
    return (refs[0][...] + refs[1][...]) + (refs[2][...] + refs[3][...])


def dp_turn_kernel(q0, q1, q2, q3, loss_ref, total_ref, note_ref):
    total = four((q0, q1, q2, q3))
    total_ref[...] = total
    rows = total.shape[0]
    note_ref[:rows, :] = total
    for k in range(4):
        note_ref[rows + k : rows + k + 1, :] = loss_ref[2 * k + 1 : 2 * k + 2, :]
    note_ref[rows + 4 :, :] = jnp.zeros((4, total.shape[1]), F32)


def pair_turn_kernel(me_ref, total_ref, got_ref, loss_ref, *outs):
    rows, width = total_ref.shape
    half = rows // 2
    at = pl.ds(pl.multiple_of((me_ref[0] & 1) * half, half), half)
    for k, ref in enumerate(outs):
        ref[:half, :] = total_ref[at, :] + got_ref[at, :]
        ref[half : half + 1, :] = loss_ref[2 * k : 2 * k + 1, :]
        ref[half + 1 : half + 2, :] = got_ref[rows + k : rows + k + 1, :]
        ref[half + 2 :, :] = jnp.zeros((6, width), F32)


def z_turn_kernel(*refs):
    *notes, total_ref, loss_ref = refs
    half = total_ref.shape[0]
    total_ref[...] = four([note.at[:half, :] for note in notes])
    for k, note in enumerate(notes):
        loss_ref[2 * k : 2 * k + 2, :] = note[half : half + 2, :]


def join_kernel(me_ref, own_ref, other_ref, both_ref):
    half = own_ref.shape[0]
    core = me_ref[0] & 1
    both_ref[pl.ds(pl.multiple_of(core * half, half), half), :] = own_ref[...]
    both_ref[pl.ds(pl.multiple_of((1 - core) * half, half), half), :] = other_ref[...]


def assemble_kernel(mine_ref, *refs):
    *held, _, trunk_ref = refs
    for j, ref in enumerate(held):
        rows = ref.shape[0]
        at = pl.multiple_of((mine_ref[0] ^ j) * rows, rows)
        trunk_ref[pl.ds(at, rows), :] = ref[...]


def turn(kernel, held, shapes, name, index=None):
    first = [] if index is None else [index]
    width = held[0].shape[1]
    return pl.pallas_call(
        kernel,
        out_shape=[jax.ShapeDtypeStruct((rows, width), F32) for rows in shapes],
        in_specs=[whole(pltpu.SMEM)] * len(first) + [whole()] * len(held),
        out_specs=[whole()] * len(shapes),
        compiler_params=pltpu.CompilerParams(vmem_limit_bytes=4 * MIB),
        name=name,
    )(*first, *held)


def send_kernel(acc_ref, ahead_ref, up_ref, down_ref):
    for k in range(2):
        up_ref[k] = acc_ref[2 * k + 1, 0].astype(BF16)
        down_ref[k] = acc_ref[k + 2, 1].astype(BF16)


def pass_on_kernel(acc_ref, got_up_ref, got_down_ref, ahead_ref, up_ref, down_ref):
    up_ref[...] = (acc_ref[2, 0] + got_up_ref[1].astype(F32)).astype(BF16)
    down_ref[...] = (acc_ref[1, 1] + got_down_ref[1].astype(F32)).astype(BF16)


def messages(kernel, held, ahead, shape, name):
    return pl.pallas_call(
        kernel,
        out_shape=[jax.ShapeDtypeStruct(shape, BF16)] * 2,
        in_specs=[whole()] * len(held) + [whole(pl.ANY)],
        out_specs=[whole()] * 2,
        compiler_params=pltpu.CompilerParams(vmem_limit_bytes=16 * MIB),
        name=name,
    )(*held, ahead)


def row_loss_kernel(place_ref, loss_ref, row_loss_ref):
    experts, capacity = loss_ref.shape
    loss = loss_ref[...]
    for g in range(place_ref.shape[0]):
        place = place_ref[g : g + 1, :]
        block = place // capacity
        slot = place - block * capacity
        picks = jnp.where(iota((capacity, LANES), 0) == slot, 1.0, 0.0)
        found = lax.dot_general(
            loss,
            picks,
            (((1,), (0,)), ((), ())),
            precision=lax.Precision.HIGHEST,
            preferred_element_type=F32,
        )
        mine = jnp.where(iota((experts, LANES), 0) == block, found, 0.0)
        row_loss_ref[g : g + 1, :] = jnp.sum(mine, axis=0, keepdims=True)


def loss_by_row(place, loss):
    return pl.pallas_call(
        row_loss_kernel,
        out_shape=jax.ShapeDtypeStruct(place.shape, F32),
        in_specs=[whole()] * 2,
        out_specs=whole(),
        compiler_params=pltpu.CompilerParams(vmem_limit_bytes=16 * MIB),
        name="row_loss",
    )(place, loss)


def adam_update(params, first, second, grads):
    first_new = beta_one * first + (1.0 - beta_one) * grads
    second_new = beta_two * second + (1.0 - beta_two) * grads * grads
    first_hat = first_new / (1.0 - beta_one**adam_step)
    second_hat = second_new / (1.0 - beta_two**adam_step)
    return (
        params - learn_rate * first_hat / (jnp.sqrt(second_hat) + adam_eps),
        first_new,
        second_new,
    )


def adam_kernel(*refs):
    params_ref, first_ref, second_ref, acc_ref, *got = refs[:8]
    *outs, done_ref = refs[8:]
    for k in range(2):
        grads = acc_ref[0, k] + got[k][0].astype(F32) + got[2 + k][...].astype(F32)
        news = adam_update(params_ref[0, k], first_ref[0, k], second_ref[0, k], grads)
        for ref, new in zip(outs, news):
            ref[0, k] = new
    done_ref[...] = jnp.zeros(done_ref.shape, F32)


def adam(params, first, second, acc, got):
    shape = jax.ShapeDtypeStruct(params.shape, F32)
    return pl.pallas_call(
        adam_kernel,
        out_shape=[shape] * 3 + [jax.ShapeDtypeStruct((8, LANES), F32)],
        in_specs=[whole()] * 8,
        out_specs=[whole()] * 4,
        compiler_params=pltpu.CompilerParams(vmem_limit_bytes=24 * MIB),
        cost_estimate=pl.CostEstimate(
            flops=20 * params.size, bytes_accessed=8 * params.size, transcendentals=params.size
        ),
        name="adam",
    )(params, first, second, acc, *got)


def swap(value, axis, s):
    if s == 0:
        return value
    return lax.ppermute(value, axis, [(i, i ^ s) for i in range(lax.axis_size(axis))])


def on_device(
    cell_table,
    sample_index,
    region,
    targets,
    trunk_weight,
    expert_params,
    first_moment,
    second_moment,
):
    rows = sample_index.shape[0]
    width = cell_table.shape[1]
    experts = lax.axis_size("expert")
    replicas = lax.axis_size("dp")
    capacity = 2 * rows // experts
    me = lax.axis_index("expert").astype(jnp.int32).reshape(1)
    mine = lax.axis_index("dp").astype(jnp.int32).reshape(1)

    up, down = expert_params[0, 0].astype(BF16), expert_params[0, 1].astype(BF16)
    near_up, near_down = swap(up, "dp", 1), swap(down, "dp", 2)
    *blocks, place = pack(me, sample_index, region[:, 0], cell_table, targets, experts, capacity)
    ups, downs = pair(up, near_up, place), pair(down, near_down, place)
    weights = [ups, swap(ups, "dp", 2), downs, swap(downs, "dp", 1)]
    if in_turns(experts):
        batches, later = ((0, 1), (4, 5), (2,), (3,), (6,), (7,)), (6, 7)
    else:
        batches, later = (range(experts // 2), range(experts // 2, experts)), ()
    order = [s for batch in batches for s in batch]
    arrived = {s: swap(blocks[s], "expert", s) for s in order if s not in later}
    prior, losses = None, []
    for k, batch in enumerate(batches):
        last = k == len(batches) - 1
        relays = [blocks[s] for s in later] if k == 0 else []
        outs = expert_call(
            [arrived[s] for s in batch], trunk_weight, weights, prior, losses, mine, order, last, relays
        )
        if not last:
            prior = outs[:2]
            losses.append(outs[2])
            for s, block in zip(later, outs[3:]):
                arrived[s] = swap(block, "expert", s)
    acc, *parts, losses = outs

    def send(ahead):
        up, down = messages(send_kernel, [acc], ahead, (2, *acc.shape[2:]), "send")
        return swap(up, "dp", 1), swap(down, "dp", 2)

    def pass_on(got, ahead):
        up, down = messages(pass_on_kernel, [acc, *got], ahead, acc.shape[2:], "pass_on")
        return swap(up, "dp", 2), swap(down, "dp", 1)

    if in_turns(experts):
        quarter = width // replicas
        parts = [swap(part, "dp", j) for j, part in enumerate(parts)]
        total, note = turn(dp_turn_kernel, parts + [losses], (quarter, quarter + 8), "dp_turn")
        got = send(total)
        notes = turn(
            pair_turn_kernel,
            [total, swap(note, "expert", 1), losses],
            (quarter // 2 + 8,) * 4,
            "pair_turn",
            me,
        )
        notes = [swap(note, "expert", 2 * k) for k, note in enumerate(notes)]
        total, loss = turn(z_turn_kernel, notes, (quarter // 2, experts), "z_turn")
        more_up, more_down = pass_on(got, total)
        (total,) = turn(join_kernel, [total, swap(total, "expert", 1)], (quarter,), "join", me)
        parts = [swap(total, "dp", j) for j in range(replicas)]
        *news, done = adam(
            expert_params, first_moment, second_moment, acc, [*got, more_up, more_down]
        )
        (trunk_grad,) = turn(assemble_kernel, parts + [done], (width,), "assemble_trunk", mine)
    else:
        got = send(losses)
        more_up, more_down = pass_on(got, losses)
        *news, _ = adam(
            expert_params, first_moment, second_moment, acc, [*got, more_up, more_down]
        )
        trunk_grad = lax.psum(parts[0], ("dp", "expert"))
        places = jnp.arange(experts, dtype=jnp.int32) ^ me
        losses = losses.reshape(experts, capacity)[places]
        loss = lax.all_to_all(losses, "expert", split_axis=0, concat_axis=0, tiled=True)[places]
    row_loss = loss_by_row(place, loss)

    return (trunk_grad, row_loss.reshape(rows), *news)


def solution(mesh):
    placed = (
        P(("dp", "expert"), None),
        P(("dp", "expert")),
        P(("dp", "expert"), None),
        P(("dp", "expert"), None),
        P(),
        P("expert", None, None, "dp"),
        P("expert", None, None, "dp"),
        P("expert", None, None, "dp"),
    )
    return jax.shard_map(
        on_device,
        mesh=mesh,
        in_specs=placed,
        out_specs=(
            P(),
            P(("dp", "expert")),
            P("expert", None, None, "dp"),
            P("expert", None, None, "dp"),
            P("expert", None, None, "dp"),
        ),
        check_vma=False,
    )
```

```python
import functools

import jax
import jax.numpy as jnp
from jax import lax
from jax.experimental import pallas as pl
from jax.experimental.pallas import tpu as pltpu
from jax.sharding import PartitionSpec as P

loss_scale = 1.0 / 32.0
beta_one = 0.9
beta_two = 0.999
learn_rate = 0.05
adam_eps = 1e-08
adam_step = 10

LANES = 128
F32 = jnp.float32
BF16 = jnp.bfloat16
MIB = 1 << 20
LOSSES = 256


def iota(shape, dim):
    return lax.broadcasted_iota(jnp.int32, shape, dim)


def dot(a, b, ca=1, cb=0):
    return lax.dot_general(a, b, (((ca,), (cb,)), ((), ())), preferred_element_type=F32)


def whole(memory_space=pltpu.VMEM):
    return pl.BlockSpec(memory_space=memory_space)


def pack_kernel(experts, capacity, me_ref, mine_ref, index_ref, region_ref, table_ref, target_ref, *refs):
    blocks, place_ref, rows_ref = refs[:experts], refs[experts], refs[experts + 1]
    me = me_ref[0]
    groups = index_ref.shape[0]
    cells, width = table_ref.shape
    expert_id = iota((experts, LANES), 0)
    starts = ((expert_id ^ me) * capacity).astype(F32)
    ahead = jnp.where(iota((LANES, LANES), 0) <= iota((LANES, LANES), 1), 1.0, 0.0).astype(BF16)
    counted = jnp.zeros((experts, LANES), F32)
    places = []
    for g in range(groups):
        hot = jnp.where(region_ref[g : g + 1, :] == expert_id, 1.0, 0.0)
        upto = dot(hot.astype(BF16), ahead)
        places.append(jnp.sum(hot * (upto - 1.0 + counted + starts), axis=0, keepdims=True))
        counted = counted + jnp.broadcast_to(upto[:, LANES - 1 :], (experts, LANES))
    for g in range(groups):
        place_ref[g : g + 1, :] = places[g].astype(jnp.int32)
    place = jnp.concatenate(places, axis=1)

    step = 2
    cell_id = iota((LANES * step, LANES), 1).astype(F32)
    for g in range(0, groups, step):
        column = jnp.concatenate(
            [
                jnp.broadcast_to(index_ref[h : h + 1, :].astype(F32), (LANES, LANES)).T
                for h in range(g, g + step)
            ],
            axis=0,
        )
        picks = jnp.concatenate(
            [
                jnp.where(column == cell_id + float(LANES * t), 1.0, 0.0).astype(BF16)
                for t in range(cells // LANES)
            ],
            axis=1,
        )
        at = slice(g * LANES, (g + step) * LANES)
        rows_ref[at, :width] = dot(picks, table_ref[...]).astype(BF16)
        rows_ref[at, width:] = target_ref[at, :]

    slot_id = iota((capacity, place.shape[1]), 0).astype(F32)
    for s in range(experts):
        spread = jnp.where(place == slot_id + float(s * capacity), 1.0, 0.0).astype(BF16)
        blocks[s][...] = dot(spread, rows_ref[...]).astype(BF16)


def pack(me, mine, index, region, table, targets, experts, capacity):
    rows, width = targets.shape
    groups = rows // LANES
    return pl.pallas_call(
        functools.partial(pack_kernel, experts, capacity),
        out_shape=[jax.ShapeDtypeStruct((capacity, 2 * width), BF16)] * experts
        + [jax.ShapeDtypeStruct((groups, LANES), jnp.int32)],
        in_specs=[whole(pltpu.SMEM)] * 2 + [whole()] * 4,
        out_specs=[whole()] * (experts + 1),
        scratch_shapes=[pltpu.VMEM((rows, 2 * width), BF16)],
        compiler_params=pltpu.CompilerParams(vmem_limit_bytes=24 * MIB),
        cost_estimate=pl.CostEstimate(
            flops=2 * rows * width * (table.shape[0] + 2 * experts * capacity),
            bytes_accessed=6 * MIB,
            transcendentals=0,
        ),
        name="pack_rows",
    )(me, mine, index.reshape(groups, LANES), region.reshape(groups, LANES), table, targets)


def pair_kernel(one_ref, other_ref, ahead_ref, both_ref):
    both_ref[0] = one_ref[...]
    both_ref[1] = other_ref[...]


def pair(one, other, ahead):
    return pl.pallas_call(
        pair_kernel,
        out_shape=jax.ShapeDtypeStruct((2, *one.shape), one.dtype),
        in_specs=[whole()] * 2 + [whole(pl.ANY)],
        out_specs=whole(),
        compiler_params=pltpu.CompilerParams(vmem_limit_bytes=4 * MIB),
        name="pair",
    )(one, other, ahead)


def sigmoid(v):
    return 0.5 * jnp.tanh(0.5 * v) + 0.5


def expert_kernel(counts, order, first, last, *refs):
    blocks, shares, experts, steps, step_rows, relays = counts
    refs = list(refs)

    def take(n):
        got = refs[:n]
        del refs[:n]
        return got

    xs = take(blocks)
    trunk_ref, ups_near, ups_far, downs_near, downs_far = take(5)
    ups = (ups_near.at[0], ups_near.at[1], ups_far.at[0], ups_far.at[1])
    downs = (downs_near.at[0], downs_far.at[0], downs_near.at[1], downs_far.at[1])
    if not first:
        prior_ref, prior_trunk_ref = take(2)
    held = take(relays)
    if last:
        loss_refs = take(last - 1)
        (mine_ref,) = take(1)
        (acc_ref,) = take(1)
        trunk_parts = take(shares if in_turns(experts) else 1)
        (all_loss_ref,) = take(1)
    else:
        acc_ref, acc_trunk_ref, loss_ref = take(3)
        for source, copy in zip(held, take(relays)):
            copy[...] = source[...]
    x_ref, hid_ref, slope_ref = take(3)
    if last:
        acc_trunk_ref, loss_ref = take(2)

    width = trunk_ref.shape[0]
    share = ups_near.shape[2]
    block_rows = xs[0].shape[0]
    for i, ref in enumerate(xs):
        x_ref[i * block_rows : (i + 1) * block_rows, :] = ref[...]
    looped = steps > 3
    if looped and first:
        acc_ref[...] = jnp.zeros(acc_ref.shape, F32)
        acc_trunk_ref[...] = jnp.zeros(acc_trunk_ref.shape, F32)
    elif looped:
        acc_ref[...] = prior_ref[...]
        acc_trunk_ref[...] = prior_trunk_ref[...]

    def add(i, ref, source, at, value):
        if looped or i > 0:
            ref[at] += value
        elif first:
            ref[at] = value
        else:
            ref[at] = source[at] + value

    prior = None if first else prior_ref
    prior_trunk = None if first else prior_trunk_ref

    def step(i, carry):
        if looped:
            at = pl.ds(pl.multiple_of(i * step_rows, step_rows), step_rows)
        else:
            at = slice(i * step_rows, (i + 1) * step_rows)
        feats = x_ref[at, :width]
        feats_f = feats.astype(F32)
        trunk_pre = dot(feats, trunk_ref[...])
        gate = sigmoid(trunk_pre)
        act = trunk_pre * gate
        trunk_slope = gate + act * (1.0 - gate)
        out_f = feats_f + act
        out = out_f.astype(BF16)
        predicted = jnp.zeros((step_rows, width), F32)
        for j in range(shares):
            up = dot(out, ups[j][...])
            s = sigmoid(up)
            h = up * s
            slope_ref[:, j * share : (j + 1) * share] = s + h * (1.0 - s)
            h = h.astype(BF16)
            hid_ref[:, j * share : (j + 1) * share] = h
            predicted = predicted + dot(h, downs[j][...], 1, 1)
        errors = predicted - x_ref[at, width:].astype(F32)
        squares = errors * errors
        half = squares[:, :LANES]
        for k in range(1, width // LANES):
            half = half + squares[:, k * LANES : (k + 1) * LANES]
        lost = jnp.sum(half.T, axis=0, keepdims=True) * (0.5 * loss_scale)
        for k in range(step_rows // LOSSES):
            row = pl.ds(i * (step_rows // LOSSES) + k, 1)
            loss_ref[row, :] = lost[:, k * LOSSES : (k + 1) * LOSSES]
        scaled_f = errors * loss_scale
        scaled = scaled_f.astype(BF16)
        scaled_t = scaled_f.T.astype(BF16)
        out_t = out_f.T.astype(BF16)
        row_grad = jnp.zeros((step_rows, width), F32)
        for j in range(shares):
            part = slice(j * share, (j + 1) * share)
            add(i, acc_ref, prior, (j, 1), dot(scaled_t, hid_ref[:, part]))
            pre = (dot(scaled, downs[j][...]) * slope_ref[:, part]).astype(BF16)
            add(i, acc_ref, prior, (j, 0), dot(out_t, pre))
            row_grad = row_grad + dot(pre, ups[j][...], 1, 1)
        slope = (row_grad.astype(BF16).astype(F32) * trunk_slope).astype(BF16)
        add(i, acc_trunk_ref, prior_trunk, ..., dot(feats_f.T.astype(BF16), slope))
        return carry

    if looped:
        lax.fori_loop(0, steps, step, 0)
    else:
        for i in range(steps):
            step(i, 0)
    if last:
        all_losses = list(loss_refs) + [loss_ref]
        if not in_turns(experts):
            trunk_parts[0][...] = acc_trunk_ref[...]
            for row in range(all_loss_ref.shape[0]):
                all_loss_ref[row : row + 1, :] = loss_row(all_losses, row)
            return
        quarter = width // shares
        for j, ref in enumerate(trunk_parts):
            at = pl.multiple_of((mine_ref[0] ^ j) * quarter, quarter)
            ref[...] = acc_trunk_ref[pl.ds(at, quarter), :]
        for s in range(experts):
            all_loss_ref[s : s + 1, :] = loss_row(all_losses, order.index(s))


def in_turns(experts):
    return experts == 8


def loss_row(refs, row):
    for ref in refs:
        if row < ref.shape[0]:
            return ref[row : row + 1, :]
        row -= ref.shape[0]


def expert_call(xs, trunk_weight, weights, prior, losses, mine, order, last, relays=()):
    experts = len(order)
    block_rows = xs[0].shape[0]
    width = trunk_weight.shape[0]
    shares, share = len(weights), weights[0].shape[2]
    rows = block_rows * len(xs)
    step_rows = min(512, rows)
    steps = rows // step_rows
    first = prior is None
    acc = jax.ShapeDtypeStruct((shares, 2, width, share), F32)
    acc_trunk = jax.ShapeDtypeStruct((width, width), F32)
    loss = jax.ShapeDtypeStruct((rows // LOSSES, LOSSES), F32)
    args = list(xs) + [trunk_weight, *weights]
    if not first:
        args += list(prior)
    args += relays
    in_specs = [whole()] * len(args)
    scratch = [
        pltpu.VMEM((rows, 2 * width), BF16),
        pltpu.VMEM((step_rows, shares * share), BF16),
        pltpu.VMEM((step_rows, shares * share), F32),
    ]
    if last:
        args += list(losses) + [mine]
        in_specs += [whole()] * len(losses) + [whole(pltpu.SMEM)]
        outs = [acc]
        if in_turns(experts):
            outs += [jax.ShapeDtypeStruct((width // shares, width), F32)] * shares
        else:
            outs += [acc_trunk]
        outs += [jax.ShapeDtypeStruct((experts * block_rows // LOSSES, LOSSES), F32)]
        scratch += [pltpu.VMEM(a.shape, a.dtype) for a in (acc_trunk, loss)]
    else:
        outs = [acc, acc_trunk, loss]
        outs += [jax.ShapeDtypeStruct(relay.shape, relay.dtype) for relay in relays]
    counts = (len(xs), shares, experts, steps, step_rows, len(relays))
    return pl.pallas_call(
        functools.partial(expert_kernel, counts, order, first, len(losses) + 1 if last else 0),
        out_shape=outs,
        in_specs=in_specs,
        out_specs=[whole()] * len(outs),
        scratch_shapes=scratch,
        compiler_params=pltpu.CompilerParams(vmem_limit_bytes=20 * MIB),
        cost_estimate=pl.CostEstimate(
            flops=12 * rows * width,
            bytes_accessed=rows * width,
            transcendentals=0,
        ),
        name="expert_rows",
    )(*args)


def four(refs):
    return (refs[0][...] + refs[1][...]) + (refs[2][...] + refs[3][...])


def dp_turn_kernel(q0, q1, q2, q3, loss_ref, total_ref, note_ref):
    total = four((q0, q1, q2, q3))
    total_ref[...] = total
    rows = total.shape[0]
    note_ref[:rows, :] = total
    for k in range(4):
        note_ref[rows + k : rows + k + 1, :] = loss_ref[2 * k + 1 : 2 * k + 2, :]
    note_ref[rows + 4 :, :] = jnp.zeros((4, total.shape[1]), F32)


def pair_turn_kernel(me_ref, total_ref, got_ref, loss_ref, *outs):
    rows, width = total_ref.shape
    half = rows // 2
    at = pl.ds(pl.multiple_of((me_ref[0] & 1) * half, half), half)
    for k, ref in enumerate(outs):
        ref[:half, :] = total_ref[at, :] + got_ref[at, :]
        ref[half : half + 1, :] = loss_ref[2 * k : 2 * k + 1, :]
        ref[half + 1 : half + 2, :] = got_ref[rows + k : rows + k + 1, :]
        ref[half + 2 :, :] = jnp.zeros((6, width), F32)


def z_turn_kernel(*refs):
    *notes, total_ref, loss_ref = refs
    half = total_ref.shape[0]
    total_ref[...] = four([note.at[:half, :] for note in notes])
    for k, note in enumerate(notes):
        loss_ref[2 * k : 2 * k + 2, :] = note[half : half + 2, :]


def join_kernel(me_ref, own_ref, other_ref, both_ref):
    half = own_ref.shape[0]
    core = me_ref[0] & 1
    both_ref[pl.ds(pl.multiple_of(core * half, half), half), :] = own_ref[...]
    both_ref[pl.ds(pl.multiple_of((1 - core) * half, half), half), :] = other_ref[...]


def assemble_kernel(mine_ref, *refs):
    *held, _, trunk_ref = refs
    for j, ref in enumerate(held):
        rows = ref.shape[0]
        at = pl.multiple_of((mine_ref[0] ^ j) * rows, rows)
        trunk_ref[pl.ds(at, rows), :] = ref[...]


def turn(kernel, held, shapes, name, index=None):
    first = [] if index is None else [index]
    width = held[0].shape[1]
    return pl.pallas_call(
        kernel,
        out_shape=[jax.ShapeDtypeStruct((rows, width), F32) for rows in shapes],
        in_specs=[whole(pltpu.SMEM)] * len(first) + [whole()] * len(held),
        out_specs=[whole()] * len(shapes),
        compiler_params=pltpu.CompilerParams(vmem_limit_bytes=4 * MIB),
        name=name,
    )(*first, *held)


def send_kernel(acc_ref, ahead_ref, up_ref, down_ref):
    for k in range(2):
        up_ref[k] = acc_ref[2 * k + 1, 0].astype(BF16)
        down_ref[k] = acc_ref[k + 2, 1].astype(BF16)


def pass_on_kernel(acc_ref, got_up_ref, got_down_ref, ahead_ref, up_ref, down_ref):
    up_ref[...] = (acc_ref[2, 0] + got_up_ref[1].astype(F32)).astype(BF16)
    down_ref[...] = (acc_ref[1, 1] + got_down_ref[1].astype(F32)).astype(BF16)


def messages(kernel, held, ahead, shape, name):
    return pl.pallas_call(
        kernel,
        out_shape=[jax.ShapeDtypeStruct(shape, BF16)] * 2,
        in_specs=[whole()] * len(held) + [whole(pl.ANY)],
        out_specs=[whole()] * 2,
        compiler_params=pltpu.CompilerParams(vmem_limit_bytes=16 * MIB),
        name=name,
    )(*held, ahead)


def row_loss_kernel(place_ref, loss_ref, row_loss_ref):
    experts, capacity = loss_ref.shape
    loss = loss_ref[...]
    for g in range(place_ref.shape[0]):
        place = place_ref[g : g + 1, :]
        block = place // capacity
        slot = place - block * capacity
        picks = jnp.where(iota((capacity, LANES), 0) == slot, 1.0, 0.0)
        found = lax.dot_general(
            loss,
            picks,
            (((1,), (0,)), ((), ())),
            precision=lax.Precision.HIGHEST,
            preferred_element_type=F32,
        )
        mine = jnp.where(iota((experts, LANES), 0) == block, found, 0.0)
        row_loss_ref[g : g + 1, :] = jnp.sum(mine, axis=0, keepdims=True)


def loss_by_row(place, loss):
    return pl.pallas_call(
        row_loss_kernel,
        out_shape=jax.ShapeDtypeStruct(place.shape, F32),
        in_specs=[whole()] * 2,
        out_specs=whole(),
        compiler_params=pltpu.CompilerParams(vmem_limit_bytes=16 * MIB),
        name="row_loss",
    )(place, loss)


def adam_update(params, first, second, grads):
    first_new = beta_one * first + (1.0 - beta_one) * grads
    second_new = beta_two * second + (1.0 - beta_two) * grads * grads
    first_hat = first_new / (1.0 - beta_one**adam_step)
    second_hat = second_new / (1.0 - beta_two**adam_step)
    return (
        params - learn_rate * first_hat / (jnp.sqrt(second_hat) + adam_eps),
        first_new,
        second_new,
    )


def adam_kernel(*refs):
    params_ref, first_ref, second_ref, acc_ref, *got = refs[:8]
    *outs, done_ref = refs[8:]
    for k in range(2):
        grads = acc_ref[0, k] + got[k][0].astype(F32) + got[2 + k][...].astype(F32)
        news = adam_update(params_ref[0, k], first_ref[0, k], second_ref[0, k], grads)
        for ref, new in zip(outs, news):
            ref[0, k] = new
    done_ref[...] = jnp.zeros(done_ref.shape, F32)


def adam(params, first, second, acc, got):
    shape = jax.ShapeDtypeStruct(params.shape, F32)
    return pl.pallas_call(
        adam_kernel,
        out_shape=[shape] * 3 + [jax.ShapeDtypeStruct((8, LANES), F32)],
        in_specs=[whole()] * 8,
        out_specs=[whole()] * 4,
        compiler_params=pltpu.CompilerParams(vmem_limit_bytes=24 * MIB),
        cost_estimate=pl.CostEstimate(
            flops=20 * params.size, bytes_accessed=8 * params.size, transcendentals=params.size
        ),
        name="adam",
    )(params, first, second, acc, *got)


def swap(value, axis, s):
    if s == 0:
        return value
    return lax.ppermute(value, axis, [(i, i ^ s) for i in range(lax.axis_size(axis))])


def on_device(
    cell_table,
    sample_index,
    region,
    targets,
    trunk_weight,
    expert_params,
    first_moment,
    second_moment,
):
    rows = sample_index.shape[0]
    width = cell_table.shape[1]
    experts = lax.axis_size("expert")
    replicas = lax.axis_size("dp")
    capacity = 2 * rows // experts
    me = lax.axis_index("expert").astype(jnp.int32).reshape(1)
    mine = lax.axis_index("dp").astype(jnp.int32).reshape(1)

    up, down = expert_params[0, 0].astype(BF16), expert_params[0, 1].astype(BF16)
    near_up, near_down = swap(up, "dp", 1), swap(down, "dp", 2)
    *blocks, place = pack(me, mine, sample_index, region[:, 0], cell_table, targets, experts, capacity)
    ups, downs = pair(up, near_up, place), pair(down, near_down, place)
    weights = [ups, swap(ups, "dp", 2), downs, swap(downs, "dp", 1)]
    if in_turns(experts):
        batches, later = ((0, 1), (4, 5), (2,), (3,), (6,), (7,)), (6, 7)
    else:
        batches, later = (range(experts // 2), range(experts // 2, experts)), ()
    order = [s for batch in batches for s in batch]
    arrived = {s: swap(blocks[s], "expert", s) for s in order if s not in later}
    prior, losses = None, []
    for k, batch in enumerate(batches):
        last = k == len(batches) - 1
        relays = [blocks[s] for s in later] if k == 0 else []
        outs = expert_call(
            [arrived[s] for s in batch], trunk_weight, weights, prior, losses, mine, order, last, relays
        )
        if not last:
            prior = outs[:2]
            losses.append(outs[2])
            for s, block in zip(later, outs[3:]):
                arrived[s] = swap(block, "expert", s)
    acc, *parts, losses = outs

    def send(ahead):
        up, down = messages(send_kernel, [acc], ahead, (2, *acc.shape[2:]), "send")
        return swap(up, "dp", 1), swap(down, "dp", 2)

    def pass_on(got, ahead):
        up, down = messages(pass_on_kernel, [acc, *got], ahead, acc.shape[2:], "pass_on")
        return swap(up, "dp", 2), swap(down, "dp", 1)

    if in_turns(experts):
        quarter = width // replicas
        parts = [swap(part, "dp", j) for j, part in enumerate(parts)]
        total, note = turn(dp_turn_kernel, parts + [losses], (quarter, quarter + 8), "dp_turn")
        got = send(total)
        notes = turn(
            pair_turn_kernel,
            [total, swap(note, "expert", 1), losses],
            (quarter // 2 + 8,) * 4,
            "pair_turn",
            me,
        )
        notes = [swap(note, "expert", 2 * k) for k, note in enumerate(notes)]
        total, loss = turn(z_turn_kernel, notes, (quarter // 2, experts), "z_turn")
        more_up, more_down = pass_on(got, total)
        (total,) = turn(join_kernel, [total, swap(total, "expert", 1)], (quarter,), "join", me)
        parts = [swap(total, "dp", j) for j in range(replicas)]
        *news, done = adam(
            expert_params, first_moment, second_moment, acc, [*got, more_up, more_down]
        )
        (trunk_grad,) = turn(assemble_kernel, parts + [done], (width,), "assemble_trunk", mine)
    else:
        got = send(losses)
        more_up, more_down = pass_on(got, losses)
        *news, _ = adam(
            expert_params, first_moment, second_moment, acc, [*got, more_up, more_down]
        )
        trunk_grad = lax.psum(parts[0], ("dp", "expert"))
        places = jnp.arange(experts, dtype=jnp.int32) ^ me
        losses = losses.reshape(experts, capacity)[places]
        loss = lax.all_to_all(losses, "expert", split_axis=0, concat_axis=0, tiled=True)[places]
    row_loss = loss_by_row(place, loss)

    return (trunk_grad, row_loss.reshape(rows), *news)


def solution(mesh):
    placed = (
        P(("dp", "expert"), None),
        P(("dp", "expert")),
        P(("dp", "expert"), None),
        P(("dp", "expert"), None),
        P(),
        P("expert", None, None, "dp"),
        P("expert", None, None, "dp"),
        P("expert", None, None, "dp"),
    )
    return jax.shard_map(
        on_device,
        mesh=mesh,
        in_specs=placed,
        out_specs=(
            P(),
            P(("dp", "expert")),
            P("expert", None, None, "dp"),
            P("expert", None, None, "dp"),
            P("expert", None, None, "dp"),
        ),
        check_vma=False,
    )
```

```python
import functools

import jax
import jax.numpy as jnp
from jax import lax
from jax.experimental import pallas as pl
from jax.experimental.pallas import tpu as pltpu
from jax.sharding import PartitionSpec as P

loss_scale = 1.0 / 32.0
beta_one = 0.9
beta_two = 0.999
learn_rate = 0.05
adam_eps = 1e-08
adam_step = 10

LANES = 128
F32 = jnp.float32
BF16 = jnp.bfloat16
MIB = 1 << 20
LOSSES = 256


def iota(shape, dim):
    return lax.broadcasted_iota(jnp.int32, shape, dim)


def dot(a, b, ca=1, cb=0):
    return lax.dot_general(a, b, (((ca,), (cb,)), ((), ())), preferred_element_type=F32)


def whole(memory_space=pltpu.VMEM):
    return pl.BlockSpec(memory_space=memory_space)


def pack_kernel(experts, capacity, me_ref, mine_ref, index_ref, region_ref, table_ref, target_ref, *refs):
    blocks, place_ref, rows_ref = refs[:experts], refs[experts], refs[experts + 1]
    me = me_ref[0]
    groups = index_ref.shape[0]
    cells, width = table_ref.shape
    expert_id = iota((experts, LANES), 0)
    starts = ((expert_id ^ me) * capacity).astype(F32)
    ahead = jnp.where(iota((LANES, LANES), 0) <= iota((LANES, LANES), 1), 1.0, 0.0).astype(BF16)
    counted = jnp.zeros((experts, LANES), F32)
    places = []
    for g in range(groups):
        hot = jnp.where(region_ref[g : g + 1, :] == expert_id, 1.0, 0.0)
        upto = dot(hot.astype(BF16), ahead)
        places.append(jnp.sum(hot * (upto - 1.0 + counted + starts), axis=0, keepdims=True))
        counted = counted + jnp.broadcast_to(upto[:, LANES - 1 :], (experts, LANES))
    for g in range(groups):
        place_ref[g : g + 1, :] = places[g].astype(jnp.int32)
    place = jnp.concatenate(places, axis=1)

    step = 2
    cell_id = iota((LANES * step, LANES), 1).astype(F32)
    for g in range(0, groups, step):
        column = jnp.concatenate(
            [
                jnp.broadcast_to(index_ref[h : h + 1, :].astype(F32), (LANES, LANES)).T
                for h in range(g, g + step)
            ],
            axis=0,
        )
        picks = jnp.concatenate(
            [
                jnp.where(column == cell_id + float(LANES * t), 1.0, 0.0).astype(BF16)
                for t in range(cells // LANES)
            ],
            axis=1,
        )
        at = slice(g * LANES, (g + step) * LANES)
        rows_ref[at, :width] = dot(picks, table_ref[...]).astype(BF16)
        rows_ref[at, width:] = target_ref[at, :]

    slot_id = iota((capacity, place.shape[1]), 0).astype(F32)
    for s in range(experts):
        spread = jnp.where(place == slot_id + float(s * capacity), 1.0, 0.0).astype(BF16)
        blocks[s][...] = dot(spread, rows_ref[...]).astype(BF16)


def pack(me, mine, index, region, table, targets, experts, capacity):
    rows, width = targets.shape
    groups = rows // LANES
    return pl.pallas_call(
        functools.partial(pack_kernel, experts, capacity),
        out_shape=[jax.ShapeDtypeStruct((capacity, 2 * width), BF16)] * experts
        + [jax.ShapeDtypeStruct((groups, LANES), jnp.int32)],
        in_specs=[whole(pltpu.SMEM)] * 2 + [whole()] * 4,
        out_specs=[whole()] * (experts + 1),
        scratch_shapes=[pltpu.VMEM((rows, 2 * width), BF16)],
        compiler_params=pltpu.CompilerParams(vmem_limit_bytes=24 * MIB),
        cost_estimate=pl.CostEstimate(
            flops=2 * rows * width * (table.shape[0] + 2 * experts * capacity),
            bytes_accessed=6 * MIB,
            transcendentals=0,
        ),
        name="pack_rows",
    )(me, mine, index.reshape(groups, LANES), region.reshape(groups, LANES), table, targets)


def pair_kernel(one_ref, other_ref, ahead_ref, both_ref):
    both_ref[0] = one_ref[...]
    both_ref[1] = other_ref[...]


def pair(one, other, ahead):
    return pl.pallas_call(
        pair_kernel,
        out_shape=jax.ShapeDtypeStruct((2, *one.shape), one.dtype),
        in_specs=[whole()] * 2 + [whole(pl.ANY)],
        out_specs=whole(),
        compiler_params=pltpu.CompilerParams(vmem_limit_bytes=4 * MIB),
        name="pair",
    )(one, other, ahead)


def sigmoid(v):
    return 0.5 * jnp.tanh(0.5 * v) + 0.5


def expert_kernel(counts, order, first, last, *refs):
    blocks, shares, experts, steps, step_rows, relays = counts
    refs = list(refs)

    def take(n):
        got = refs[:n]
        del refs[:n]
        return got

    xs = take(blocks)
    trunk_ref, ups_near, ups_far, downs_near, downs_far = take(5)
    ups = (ups_near.at[0], ups_near.at[1], ups_far.at[0], ups_far.at[1])
    downs = (downs_near.at[0], downs_far.at[0], downs_near.at[1], downs_far.at[1])
    if not first:
        prior_ref, prior_trunk_ref = take(2)
    held = take(relays)
    if last:
        loss_refs = take(last - 1)
        (mine_ref,) = take(1)
        (acc_ref,) = take(1)
        trunk_parts = take(shares if in_turns(experts) else 1)
        (all_loss_ref,) = take(1)
    else:
        acc_ref, acc_trunk_ref, loss_ref = take(3)
        for source, copy in zip(held, take(relays)):
            copy[...] = source[...]
    x_ref, hid_ref, slope_ref = take(3)
    if last:
        acc_trunk_ref, loss_ref = take(2)

    width = trunk_ref.shape[0]
    share = ups_near.shape[2]
    block_rows = xs[0].shape[0]
    for i, ref in enumerate(xs):
        x_ref[i * block_rows : (i + 1) * block_rows, :] = ref[...]
    looped = steps > 3
    if looped and first:
        acc_ref[...] = jnp.zeros(acc_ref.shape, F32)
        acc_trunk_ref[...] = jnp.zeros(acc_trunk_ref.shape, F32)
    elif looped:
        acc_ref[...] = prior_ref[...]
        acc_trunk_ref[...] = prior_trunk_ref[...]

    def add(i, ref, source, at, value):
        if looped or i > 0:
            ref[at] += value
        elif first:
            ref[at] = value
        else:
            ref[at] = source[at] + value

    prior = None if first else prior_ref
    prior_trunk = None if first else prior_trunk_ref

    def step(i, carry):
        if looped:
            at = pl.ds(pl.multiple_of(i * step_rows, step_rows), step_rows)
        else:
            at = slice(i * step_rows, (i + 1) * step_rows)
        feats = x_ref[at, :width]
        feats_f = feats.astype(F32)
        trunk_pre = dot(feats, trunk_ref[...])
        gate = sigmoid(trunk_pre)
        act = trunk_pre * gate
        trunk_slope = gate + act * (1.0 - gate)
        out_f = feats_f + act
        out = out_f.astype(BF16)
        predicted = jnp.zeros((step_rows, width), F32)
        for j in range(shares):
            up = dot(out, ups[j][...])
            s = sigmoid(up)
            h = up * s
            slope_ref[:, j * share : (j + 1) * share] = s + h * (1.0 - s)
            h = h.astype(BF16)
            hid_ref[:, j * share : (j + 1) * share] = h
            predicted = predicted + dot(h, downs[j][...], 1, 1)
        errors = predicted - x_ref[at, width:].astype(F32)
        squares = errors * errors
        half = squares[:, :LANES]
        for k in range(1, width // LANES):
            half = half + squares[:, k * LANES : (k + 1) * LANES]
        lost = jnp.sum(half.T, axis=0, keepdims=True) * (0.5 * loss_scale)
        for k in range(step_rows // LOSSES):
            row = pl.ds(i * (step_rows // LOSSES) + k, 1)
            loss_ref[row, :] = lost[:, k * LOSSES : (k + 1) * LOSSES]
        scaled_f = errors * loss_scale
        scaled = scaled_f.astype(BF16)
        scaled_t = scaled_f.T.astype(BF16)
        out_t = out_f.T.astype(BF16)
        row_grad = jnp.zeros((step_rows, width), F32)
        for j in range(shares):
            part = slice(j * share, (j + 1) * share)
            add(i, acc_ref, prior, (j, 1), dot(scaled_t, hid_ref[:, part]))
            pre = (dot(scaled, downs[j][...]) * slope_ref[:, part]).astype(BF16)
            add(i, acc_ref, prior, (j, 0), dot(out_t, pre))
            row_grad = row_grad + dot(pre, ups[j][...], 1, 1)
        slope = (row_grad.astype(BF16).astype(F32) * trunk_slope).astype(BF16)
        add(i, acc_trunk_ref, prior_trunk, ..., dot(feats_f.T.astype(BF16), slope))
        return carry

    if looped:
        lax.fori_loop(0, steps, step, 0)
    else:
        for i in range(steps):
            step(i, 0)
    if last:
        all_losses = list(loss_refs) + [loss_ref]
        if not in_turns(experts):
            trunk_parts[0][...] = acc_trunk_ref[...]
            for row in range(all_loss_ref.shape[0]):
                all_loss_ref[row : row + 1, :] = loss_row(all_losses, row)
            return
        quarter = width // shares
        for j, ref in enumerate(trunk_parts):
            at = pl.multiple_of((mine_ref[0] ^ j) * quarter, quarter)
            ref[...] = acc_trunk_ref[pl.ds(at, quarter), :]
        for s in range(experts):
            all_loss_ref[s : s + 1, :] = loss_row(all_losses, order.index(s))


def in_turns(experts):
    return experts == 8


def loss_row(refs, row):
    for ref in refs:
        if row < ref.shape[0]:
            return ref[row : row + 1, :]
        row -= ref.shape[0]


def expert_call(xs, trunk_weight, weights, prior, losses, mine, order, last, relays=()):
    experts = len(order)
    block_rows = xs[0].shape[0]
    width = trunk_weight.shape[0]
    shares, share = len(weights), weights[0].shape[2]
    rows = block_rows * len(xs)
    step_rows = min(512, rows)
    steps = rows // step_rows
    first = prior is None
    acc = jax.ShapeDtypeStruct((shares, 2, width, share), F32)
    acc_trunk = jax.ShapeDtypeStruct((width, width), F32)
    loss = jax.ShapeDtypeStruct((rows // LOSSES, LOSSES), F32)
    args = list(xs) + [trunk_weight, *weights]
    if not first:
        args += list(prior)
    args += relays
    in_specs = [whole()] * len(args)
    scratch = [
        pltpu.VMEM((rows, 2 * width), BF16),
        pltpu.VMEM((step_rows, shares * share), BF16),
        pltpu.VMEM((step_rows, shares * share), F32),
    ]
    if last:
        args += list(losses) + [mine]
        in_specs += [whole()] * len(losses) + [whole(pltpu.SMEM)]
        outs = [acc]
        if in_turns(experts):
            outs += [jax.ShapeDtypeStruct((width // shares, width), F32)] * shares
        else:
            outs += [acc_trunk]
        outs += [jax.ShapeDtypeStruct((experts * block_rows // LOSSES, LOSSES), F32)]
        scratch += [pltpu.VMEM(a.shape, a.dtype) for a in (acc_trunk, loss)]
    else:
        outs = [acc, acc_trunk, loss]
        outs += [jax.ShapeDtypeStruct(relay.shape, relay.dtype) for relay in relays]
    counts = (len(xs), shares, experts, steps, step_rows, len(relays))
    return pl.pallas_call(
        functools.partial(expert_kernel, counts, order, first, len(losses) + 1 if last else 0),
        out_shape=outs,
        in_specs=in_specs,
        out_specs=[whole()] * len(outs),
        scratch_shapes=scratch,
        compiler_params=pltpu.CompilerParams(vmem_limit_bytes=20 * MIB),
        cost_estimate=pl.CostEstimate(
            flops=12 * rows * width,
            bytes_accessed=rows * width,
            transcendentals=0,
        ),
        name="expert_rows",
    )(*args)


def four(refs):
    return (refs[0][...] + refs[1][...]) + (refs[2][...] + refs[3][...])


def dp_turn_kernel(q0, q1, q2, q3, loss_ref, total_ref, note_ref):
    total = four((q0, q1, q2, q3))
    total_ref[...] = total
    rows = total.shape[0]
    note_ref[:rows, :] = total
    for k in range(4):
        note_ref[rows + k : rows + k + 1, :] = loss_ref[2 * k + 1 : 2 * k + 2, :]
    note_ref[rows + 4 :, :] = jnp.zeros((4, total.shape[1]), F32)


def pair_turn_kernel(me_ref, total_ref, got_ref, loss_ref, *outs):
    rows, width = total_ref.shape
    half = rows // 2
    at = pl.ds(pl.multiple_of((me_ref[0] & 1) * half, half), half)
    for k, ref in enumerate(outs):
        ref[:half, :] = total_ref[at, :] + got_ref[at, :]
        ref[half : half + 1, :] = loss_ref[2 * k : 2 * k + 1, :]
        ref[half + 1 : half + 2, :] = got_ref[rows + k : rows + k + 1, :]
        ref[half + 2 :, :] = jnp.zeros((6, width), F32)


def z_turn_kernel(*refs):
    *notes, total_ref, loss_ref = refs
    half = total_ref.shape[0]
    total_ref[...] = four([note.at[:half, :] for note in notes])
    for k, note in enumerate(notes):
        loss_ref[2 * k : 2 * k + 2, :] = note[half : half + 2, :]


def join_kernel(me_ref, own_ref, other_ref, both_ref):
    half = own_ref.shape[0]
    core = me_ref[0] & 1
    both_ref[pl.ds(pl.multiple_of(core * half, half), half), :] = own_ref[...]
    both_ref[pl.ds(pl.multiple_of((1 - core) * half, half), half), :] = other_ref[...]


def assemble_kernel(mine_ref, *refs):
    *held, _, trunk_ref = refs
    for j, ref in enumerate(held):
        rows = ref.shape[0]
        at = pl.multiple_of((mine_ref[0] ^ j) * rows, rows)
        trunk_ref[pl.ds(at, rows), :] = ref[...]


def turn(kernel, held, shapes, name, index=None):
    first = [] if index is None else [index]
    width = held[0].shape[1]
    return pl.pallas_call(
        kernel,
        out_shape=[jax.ShapeDtypeStruct((rows, width), F32) for rows in shapes],
        in_specs=[whole(pltpu.SMEM)] * len(first) + [whole()] * len(held),
        out_specs=[whole()] * len(shapes),
        compiler_params=pltpu.CompilerParams(vmem_limit_bytes=4 * MIB),
        name=name,
    )(*first, *held)


def send_kernel(acc_ref, ahead_ref, up_ref, down_ref):
    for k in range(2):
        up_ref[k] = acc_ref[2 * k + 1, 0].astype(BF16)
        down_ref[k] = acc_ref[k + 2, 1].astype(BF16)


def pass_on_kernel(acc_ref, got_up_ref, got_down_ref, ahead_ref, up_ref, down_ref):
    up_ref[...] = (acc_ref[2, 0] + got_up_ref[1].astype(F32)).astype(BF16)
    down_ref[...] = (acc_ref[1, 1] + got_down_ref[1].astype(F32)).astype(BF16)


def messages(kernel, held, ahead, shape, name):
    return pl.pallas_call(
        kernel,
        out_shape=[jax.ShapeDtypeStruct(shape, BF16)] * 2,
        in_specs=[whole()] * len(held) + [whole(pl.ANY)],
        out_specs=[whole()] * 2,
        compiler_params=pltpu.CompilerParams(vmem_limit_bytes=16 * MIB),
        name=name,
    )(*held, ahead)


def row_loss_kernel(place_ref, loss_ref, row_loss_ref):
    experts, capacity = loss_ref.shape
    loss = loss_ref[...]
    for g in range(place_ref.shape[0]):
        place = place_ref[g : g + 1, :]
        block = place // capacity
        slot = place - block * capacity
        picks = jnp.where(iota((capacity, LANES), 0) == slot, 1.0, 0.0)
        found = lax.dot_general(
            loss,
            picks,
            (((1,), (0,)), ((), ())),
            precision=lax.Precision.HIGHEST,
            preferred_element_type=F32,
        )
        mine = jnp.where(iota((experts, LANES), 0) == block, found, 0.0)
        row_loss_ref[g : g + 1, :] = jnp.sum(mine, axis=0, keepdims=True)


def loss_by_row(place, loss):
    return pl.pallas_call(
        row_loss_kernel,
        out_shape=jax.ShapeDtypeStruct(place.shape, F32),
        in_specs=[whole()] * 2,
        out_specs=whole(),
        compiler_params=pltpu.CompilerParams(vmem_limit_bytes=16 * MIB),
        name="row_loss",
    )(place, loss)


def adam_update(params, first, second, grads):
    first_new = beta_one * first + (1.0 - beta_one) * grads
    second_new = beta_two * second + (1.0 - beta_two) * grads * grads
    first_hat = first_new / (1.0 - beta_one**adam_step)
    second_hat = second_new / (1.0 - beta_two**adam_step)
    return (
        params - learn_rate * first_hat / (jnp.sqrt(second_hat) + adam_eps),
        first_new,
        second_new,
    )


def adam_kernel(*refs):
    params_ref, first_ref, second_ref, acc_ref, *got = refs[:8]
    *outs, done_ref = refs[8:]
    for k in range(2):
        grads = acc_ref[0, k] + got[k][0].astype(F32) + got[2 + k][...].astype(F32)
        news = adam_update(params_ref[0, k], first_ref[0, k], second_ref[0, k], grads)
        for ref, new in zip(outs, news):
            ref[0, k] = new
    done_ref[...] = jnp.zeros(done_ref.shape, F32)


def adam(params, first, second, acc, got):
    shape = jax.ShapeDtypeStruct(params.shape, F32)
    return pl.pallas_call(
        adam_kernel,
        out_shape=[shape] * 3 + [jax.ShapeDtypeStruct((8, LANES), F32)],
        in_specs=[whole()] * 8,
        out_specs=[whole()] * 4,
        compiler_params=pltpu.CompilerParams(vmem_limit_bytes=24 * MIB),
        cost_estimate=pl.CostEstimate(
            flops=20 * params.size, bytes_accessed=8 * params.size, transcendentals=params.size
        ),
        name="adam",
    )(params, first, second, acc, *got)


def swap(value, axis, s):
    if s == 0:
        return value
    return lax.ppermute(value, axis, [(i, i ^ s) for i in range(lax.axis_size(axis))])


def on_device(
    cell_table,
    sample_index,
    region,
    targets,
    trunk_weight,
    expert_params,
    first_moment,
    second_moment,
):
    rows = sample_index.shape[0]
    width = cell_table.shape[1]
    experts = lax.axis_size("expert")
    replicas = lax.axis_size("dp")
    capacity = 2 * rows // experts
    me = lax.axis_index("expert").astype(jnp.int32).reshape(1)
    mine = lax.axis_index("dp").astype(jnp.int32).reshape(1)

    up, down = expert_params[0, 0].astype(BF16), expert_params[0, 1].astype(BF16)
    near_up, near_down = swap(up, "dp", 1), swap(down, "dp", 2)
    *blocks, place = pack(me, mine, sample_index, region[:, 0], cell_table, targets, experts, capacity)
    ups, downs = pair(up, near_up, place), pair(down, near_down, place)
    weights = [ups, swap(ups, "dp", 2), downs, swap(downs, "dp", 1)]
    if in_turns(experts):
        batches, later = ((0, 4), (1, 5), (2, 3), (6, 7)), ()
    else:
        batches, later = (range(experts // 2), range(experts // 2, experts)), ()
    order = [s for batch in batches for s in batch]
    arrived = {s: swap(blocks[s], "expert", s) for s in order if s not in later}
    prior, losses = None, []
    for k, batch in enumerate(batches):
        last = k == len(batches) - 1
        relays = [blocks[s] for s in later] if k == 0 else []
        outs = expert_call(
            [arrived[s] for s in batch], trunk_weight, weights, prior, losses, mine, order, last, relays
        )
        if not last:
            prior = outs[:2]
            losses.append(outs[2])
            for s, block in zip(later, outs[3:]):
                arrived[s] = swap(block, "expert", s)
    acc, *parts, losses = outs

    def send(ahead):
        up, down = messages(send_kernel, [acc], ahead, (2, *acc.shape[2:]), "send")
        return swap(up, "dp", 1), swap(down, "dp", 2)

    def pass_on(got, ahead):
        up, down = messages(pass_on_kernel, [acc, *got], ahead, acc.shape[2:], "pass_on")
        return swap(up, "dp", 2), swap(down, "dp", 1)

    if in_turns(experts):
        quarter = width // replicas
        parts = [swap(part, "dp", j) for j, part in enumerate(parts)]
        total, note = turn(dp_turn_kernel, parts + [losses], (quarter, quarter + 8), "dp_turn")
        got = send(total)
        notes = turn(
            pair_turn_kernel,
            [total, swap(note, "expert", 1), losses],
            (quarter // 2 + 8,) * 4,
            "pair_turn",
            me,
        )
        notes = [swap(note, "expert", 2 * k) for k, note in enumerate(notes)]
        total, loss = turn(z_turn_kernel, notes, (quarter // 2, experts), "z_turn")
        more_up, more_down = pass_on(got, total)
        (total,) = turn(join_kernel, [total, swap(total, "expert", 1)], (quarter,), "join", me)
        parts = [swap(total, "dp", j) for j in range(replicas)]
        *news, done = adam(
            expert_params, first_moment, second_moment, acc, [*got, more_up, more_down]
        )
        (trunk_grad,) = turn(assemble_kernel, parts + [done], (width,), "assemble_trunk", mine)
    else:
        got = send(losses)
        more_up, more_down = pass_on(got, losses)
        *news, _ = adam(
            expert_params, first_moment, second_moment, acc, [*got, more_up, more_down]
        )
        trunk_grad = lax.psum(parts[0], ("dp", "expert"))
        places = jnp.arange(experts, dtype=jnp.int32) ^ me
        losses = losses.reshape(experts, capacity)[places]
        loss = lax.all_to_all(losses, "expert", split_axis=0, concat_axis=0, tiled=True)[places]
    row_loss = loss_by_row(place, loss)

    return (trunk_grad, row_loss.reshape(rows), *news)


def solution(mesh):
    placed = (
        P(("dp", "expert"), None),
        P(("dp", "expert")),
        P(("dp", "expert"), None),
        P(("dp", "expert"), None),
        P(),
        P("expert", None, None, "dp"),
        P("expert", None, None, "dp"),
        P("expert", None, None, "dp"),
    )
    return jax.shard_map(
        on_device,
        mesh=mesh,
        in_specs=placed,
        out_specs=(
            P(),
            P(("dp", "expert")),
            P("expert", None, None, "dp"),
            P("expert", None, None, "dp"),
            P("expert", None, None, "dp"),
        ),
        check_vma=False,
    )
```

```python
import functools

import jax
import jax.numpy as jnp
from jax import lax
from jax.experimental import pallas as pl
from jax.experimental.pallas import tpu as pltpu
from jax.sharding import PartitionSpec as P

loss_scale = 1.0 / 32.0
beta_one = 0.9
beta_two = 0.999
learn_rate = 0.05
adam_eps = 1e-08
adam_step = 10

LANES = 128
F32 = jnp.float32
BF16 = jnp.bfloat16
MIB = 1 << 20
LOSSES = 256


def iota(shape, dim):
    return lax.broadcasted_iota(jnp.int32, shape, dim)


def dot(a, b, ca=1, cb=0):
    return lax.dot_general(a, b, (((ca,), (cb,)), ((), ())), preferred_element_type=F32)


def whole(memory_space=pltpu.VMEM):
    return pl.BlockSpec(memory_space=memory_space)


def pack_kernel(experts, capacity, me_ref, mine_ref, index_ref, region_ref, table_ref, target_ref, *refs):
    blocks, place_ref, rows_ref = refs[:experts], refs[experts], refs[experts + 1]
    me = me_ref[0]
    groups = index_ref.shape[0]
    cells, width = table_ref.shape
    expert_id = iota((experts, LANES), 0)
    starts = ((expert_id ^ me) * capacity).astype(F32)
    ahead = jnp.where(iota((LANES, LANES), 0) <= iota((LANES, LANES), 1), 1.0, 0.0).astype(BF16)
    counted = jnp.zeros((experts, LANES), F32)
    places = []
    for g in range(groups):
        hot = jnp.where(region_ref[g : g + 1, :] == expert_id, 1.0, 0.0)
        upto = dot(hot.astype(BF16), ahead)
        places.append(jnp.sum(hot * (upto - 1.0 + counted + starts), axis=0, keepdims=True))
        counted = counted + jnp.broadcast_to(upto[:, LANES - 1 :], (experts, LANES))
    for g in range(groups):
        place_ref[g : g + 1, :] = places[g].astype(jnp.int32)
    place = jnp.concatenate(places, axis=1)

    step = 2
    cell_id = iota((LANES * step, LANES), 1).astype(F32)
    for g in range(0, groups, step):
        column = jnp.concatenate(
            [
                jnp.broadcast_to(index_ref[h : h + 1, :].astype(F32), (LANES, LANES)).T
                for h in range(g, g + step)
            ],
            axis=0,
        )
        picks = jnp.concatenate(
            [
                jnp.where(column == cell_id + float(LANES * t), 1.0, 0.0).astype(BF16)
                for t in range(cells // LANES)
            ],
            axis=1,
        )
        at = slice(g * LANES, (g + step) * LANES)
        rows_ref[at, :width] = dot(picks, table_ref[...]).astype(BF16)
        rows_ref[at, width:] = target_ref[at, :]

    slot_id = iota((capacity, place.shape[1]), 0).astype(F32)
    for s in range(experts):
        spread = jnp.where(place == slot_id + float(s * capacity), 1.0, 0.0).astype(BF16)
        blocks[s][...] = dot(spread, rows_ref[...]).astype(BF16)


def pack(me, mine, index, region, table, targets, experts, capacity):
    rows, width = targets.shape
    groups = rows // LANES
    return pl.pallas_call(
        functools.partial(pack_kernel, experts, capacity),
        out_shape=[jax.ShapeDtypeStruct((capacity, 2 * width), BF16)] * experts
        + [jax.ShapeDtypeStruct((groups, LANES), jnp.int32)],
        in_specs=[whole(pltpu.SMEM)] * 2 + [whole()] * 4,
        out_specs=[whole()] * (experts + 1),
        scratch_shapes=[pltpu.VMEM((rows, 2 * width), BF16)],
        compiler_params=pltpu.CompilerParams(vmem_limit_bytes=24 * MIB),
        cost_estimate=pl.CostEstimate(
            flops=2 * rows * width * (table.shape[0] + 2 * experts * capacity),
            bytes_accessed=6 * MIB,
            transcendentals=0,
        ),
        name="pack_rows",
    )(me, mine, index.reshape(groups, LANES), region.reshape(groups, LANES), table, targets)


def pair_kernel(one_ref, other_ref, ahead_ref, both_ref):
    both_ref[0] = one_ref[...]
    both_ref[1] = other_ref[...]


def pair(one, other, ahead):
    return pl.pallas_call(
        pair_kernel,
        out_shape=jax.ShapeDtypeStruct((2, *one.shape), one.dtype),
        in_specs=[whole()] * 2 + [whole(pl.ANY)],
        out_specs=whole(),
        compiler_params=pltpu.CompilerParams(vmem_limit_bytes=4 * MIB),
        name="pair",
    )(one, other, ahead)


def sigmoid(v):
    return 0.5 * jnp.tanh(0.5 * v) + 0.5


def expert_kernel(counts, order, first, last, *refs):
    blocks, shares, experts, steps, step_rows, relays = counts
    refs = list(refs)

    def take(n):
        got = refs[:n]
        del refs[:n]
        return got

    xs = take(blocks)
    trunk_ref, ups_near, ups_far, downs_near, downs_far = take(5)
    ups = (ups_near.at[0], ups_near.at[1], ups_far.at[0], ups_far.at[1])
    downs = (downs_near.at[0], downs_far.at[0], downs_near.at[1], downs_far.at[1])
    if not first:
        prior_ref, prior_trunk_ref = take(2)
    held = take(relays)
    if last:
        loss_refs = take(last - 1)
        (mine_ref,) = take(1)
        (acc_ref,) = take(1)
        trunk_parts = take(shares if in_turns(experts) else 1)
        (all_loss_ref,) = take(1)
    else:
        acc_ref, acc_trunk_ref, loss_ref = take(3)
        for source, copy in zip(held, take(relays)):
            copy[...] = source[...]
    x_ref, hid_ref, slope_ref = take(3)
    if last:
        acc_trunk_ref, loss_ref = take(2)

    width = trunk_ref.shape[0]
    share = ups_near.shape[2]
    block_rows = xs[0].shape[0]
    for i, ref in enumerate(xs):
        x_ref[i * block_rows : (i + 1) * block_rows, :] = ref[...]
    looped = steps > 3
    if looped and first:
        acc_ref[...] = jnp.zeros(acc_ref.shape, F32)
        acc_trunk_ref[...] = jnp.zeros(acc_trunk_ref.shape, F32)
    elif looped:
        acc_ref[...] = prior_ref[...]
        acc_trunk_ref[...] = prior_trunk_ref[...]

    def add(i, ref, source, at, value):
        if looped or i > 0:
            ref[at] += value
        elif first:
            ref[at] = value
        else:
            ref[at] = source[at] + value

    prior = None if first else prior_ref
    prior_trunk = None if first else prior_trunk_ref

    def step(i, carry):
        if looped:
            at = pl.ds(pl.multiple_of(i * step_rows, step_rows), step_rows)
        else:
            at = slice(i * step_rows, (i + 1) * step_rows)
        feats = x_ref[at, :width]
        feats_f = feats.astype(F32)
        trunk_pre = dot(feats, trunk_ref[...])
        gate = sigmoid(trunk_pre)
        act = trunk_pre * gate
        trunk_slope = gate + act * (1.0 - gate)
        out_f = feats_f + act
        out = out_f.astype(BF16)
        predicted = jnp.zeros((step_rows, width), F32)
        for j in range(shares):
            up = dot(out, ups[j][...])
            s = sigmoid(up)
            h = up * s
            slope_ref[:, j * share : (j + 1) * share] = s + h * (1.0 - s)
            h = h.astype(BF16)
            hid_ref[:, j * share : (j + 1) * share] = h
            predicted = predicted + dot(h, downs[j][...], 1, 1)
        errors = predicted - x_ref[at, width:].astype(F32)
        squares = errors * errors
        half = squares[:, :LANES]
        for k in range(1, width // LANES):
            half = half + squares[:, k * LANES : (k + 1) * LANES]
        lost = jnp.sum(half.T, axis=0, keepdims=True) * (0.5 * loss_scale)
        for k in range(step_rows // LOSSES):
            row = pl.ds(i * (step_rows // LOSSES) + k, 1)
            loss_ref[row, :] = lost[:, k * LOSSES : (k + 1) * LOSSES]
        scaled_f = errors * loss_scale
        scaled = scaled_f.astype(BF16)
        scaled_t = scaled_f.T.astype(BF16)
        out_t = out_f.T.astype(BF16)
        row_grad = jnp.zeros((step_rows, width), F32)
        for j in range(shares):
            part = slice(j * share, (j + 1) * share)
            add(i, acc_ref, prior, (j, 1), dot(scaled_t, hid_ref[:, part]))
            pre = (dot(scaled, downs[j][...]) * slope_ref[:, part]).astype(BF16)
            add(i, acc_ref, prior, (j, 0), dot(out_t, pre))
            row_grad = row_grad + dot(pre, ups[j][...], 1, 1)
        slope = (row_grad.astype(BF16).astype(F32) * trunk_slope).astype(BF16)
        add(i, acc_trunk_ref, prior_trunk, ..., dot(feats_f.T.astype(BF16), slope))
        return carry

    if looped:
        lax.fori_loop(0, steps, step, 0)
    else:
        for i in range(steps):
            step(i, 0)
    if last:
        all_losses = list(loss_refs) + [loss_ref]
        if not in_turns(experts):
            trunk_parts[0][...] = acc_trunk_ref[...]
            for row in range(all_loss_ref.shape[0]):
                all_loss_ref[row : row + 1, :] = loss_row(all_losses, row)
            return
        quarter = width // shares
        for j, ref in enumerate(trunk_parts):
            at = pl.multiple_of((mine_ref[0] ^ j) * quarter, quarter)
            ref[...] = acc_trunk_ref[pl.ds(at, quarter), :]
        for s in range(experts):
            all_loss_ref[s : s + 1, :] = loss_row(all_losses, order.index(s))


def in_turns(experts):
    return experts == 8


def loss_row(refs, row):
    for ref in refs:
        if row < ref.shape[0]:
            return ref[row : row + 1, :]
        row -= ref.shape[0]


def expert_call(xs, trunk_weight, weights, prior, losses, mine, order, last, relays=()):
    experts = len(order)
    block_rows = xs[0].shape[0]
    width = trunk_weight.shape[0]
    shares, share = len(weights), weights[0].shape[2]
    rows = block_rows * len(xs)
    step_rows = min(512, rows)
    steps = rows // step_rows
    first = prior is None
    acc = jax.ShapeDtypeStruct((shares, 2, width, share), F32)
    acc_trunk = jax.ShapeDtypeStruct((width, width), F32)
    loss = jax.ShapeDtypeStruct((rows // LOSSES, LOSSES), F32)
    args = list(xs) + [trunk_weight, *weights]
    if not first:
        args += list(prior)
    args += relays
    in_specs = [whole()] * len(args)
    scratch = [
        pltpu.VMEM((rows, 2 * width), BF16),
        pltpu.VMEM((step_rows, shares * share), BF16),
        pltpu.VMEM((step_rows, shares * share), F32),
    ]
    if last:
        args += list(losses) + [mine]
        in_specs += [whole()] * len(losses) + [whole(pltpu.SMEM)]
        outs = [acc]
        if in_turns(experts):
            outs += [jax.ShapeDtypeStruct((width // shares, width), F32)] * shares
        else:
            outs += [acc_trunk]
        outs += [jax.ShapeDtypeStruct((experts * block_rows // LOSSES, LOSSES), F32)]
        scratch += [pltpu.VMEM(a.shape, a.dtype) for a in (acc_trunk, loss)]
    else:
        outs = [acc, acc_trunk, loss]
        outs += [jax.ShapeDtypeStruct(relay.shape, relay.dtype) for relay in relays]
    counts = (len(xs), shares, experts, steps, step_rows, len(relays))
    return pl.pallas_call(
        functools.partial(expert_kernel, counts, order, first, len(losses) + 1 if last else 0),
        out_shape=outs,
        in_specs=in_specs,
        out_specs=[whole()] * len(outs),
        scratch_shapes=scratch,
        compiler_params=pltpu.CompilerParams(vmem_limit_bytes=20 * MIB),
        cost_estimate=pl.CostEstimate(
            flops=12 * rows * width,
            bytes_accessed=rows * width,
            transcendentals=0,
        ),
        name="expert_rows",
    )(*args)


def four(refs):
    return (refs[0][...] + refs[1][...]) + (refs[2][...] + refs[3][...])


def dp_turn_kernel(q0, q1, q2, q3, loss_ref, total_ref, note_ref):
    total = four((q0, q1, q2, q3))
    total_ref[...] = total
    rows = total.shape[0]
    note_ref[:rows, :] = total
    for k in range(4):
        note_ref[rows + k : rows + k + 1, :] = loss_ref[2 * k + 1 : 2 * k + 2, :]
    note_ref[rows + 4 :, :] = jnp.zeros((4, total.shape[1]), F32)


def pair_turn_kernel(me_ref, total_ref, got_ref, loss_ref, *outs):
    rows, width = total_ref.shape
    half = rows // 2
    at = pl.ds(pl.multiple_of((me_ref[0] & 1) * half, half), half)
    for k, ref in enumerate(outs):
        ref[:half, :] = total_ref[at, :] + got_ref[at, :]
        ref[half : half + 1, :] = loss_ref[2 * k : 2 * k + 1, :]
        ref[half + 1 : half + 2, :] = got_ref[rows + k : rows + k + 1, :]
        ref[half + 2 :, :] = jnp.zeros((6, width), F32)


def z_turn_kernel(*refs):
    *notes, total_ref, loss_ref = refs
    half = total_ref.shape[0]
    total_ref[...] = four([note.at[:half, :] for note in notes])
    for k, note in enumerate(notes):
        loss_ref[2 * k : 2 * k + 2, :] = note[half : half + 2, :]


def join_kernel(me_ref, own_ref, other_ref, _, both_ref):
    half = own_ref.shape[0]
    core = me_ref[0] & 1
    both_ref[pl.ds(pl.multiple_of(core * half, half), half), :] = own_ref[...]
    both_ref[pl.ds(pl.multiple_of((1 - core) * half, half), half), :] = other_ref[...]


def assemble_kernel(mine_ref, *refs):
    *held, _, trunk_ref = refs
    for j, ref in enumerate(held):
        rows = ref.shape[0]
        at = pl.multiple_of((mine_ref[0] ^ j) * rows, rows)
        trunk_ref[pl.ds(at, rows), :] = ref[...]


def turn(kernel, held, shapes, name, index=None):
    first = [] if index is None else [index]
    width = held[0].shape[1]
    return pl.pallas_call(
        kernel,
        out_shape=[jax.ShapeDtypeStruct((rows, width), F32) for rows in shapes],
        in_specs=[whole(pltpu.SMEM)] * len(first) + [whole()] * len(held),
        out_specs=[whole()] * len(shapes),
        compiler_params=pltpu.CompilerParams(vmem_limit_bytes=4 * MIB),
        name=name,
    )(*first, *held)


def send_kernel(acc_ref, ahead_ref, up_ref, down_ref):
    for k in range(2):
        up_ref[k] = acc_ref[2 * k + 1, 0].astype(BF16)
        down_ref[k] = acc_ref[k + 2, 1].astype(BF16)


def pass_on_kernel(acc_ref, got_up_ref, got_down_ref, ahead_ref, up_ref, down_ref):
    up_ref[...] = (acc_ref[2, 0] + got_up_ref[1].astype(F32)).astype(BF16)
    down_ref[...] = (acc_ref[1, 1] + got_down_ref[1].astype(F32)).astype(BF16)


def messages(kernel, held, ahead, shape, name):
    return pl.pallas_call(
        kernel,
        out_shape=[jax.ShapeDtypeStruct(shape, BF16)] * 2,
        in_specs=[whole()] * len(held) + [whole(pl.ANY)],
        out_specs=[whole()] * 2,
        compiler_params=pltpu.CompilerParams(vmem_limit_bytes=16 * MIB),
        name=name,
    )(*held, ahead)


def row_loss_kernel(place_ref, loss_ref, row_loss_ref):
    experts, capacity = loss_ref.shape
    groups = place_ref.shape[0]
    place = jnp.concatenate([place_ref[g : g + 1, :] for g in range(groups)], axis=1)
    block = place // capacity
    slot = place - block * capacity
    picks = jnp.where(iota((capacity, place.shape[1]), 0) == slot, 1.0, 0.0)
    found = lax.dot_general(
        loss_ref[...],
        picks,
        (((1,), (0,)), ((), ())),
        precision=lax.Precision.HIGHEST,
        preferred_element_type=F32,
    )
    mine = jnp.sum(
        jnp.where(iota((experts, place.shape[1]), 0) == block, found, 0.0), axis=0, keepdims=True
    )
    for g in range(groups):
        row_loss_ref[g : g + 1, :] = mine[:, g * LANES : (g + 1) * LANES]


def loss_by_row(place, loss):
    return pl.pallas_call(
        row_loss_kernel,
        out_shape=jax.ShapeDtypeStruct(place.shape, F32),
        in_specs=[whole()] * 2,
        out_specs=whole(),
        compiler_params=pltpu.CompilerParams(vmem_limit_bytes=16 * MIB),
        name="row_loss",
    )(place, loss)


def adam_update(params, first, second, grads):
    first_new = beta_one * first + (1.0 - beta_one) * grads
    second_new = beta_two * second + (1.0 - beta_two) * grads * grads
    first_hat = first_new / (1.0 - beta_one**adam_step)
    second_hat = second_new / (1.0 - beta_two**adam_step)
    return (
        params - learn_rate * first_hat / (jnp.sqrt(second_hat) + adam_eps),
        first_new,
        second_new,
    )


def adam_kernel(*refs):
    params_ref, first_ref, second_ref, acc_ref, *got = refs[:8]
    *outs, done_ref = refs[8:]
    for k in range(2):
        grads = acc_ref[0, k] + got[k][0].astype(F32) + got[2 + k][...].astype(F32)
        news = adam_update(params_ref[0, k], first_ref[0, k], second_ref[0, k], grads)
        for ref, new in zip(outs, news):
            ref[0, k] = new
    done_ref[...] = jnp.zeros(done_ref.shape, F32)


def adam(params, first, second, acc, got):
    shape = jax.ShapeDtypeStruct(params.shape, F32)
    return pl.pallas_call(
        adam_kernel,
        out_shape=[shape] * 3 + [jax.ShapeDtypeStruct((8, LANES), F32)],
        in_specs=[whole()] * 8,
        out_specs=[whole()] * 4,
        compiler_params=pltpu.CompilerParams(vmem_limit_bytes=24 * MIB),
        cost_estimate=pl.CostEstimate(
            flops=20 * params.size, bytes_accessed=8 * params.size, transcendentals=params.size
        ),
        name="adam",
    )(params, first, second, acc, *got)


def swap(value, axis, s):
    if s == 0:
        return value
    return lax.ppermute(value, axis, [(i, i ^ s) for i in range(lax.axis_size(axis))])


def on_device(
    cell_table,
    sample_index,
    region,
    targets,
    trunk_weight,
    expert_params,
    first_moment,
    second_moment,
):
    rows = sample_index.shape[0]
    width = cell_table.shape[1]
    experts = lax.axis_size("expert")
    replicas = lax.axis_size("dp")
    capacity = 2 * rows // experts
    me = lax.axis_index("expert").astype(jnp.int32).reshape(1)
    mine = lax.axis_index("dp").astype(jnp.int32).reshape(1)

    up, down = expert_params[0, 0].astype(BF16), expert_params[0, 1].astype(BF16)
    near_up, near_down = swap(up, "dp", 1), swap(down, "dp", 2)
    *blocks, place = pack(me, mine, sample_index, region[:, 0], cell_table, targets, experts, capacity)
    ups, downs = pair(up, near_up, place), pair(down, near_down, place)
    weights = [ups, swap(ups, "dp", 2), downs, swap(downs, "dp", 1)]
    if in_turns(experts):
        batches, later = ((0, 4), (1, 5), (2,), (6,), (3,), (7,)), ()
    else:
        batches, later = (range(experts // 2), range(experts // 2, experts)), ()
    order = [s for batch in batches for s in batch]
    arrived = {s: swap(blocks[s], "expert", s) for s in order if s not in later}
    prior, losses = None, []
    for k, batch in enumerate(batches):
        last = k == len(batches) - 1
        relays = [blocks[s] for s in later] if k == 0 else []
        outs = expert_call(
            [arrived[s] for s in batch], trunk_weight, weights, prior, losses, mine, order, last, relays
        )
        if not last:
            prior = outs[:2]
            losses.append(outs[2])
            for s, block in zip(later, outs[3:]):
                arrived[s] = swap(block, "expert", s)
    acc, *parts, losses = outs

    def send(ahead):
        up, down = messages(send_kernel, [acc], ahead, (2, *acc.shape[2:]), "send")
        return swap(up, "dp", 1), swap(down, "dp", 2)

    def pass_on(got, ahead):
        up, down = messages(pass_on_kernel, [acc, *got], ahead, acc.shape[2:], "pass_on")
        return swap(up, "dp", 2), swap(down, "dp", 1)

    if in_turns(experts):
        quarter = width // replicas
        parts = [swap(part, "dp", j) for j, part in enumerate(parts)]
        total, note = turn(dp_turn_kernel, parts + [losses], (quarter, quarter + 8), "dp_turn")
        got = send(total)
        notes = turn(
            pair_turn_kernel,
            [total, swap(note, "expert", 1), losses],
            (quarter // 2 + 8,) * 4,
            "pair_turn",
            me,
        )
        notes = [swap(note, "expert", 2 * k) for k, note in enumerate(notes)]
        total, loss = turn(z_turn_kernel, notes, (quarter // 2, experts), "z_turn")
        more_up, more_down = pass_on(got, total)
        row_loss = loss_by_row(place, loss)
        other = swap(total, "expert", 1)
        (total,) = turn(join_kernel, [total, other, row_loss], (quarter,), "join", me)
        parts = [swap(total, "dp", j) for j in range(replicas)]
        *news, done = adam(
            expert_params, first_moment, second_moment, acc, [*got, more_up, more_down]
        )
        (trunk_grad,) = turn(assemble_kernel, parts + [done], (width,), "assemble_trunk", mine)
    else:
        got = send(losses)
        more_up, more_down = pass_on(got, losses)
        *news, _ = adam(
            expert_params, first_moment, second_moment, acc, [*got, more_up, more_down]
        )
        trunk_grad = lax.psum(parts[0], ("dp", "expert"))
        places = jnp.arange(experts, dtype=jnp.int32) ^ me
        losses = losses.reshape(experts, capacity)[places]
        loss = lax.all_to_all(losses, "expert", split_axis=0, concat_axis=0, tiled=True)[places]
        row_loss = loss_by_row(place, loss)

    return (trunk_grad, row_loss.reshape(rows), *news)


def solution(mesh):
    placed = (
        P(("dp", "expert"), None),
        P(("dp", "expert")),
        P(("dp", "expert"), None),
        P(("dp", "expert"), None),
        P(),
        P("expert", None, None, "dp"),
        P("expert", None, None, "dp"),
        P("expert", None, None, "dp"),
    )
    return jax.shard_map(
        on_device,
        mesh=mesh,
        in_specs=placed,
        out_specs=(
            P(),
            P(("dp", "expert")),
            P("expert", None, None, "dp"),
            P("expert", None, None, "dp"),
            P("expert", None, None, "dp"),
        ),
        check_vma=False,
    )
```

```python
import functools

import jax
import jax.numpy as jnp
from jax import lax
from jax.experimental import pallas as pl
from jax.experimental.pallas import tpu as pltpu
from jax.sharding import PartitionSpec as P

loss_scale = 1.0 / 32.0
beta_one = 0.9
beta_two = 0.999
learn_rate = 0.05
adam_eps = 1e-08
adam_step = 10

LANES = 128
F32 = jnp.float32
BF16 = jnp.bfloat16
MIB = 1 << 20
LOSSES = 256


def iota(shape, dim):
    return lax.broadcasted_iota(jnp.int32, shape, dim)


def dot(a, b, ca=1, cb=0):
    return lax.dot_general(a, b, (((ca,), (cb,)), ((), ())), preferred_element_type=F32)


def whole(memory_space=pltpu.VMEM):
    return pl.BlockSpec(memory_space=memory_space)


def pack_kernel(experts, capacity, me_ref, mine_ref, index_ref, region_ref, table_ref, target_ref, *refs):
    blocks, place_ref, rows_ref = refs[:experts], refs[experts], refs[experts + 1]
    me = me_ref[0]
    groups = index_ref.shape[0]
    cells, width = table_ref.shape
    expert_id = iota((experts, LANES), 0)
    starts = ((expert_id ^ me) * capacity).astype(F32)
    ahead = jnp.where(iota((LANES, LANES), 0) <= iota((LANES, LANES), 1), 1.0, 0.0).astype(BF16)
    counted = jnp.zeros((experts, LANES), F32)
    places = []
    for g in range(groups):
        hot = jnp.where(region_ref[g : g + 1, :] == expert_id, 1.0, 0.0)
        upto = dot(hot.astype(BF16), ahead)
        places.append(jnp.sum(hot * (upto - 1.0 + counted + starts), axis=0, keepdims=True))
        counted = counted + jnp.broadcast_to(upto[:, LANES - 1 :], (experts, LANES))
    for g in range(groups):
        place_ref[g : g + 1, :] = places[g].astype(jnp.int32)
    place = jnp.concatenate(places, axis=1)

    step = 2
    cell_id = iota((LANES * step, LANES), 1).astype(F32)
    for g in range(0, groups, step):
        column = jnp.concatenate(
            [
                jnp.broadcast_to(index_ref[h : h + 1, :].astype(F32), (LANES, LANES)).T
                for h in range(g, g + step)
            ],
            axis=0,
        )
        picks = jnp.concatenate(
            [
                jnp.where(column == cell_id + float(LANES * t), 1.0, 0.0).astype(BF16)
                for t in range(cells // LANES)
            ],
            axis=1,
        )
        at = slice(g * LANES, (g + step) * LANES)
        rows_ref[at, :width] = dot(picks, table_ref[...]).astype(BF16)
        rows_ref[at, width:] = target_ref[at, :]

    slot_id = iota((capacity, place.shape[1]), 0).astype(F32)
    for s in range(experts):
        spread = jnp.where(place == slot_id + float(s * capacity), 1.0, 0.0).astype(BF16)
        blocks[s][...] = dot(spread, rows_ref[...]).astype(BF16)


def pack(me, mine, index, region, table, targets, experts, capacity):
    rows, width = targets.shape
    groups = rows // LANES
    return pl.pallas_call(
        functools.partial(pack_kernel, experts, capacity),
        out_shape=[jax.ShapeDtypeStruct((capacity, 2 * width), BF16)] * experts
        + [jax.ShapeDtypeStruct((groups, LANES), jnp.int32)],
        in_specs=[whole(pltpu.SMEM)] * 2 + [whole()] * 4,
        out_specs=[whole()] * (experts + 1),
        scratch_shapes=[pltpu.VMEM((rows, 2 * width), BF16)],
        compiler_params=pltpu.CompilerParams(vmem_limit_bytes=24 * MIB),
        cost_estimate=pl.CostEstimate(
            flops=2 * rows * width * (table.shape[0] + 2 * experts * capacity),
            bytes_accessed=6 * MIB,
            transcendentals=0,
        ),
        name="pack_rows",
    )(me, mine, index.reshape(groups, LANES), region.reshape(groups, LANES), table, targets)


def pair_kernel(one_ref, other_ref, ahead_ref, both_ref):
    both_ref[0] = one_ref[...]
    both_ref[1] = other_ref[...]


def pair(one, other, ahead):
    return pl.pallas_call(
        pair_kernel,
        out_shape=jax.ShapeDtypeStruct((2, *one.shape), one.dtype),
        in_specs=[whole()] * 2 + [whole(pl.ANY)],
        out_specs=whole(),
        compiler_params=pltpu.CompilerParams(vmem_limit_bytes=4 * MIB),
        name="pair",
    )(one, other, ahead)


def sigmoid(v):
    return 0.5 * jnp.tanh(0.5 * v) + 0.5


def expert_kernel(counts, order, first, last, *refs):
    blocks, shares, experts, steps, step_rows, relays = counts
    refs = list(refs)

    def take(n):
        got = refs[:n]
        del refs[:n]
        return got

    xs = take(blocks)
    trunk_ref, ups_near, ups_far, downs_near, downs_far = take(5)
    ups = (ups_near.at[0], ups_near.at[1], ups_far.at[0], ups_far.at[1])
    downs = (downs_near.at[0], downs_far.at[0], downs_near.at[1], downs_far.at[1])
    if not first:
        prior_ref, prior_trunk_ref = take(2)
    held = take(relays)
    if last:
        loss_refs = take(last - 1)
        (mine_ref,) = take(1)
        (acc_ref,) = take(1)
        trunk_parts = take(shares if in_turns(experts) else 1)
        (all_loss_ref,) = take(1)
    else:
        acc_ref, acc_trunk_ref, loss_ref = take(3)
        for source, copy in zip(held, take(relays)):
            copy[...] = source[...]
    x_ref, hid_ref, slope_ref = take(3)
    if last:
        acc_trunk_ref, loss_ref = take(2)

    width = trunk_ref.shape[0]
    share = ups_near.shape[2]
    block_rows = xs[0].shape[0]
    for i, ref in enumerate(xs):
        x_ref[i * block_rows : (i + 1) * block_rows, :] = ref[...]
    looped = steps > 3
    if looped and first:
        acc_ref[...] = jnp.zeros(acc_ref.shape, F32)
        acc_trunk_ref[...] = jnp.zeros(acc_trunk_ref.shape, F32)
    elif looped:
        acc_ref[...] = prior_ref[...]
        acc_trunk_ref[...] = prior_trunk_ref[...]

    def add(i, ref, source, at, value):
        if looped or i > 0:
            ref[at] += value
        elif first:
            ref[at] = value
        else:
            ref[at] = source[at] + value

    prior = None if first else prior_ref
    prior_trunk = None if first else prior_trunk_ref

    def step(i, carry):
        if looped:
            at = pl.ds(pl.multiple_of(i * step_rows, step_rows), step_rows)
        else:
            at = slice(i * step_rows, (i + 1) * step_rows)
        feats = x_ref[at, :width]
        feats_f = feats.astype(F32)
        trunk_pre = dot(feats, trunk_ref[...])
        gate = sigmoid(trunk_pre)
        act = trunk_pre * gate
        trunk_slope = gate + act * (1.0 - gate)
        out_f = feats_f + act
        out = out_f.astype(BF16)
        predicted = jnp.zeros((step_rows, width), F32)
        for j in range(shares):
            up = dot(out, ups[j][...])
            s = sigmoid(up)
            h = up * s
            slope_ref[:, j * share : (j + 1) * share] = s + h * (1.0 - s)
            h = h.astype(BF16)
            hid_ref[:, j * share : (j + 1) * share] = h
            predicted = predicted + dot(h, downs[j][...], 1, 1)
        errors = predicted - x_ref[at, width:].astype(F32)
        squares = errors * errors
        half = squares[:, :LANES]
        for k in range(1, width // LANES):
            half = half + squares[:, k * LANES : (k + 1) * LANES]
        lost = jnp.sum(half.T, axis=0, keepdims=True) * (0.5 * loss_scale)
        for k in range(step_rows // LOSSES):
            row = pl.ds(i * (step_rows // LOSSES) + k, 1)
            loss_ref[row, :] = lost[:, k * LOSSES : (k + 1) * LOSSES]
        scaled_f = errors * loss_scale
        scaled = scaled_f.astype(BF16)
        scaled_t = scaled_f.T.astype(BF16)
        out_t = out_f.T.astype(BF16)
        row_grad = jnp.zeros((step_rows, width), F32)
        for j in range(shares):
            part = slice(j * share, (j + 1) * share)
            add(i, acc_ref, prior, (j, 1), dot(scaled_t, hid_ref[:, part]))
            pre = (dot(scaled, downs[j][...]) * slope_ref[:, part]).astype(BF16)
            add(i, acc_ref, prior, (j, 0), dot(out_t, pre))
            row_grad = row_grad + dot(pre, ups[j][...], 1, 1)
        slope = (row_grad.astype(BF16).astype(F32) * trunk_slope).astype(BF16)
        add(i, acc_trunk_ref, prior_trunk, ..., dot(feats_f.T.astype(BF16), slope))
        return carry

    if looped:
        lax.fori_loop(0, steps, step, 0)
    else:
        for i in range(steps):
            step(i, 0)
    if last:
        all_losses = list(loss_refs) + [loss_ref]
        if not in_turns(experts):
            trunk_parts[0][...] = acc_trunk_ref[...]
            for row in range(all_loss_ref.shape[0]):
                all_loss_ref[row : row + 1, :] = loss_row(all_losses, row)
            return
        quarter = width // shares
        for j, ref in enumerate(trunk_parts):
            at = pl.multiple_of((mine_ref[0] ^ j) * quarter, quarter)
            ref[...] = acc_trunk_ref[pl.ds(at, quarter), :]
        for s in range(experts):
            all_loss_ref[s : s + 1, :] = loss_row(all_losses, order.index(s))


def in_turns(experts):
    return experts == 8


def loss_row(refs, row):
    for ref in refs:
        if row < ref.shape[0]:
            return ref[row : row + 1, :]
        row -= ref.shape[0]


def expert_call(xs, trunk_weight, weights, prior, losses, mine, order, last, relays=()):
    experts = len(order)
    block_rows = xs[0].shape[0]
    width = trunk_weight.shape[0]
    shares, share = len(weights), weights[0].shape[2]
    rows = block_rows * len(xs)
    step_rows = min(512, rows)
    steps = rows // step_rows
    first = prior is None
    acc = jax.ShapeDtypeStruct((shares, 2, width, share), F32)
    acc_trunk = jax.ShapeDtypeStruct((width, width), F32)
    loss = jax.ShapeDtypeStruct((rows // LOSSES, LOSSES), F32)
    args = list(xs) + [trunk_weight, *weights]
    if not first:
        args += list(prior)
    args += relays
    in_specs = [whole()] * len(args)
    scratch = [
        pltpu.VMEM((rows, 2 * width), BF16),
        pltpu.VMEM((step_rows, shares * share), BF16),
        pltpu.VMEM((step_rows, shares * share), F32),
    ]
    if last:
        args += list(losses) + [mine]
        in_specs += [whole()] * len(losses) + [whole(pltpu.SMEM)]
        outs = [acc]
        if in_turns(experts):
            outs += [jax.ShapeDtypeStruct((width // shares, width), F32)] * shares
        else:
            outs += [acc_trunk]
        outs += [jax.ShapeDtypeStruct((experts * block_rows // LOSSES, LOSSES), F32)]
        scratch += [pltpu.VMEM(a.shape, a.dtype) for a in (acc_trunk, loss)]
    else:
        outs = [acc, acc_trunk, loss]
        outs += [jax.ShapeDtypeStruct(relay.shape, relay.dtype) for relay in relays]
    counts = (len(xs), shares, experts, steps, step_rows, len(relays))
    return pl.pallas_call(
        functools.partial(expert_kernel, counts, order, first, len(losses) + 1 if last else 0),
        out_shape=outs,
        in_specs=in_specs,
        out_specs=[whole()] * len(outs),
        scratch_shapes=scratch,
        compiler_params=pltpu.CompilerParams(vmem_limit_bytes=20 * MIB),
        cost_estimate=pl.CostEstimate(
            flops=12 * rows * width,
            bytes_accessed=rows * width,
            transcendentals=0,
        ),
        name="expert_rows",
    )(*args)


def four(refs):
    return (refs[0][...] + refs[1][...]) + (refs[2][...] + refs[3][...])


def dp_turn_kernel(q0, q1, q2, q3, loss_ref, total_ref, note_ref):
    total = four((q0, q1, q2, q3))
    total_ref[...] = total
    rows = total.shape[0]
    note_ref[:rows, :] = total
    for k in range(4):
        note_ref[rows + k : rows + k + 1, :] = loss_ref[2 * k + 1 : 2 * k + 2, :]
    note_ref[rows + 4 :, :] = jnp.zeros((4, total.shape[1]), F32)


def pair_turn_kernel(me_ref, total_ref, got_ref, loss_ref, *outs):
    rows, width = total_ref.shape
    half = rows // 2
    at = pl.ds(pl.multiple_of((me_ref[0] & 1) * half, half), half)
    for k, ref in enumerate(outs):
        ref[:half, :] = total_ref[at, :] + got_ref[at, :]
        ref[half : half + 1, :] = loss_ref[2 * k : 2 * k + 1, :]
        ref[half + 1 : half + 2, :] = got_ref[rows + k : rows + k + 1, :]
        ref[half + 2 :, :] = jnp.zeros((6, width), F32)


def z_turn_kernel(*refs):
    *notes, total_ref, loss_ref = refs
    half = total_ref.shape[0]
    total_ref[...] = four([note.at[:half, :] for note in notes])
    for k, note in enumerate(notes):
        loss_ref[2 * k : 2 * k + 2, :] = note[half : half + 2, :]


def join_kernel(me_ref, own_ref, other_ref, _, both_ref):
    half = own_ref.shape[0]
    core = me_ref[0] & 1
    both_ref[pl.ds(pl.multiple_of(core * half, half), half), :] = own_ref[...]
    both_ref[pl.ds(pl.multiple_of((1 - core) * half, half), half), :] = other_ref[...]


def assemble_kernel(mine_ref, *refs):
    *held, _, trunk_ref = refs
    for j, ref in enumerate(held):
        rows = ref.shape[0]
        at = pl.multiple_of((mine_ref[0] ^ j) * rows, rows)
        trunk_ref[pl.ds(at, rows), :] = ref[...]


def turn(kernel, held, shapes, name, index=None):
    first = [] if index is None else [index]
    width = held[0].shape[1]
    return pl.pallas_call(
        kernel,
        out_shape=[jax.ShapeDtypeStruct((rows, width), F32) for rows in shapes],
        in_specs=[whole(pltpu.SMEM)] * len(first) + [whole()] * len(held),
        out_specs=[whole()] * len(shapes),
        compiler_params=pltpu.CompilerParams(vmem_limit_bytes=4 * MIB),
        name=name,
    )(*first, *held)


def send_kernel(acc_ref, ahead_ref, up_ref, down_ref):
    for k in range(2):
        up_ref[k] = acc_ref[2 * k + 1, 0].astype(BF16)
        down_ref[k] = acc_ref[k + 2, 1].astype(BF16)


def pass_on_kernel(acc_ref, got_up_ref, got_down_ref, ahead_ref, up_ref, down_ref):
    up_ref[...] = (acc_ref[2, 0] + got_up_ref[1].astype(F32)).astype(BF16)
    down_ref[...] = (acc_ref[1, 1] + got_down_ref[1].astype(F32)).astype(BF16)


def messages(kernel, held, ahead, shape, name):
    return pl.pallas_call(
        kernel,
        out_shape=[jax.ShapeDtypeStruct(shape, BF16)] * 2,
        in_specs=[whole()] * len(held) + [whole(pl.ANY)],
        out_specs=[whole()] * 2,
        compiler_params=pltpu.CompilerParams(vmem_limit_bytes=16 * MIB),
        name=name,
    )(*held, ahead)


def row_loss_kernel(place_ref, loss_ref, row_loss_ref, done_ref):
    experts, capacity = loss_ref.shape
    groups = place_ref.shape[0]
    place = jnp.concatenate([place_ref[g : g + 1, :] for g in range(groups)], axis=1)
    block = place // capacity
    slot = place - block * capacity
    picks = jnp.where(iota((capacity, place.shape[1]), 0) == slot, 1.0, 0.0)
    found = lax.dot_general(
        loss_ref[...],
        picks,
        (((1,), (0,)), ((), ())),
        precision=lax.Precision.HIGHEST,
        preferred_element_type=F32,
    )
    mine = jnp.sum(
        jnp.where(iota((experts, place.shape[1]), 0) == block, found, 0.0), axis=0, keepdims=True
    )
    for g in range(groups):
        row_loss_ref[g : g + 1, :] = mine[:, g * LANES : (g + 1) * LANES]
    done_ref[...] = jnp.zeros(done_ref.shape, F32)


def loss_by_row(place, loss):
    return pl.pallas_call(
        row_loss_kernel,
        out_shape=[jax.ShapeDtypeStruct(shape, F32) for shape in (place.shape, (8, LANES))],
        in_specs=[whole()] * 2,
        out_specs=[whole()] * 2,
        compiler_params=pltpu.CompilerParams(vmem_limit_bytes=16 * MIB),
        name="row_loss",
    )(place, loss)


def adam_update(params, first, second, grads):
    first_new = beta_one * first + (1.0 - beta_one) * grads
    second_new = beta_two * second + (1.0 - beta_two) * grads * grads
    first_hat = first_new / (1.0 - beta_one**adam_step)
    second_hat = second_new / (1.0 - beta_two**adam_step)
    return (
        params - learn_rate * first_hat / (jnp.sqrt(second_hat) + adam_eps),
        first_new,
        second_new,
    )


def adam_kernel(*refs):
    params_ref, first_ref, second_ref, acc_ref, *got = refs[:8]
    *outs, done_ref = refs[8:]
    for k in range(2):
        grads = acc_ref[0, k] + got[k][0].astype(F32) + got[2 + k][...].astype(F32)
        news = adam_update(params_ref[0, k], first_ref[0, k], second_ref[0, k], grads)
        for ref, new in zip(outs, news):
            ref[0, k] = new
    done_ref[...] = jnp.zeros(done_ref.shape, F32)


def adam(params, first, second, acc, got):
    shape = jax.ShapeDtypeStruct(params.shape, F32)
    return pl.pallas_call(
        adam_kernel,
        out_shape=[shape] * 3 + [jax.ShapeDtypeStruct((8, LANES), F32)],
        in_specs=[whole()] * 8,
        out_specs=[whole()] * 4,
        compiler_params=pltpu.CompilerParams(vmem_limit_bytes=24 * MIB),
        cost_estimate=pl.CostEstimate(
            flops=20 * params.size, bytes_accessed=8 * params.size, transcendentals=params.size
        ),
        name="adam",
    )(params, first, second, acc, *got)


def swap(value, axis, s):
    if s == 0:
        return value
    return lax.ppermute(value, axis, [(i, i ^ s) for i in range(lax.axis_size(axis))])


def on_device(
    cell_table,
    sample_index,
    region,
    targets,
    trunk_weight,
    expert_params,
    first_moment,
    second_moment,
):
    rows = sample_index.shape[0]
    width = cell_table.shape[1]
    experts = lax.axis_size("expert")
    replicas = lax.axis_size("dp")
    capacity = 2 * rows // experts
    me = lax.axis_index("expert").astype(jnp.int32).reshape(1)
    mine = lax.axis_index("dp").astype(jnp.int32).reshape(1)

    up, down = expert_params[0, 0].astype(BF16), expert_params[0, 1].astype(BF16)
    near_up, near_down = swap(up, "dp", 1), swap(down, "dp", 2)
    *blocks, place = pack(me, mine, sample_index, region[:, 0], cell_table, targets, experts, capacity)
    ups, downs = pair(up, near_up, place), pair(down, near_down, place)
    weights = [ups, swap(ups, "dp", 2), downs, swap(downs, "dp", 1)]
    if in_turns(experts):
        batches, later = ((0, 4), (1, 5), (2,), (6, 3), (7,)), ()
    else:
        batches, later = (range(experts // 2), range(experts // 2, experts)), ()
    order = [s for batch in batches for s in batch]
    arrived = {s: swap(blocks[s], "expert", s) for s in order if s not in later}
    prior, losses = None, []
    for k, batch in enumerate(batches):
        last = k == len(batches) - 1
        relays = [blocks[s] for s in later] if k == 0 else []
        outs = expert_call(
            [arrived[s] for s in batch], trunk_weight, weights, prior, losses, mine, order, last, relays
        )
        if not last:
            prior = outs[:2]
            losses.append(outs[2])
            for s, block in zip(later, outs[3:]):
                arrived[s] = swap(block, "expert", s)
    acc, *parts, losses = outs

    def send(ahead):
        up, down = messages(send_kernel, [acc], ahead, (2, *acc.shape[2:]), "send")
        return swap(up, "dp", 1), swap(down, "dp", 2)

    def pass_on(got, ahead):
        up, down = messages(pass_on_kernel, [acc, *got], ahead, acc.shape[2:], "pass_on")
        return swap(up, "dp", 2), swap(down, "dp", 1)

    if in_turns(experts):
        quarter = width // replicas
        parts = [swap(part, "dp", j) for j, part in enumerate(parts)]
        total, note = turn(dp_turn_kernel, parts + [losses], (quarter, quarter + 8), "dp_turn")
        got = send(total)
        notes = turn(
            pair_turn_kernel,
            [total, swap(note, "expert", 1), losses],
            (quarter // 2 + 8,) * 4,
            "pair_turn",
            me,
        )
        notes = [swap(note, "expert", 2 * k) for k, note in enumerate(notes)]
        total, loss = turn(z_turn_kernel, notes, (quarter // 2, experts), "z_turn")
        more_up, more_down = pass_on(got, total)
        row_loss, found = loss_by_row(place, loss)
        other = swap(total, "expert", 1)
        (total,) = turn(join_kernel, [total, other, found], (quarter,), "join", me)
        parts = [swap(total, "dp", j) for j in range(replicas)]
        *news, done = adam(
            expert_params, first_moment, second_moment, acc, [*got, more_up, more_down]
        )
        (trunk_grad,) = turn(assemble_kernel, parts + [done], (width,), "assemble_trunk", mine)
    else:
        got = send(losses)
        more_up, more_down = pass_on(got, losses)
        *news, _ = adam(
            expert_params, first_moment, second_moment, acc, [*got, more_up, more_down]
        )
        trunk_grad = lax.psum(parts[0], ("dp", "expert"))
        places = jnp.arange(experts, dtype=jnp.int32) ^ me
        losses = losses.reshape(experts, capacity)[places]
        loss = lax.all_to_all(losses, "expert", split_axis=0, concat_axis=0, tiled=True)[places]
        row_loss, _ = loss_by_row(place, loss)

    return (trunk_grad, row_loss.reshape(rows), *news)


def solution(mesh):
    placed = (
        P(("dp", "expert"), None),
        P(("dp", "expert")),
        P(("dp", "expert"), None),
        P(("dp", "expert"), None),
        P(),
        P("expert", None, None, "dp"),
        P("expert", None, None, "dp"),
        P("expert", None, None, "dp"),
    )
    return jax.shard_map(
        on_device,
        mesh=mesh,
        in_specs=placed,
        out_specs=(
            P(),
            P(("dp", "expert")),
            P("expert", None, None, "dp"),
            P("expert", None, None, "dp"),
            P("expert", None, None, "dp"),
        ),
        check_vma=False,
    )
```

```python
import functools

import jax
import jax.numpy as jnp
from jax import lax
from jax.experimental import pallas as pl
from jax.experimental.pallas import tpu as pltpu
from jax.sharding import PartitionSpec as P

loss_scale = 1.0 / 32.0
beta_one = 0.9
beta_two = 0.999
learn_rate = 0.05
adam_eps = 1e-08
adam_step = 10

LANES = 128
F32 = jnp.float32
BF16 = jnp.bfloat16
MIB = 1 << 20
LOSSES = 256


def iota(shape, dim):
    return lax.broadcasted_iota(jnp.int32, shape, dim)


def dot(a, b, ca=1, cb=0):
    return lax.dot_general(a, b, (((ca,), (cb,)), ((), ())), preferred_element_type=F32)


def whole(memory_space=pltpu.VMEM):
    return pl.BlockSpec(memory_space=memory_space)


def pack_kernel(experts, capacity, me_ref, mine_ref, index_ref, region_ref, table_ref, target_ref, *refs):
    blocks, place_ref, rows_ref = refs[:experts], refs[experts], refs[experts + 1]
    me = me_ref[0]
    groups = index_ref.shape[0]
    cells, width = table_ref.shape
    expert_id = iota((experts, LANES), 0)
    starts = ((expert_id ^ me) * capacity).astype(F32)
    ahead = jnp.where(iota((LANES, LANES), 0) <= iota((LANES, LANES), 1), 1.0, 0.0).astype(BF16)
    counted = jnp.zeros((experts, LANES), F32)
    places = []
    for g in range(groups):
        hot = jnp.where(region_ref[g : g + 1, :] == expert_id, 1.0, 0.0)
        upto = dot(hot.astype(BF16), ahead)
        places.append(jnp.sum(hot * (upto - 1.0 + counted + starts), axis=0, keepdims=True))
        counted = counted + jnp.broadcast_to(upto[:, LANES - 1 :], (experts, LANES))
    for g in range(groups):
        place_ref[g : g + 1, :] = places[g].astype(jnp.int32)
    place = jnp.concatenate(places, axis=1)

    step = 2
    cell_id = iota((LANES * step, LANES), 1).astype(F32)
    for g in range(0, groups, step):
        column = jnp.concatenate(
            [
                jnp.broadcast_to(index_ref[h : h + 1, :].astype(F32), (LANES, LANES)).T
                for h in range(g, g + step)
            ],
            axis=0,
        )
        picks = jnp.concatenate(
            [
                jnp.where(column == cell_id + float(LANES * t), 1.0, 0.0).astype(BF16)
                for t in range(cells // LANES)
            ],
            axis=1,
        )
        at = slice(g * LANES, (g + step) * LANES)
        rows_ref[at, :width] = dot(picks, table_ref[...]).astype(BF16)
        rows_ref[at, width:] = target_ref[at, :]

    slot_id = iota((capacity, place.shape[1]), 0).astype(F32)
    for s in range(experts):
        spread = jnp.where(place == slot_id + float(s * capacity), 1.0, 0.0).astype(BF16)
        blocks[s][...] = dot(spread, rows_ref[...]).astype(BF16)


def pack(me, mine, index, region, table, targets, experts, capacity):
    rows, width = targets.shape
    groups = rows // LANES
    return pl.pallas_call(
        functools.partial(pack_kernel, experts, capacity),
        out_shape=[jax.ShapeDtypeStruct((capacity, 2 * width), BF16)] * experts
        + [jax.ShapeDtypeStruct((groups, LANES), jnp.int32)],
        in_specs=[whole(pltpu.SMEM)] * 2 + [whole()] * 4,
        out_specs=[whole()] * (experts + 1),
        scratch_shapes=[pltpu.VMEM((rows, 2 * width), BF16)],
        compiler_params=pltpu.CompilerParams(vmem_limit_bytes=24 * MIB),
        cost_estimate=pl.CostEstimate(
            flops=2 * rows * width * (table.shape[0] + 2 * experts * capacity),
            bytes_accessed=6 * MIB,
            transcendentals=0,
        ),
        name="pack_rows",
    )(me, mine, index.reshape(groups, LANES), region.reshape(groups, LANES), table, targets)


def pair_kernel(one_ref, other_ref, ahead_ref, both_ref):
    both_ref[0] = one_ref[...]
    both_ref[1] = other_ref[...]


def pair(one, other, ahead):
    return pl.pallas_call(
        pair_kernel,
        out_shape=jax.ShapeDtypeStruct((2, *one.shape), one.dtype),
        in_specs=[whole()] * 2 + [whole(pl.ANY)],
        out_specs=whole(),
        compiler_params=pltpu.CompilerParams(vmem_limit_bytes=4 * MIB),
        name="pair",
    )(one, other, ahead)


def sigmoid(v):
    return 0.5 * jnp.tanh(0.5 * v) + 0.5


def expert_kernel(counts, order, first, last, *refs):
    blocks, shares, experts, steps, step_rows, relays = counts
    refs = list(refs)

    def take(n):
        got = refs[:n]
        del refs[:n]
        return got

    xs = take(blocks)
    trunk_ref, ups_near, ups_far, downs_near, downs_far = take(5)
    ups = (ups_near.at[0], ups_near.at[1], ups_far.at[0], ups_far.at[1])
    downs = (downs_near.at[0], downs_far.at[0], downs_near.at[1], downs_far.at[1])
    if not first:
        prior_ref, prior_trunk_ref = take(2)
    held = take(relays)
    if last:
        loss_refs = take(last - 1)
        (mine_ref,) = take(1)
        (acc_ref,) = take(1)
        trunk_parts = take(shares if in_turns(experts) else 1)
        (all_loss_ref,) = take(1)
    else:
        acc_ref, acc_trunk_ref, loss_ref = take(3)
        for source, copy in zip(held, take(relays)):
            copy[...] = source[...]
    x_ref, hid_ref, slope_ref = take(3)
    if last:
        acc_trunk_ref, loss_ref = take(2)

    width = trunk_ref.shape[0]
    share = ups_near.shape[2]
    block_rows = xs[0].shape[0]
    for i, ref in enumerate(xs):
        x_ref[i * block_rows : (i + 1) * block_rows, :] = ref[...]
    looped = steps > 3
    if looped and first:
        acc_ref[...] = jnp.zeros(acc_ref.shape, F32)
        acc_trunk_ref[...] = jnp.zeros(acc_trunk_ref.shape, F32)
    elif looped:
        acc_ref[...] = prior_ref[...]
        acc_trunk_ref[...] = prior_trunk_ref[...]

    def add(i, ref, source, at, value):
        if looped or i > 0:
            ref[at] += value
        elif first:
            ref[at] = value
        else:
            ref[at] = source[at] + value

    prior = None if first else prior_ref
    prior_trunk = None if first else prior_trunk_ref

    def step(i, carry):
        if looped:
            at = pl.ds(pl.multiple_of(i * step_rows, step_rows), step_rows)
        else:
            at = slice(i * step_rows, (i + 1) * step_rows)
        feats = x_ref[at, :width]
        feats_f = feats.astype(F32)
        trunk_pre = dot(feats, trunk_ref[...])
        gate = sigmoid(trunk_pre)
        act = trunk_pre * gate
        trunk_slope = gate + act * (1.0 - gate)
        out_f = feats_f + act
        out = out_f.astype(BF16)
        predicted = jnp.zeros((step_rows, width), F32)
        for j in range(shares):
            up = dot(out, ups[j][...])
            s = sigmoid(up)
            h = up * s
            slope_ref[:, j * share : (j + 1) * share] = s + h * (1.0 - s)
            h = h.astype(BF16)
            hid_ref[:, j * share : (j + 1) * share] = h
            predicted = predicted + dot(h, downs[j][...], 1, 1)
        errors = predicted - x_ref[at, width:].astype(F32)
        squares = errors * errors
        half = squares[:, :LANES]
        for k in range(1, width // LANES):
            half = half + squares[:, k * LANES : (k + 1) * LANES]
        lost = jnp.sum(half.T, axis=0, keepdims=True) * (0.5 * loss_scale)
        for k in range(step_rows // LOSSES):
            row = pl.ds(i * (step_rows // LOSSES) + k, 1)
            loss_ref[row, :] = lost[:, k * LOSSES : (k + 1) * LOSSES]
        scaled_f = errors * loss_scale
        scaled = scaled_f.astype(BF16)
        scaled_t = scaled_f.T.astype(BF16)
        out_t = out_f.T.astype(BF16)
        row_grad = jnp.zeros((step_rows, width), F32)
        for j in range(shares):
            part = slice(j * share, (j + 1) * share)
            add(i, acc_ref, prior, (j, 1), dot(scaled_t, hid_ref[:, part]))
            pre = (dot(scaled, downs[j][...]) * slope_ref[:, part]).astype(BF16)
            add(i, acc_ref, prior, (j, 0), dot(out_t, pre))
            row_grad = row_grad + dot(pre, ups[j][...], 1, 1)
        slope = (row_grad.astype(BF16).astype(F32) * trunk_slope).astype(BF16)
        add(i, acc_trunk_ref, prior_trunk, ..., dot(feats_f.T.astype(BF16), slope))
        return carry

    if looped:
        lax.fori_loop(0, steps, step, 0)
    else:
        for i in range(steps):
            step(i, 0)
    if last:
        all_losses = list(loss_refs) + [loss_ref]
        if not in_turns(experts):
            trunk_parts[0][...] = acc_trunk_ref[...]
            for row in range(all_loss_ref.shape[0]):
                all_loss_ref[row : row + 1, :] = loss_row(all_losses, row)
            return
        quarter = width // shares
        for j, ref in enumerate(trunk_parts):
            at = pl.multiple_of((mine_ref[0] ^ j) * quarter, quarter)
            ref[...] = acc_trunk_ref[pl.ds(at, quarter), :]
        for s in range(experts):
            all_loss_ref[s : s + 1, :] = loss_row(all_losses, order.index(s))


def in_turns(experts):
    return experts == 8


def loss_row(refs, row):
    for ref in refs:
        if row < ref.shape[0]:
            return ref[row : row + 1, :]
        row -= ref.shape[0]


def expert_call(xs, trunk_weight, weights, prior, losses, mine, order, last, relays=()):
    experts = len(order)
    block_rows = xs[0].shape[0]
    width = trunk_weight.shape[0]
    shares, share = len(weights), weights[0].shape[2]
    rows = block_rows * len(xs)
    step_rows = min(512, rows)
    steps = rows // step_rows
    first = prior is None
    acc = jax.ShapeDtypeStruct((shares, 2, width, share), F32)
    acc_trunk = jax.ShapeDtypeStruct((width, width), F32)
    loss = jax.ShapeDtypeStruct((rows // LOSSES, LOSSES), F32)
    args = list(xs) + [trunk_weight, *weights]
    if not first:
        args += list(prior)
    args += relays
    in_specs = [whole()] * len(args)
    scratch = [
        pltpu.VMEM((rows, 2 * width), BF16),
        pltpu.VMEM((step_rows, shares * share), BF16),
        pltpu.VMEM((step_rows, shares * share), F32),
    ]
    if last:
        args += list(losses) + [mine]
        in_specs += [whole()] * len(losses) + [whole(pltpu.SMEM)]
        outs = [acc]
        if in_turns(experts):
            outs += [jax.ShapeDtypeStruct((width // shares, width), F32)] * shares
        else:
            outs += [acc_trunk]
        outs += [jax.ShapeDtypeStruct((experts * block_rows // LOSSES, LOSSES), F32)]
        scratch += [pltpu.VMEM(a.shape, a.dtype) for a in (acc_trunk, loss)]
    else:
        outs = [acc, acc_trunk, loss]
        outs += [jax.ShapeDtypeStruct(relay.shape, relay.dtype) for relay in relays]
    counts = (len(xs), shares, experts, steps, step_rows, len(relays))
    return pl.pallas_call(
        functools.partial(expert_kernel, counts, order, first, len(losses) + 1 if last else 0),
        out_shape=outs,
        in_specs=in_specs,
        out_specs=[whole()] * len(outs),
        scratch_shapes=scratch,
        compiler_params=pltpu.CompilerParams(vmem_limit_bytes=20 * MIB),
        cost_estimate=pl.CostEstimate(
            flops=12 * rows * width,
            bytes_accessed=rows * width,
            transcendentals=0,
        ),
        name="expert_rows",
    )(*args)


def four(refs):
    return (refs[0][...] + refs[1][...]) + (refs[2][...] + refs[3][...])


def dp_turn_kernel(q0, q1, q2, q3, loss_ref, total_ref, note_ref):
    total = four((q0, q1, q2, q3))
    total_ref[...] = total
    rows = total.shape[0]
    note_ref[:rows, :] = total
    for k in range(4):
        note_ref[rows + k : rows + k + 1, :] = loss_ref[2 * k + 1 : 2 * k + 2, :]
    note_ref[rows + 4 :, :] = jnp.zeros((4, total.shape[1]), F32)


def pair_turn_kernel(me_ref, total_ref, got_ref, loss_ref, *outs):
    rows, width = total_ref.shape
    half = rows // 2
    at = pl.ds(pl.multiple_of((me_ref[0] & 1) * half, half), half)
    for k, ref in enumerate(outs):
        ref[:half, :] = total_ref[at, :] + got_ref[at, :]
        ref[half : half + 1, :] = loss_ref[2 * k : 2 * k + 1, :]
        ref[half + 1 : half + 2, :] = got_ref[rows + k : rows + k + 1, :]
        ref[half + 2 :, :] = jnp.zeros((6, width), F32)


def z_turn_kernel(*refs):
    *notes, total_ref, loss_ref = refs
    half = total_ref.shape[0]
    total_ref[...] = four([note.at[:half, :] for note in notes])
    for k, note in enumerate(notes):
        loss_ref[2 * k : 2 * k + 2, :] = note[half : half + 2, :]


def join_kernel(me_ref, own_ref, other_ref, _, both_ref):
    half = own_ref.shape[0]
    core = me_ref[0] & 1
    both_ref[pl.ds(pl.multiple_of(core * half, half), half), :] = own_ref[...]
    both_ref[pl.ds(pl.multiple_of((1 - core) * half, half), half), :] = other_ref[...]


def assemble_kernel(mine_ref, *refs):
    *held, _, trunk_ref = refs
    for j, ref in enumerate(held):
        rows = ref.shape[0]
        at = pl.multiple_of((mine_ref[0] ^ j) * rows, rows)
        trunk_ref[pl.ds(at, rows), :] = ref[...]


def turn(kernel, held, shapes, name, index=None):
    first = [] if index is None else [index]
    width = held[0].shape[1]
    return pl.pallas_call(
        kernel,
        out_shape=[jax.ShapeDtypeStruct((rows, width), F32) for rows in shapes],
        in_specs=[whole(pltpu.SMEM)] * len(first) + [whole()] * len(held),
        out_specs=[whole()] * len(shapes),
        compiler_params=pltpu.CompilerParams(vmem_limit_bytes=4 * MIB),
        name=name,
    )(*first, *held)


def send_kernel(acc_ref, ahead_ref, up_ref, down_ref):
    for k in range(2):
        up_ref[k] = acc_ref[2 * k + 1, 0].astype(BF16)
        down_ref[k] = acc_ref[k + 2, 1].astype(BF16)


def pass_on_kernel(acc_ref, got_up_ref, got_down_ref, ahead_ref, up_ref, down_ref):
    up_ref[...] = (acc_ref[2, 0] + got_up_ref[1].astype(F32)).astype(BF16)
    down_ref[...] = (acc_ref[1, 1] + got_down_ref[1].astype(F32)).astype(BF16)


def messages(kernel, held, ahead, shape, name):
    return pl.pallas_call(
        kernel,
        out_shape=[jax.ShapeDtypeStruct(shape, BF16)] * 2,
        in_specs=[whole()] * len(held) + [whole(pl.ANY)],
        out_specs=[whole()] * 2,
        compiler_params=pltpu.CompilerParams(vmem_limit_bytes=16 * MIB),
        name=name,
    )(*held, ahead)


def row_loss_kernel(place_ref, loss_ref, row_loss_ref, done_ref):
    experts, capacity = loss_ref.shape
    groups = place_ref.shape[0]
    place = jnp.concatenate([place_ref[g : g + 1, :] for g in range(groups)], axis=1)
    block = place // capacity
    slot = place - block * capacity
    picks = jnp.where(iota((capacity, place.shape[1]), 0) == slot, 1.0, 0.0)
    found = lax.dot_general(
        loss_ref[...],
        picks,
        (((1,), (0,)), ((), ())),
        precision=lax.Precision.HIGHEST,
        preferred_element_type=F32,
    )
    mine = jnp.sum(
        jnp.where(iota((experts, place.shape[1]), 0) == block, found, 0.0), axis=0, keepdims=True
    )
    for g in range(groups):
        row_loss_ref[g : g + 1, :] = mine[:, g * LANES : (g + 1) * LANES]
    done_ref[...] = jnp.zeros(done_ref.shape, F32)


def loss_by_row(place, loss):
    return pl.pallas_call(
        row_loss_kernel,
        out_shape=[jax.ShapeDtypeStruct(shape, F32) for shape in (place.shape, (8, LANES))],
        in_specs=[whole()] * 2,
        out_specs=[whole()] * 2,
        compiler_params=pltpu.CompilerParams(vmem_limit_bytes=16 * MIB),
        name="row_loss",
    )(place, loss)


def adam_update(params, first, second, grads):
    first_new = beta_one * first + (1.0 - beta_one) * grads
    second_new = beta_two * second + (1.0 - beta_two) * grads * grads
    first_hat = first_new / (1.0 - beta_one**adam_step)
    second_hat = second_new / (1.0 - beta_two**adam_step)
    return (
        params - learn_rate * first_hat / (jnp.sqrt(second_hat) + adam_eps),
        first_new,
        second_new,
    )


def adam_kernel(*refs):
    params_ref, first_ref, second_ref, acc_ref, *got = refs[:8]
    *outs, done_ref = refs[8:]
    for k in range(2):
        grads = acc_ref[0, k] + got[k][0].astype(F32) + got[2 + k][...].astype(F32)
        news = adam_update(params_ref[0, k], first_ref[0, k], second_ref[0, k], grads)
        for ref, new in zip(outs, news):
            ref[0, k] = new
    done_ref[...] = jnp.zeros(done_ref.shape, F32)


def adam(params, first, second, acc, got):
    shape = jax.ShapeDtypeStruct(params.shape, F32)
    return pl.pallas_call(
        adam_kernel,
        out_shape=[shape] * 3 + [jax.ShapeDtypeStruct((8, LANES), F32)],
        in_specs=[whole()] * 8,
        out_specs=[whole()] * 4,
        compiler_params=pltpu.CompilerParams(vmem_limit_bytes=24 * MIB),
        cost_estimate=pl.CostEstimate(
            flops=20 * params.size, bytes_accessed=8 * params.size, transcendentals=params.size
        ),
        name="adam",
    )(params, first, second, acc, *got)


def swap(value, axis, s):
    if s == 0:
        return value
    return lax.ppermute(value, axis, [(i, i ^ s) for i in range(lax.axis_size(axis))])


def on_device(
    cell_table,
    sample_index,
    region,
    targets,
    trunk_weight,
    expert_params,
    first_moment,
    second_moment,
):
    rows = sample_index.shape[0]
    width = cell_table.shape[1]
    experts = lax.axis_size("expert")
    replicas = lax.axis_size("dp")
    capacity = 2 * rows // experts
    me = lax.axis_index("expert").astype(jnp.int32).reshape(1)
    mine = lax.axis_index("dp").astype(jnp.int32).reshape(1)

    up, down = expert_params[0, 0].astype(BF16), expert_params[0, 1].astype(BF16)
    near_up, near_down = swap(up, "dp", 1), swap(down, "dp", 2)
    *blocks, place = pack(me, mine, sample_index, region[:, 0], cell_table, targets, experts, capacity)
    ups, downs = pair(up, near_up, place), pair(down, near_down, place)
    weights = [ups, swap(ups, "dp", 2), downs, swap(downs, "dp", 1)]
    if in_turns(experts):
        batches, later = ((0, 4), (1, 5), (2,), (6,), (7, 3)), ()
    else:
        batches, later = (range(experts // 2), range(experts // 2, experts)), ()
    order = [s for batch in batches for s in batch]
    arrived = {s: swap(blocks[s], "expert", s) for s in order if s not in later}
    prior, losses = None, []
    for k, batch in enumerate(batches):
        last = k == len(batches) - 1
        relays = [blocks[s] for s in later] if k == 0 else []
        outs = expert_call(
            [arrived[s] for s in batch], trunk_weight, weights, prior, losses, mine, order, last, relays
        )
        if not last:
            prior = outs[:2]
            losses.append(outs[2])
            for s, block in zip(later, outs[3:]):
                arrived[s] = swap(block, "expert", s)
    acc, *parts, losses = outs

    def send(ahead):
        up, down = messages(send_kernel, [acc], ahead, (2, *acc.shape[2:]), "send")
        return swap(up, "dp", 1), swap(down, "dp", 2)

    def pass_on(got, ahead):
        up, down = messages(pass_on_kernel, [acc, *got], ahead, acc.shape[2:], "pass_on")
        return swap(up, "dp", 2), swap(down, "dp", 1)

    if in_turns(experts):
        quarter = width // replicas
        parts = [swap(part, "dp", j) for j, part in enumerate(parts)]
        total, note = turn(dp_turn_kernel, parts + [losses], (quarter, quarter + 8), "dp_turn")
        got = send(total)
        notes = turn(
            pair_turn_kernel,
            [total, swap(note, "expert", 1), losses],
            (quarter // 2 + 8,) * 4,
            "pair_turn",
            me,
        )
        notes = [swap(note, "expert", 2 * k) for k, note in enumerate(notes)]
        total, loss = turn(z_turn_kernel, notes, (quarter // 2, experts), "z_turn")
        more_up, more_down = pass_on(got, total)
        row_loss, found = loss_by_row(place, loss)
        other = swap(total, "expert", 1)
        (total,) = turn(join_kernel, [total, other, found], (quarter,), "join", me)
        parts = [swap(total, "dp", j) for j in range(replicas)]
        *news, done = adam(
            expert_params, first_moment, second_moment, acc, [*got, more_up, more_down]
        )
        (trunk_grad,) = turn(assemble_kernel, parts + [done], (width,), "assemble_trunk", mine)
    else:
        got = send(losses)
        more_up, more_down = pass_on(got, losses)
        *news, _ = adam(
            expert_params, first_moment, second_moment, acc, [*got, more_up, more_down]
        )
        trunk_grad = lax.psum(parts[0], ("dp", "expert"))
        places = jnp.arange(experts, dtype=jnp.int32) ^ me
        losses = losses.reshape(experts, capacity)[places]
        loss = lax.all_to_all(losses, "expert", split_axis=0, concat_axis=0, tiled=True)[places]
        row_loss, _ = loss_by_row(place, loss)

    return (trunk_grad, row_loss.reshape(rows), *news)


def solution(mesh):
    placed = (
        P(("dp", "expert"), None),
        P(("dp", "expert")),
        P(("dp", "expert"), None),
        P(("dp", "expert"), None),
        P(),
        P("expert", None, None, "dp"),
        P("expert", None, None, "dp"),
        P("expert", None, None, "dp"),
    )
    return jax.shard_map(
        on_device,
        mesh=mesh,
        in_specs=placed,
        out_specs=(
            P(),
            P(("dp", "expert")),
            P("expert", None, None, "dp"),
            P("expert", None, None, "dp"),
            P("expert", None, None, "dp"),
        ),
        check_vma=False,
    )
```

```python
import functools

import jax
import jax.numpy as jnp
from jax import lax
from jax.experimental import pallas as pl
from jax.experimental.pallas import tpu as pltpu
from jax.sharding import PartitionSpec as P

loss_scale = 1.0 / 32.0
beta_one = 0.9
beta_two = 0.999
learn_rate = 0.05
adam_eps = 1e-08
adam_step = 10

LANES = 128
F32 = jnp.float32
BF16 = jnp.bfloat16
MIB = 1 << 20
LOSSES = 256


def iota(shape, dim):
    return lax.broadcasted_iota(jnp.int32, shape, dim)


def dot(a, b, ca=1, cb=0):
    return lax.dot_general(a, b, (((ca,), (cb,)), ((), ())), preferred_element_type=F32)


def whole(memory_space=pltpu.VMEM):
    return pl.BlockSpec(memory_space=memory_space)


def pack_kernel(experts, capacity, me_ref, mine_ref, index_ref, region_ref, table_ref, target_ref, *refs):
    blocks, place_ref, rows_ref = refs[:experts], refs[experts], refs[experts + 1]
    me = me_ref[0]
    groups = index_ref.shape[0]
    cells, width = table_ref.shape
    expert_id = iota((experts, LANES), 0)
    starts = ((expert_id ^ me) * capacity).astype(F32)
    ahead = jnp.where(iota((LANES, LANES), 0) <= iota((LANES, LANES), 1), 1.0, 0.0).astype(BF16)
    counted = jnp.zeros((experts, LANES), F32)
    places = []
    for g in range(groups):
        hot = jnp.where(region_ref[g : g + 1, :] == expert_id, 1.0, 0.0)
        upto = dot(hot.astype(BF16), ahead)
        places.append(jnp.sum(hot * (upto - 1.0 + counted + starts), axis=0, keepdims=True))
        counted = counted + jnp.broadcast_to(upto[:, LANES - 1 :], (experts, LANES))
    for g in range(groups):
        place_ref[g : g + 1, :] = places[g].astype(jnp.int32)
    place = jnp.concatenate(places, axis=1)

    step = 2
    cell_id = iota((LANES * step, LANES), 1).astype(F32)
    for g in range(0, groups, step):
        column = jnp.concatenate(
            [
                jnp.broadcast_to(index_ref[h : h + 1, :].astype(F32), (LANES, LANES)).T
                for h in range(g, g + step)
            ],
            axis=0,
        )
        picks = jnp.concatenate(
            [
                jnp.where(column == cell_id + float(LANES * t), 1.0, 0.0).astype(BF16)
                for t in range(cells // LANES)
            ],
            axis=1,
        )
        at = slice(g * LANES, (g + step) * LANES)
        rows_ref[at, :width] = dot(picks, table_ref[...]).astype(BF16)
        rows_ref[at, width:] = target_ref[at, :]

    slot_id = iota((capacity, place.shape[1]), 0).astype(F32)
    for s in range(experts):
        spread = jnp.where(place == slot_id + float(s * capacity), 1.0, 0.0).astype(BF16)
        blocks[s][...] = dot(spread, rows_ref[...]).astype(BF16)


def pack(me, mine, index, region, table, targets, experts, capacity):
    rows, width = targets.shape
    groups = rows // LANES
    return pl.pallas_call(
        functools.partial(pack_kernel, experts, capacity),
        out_shape=[jax.ShapeDtypeStruct((capacity, 2 * width), BF16)] * experts
        + [jax.ShapeDtypeStruct((groups, LANES), jnp.int32)],
        in_specs=[whole(pltpu.SMEM)] * 2 + [whole()] * 4,
        out_specs=[whole()] * (experts + 1),
        scratch_shapes=[pltpu.VMEM((rows, 2 * width), BF16)],
        compiler_params=pltpu.CompilerParams(vmem_limit_bytes=24 * MIB),
        cost_estimate=pl.CostEstimate(
            flops=2 * rows * width * (table.shape[0] + 2 * experts * capacity),
            bytes_accessed=6 * MIB,
            transcendentals=0,
        ),
        name="pack_rows",
    )(me, mine, index.reshape(groups, LANES), region.reshape(groups, LANES), table, targets)


def pair_kernel(one_ref, other_ref, ahead_ref, both_ref):
    both_ref[0] = one_ref[...]
    both_ref[1] = other_ref[...]


def pair(one, other, ahead):
    return pl.pallas_call(
        pair_kernel,
        out_shape=jax.ShapeDtypeStruct((2, *one.shape), one.dtype),
        in_specs=[whole()] * 2 + [whole(pl.ANY)],
        out_specs=whole(),
        compiler_params=pltpu.CompilerParams(vmem_limit_bytes=4 * MIB),
        name="pair",
    )(one, other, ahead)


def sigmoid(v):
    return 0.5 * jnp.tanh(0.5 * v) + 0.5


def expert_kernel(counts, order, first, last, *refs):
    blocks, shares, experts, steps, step_rows, relays = counts
    refs = list(refs)

    def take(n):
        got = refs[:n]
        del refs[:n]
        return got

    xs = take(blocks)
    trunk_ref, ups_near, ups_far, downs_near, downs_far = take(5)
    ups = (ups_near.at[0], ups_near.at[1], ups_far.at[0], ups_far.at[1])
    downs = (downs_near.at[0], downs_far.at[0], downs_near.at[1], downs_far.at[1])
    if not first:
        prior_ref, prior_trunk_ref = take(2)
    held = take(relays)
    if last:
        loss_refs = take(last - 1)
        (mine_ref,) = take(1)
        (acc_ref,) = take(1)
        trunk_parts = take(shares if in_turns(experts) else 1)
        (all_loss_ref,) = take(1)
    else:
        acc_ref, acc_trunk_ref, loss_ref = take(3)
        for source, copy in zip(held, take(relays)):
            copy[...] = source[...]
    x_ref, hid_ref, slope_ref = take(3)
    if last:
        acc_trunk_ref, loss_ref = take(2)

    width = trunk_ref.shape[0]
    share = ups_near.shape[2]
    block_rows = xs[0].shape[0]
    for i, ref in enumerate(xs):
        x_ref[i * block_rows : (i + 1) * block_rows, :] = ref[...]
    looped = steps > 3
    if looped and first:
        acc_ref[...] = jnp.zeros(acc_ref.shape, F32)
        acc_trunk_ref[...] = jnp.zeros(acc_trunk_ref.shape, F32)
    elif looped:
        acc_ref[...] = prior_ref[...]
        acc_trunk_ref[...] = prior_trunk_ref[...]

    def add(i, ref, source, at, value):
        if looped or i > 0:
            ref[at] += value
        elif first:
            ref[at] = value
        else:
            ref[at] = source[at] + value

    prior = None if first else prior_ref
    prior_trunk = None if first else prior_trunk_ref

    def step(i, carry):
        if looped:
            at = pl.ds(pl.multiple_of(i * step_rows, step_rows), step_rows)
        else:
            at = slice(i * step_rows, (i + 1) * step_rows)
        feats = x_ref[at, :width]
        feats_f = feats.astype(F32)
        trunk_pre = dot(feats, trunk_ref[...])
        gate = sigmoid(trunk_pre)
        act = trunk_pre * gate
        trunk_slope = gate + act * (1.0 - gate)
        out_f = feats_f + act
        out = out_f.astype(BF16)
        predicted = jnp.zeros((step_rows, width), F32)
        for j in range(shares):
            up = dot(out, ups[j][...])
            s = sigmoid(up)
            h = up * s
            slope_ref[:, j * share : (j + 1) * share] = s + h * (1.0 - s)
            h = h.astype(BF16)
            hid_ref[:, j * share : (j + 1) * share] = h
            predicted = predicted + dot(h, downs[j][...], 1, 1)
        errors = predicted - x_ref[at, width:].astype(F32)
        squares = errors * errors
        half = squares[:, :LANES]
        for k in range(1, width // LANES):
            half = half + squares[:, k * LANES : (k + 1) * LANES]
        lost = jnp.sum(half.T, axis=0, keepdims=True) * (0.5 * loss_scale)
        for k in range(step_rows // LOSSES):
            row = pl.ds(i * (step_rows // LOSSES) + k, 1)
            loss_ref[row, :] = lost[:, k * LOSSES : (k + 1) * LOSSES]
        scaled_f = errors * loss_scale
        scaled = scaled_f.astype(BF16)
        scaled_t = scaled_f.T.astype(BF16)
        out_t = out_f.T.astype(BF16)
        row_grad = jnp.zeros((step_rows, width), F32)
        for j in range(shares):
            part = slice(j * share, (j + 1) * share)
            add(i, acc_ref, prior, (j, 1), dot(scaled_t, hid_ref[:, part]))
            pre = (dot(scaled, downs[j][...]) * slope_ref[:, part]).astype(BF16)
            add(i, acc_ref, prior, (j, 0), dot(out_t, pre))
            row_grad = row_grad + dot(pre, ups[j][...], 1, 1)
        slope = (row_grad.astype(BF16).astype(F32) * trunk_slope).astype(BF16)
        add(i, acc_trunk_ref, prior_trunk, ..., dot(feats_f.T.astype(BF16), slope))
        return carry

    if looped:
        lax.fori_loop(0, steps, step, 0)
    else:
        for i in range(steps):
            step(i, 0)
    if last:
        all_losses = list(loss_refs) + [loss_ref]
        if not in_turns(experts):
            trunk_parts[0][...] = acc_trunk_ref[...]
            for row in range(all_loss_ref.shape[0]):
                all_loss_ref[row : row + 1, :] = loss_row(all_losses, row)
            return
        quarter = width // shares
        for j, ref in enumerate(trunk_parts):
            at = pl.multiple_of((mine_ref[0] ^ j) * quarter, quarter)
            ref[...] = acc_trunk_ref[pl.ds(at, quarter), :]
        for s in range(experts):
            all_loss_ref[s : s + 1, :] = loss_row(all_losses, order.index(s))


def in_turns(experts):
    return experts == 8


def loss_row(refs, row):
    for ref in refs:
        if row < ref.shape[0]:
            return ref[row : row + 1, :]
        row -= ref.shape[0]


def expert_call(xs, trunk_weight, weights, prior, losses, mine, order, last, relays=()):
    experts = len(order)
    block_rows = xs[0].shape[0]
    width = trunk_weight.shape[0]
    shares, share = len(weights), weights[0].shape[2]
    rows = block_rows * len(xs)
    step_rows = min(512, rows)
    steps = rows // step_rows
    first = prior is None
    acc = jax.ShapeDtypeStruct((shares, 2, width, share), F32)
    acc_trunk = jax.ShapeDtypeStruct((width, width), F32)
    loss = jax.ShapeDtypeStruct((rows // LOSSES, LOSSES), F32)
    args = list(xs) + [trunk_weight, *weights]
    if not first:
        args += list(prior)
    args += relays
    in_specs = [whole()] * len(args)
    scratch = [
        pltpu.VMEM((rows, 2 * width), BF16),
        pltpu.VMEM((step_rows, shares * share), BF16),
        pltpu.VMEM((step_rows, shares * share), F32),
    ]
    if last:
        args += list(losses) + [mine]
        in_specs += [whole()] * len(losses) + [whole(pltpu.SMEM)]
        outs = [acc]
        if in_turns(experts):
            outs += [jax.ShapeDtypeStruct((width // shares, width), F32)] * shares
        else:
            outs += [acc_trunk]
        outs += [jax.ShapeDtypeStruct((experts * block_rows // LOSSES, LOSSES), F32)]
        scratch += [pltpu.VMEM(a.shape, a.dtype) for a in (acc_trunk, loss)]
    else:
        outs = [acc, acc_trunk, loss]
        outs += [jax.ShapeDtypeStruct(relay.shape, relay.dtype) for relay in relays]
    counts = (len(xs), shares, experts, steps, step_rows, len(relays))
    return pl.pallas_call(
        functools.partial(expert_kernel, counts, order, first, len(losses) + 1 if last else 0),
        out_shape=outs,
        in_specs=in_specs,
        out_specs=[whole()] * len(outs),
        scratch_shapes=scratch,
        compiler_params=pltpu.CompilerParams(vmem_limit_bytes=20 * MIB),
        cost_estimate=pl.CostEstimate(
            flops=12 * rows * width,
            bytes_accessed=rows * width,
            transcendentals=0,
        ),
        name="expert_rows",
    )(*args)


def four(refs):
    return (refs[0][...] + refs[1][...]) + (refs[2][...] + refs[3][...])


def dp_turn_kernel(q0, q1, q2, q3, loss_ref, total_ref, note_ref):
    total = four((q0, q1, q2, q3))
    total_ref[...] = total
    rows = total.shape[0]
    note_ref[:rows, :] = total
    for k in range(4):
        note_ref[rows + k : rows + k + 1, :] = loss_ref[2 * k + 1 : 2 * k + 2, :]
    note_ref[rows + 4 :, :] = jnp.zeros((4, total.shape[1]), F32)


def pair_turn_kernel(me_ref, total_ref, got_ref, loss_ref, *outs):
    rows, width = total_ref.shape
    half = rows // 2
    at = pl.ds(pl.multiple_of((me_ref[0] & 1) * half, half), half)
    for k, ref in enumerate(outs):
        ref[:half, :] = total_ref[at, :] + got_ref[at, :]
        ref[half : half + 1, :] = loss_ref[2 * k : 2 * k + 1, :]
        ref[half + 1 : half + 2, :] = got_ref[rows + k : rows + k + 1, :]
        ref[half + 2 :, :] = jnp.zeros((6, width), F32)


def z_turn_kernel(*refs):
    *notes, total_ref, loss_ref = refs
    half = total_ref.shape[0]
    total_ref[...] = four([note.at[:half, :] for note in notes])
    for k, note in enumerate(notes):
        loss_ref[2 * k : 2 * k + 2, :] = note[half : half + 2, :]


def join_kernel(me_ref, own_ref, other_ref, _, both_ref):
    half = own_ref.shape[0]
    core = me_ref[0] & 1
    both_ref[pl.ds(pl.multiple_of(core * half, half), half), :] = own_ref[...]
    both_ref[pl.ds(pl.multiple_of((1 - core) * half, half), half), :] = other_ref[...]


def assemble_kernel(mine_ref, *refs):
    *held, _, trunk_ref = refs
    for j, ref in enumerate(held):
        rows = ref.shape[0]
        at = pl.multiple_of((mine_ref[0] ^ j) * rows, rows)
        trunk_ref[pl.ds(at, rows), :] = ref[...]


def turn(kernel, held, shapes, name, index=None):
    first = [] if index is None else [index]
    width = held[0].shape[1]
    return pl.pallas_call(
        kernel,
        out_shape=[jax.ShapeDtypeStruct((rows, width), F32) for rows in shapes],
        in_specs=[whole(pltpu.SMEM)] * len(first) + [whole()] * len(held),
        out_specs=[whole()] * len(shapes),
        compiler_params=pltpu.CompilerParams(vmem_limit_bytes=4 * MIB),
        name=name,
    )(*first, *held)


def send_kernel(acc_ref, ahead_ref, up_ref, down_ref):
    for k in range(2):
        up_ref[k] = acc_ref[2 * k + 1, 0].astype(BF16)
        down_ref[k] = acc_ref[k + 2, 1].astype(BF16)


def pass_on_kernel(acc_ref, got_up_ref, got_down_ref, ahead_ref, up_ref, down_ref):
    up_ref[...] = (acc_ref[2, 0] + got_up_ref[1].astype(F32)).astype(BF16)
    down_ref[...] = (acc_ref[1, 1] + got_down_ref[1].astype(F32)).astype(BF16)


def messages(kernel, held, ahead, shape, name):
    return pl.pallas_call(
        kernel,
        out_shape=[jax.ShapeDtypeStruct(shape, BF16)] * 2,
        in_specs=[whole()] * len(held) + [whole(pl.ANY)],
        out_specs=[whole()] * 2,
        compiler_params=pltpu.CompilerParams(vmem_limit_bytes=16 * MIB),
        name=name,
    )(*held, ahead)


def row_loss_kernel(place_ref, loss_ref, row_loss_ref, done_ref):
    experts, capacity = loss_ref.shape
    groups = place_ref.shape[0]
    place = jnp.concatenate([place_ref[g : g + 1, :] for g in range(groups)], axis=1)
    block = place // capacity
    slot = place - block * capacity
    picks = jnp.where(iota((capacity, place.shape[1]), 0) == slot, 1.0, 0.0)
    found = lax.dot_general(
        loss_ref[...],
        picks,
        (((1,), (0,)), ((), ())),
        precision=lax.Precision.HIGHEST,
        preferred_element_type=F32,
    )
    mine = jnp.sum(
        jnp.where(iota((experts, place.shape[1]), 0) == block, found, 0.0), axis=0, keepdims=True
    )
    for g in range(groups):
        row_loss_ref[g : g + 1, :] = mine[:, g * LANES : (g + 1) * LANES]
    done_ref[...] = jnp.zeros(done_ref.shape, F32)


def loss_by_row(place, loss):
    return pl.pallas_call(
        row_loss_kernel,
        out_shape=[jax.ShapeDtypeStruct(shape, F32) for shape in (place.shape, (8, LANES))],
        in_specs=[whole()] * 2,
        out_specs=[whole()] * 2,
        compiler_params=pltpu.CompilerParams(vmem_limit_bytes=16 * MIB),
        name="row_loss",
    )(place, loss)


def adam_update(params, first, second, grads):
    first_new = beta_one * first + (1.0 - beta_one) * grads
    second_new = beta_two * second + (1.0 - beta_two) * grads * grads
    first_hat = first_new / (1.0 - beta_one**adam_step)
    second_hat = second_new / (1.0 - beta_two**adam_step)
    return (
        params - learn_rate * first_hat / (jnp.sqrt(second_hat) + adam_eps),
        first_new,
        second_new,
    )


def adam_kernel(*refs):
    params_ref, first_ref, second_ref, acc_ref, *got = refs[:8]
    *outs, done_ref = refs[8:]
    for k in range(2):
        grads = acc_ref[0, k] + got[k][0].astype(F32) + got[2 + k][...].astype(F32)
        news = adam_update(params_ref[0, k], first_ref[0, k], second_ref[0, k], grads)
        for ref, new in zip(outs, news):
            ref[0, k] = new
    done_ref[...] = jnp.zeros(done_ref.shape, F32)


def adam(params, first, second, acc, got):
    shape = jax.ShapeDtypeStruct(params.shape, F32)
    return pl.pallas_call(
        adam_kernel,
        out_shape=[shape] * 3 + [jax.ShapeDtypeStruct((8, LANES), F32)],
        in_specs=[whole()] * 8,
        out_specs=[whole()] * 4,
        compiler_params=pltpu.CompilerParams(vmem_limit_bytes=24 * MIB),
        cost_estimate=pl.CostEstimate(
            flops=20 * params.size, bytes_accessed=8 * params.size, transcendentals=params.size
        ),
        name="adam",
    )(params, first, second, acc, *got)


def swap(value, axis, s):
    if s == 0:
        return value
    return lax.ppermute(value, axis, [(i, i ^ s) for i in range(lax.axis_size(axis))])


def on_device(
    cell_table,
    sample_index,
    region,
    targets,
    trunk_weight,
    expert_params,
    first_moment,
    second_moment,
):
    rows = sample_index.shape[0]
    width = cell_table.shape[1]
    experts = lax.axis_size("expert")
    replicas = lax.axis_size("dp")
    capacity = 2 * rows // experts
    me = lax.axis_index("expert").astype(jnp.int32).reshape(1)
    mine = lax.axis_index("dp").astype(jnp.int32).reshape(1)

    up, down = expert_params[0, 0].astype(BF16), expert_params[0, 1].astype(BF16)
    near_up, near_down = swap(up, "dp", 1), swap(down, "dp", 2)
    *blocks, place = pack(me, mine, sample_index, region[:, 0], cell_table, targets, experts, capacity)
    ups, downs = pair(up, near_up, place), pair(down, near_down, place)
    weights = [ups, swap(ups, "dp", 2), downs, swap(downs, "dp", 1)]
    if in_turns(experts):
        batches, later = ((0, 1), (4, 5), (2,), (6, 3), (7,)), ()
    else:
        batches, later = (range(experts // 2), range(experts // 2, experts)), ()
    order = [s for batch in batches for s in batch]
    arrived = {s: swap(blocks[s], "expert", s) for s in order if s not in later}
    prior, losses = None, []
    for k, batch in enumerate(batches):
        last = k == len(batches) - 1
        relays = [blocks[s] for s in later] if k == 0 else []
        outs = expert_call(
            [arrived[s] for s in batch], trunk_weight, weights, prior, losses, mine, order, last, relays
        )
        if not last:
            prior = outs[:2]
            losses.append(outs[2])
            for s, block in zip(later, outs[3:]):
                arrived[s] = swap(block, "expert", s)
    acc, *parts, losses = outs

    def send(ahead):
        up, down = messages(send_kernel, [acc], ahead, (2, *acc.shape[2:]), "send")
        return swap(up, "dp", 1), swap(down, "dp", 2)

    def pass_on(got, ahead):
        up, down = messages(pass_on_kernel, [acc, *got], ahead, acc.shape[2:], "pass_on")
        return swap(up, "dp", 2), swap(down, "dp", 1)

    if in_turns(experts):
        quarter = width // replicas
        parts = [swap(part, "dp", j) for j, part in enumerate(parts)]
        total, note = turn(dp_turn_kernel, parts + [losses], (quarter, quarter + 8), "dp_turn")
        got = send(total)
        notes = turn(
            pair_turn_kernel,
            [total, swap(note, "expert", 1), losses],
            (quarter // 2 + 8,) * 4,
            "pair_turn",
            me,
        )
        notes = [swap(note, "expert", 2 * k) for k, note in enumerate(notes)]
        total, loss = turn(z_turn_kernel, notes, (quarter // 2, experts), "z_turn")
        more_up, more_down = pass_on(got, total)
        row_loss, found = loss_by_row(place, loss)
        other = swap(total, "expert", 1)
        (total,) = turn(join_kernel, [total, other, found], (quarter,), "join", me)
        parts = [swap(total, "dp", j) for j in range(replicas)]
        *news, done = adam(
            expert_params, first_moment, second_moment, acc, [*got, more_up, more_down]
        )
        (trunk_grad,) = turn(assemble_kernel, parts + [done], (width,), "assemble_trunk", mine)
    else:
        got = send(losses)
        more_up, more_down = pass_on(got, losses)
        *news, _ = adam(
            expert_params, first_moment, second_moment, acc, [*got, more_up, more_down]
        )
        trunk_grad = lax.psum(parts[0], ("dp", "expert"))
        places = jnp.arange(experts, dtype=jnp.int32) ^ me
        losses = losses.reshape(experts, capacity)[places]
        loss = lax.all_to_all(losses, "expert", split_axis=0, concat_axis=0, tiled=True)[places]
        row_loss, _ = loss_by_row(place, loss)

    return (trunk_grad, row_loss.reshape(rows), *news)


def solution(mesh):
    placed = (
        P(("dp", "expert"), None),
        P(("dp", "expert")),
        P(("dp", "expert"), None),
        P(("dp", "expert"), None),
        P(),
        P("expert", None, None, "dp"),
        P("expert", None, None, "dp"),
        P("expert", None, None, "dp"),
    )
    return jax.shard_map(
        on_device,
        mesh=mesh,
        in_specs=placed,
        out_specs=(
            P(),
            P(("dp", "expert")),
            P("expert", None, None, "dp"),
            P("expert", None, None, "dp"),
            P("expert", None, None, "dp"),
        ),
        check_vma=False,
    )
```

```python
import functools

import jax
import jax.numpy as jnp
from jax import lax
from jax.experimental import pallas as pl
from jax.experimental.pallas import tpu as pltpu
from jax.sharding import PartitionSpec as P

loss_scale = 1.0 / 32.0
beta_one = 0.9
beta_two = 0.999
learn_rate = 0.05
adam_eps = 1e-08
adam_step = 10

LANES = 128
F32 = jnp.float32
BF16 = jnp.bfloat16
MIB = 1 << 20
LOSSES = 256


def iota(shape, dim):
    return lax.broadcasted_iota(jnp.int32, shape, dim)


def dot(a, b, ca=1, cb=0):
    return lax.dot_general(a, b, (((ca,), (cb,)), ((), ())), preferred_element_type=F32)


def whole(memory_space=pltpu.VMEM):
    return pl.BlockSpec(memory_space=memory_space)


def pack_kernel(experts, capacity, me_ref, mine_ref, index_ref, region_ref, table_ref, target_ref, *refs):
    blocks, place_ref, rows_ref = refs[:experts], refs[experts], refs[experts + 1]
    me = me_ref[0]
    groups = index_ref.shape[0]
    cells, width = table_ref.shape
    expert_id = iota((experts, LANES), 0)
    starts = ((expert_id ^ me) * capacity).astype(F32)
    ahead = jnp.where(iota((LANES, LANES), 0) <= iota((LANES, LANES), 1), 1.0, 0.0).astype(BF16)
    counted = jnp.zeros((experts, LANES), F32)
    places = []
    for g in range(groups):
        hot = jnp.where(region_ref[g : g + 1, :] == expert_id, 1.0, 0.0)
        upto = dot(hot.astype(BF16), ahead)
        places.append(jnp.sum(hot * (upto - 1.0 + counted + starts), axis=0, keepdims=True))
        counted = counted + jnp.broadcast_to(upto[:, LANES - 1 :], (experts, LANES))
    for g in range(groups):
        place_ref[g : g + 1, :] = places[g].astype(jnp.int32)
    place = jnp.concatenate(places, axis=1)

    step = 2
    cell_id = iota((LANES * step, LANES), 1).astype(F32)
    for g in range(0, groups, step):
        column = jnp.concatenate(
            [
                jnp.broadcast_to(index_ref[h : h + 1, :].astype(F32), (LANES, LANES)).T
                for h in range(g, g + step)
            ],
            axis=0,
        )
        picks = jnp.concatenate(
            [
                jnp.where(column == cell_id + float(LANES * t), 1.0, 0.0).astype(BF16)
                for t in range(cells // LANES)
            ],
            axis=1,
        )
        at = slice(g * LANES, (g + step) * LANES)
        rows_ref[at, :width] = dot(picks, table_ref[...]).astype(BF16)
        rows_ref[at, width:] = target_ref[at, :]

    slot_id = iota((capacity, place.shape[1]), 0).astype(F32)
    for s in range(experts):
        spread = jnp.where(place == slot_id + float(s * capacity), 1.0, 0.0).astype(BF16)
        blocks[s][...] = dot(spread, rows_ref[...]).astype(BF16)


def pack(me, mine, index, region, table, targets, experts, capacity):
    rows, width = targets.shape
    groups = rows // LANES
    return pl.pallas_call(
        functools.partial(pack_kernel, experts, capacity),
        out_shape=[jax.ShapeDtypeStruct((capacity, 2 * width), BF16)] * experts
        + [jax.ShapeDtypeStruct((groups, LANES), jnp.int32)],
        in_specs=[whole(pltpu.SMEM)] * 2 + [whole()] * 4,
        out_specs=[whole()] * (experts + 1),
        scratch_shapes=[pltpu.VMEM((rows, 2 * width), BF16)],
        compiler_params=pltpu.CompilerParams(vmem_limit_bytes=24 * MIB),
        cost_estimate=pl.CostEstimate(
            flops=2 * rows * width * (table.shape[0] + 2 * experts * capacity),
            bytes_accessed=6 * MIB,
            transcendentals=0,
        ),
        name="pack_rows",
    )(me, mine, index.reshape(groups, LANES), region.reshape(groups, LANES), table, targets)


def pair_kernel(one_ref, other_ref, ahead_ref, both_ref):
    both_ref[0] = one_ref[...]
    both_ref[1] = other_ref[...]


def pair(one, other, ahead):
    return pl.pallas_call(
        pair_kernel,
        out_shape=jax.ShapeDtypeStruct((2, *one.shape), one.dtype),
        in_specs=[whole()] * 2 + [whole(pl.ANY)],
        out_specs=whole(),
        compiler_params=pltpu.CompilerParams(vmem_limit_bytes=4 * MIB),
        name="pair",
    )(one, other, ahead)


def sigmoid(v):
    return 0.5 * jnp.tanh(0.5 * v) + 0.5


def expert_kernel(counts, order, first, last, *refs):
    blocks, shares, experts, steps, step_rows, relays = counts
    refs = list(refs)

    def take(n):
        got = refs[:n]
        del refs[:n]
        return got

    xs = take(blocks)
    trunk_ref, ups_near, ups_far, downs_near, downs_far = take(5)
    ups = (ups_near.at[0], ups_near.at[1], ups_far.at[0], ups_far.at[1])
    downs = (downs_near.at[0], downs_far.at[0], downs_near.at[1], downs_far.at[1])
    if not first:
        prior_ref, prior_trunk_ref = take(2)
    held = take(relays)
    if last:
        loss_refs = take(last - 1)
        (mine_ref,) = take(1)
        (acc_ref,) = take(1)
        trunk_parts = take(shares if in_turns(experts) else 1)
        (all_loss_ref,) = take(1)
    else:
        acc_ref, acc_trunk_ref, loss_ref = take(3)
        for source, copy in zip(held, take(relays)):
            copy[...] = source[...]
    x_ref, hid_ref, slope_ref = take(3)
    if last:
        acc_trunk_ref, loss_ref = take(2)

    width = trunk_ref.shape[0]
    share = ups_near.shape[2]
    block_rows = xs[0].shape[0]
    for i, ref in enumerate(xs):
        x_ref[i * block_rows : (i + 1) * block_rows, :] = ref[...]
    looped = steps > 3
    if looped and first:
        acc_ref[...] = jnp.zeros(acc_ref.shape, F32)
        acc_trunk_ref[...] = jnp.zeros(acc_trunk_ref.shape, F32)
    elif looped:
        acc_ref[...] = prior_ref[...]
        acc_trunk_ref[...] = prior_trunk_ref[...]

    def add(i, ref, source, at, value):
        if looped or i > 0:
            ref[at] += value
        elif first:
            ref[at] = value
        else:
            ref[at] = source[at] + value

    prior = None if first else prior_ref
    prior_trunk = None if first else prior_trunk_ref

    def step(i, carry):
        if looped:
            at = pl.ds(pl.multiple_of(i * step_rows, step_rows), step_rows)
        else:
            at = slice(i * step_rows, (i + 1) * step_rows)
        feats = x_ref[at, :width]
        feats_f = feats.astype(F32)
        trunk_pre = dot(feats, trunk_ref[...])
        gate = sigmoid(trunk_pre)
        act = trunk_pre * gate
        trunk_slope = gate + act * (1.0 - gate)
        out_f = feats_f + act
        out = out_f.astype(BF16)
        predicted = jnp.zeros((step_rows, width), F32)
        for j in range(shares):
            up = dot(out, ups[j][...])
            s = sigmoid(up)
            h = up * s
            slope_ref[:, j * share : (j + 1) * share] = s + h * (1.0 - s)
            h = h.astype(BF16)
            hid_ref[:, j * share : (j + 1) * share] = h
            predicted = predicted + dot(h, downs[j][...], 1, 1)
        errors = predicted - x_ref[at, width:].astype(F32)
        squares = errors * errors
        half = squares[:, :LANES]
        for k in range(1, width // LANES):
            half = half + squares[:, k * LANES : (k + 1) * LANES]
        lost = jnp.sum(half.T, axis=0, keepdims=True) * (0.5 * loss_scale)
        for k in range(step_rows // LOSSES):
            row = pl.ds(i * (step_rows // LOSSES) + k, 1)
            loss_ref[row, :] = lost[:, k * LOSSES : (k + 1) * LOSSES]
        scaled_f = errors * loss_scale
        scaled = scaled_f.astype(BF16)
        scaled_t = scaled_f.T.astype(BF16)
        out_t = out_f.T.astype(BF16)
        row_grad = jnp.zeros((step_rows, width), F32)
        for j in range(shares):
            part = slice(j * share, (j + 1) * share)
            add(i, acc_ref, prior, (j, 1), dot(scaled_t, hid_ref[:, part]))
            pre = (dot(scaled, downs[j][...]) * slope_ref[:, part]).astype(BF16)
            add(i, acc_ref, prior, (j, 0), dot(out_t, pre))
            row_grad = row_grad + dot(pre, ups[j][...], 1, 1)
        slope = (row_grad.astype(BF16).astype(F32) * trunk_slope).astype(BF16)
        add(i, acc_trunk_ref, prior_trunk, ..., dot(feats_f.T.astype(BF16), slope))
        return carry

    if looped:
        lax.fori_loop(0, steps, step, 0)
    else:
        for i in range(steps):
            step(i, 0)
    if last:
        all_losses = list(loss_refs) + [loss_ref]
        if not in_turns(experts):
            trunk_parts[0][...] = acc_trunk_ref[...]
            for row in range(all_loss_ref.shape[0]):
                all_loss_ref[row : row + 1, :] = loss_row(all_losses, row)
            return
        quarter = width // shares
        for j, ref in enumerate(trunk_parts):
            at = pl.multiple_of((mine_ref[0] ^ j) * quarter, quarter)
            ref[...] = acc_trunk_ref[pl.ds(at, quarter), :]
        for s in range(experts):
            all_loss_ref[s : s + 1, :] = loss_row(all_losses, order.index(s))


def in_turns(experts):
    return experts == 8


def loss_row(refs, row):
    for ref in refs:
        if row < ref.shape[0]:
            return ref[row : row + 1, :]
        row -= ref.shape[0]


def expert_call(xs, trunk_weight, weights, prior, losses, mine, order, last, relays=()):
    experts = len(order)
    block_rows = xs[0].shape[0]
    width = trunk_weight.shape[0]
    shares, share = len(weights), weights[0].shape[2]
    rows = block_rows * len(xs)
    step_rows = min(512, rows)
    steps = rows // step_rows
    first = prior is None
    acc = jax.ShapeDtypeStruct((shares, 2, width, share), F32)
    acc_trunk = jax.ShapeDtypeStruct((width, width), F32)
    loss = jax.ShapeDtypeStruct((rows // LOSSES, LOSSES), F32)
    args = list(xs) + [trunk_weight, *weights]
    if not first:
        args += list(prior)
    args += relays
    in_specs = [whole()] * len(args)
    scratch = [
        pltpu.VMEM((rows, 2 * width), BF16),
        pltpu.VMEM((step_rows, shares * share), BF16),
        pltpu.VMEM((step_rows, shares * share), F32),
    ]
    if last:
        args += list(losses) + [mine]
        in_specs += [whole()] * len(losses) + [whole(pltpu.SMEM)]
        outs = [acc]
        if in_turns(experts):
            outs += [jax.ShapeDtypeStruct((width // shares, width), F32)] * shares
        else:
            outs += [acc_trunk]
        outs += [jax.ShapeDtypeStruct((experts * block_rows // LOSSES, LOSSES), F32)]
        scratch += [pltpu.VMEM(a.shape, a.dtype) for a in (acc_trunk, loss)]
    else:
        outs = [acc, acc_trunk, loss]
        outs += [jax.ShapeDtypeStruct(relay.shape, relay.dtype) for relay in relays]
    counts = (len(xs), shares, experts, steps, step_rows, len(relays))
    return pl.pallas_call(
        functools.partial(expert_kernel, counts, order, first, len(losses) + 1 if last else 0),
        out_shape=outs,
        in_specs=in_specs,
        out_specs=[whole()] * len(outs),
        scratch_shapes=scratch,
        compiler_params=pltpu.CompilerParams(vmem_limit_bytes=20 * MIB),
        cost_estimate=pl.CostEstimate(
            flops=12 * rows * width,
            bytes_accessed=rows * width,
            transcendentals=0,
        ),
        name="expert_rows",
    )(*args)


def four(refs):
    return (refs[0][...] + refs[1][...]) + (refs[2][...] + refs[3][...])


def dp_turn_kernel(q0, q1, q2, q3, loss_ref, total_ref, note_ref):
    total = four((q0, q1, q2, q3))
    total_ref[...] = total
    rows = total.shape[0]
    note_ref[:rows, :] = total
    for k in range(4):
        note_ref[rows + k : rows + k + 1, :] = loss_ref[2 * k + 1 : 2 * k + 2, :]
    note_ref[rows + 4 :, :] = jnp.zeros((4, total.shape[1]), F32)


def pair_turn_kernel(me_ref, total_ref, got_ref, loss_ref, *outs):
    rows, width = total_ref.shape
    half = rows // 2
    at = pl.ds(pl.multiple_of((me_ref[0] & 1) * half, half), half)
    for k, ref in enumerate(outs):
        ref[:half, :] = total_ref[at, :] + got_ref[at, :]
        ref[half : half + 1, :] = loss_ref[2 * k : 2 * k + 1, :]
        ref[half + 1 : half + 2, :] = got_ref[rows + k : rows + k + 1, :]
        ref[half + 2 :, :] = jnp.zeros((6, width), F32)


def z_turn_kernel(*refs):
    *notes, total_ref, loss_ref = refs
    half = total_ref.shape[0]
    total_ref[...] = four([note.at[:half, :] for note in notes])
    for k, note in enumerate(notes):
        loss_ref[2 * k : 2 * k + 2, :] = note[half : half + 2, :]


def stack_kernel(*refs):
    *held, _, all_ref = refs
    for j, ref in enumerate(held):
        rows = ref.shape[0]
        all_ref[j * rows : (j + 1) * rows, :] = ref[...]


def assemble_kernel(me_ref, mine_ref, own_ref, other_ref, _, trunk_ref):
    core = me_ref[0] & 1
    half = own_ref.shape[0] // 4
    for ref, side in ((own_ref, core), (other_ref, 1 - core)):
        for j in range(4):
            at = pl.multiple_of(((mine_ref[0] ^ j) * 2 + side) * half, half)
            trunk_ref[pl.ds(at, half), :] = ref[j * half : (j + 1) * half, :]


def turn(kernel, held, shapes, name, indices=()):
    first = list(indices)
    width = held[0].shape[1]
    return pl.pallas_call(
        kernel,
        out_shape=[jax.ShapeDtypeStruct((rows, width), F32) for rows in shapes],
        in_specs=[whole(pltpu.SMEM)] * len(first) + [whole()] * len(held),
        out_specs=[whole()] * len(shapes),
        compiler_params=pltpu.CompilerParams(vmem_limit_bytes=4 * MIB),
        name=name,
    )(*first, *held)


def send_kernel(acc_ref, ahead_ref, up_ref, down_ref):
    for k in range(2):
        up_ref[k] = acc_ref[2 * k + 1, 0].astype(BF16)
        down_ref[k] = acc_ref[k + 2, 1].astype(BF16)


def pass_on_kernel(acc_ref, got_up_ref, got_down_ref, ahead_ref, up_ref, down_ref):
    up_ref[...] = (acc_ref[2, 0] + got_up_ref[1].astype(F32)).astype(BF16)
    down_ref[...] = (acc_ref[1, 1] + got_down_ref[1].astype(F32)).astype(BF16)


def messages(kernel, held, ahead, shape, name):
    return pl.pallas_call(
        kernel,
        out_shape=[jax.ShapeDtypeStruct(shape, BF16)] * 2,
        in_specs=[whole()] * len(held) + [whole(pl.ANY)],
        out_specs=[whole()] * 2,
        compiler_params=pltpu.CompilerParams(vmem_limit_bytes=16 * MIB),
        name=name,
    )(*held, ahead)


def row_loss_kernel(place_ref, loss_ref, row_loss_ref, done_ref):
    experts, capacity = loss_ref.shape
    groups = place_ref.shape[0]
    place = jnp.concatenate([place_ref[g : g + 1, :] for g in range(groups)], axis=1)
    block = place // capacity
    slot = place - block * capacity
    picks = jnp.where(iota((capacity, place.shape[1]), 0) == slot, 1.0, 0.0)
    found = lax.dot_general(
        loss_ref[...],
        picks,
        (((1,), (0,)), ((), ())),
        precision=lax.Precision.HIGHEST,
        preferred_element_type=F32,
    )
    mine = jnp.sum(
        jnp.where(iota((experts, place.shape[1]), 0) == block, found, 0.0), axis=0, keepdims=True
    )
    for g in range(groups):
        row_loss_ref[g : g + 1, :] = mine[:, g * LANES : (g + 1) * LANES]
    done_ref[...] = jnp.zeros(done_ref.shape, F32)


def loss_by_row(place, loss):
    return pl.pallas_call(
        row_loss_kernel,
        out_shape=[jax.ShapeDtypeStruct(shape, F32) for shape in (place.shape, (8, LANES))],
        in_specs=[whole()] * 2,
        out_specs=[whole()] * 2,
        compiler_params=pltpu.CompilerParams(vmem_limit_bytes=16 * MIB),
        name="row_loss",
    )(place, loss)


def adam_update(params, first, second, grads):
    first_new = beta_one * first + (1.0 - beta_one) * grads
    second_new = beta_two * second + (1.0 - beta_two) * grads * grads
    first_hat = first_new / (1.0 - beta_one**adam_step)
    second_hat = second_new / (1.0 - beta_two**adam_step)
    return (
        params - learn_rate * first_hat / (jnp.sqrt(second_hat) + adam_eps),
        first_new,
        second_new,
    )


def adam_kernel(*refs):
    params_ref, first_ref, second_ref, acc_ref, *got = refs[:8]
    *outs, done_ref = refs[8:]
    for k in range(2):
        grads = acc_ref[0, k] + got[k][0].astype(F32) + got[2 + k][...].astype(F32)
        news = adam_update(params_ref[0, k], first_ref[0, k], second_ref[0, k], grads)
        for ref, new in zip(outs, news):
            ref[0, k] = new
    done_ref[...] = jnp.zeros(done_ref.shape, F32)


def adam(params, first, second, acc, got):
    shape = jax.ShapeDtypeStruct(params.shape, F32)
    return pl.pallas_call(
        adam_kernel,
        out_shape=[shape] * 3 + [jax.ShapeDtypeStruct((8, LANES), F32)],
        in_specs=[whole()] * 8,
        out_specs=[whole()] * 4,
        compiler_params=pltpu.CompilerParams(vmem_limit_bytes=24 * MIB),
        cost_estimate=pl.CostEstimate(
            flops=20 * params.size, bytes_accessed=8 * params.size, transcendentals=params.size
        ),
        name="adam",
    )(params, first, second, acc, *got)


def swap(value, axis, s):
    if s == 0:
        return value
    return lax.ppermute(value, axis, [(i, i ^ s) for i in range(lax.axis_size(axis))])


def on_device(
    cell_table,
    sample_index,
    region,
    targets,
    trunk_weight,
    expert_params,
    first_moment,
    second_moment,
):
    rows = sample_index.shape[0]
    width = cell_table.shape[1]
    experts = lax.axis_size("expert")
    replicas = lax.axis_size("dp")
    capacity = 2 * rows // experts
    me = lax.axis_index("expert").astype(jnp.int32).reshape(1)
    mine = lax.axis_index("dp").astype(jnp.int32).reshape(1)

    up, down = expert_params[0, 0].astype(BF16), expert_params[0, 1].astype(BF16)
    near_up, near_down = swap(up, "dp", 1), swap(down, "dp", 2)
    *blocks, place = pack(me, mine, sample_index, region[:, 0], cell_table, targets, experts, capacity)
    ups, downs = pair(up, near_up, place), pair(down, near_down, place)
    weights = [ups, swap(ups, "dp", 2), downs, swap(downs, "dp", 1)]
    if in_turns(experts):
        batches, later = ((0, 4), (1, 5), (2,), (6, 3), (7,)), ()
    else:
        batches, later = (range(experts // 2), range(experts // 2, experts)), ()
    order = [s for batch in batches for s in batch]
    arrived = {s: swap(blocks[s], "expert", s) for s in order if s not in later}
    prior, losses = None, []
    for k, batch in enumerate(batches):
        last = k == len(batches) - 1
        relays = [blocks[s] for s in later] if k == 0 else []
        outs = expert_call(
            [arrived[s] for s in batch], trunk_weight, weights, prior, losses, mine, order, last, relays
        )
        if not last:
            prior = outs[:2]
            losses.append(outs[2])
            for s, block in zip(later, outs[3:]):
                arrived[s] = swap(block, "expert", s)
    acc, *parts, losses = outs

    def send(ahead):
        up, down = messages(send_kernel, [acc], ahead, (2, *acc.shape[2:]), "send")
        return swap(up, "dp", 1), swap(down, "dp", 2)

    def pass_on(got, ahead):
        up, down = messages(pass_on_kernel, [acc, *got], ahead, acc.shape[2:], "pass_on")
        return swap(up, "dp", 2), swap(down, "dp", 1)

    if in_turns(experts):
        quarter = width // replicas
        parts = [swap(part, "dp", j) for j, part in enumerate(parts)]
        total, note = turn(dp_turn_kernel, parts + [losses], (quarter, quarter + 8), "dp_turn")
        got = send(total)
        notes = turn(
            pair_turn_kernel,
            [total, swap(note, "expert", 1), losses],
            (quarter // 2 + 8,) * 4,
            "pair_turn",
            (me,),
        )
        notes = [swap(note, "expert", 2 * k) for k, note in enumerate(notes)]
        total, loss = turn(z_turn_kernel, notes, (quarter // 2, experts), "z_turn")
        more_up, more_down = pass_on(got, total)
        row_loss, found = loss_by_row(place, loss)
        parts = [swap(total, "dp", j) for j in range(replicas)]
        (parts,) = turn(stack_kernel, parts + [found], (width // 2,), "stack_parts")
        other = swap(parts, "expert", 1)
        *news, done = adam(
            expert_params, first_moment, second_moment, acc, [*got, more_up, more_down]
        )
        (trunk_grad,) = turn(
            assemble_kernel, [parts, other, done], (width,), "assemble_trunk", (me, mine)
        )
    else:
        got = send(losses)
        more_up, more_down = pass_on(got, losses)
        *news, _ = adam(
            expert_params, first_moment, second_moment, acc, [*got, more_up, more_down]
        )
        trunk_grad = lax.psum(parts[0], ("dp", "expert"))
        places = jnp.arange(experts, dtype=jnp.int32) ^ me
        losses = losses.reshape(experts, capacity)[places]
        loss = lax.all_to_all(losses, "expert", split_axis=0, concat_axis=0, tiled=True)[places]
        row_loss, _ = loss_by_row(place, loss)

    return (trunk_grad, row_loss.reshape(rows), *news)


def solution(mesh):
    placed = (
        P(("dp", "expert"), None),
        P(("dp", "expert")),
        P(("dp", "expert"), None),
        P(("dp", "expert"), None),
        P(),
        P("expert", None, None, "dp"),
        P("expert", None, None, "dp"),
        P("expert", None, None, "dp"),
    )
    return jax.shard_map(
        on_device,
        mesh=mesh,
        in_specs=placed,
        out_specs=(
            P(),
            P(("dp", "expert")),
            P("expert", None, None, "dp"),
            P("expert", None, None, "dp"),
            P("expert", None, None, "dp"),
        ),
        check_vma=False,
    )
```

```python
import functools

import jax
import jax.numpy as jnp
from jax import lax
from jax.experimental import pallas as pl
from jax.experimental.pallas import tpu as pltpu
from jax.sharding import PartitionSpec as P

loss_scale = 1.0 / 32.0
beta_one = 0.9
beta_two = 0.999
learn_rate = 0.05
adam_eps = 1e-08
adam_step = 10

LANES = 128
F32 = jnp.float32
BF16 = jnp.bfloat16
MIB = 1 << 20
LOSSES = 256


def iota(shape, dim):
    return lax.broadcasted_iota(jnp.int32, shape, dim)


def dot(a, b, ca=1, cb=0):
    return lax.dot_general(a, b, (((ca,), (cb,)), ((), ())), preferred_element_type=F32)


def whole(memory_space=pltpu.VMEM):
    return pl.BlockSpec(memory_space=memory_space)


def pack_kernel(experts, capacity, me_ref, mine_ref, index_ref, region_ref, table_ref, target_ref, *refs):
    blocks, place_ref, rows_ref = refs[:experts], refs[experts], refs[experts + 1]
    me = me_ref[0]
    groups = index_ref.shape[0]
    cells, width = table_ref.shape
    expert_id = iota((experts, LANES), 0)
    starts = ((expert_id ^ me) * capacity).astype(F32)
    ahead = jnp.where(iota((LANES, LANES), 0) <= iota((LANES, LANES), 1), 1.0, 0.0).astype(BF16)
    counted = jnp.zeros((experts, LANES), F32)
    places = []
    for g in range(groups):
        hot = jnp.where(region_ref[g : g + 1, :] == expert_id, 1.0, 0.0)
        upto = dot(hot.astype(BF16), ahead)
        places.append(jnp.sum(hot * (upto - 1.0 + counted + starts), axis=0, keepdims=True))
        counted = counted + jnp.broadcast_to(upto[:, LANES - 1 :], (experts, LANES))
    for g in range(groups):
        place_ref[g : g + 1, :] = places[g].astype(jnp.int32)
    place = jnp.concatenate(places, axis=1)

    step = 2
    cell_id = iota((LANES * step, LANES), 1).astype(F32)
    for g in range(0, groups, step):
        column = jnp.concatenate(
            [
                jnp.broadcast_to(index_ref[h : h + 1, :].astype(F32), (LANES, LANES)).T
                for h in range(g, g + step)
            ],
            axis=0,
        )
        picks = jnp.concatenate(
            [
                jnp.where(column == cell_id + float(LANES * t), 1.0, 0.0).astype(BF16)
                for t in range(cells // LANES)
            ],
            axis=1,
        )
        at = slice(g * LANES, (g + step) * LANES)
        rows_ref[at, :width] = dot(picks, table_ref[...]).astype(BF16)
        rows_ref[at, width:] = target_ref[at, :]

    slot_id = iota((capacity, place.shape[1]), 0).astype(F32)
    for s in range(experts):
        spread = jnp.where(place == slot_id + float(s * capacity), 1.0, 0.0).astype(BF16)
        blocks[s][...] = dot(spread, rows_ref[...]).astype(BF16)


def pack(me, mine, index, region, table, targets, experts, capacity):
    rows, width = targets.shape
    groups = rows // LANES
    return pl.pallas_call(
        functools.partial(pack_kernel, experts, capacity),
        out_shape=[jax.ShapeDtypeStruct((capacity, 2 * width), BF16)] * experts
        + [jax.ShapeDtypeStruct((groups, LANES), jnp.int32)],
        in_specs=[whole(pltpu.SMEM)] * 2 + [whole()] * 4,
        out_specs=[whole()] * (experts + 1),
        scratch_shapes=[pltpu.VMEM((rows, 2 * width), BF16)],
        compiler_params=pltpu.CompilerParams(vmem_limit_bytes=24 * MIB),
        cost_estimate=pl.CostEstimate(
            flops=2 * rows * width * (table.shape[0] + 2 * experts * capacity),
            bytes_accessed=6 * MIB,
            transcendentals=0,
        ),
        name="pack_rows",
    )(me, mine, index.reshape(groups, LANES), region.reshape(groups, LANES), table, targets)


def pair_kernel(one_ref, other_ref, ahead_ref, both_ref):
    both_ref[0] = one_ref[...]
    both_ref[1] = other_ref[...]


def pair(one, other, ahead):
    return pl.pallas_call(
        pair_kernel,
        out_shape=jax.ShapeDtypeStruct((2, *one.shape), one.dtype),
        in_specs=[whole()] * 2 + [whole(pl.ANY)],
        out_specs=whole(),
        compiler_params=pltpu.CompilerParams(vmem_limit_bytes=4 * MIB),
        name="pair",
    )(one, other, ahead)


def sigmoid(v):
    return 0.5 * jnp.tanh(0.5 * v) + 0.5


def expert_kernel(counts, order, first, last, *refs):
    blocks, shares, experts, steps, step_rows, relays = counts
    refs = list(refs)

    def take(n):
        got = refs[:n]
        del refs[:n]
        return got

    xs = take(blocks)
    trunk_ref, ups_near, ups_far, downs_near, downs_far = take(5)
    ups = (ups_near.at[0], ups_near.at[1], ups_far.at[0], ups_far.at[1])
    downs = (downs_near.at[0], downs_far.at[0], downs_near.at[1], downs_far.at[1])
    if not first:
        prior_ref, prior_trunk_ref = take(2)
    held = take(relays)
    if last:
        loss_refs = take(last - 1)
        (mine_ref,) = take(1)
        (acc_ref,) = take(1)
        trunk_parts = take(shares if in_turns(experts) else 1)
        (all_loss_ref,) = take(1)
    else:
        acc_ref, acc_trunk_ref, loss_ref = take(3)
        for source, copy in zip(held, take(relays)):
            copy[...] = source[...]
    x_ref, hid_ref, slope_ref = take(3)
    if last:
        acc_trunk_ref, loss_ref = take(2)

    width = trunk_ref.shape[0]
    share = ups_near.shape[2]
    block_rows = xs[0].shape[0]
    for i, ref in enumerate(xs):
        x_ref[i * block_rows : (i + 1) * block_rows, :] = ref[...]
    looped = steps > 3
    if looped and first:
        acc_ref[...] = jnp.zeros(acc_ref.shape, F32)
        acc_trunk_ref[...] = jnp.zeros(acc_trunk_ref.shape, F32)
    elif looped:
        acc_ref[...] = prior_ref[...]
        acc_trunk_ref[...] = prior_trunk_ref[...]

    def add(i, ref, source, at, value):
        if looped or i > 0:
            ref[at] += value
        elif first:
            ref[at] = value
        else:
            ref[at] = source[at] + value

    prior = None if first else prior_ref
    prior_trunk = None if first else prior_trunk_ref

    def step(i, carry):
        if looped:
            at = pl.ds(pl.multiple_of(i * step_rows, step_rows), step_rows)
        else:
            at = slice(i * step_rows, (i + 1) * step_rows)
        feats = x_ref[at, :width]
        feats_f = feats.astype(F32)
        trunk_pre = dot(feats, trunk_ref[...])
        gate = sigmoid(trunk_pre)
        act = trunk_pre * gate
        trunk_slope = gate + act * (1.0 - gate)
        out_f = feats_f + act
        out = out_f.astype(BF16)
        predicted = jnp.zeros((step_rows, width), F32)
        for j in range(shares):
            up = dot(out, ups[j][...])
            s = sigmoid(up)
            h = up * s
            slope_ref[:, j * share : (j + 1) * share] = s + h * (1.0 - s)
            h = h.astype(BF16)
            hid_ref[:, j * share : (j + 1) * share] = h
            predicted = predicted + dot(h, downs[j][...], 1, 1)
        errors = predicted - x_ref[at, width:].astype(F32)
        squares = errors * errors
        half = squares[:, :LANES]
        for k in range(1, width // LANES):
            half = half + squares[:, k * LANES : (k + 1) * LANES]
        lost = jnp.sum(half.T, axis=0, keepdims=True) * (0.5 * loss_scale)
        for k in range(step_rows // LOSSES):
            row = pl.ds(i * (step_rows // LOSSES) + k, 1)
            loss_ref[row, :] = lost[:, k * LOSSES : (k + 1) * LOSSES]
        scaled_f = errors * loss_scale
        scaled = scaled_f.astype(BF16)
        scaled_t = scaled_f.T.astype(BF16)
        out_t = out_f.T.astype(BF16)
        row_grad = jnp.zeros((step_rows, width), F32)
        for j in range(shares):
            part = slice(j * share, (j + 1) * share)
            add(i, acc_ref, prior, (j, 1), dot(scaled_t, hid_ref[:, part]))
            pre = (dot(scaled, downs[j][...]) * slope_ref[:, part]).astype(BF16)
            add(i, acc_ref, prior, (j, 0), dot(out_t, pre))
            row_grad = row_grad + dot(pre, ups[j][...], 1, 1)
        slope = (row_grad.astype(BF16).astype(F32) * trunk_slope).astype(BF16)
        add(i, acc_trunk_ref, prior_trunk, ..., dot(feats_f.T.astype(BF16), slope))
        return carry

    if looped:
        lax.fori_loop(0, steps, step, 0)
    else:
        for i in range(steps):
            step(i, 0)
    if last:
        all_losses = list(loss_refs) + [loss_ref]
        if not in_turns(experts):
            trunk_parts[0][...] = acc_trunk_ref[...]
            for row in range(all_loss_ref.shape[0]):
                all_loss_ref[row : row + 1, :] = loss_row(all_losses, row)
            return
        quarter = width // shares
        for j, ref in enumerate(trunk_parts):
            at = pl.multiple_of((mine_ref[0] ^ j) * quarter, quarter)
            ref[...] = acc_trunk_ref[pl.ds(at, quarter), :]
        for s in range(experts):
            all_loss_ref[s : s + 1, :] = loss_row(all_losses, order.index(s))


def in_turns(experts):
    return experts == 8


def loss_row(refs, row):
    for ref in refs:
        if row < ref.shape[0]:
            return ref[row : row + 1, :]
        row -= ref.shape[0]


def expert_call(xs, trunk_weight, weights, prior, losses, mine, order, last, relays=()):
    experts = len(order)
    block_rows = xs[0].shape[0]
    width = trunk_weight.shape[0]
    shares, share = len(weights), weights[0].shape[2]
    rows = block_rows * len(xs)
    step_rows = min(512, rows)
    steps = rows // step_rows
    first = prior is None
    acc = jax.ShapeDtypeStruct((shares, 2, width, share), F32)
    acc_trunk = jax.ShapeDtypeStruct((width, width), F32)
    loss = jax.ShapeDtypeStruct((rows // LOSSES, LOSSES), F32)
    args = list(xs) + [trunk_weight, *weights]
    if not first:
        args += list(prior)
    args += relays
    in_specs = [whole()] * len(args)
    scratch = [
        pltpu.VMEM((rows, 2 * width), BF16),
        pltpu.VMEM((step_rows, shares * share), BF16),
        pltpu.VMEM((step_rows, shares * share), F32),
    ]
    if last:
        args += list(losses) + [mine]
        in_specs += [whole()] * len(losses) + [whole(pltpu.SMEM)]
        outs = [acc]
        if in_turns(experts):
            outs += [jax.ShapeDtypeStruct((width // shares, width), F32)] * shares
        else:
            outs += [acc_trunk]
        outs += [jax.ShapeDtypeStruct((experts * block_rows // LOSSES, LOSSES), F32)]
        scratch += [pltpu.VMEM(a.shape, a.dtype) for a in (acc_trunk, loss)]
    else:
        outs = [acc, acc_trunk, loss]
        outs += [jax.ShapeDtypeStruct(relay.shape, relay.dtype) for relay in relays]
    counts = (len(xs), shares, experts, steps, step_rows, len(relays))
    return pl.pallas_call(
        functools.partial(expert_kernel, counts, order, first, len(losses) + 1 if last else 0),
        out_shape=outs,
        in_specs=in_specs,
        out_specs=[whole()] * len(outs),
        scratch_shapes=scratch,
        compiler_params=pltpu.CompilerParams(vmem_limit_bytes=20 * MIB),
        cost_estimate=pl.CostEstimate(
            flops=12 * rows * width,
            bytes_accessed=rows * width,
            transcendentals=0,
        ),
        name="expert_rows",
    )(*args)


def four(refs):
    return (refs[0][...] + refs[1][...]) + (refs[2][...] + refs[3][...])


def dp_turn_kernel(q0, q1, q2, q3, loss_ref, total_ref, note_ref):
    total = four((q0, q1, q2, q3))
    total_ref[...] = total
    rows = total.shape[0]
    note_ref[:rows, :] = total
    for k in range(4):
        note_ref[rows + k : rows + k + 1, :] = loss_ref[2 * k + 1 : 2 * k + 2, :]
    note_ref[rows + 4 :, :] = jnp.zeros((4, total.shape[1]), F32)


def pair_turn_kernel(me_ref, total_ref, got_ref, loss_ref, *outs):
    rows, width = total_ref.shape
    half = rows // 2
    at = pl.ds(pl.multiple_of((me_ref[0] & 1) * half, half), half)
    for k, ref in enumerate(outs):
        ref[:half, :] = total_ref[at, :] + got_ref[at, :]
        ref[half : half + 1, :] = loss_ref[2 * k : 2 * k + 1, :]
        ref[half + 1 : half + 2, :] = got_ref[rows + k : rows + k + 1, :]
        ref[half + 2 :, :] = jnp.zeros((6, width), F32)


def z_turn_kernel(*refs):
    *notes, total_ref, loss_ref = refs
    half = total_ref.shape[0]
    total_ref[...] = four([note.at[:half, :] for note in notes])
    for k, note in enumerate(notes):
        loss_ref[2 * k : 2 * k + 2, :] = note[half : half + 2, :]


def stack_kernel(*refs):
    *held, _, all_ref = refs
    for j, ref in enumerate(held):
        rows = ref.shape[0]
        all_ref[j * rows : (j + 1) * rows, :] = ref[...]


def assemble_kernel(me_ref, mine_ref, own_ref, other_ref, _, trunk_ref):
    core = me_ref[0] & 1
    half = own_ref.shape[0] // 4
    for ref, side in ((own_ref, core), (other_ref, 1 - core)):
        for j in range(4):
            at = pl.multiple_of(((mine_ref[0] ^ j) * 2 + side) * half, half)
            trunk_ref[pl.ds(at, half), :] = ref[j * half : (j + 1) * half, :]


def turn(kernel, held, shapes, name, indices=()):
    first = list(indices)
    width = held[0].shape[1]
    return pl.pallas_call(
        kernel,
        out_shape=[jax.ShapeDtypeStruct((rows, width), F32) for rows in shapes],
        in_specs=[whole(pltpu.SMEM)] * len(first) + [whole()] * len(held),
        out_specs=[whole()] * len(shapes),
        compiler_params=pltpu.CompilerParams(vmem_limit_bytes=4 * MIB),
        name=name,
    )(*first, *held)


def send_kernel(acc_ref, ahead_ref, up_ref, down_ref):
    for k in range(2):
        up_ref[k] = acc_ref[2 * k + 1, 0].astype(BF16)
        down_ref[k] = acc_ref[k + 2, 1].astype(BF16)


def pass_on_kernel(acc_ref, got_up_ref, got_down_ref, ahead_ref, up_ref, down_ref):
    up_ref[...] = (acc_ref[2, 0] + got_up_ref[1].astype(F32)).astype(BF16)
    down_ref[...] = (acc_ref[1, 1] + got_down_ref[1].astype(F32)).astype(BF16)


def messages(kernel, held, ahead, shape, name):
    return pl.pallas_call(
        kernel,
        out_shape=[jax.ShapeDtypeStruct(shape, BF16)] * 2,
        in_specs=[whole()] * len(held) + [whole(pl.ANY)],
        out_specs=[whole()] * 2,
        compiler_params=pltpu.CompilerParams(vmem_limit_bytes=16 * MIB),
        name=name,
    )(*held, ahead)


def row_loss_kernel(place_ref, loss_ref, row_loss_ref, done_ref):
    experts, capacity = loss_ref.shape
    groups = place_ref.shape[0]
    place = jnp.concatenate([place_ref[g : g + 1, :] for g in range(groups)], axis=1)
    block = place // capacity
    slot = place - block * capacity
    picks = jnp.where(iota((capacity, place.shape[1]), 0) == slot, 1.0, 0.0)
    found = lax.dot_general(
        loss_ref[...],
        picks,
        (((1,), (0,)), ((), ())),
        precision=lax.Precision.HIGHEST,
        preferred_element_type=F32,
    )
    mine = jnp.sum(
        jnp.where(iota((experts, place.shape[1]), 0) == block, found, 0.0), axis=0, keepdims=True
    )
    for g in range(groups):
        row_loss_ref[g : g + 1, :] = mine[:, g * LANES : (g + 1) * LANES]
    done_ref[...] = jnp.zeros(done_ref.shape, F32)


def loss_by_row(place, loss):
    return pl.pallas_call(
        row_loss_kernel,
        out_shape=[jax.ShapeDtypeStruct(shape, F32) for shape in (place.shape, (8, LANES))],
        in_specs=[whole()] * 2,
        out_specs=[whole()] * 2,
        compiler_params=pltpu.CompilerParams(vmem_limit_bytes=16 * MIB),
        name="row_loss",
    )(place, loss)


def adam_update(params, first, second, grads):
    first_new = beta_one * first + (1.0 - beta_one) * grads
    second_new = beta_two * second + (1.0 - beta_two) * grads * grads
    first_hat = first_new / (1.0 - beta_one**adam_step)
    second_hat = second_new / (1.0 - beta_two**adam_step)
    return (
        params - learn_rate * first_hat / (jnp.sqrt(second_hat) + adam_eps),
        first_new,
        second_new,
    )


def adam_kernel(*refs):
    params_ref, first_ref, second_ref, acc_ref, *got = refs[:8]
    *outs, done_ref = refs[8:]
    for k in range(2):
        grads = acc_ref[0, k] + got[k][0].astype(F32) + got[2 + k][...].astype(F32)
        news = adam_update(params_ref[0, k], first_ref[0, k], second_ref[0, k], grads)
        for ref, new in zip(outs, news):
            ref[0, k] = new
    done_ref[...] = jnp.zeros(done_ref.shape, F32)


def adam(params, first, second, acc, got):
    shape = jax.ShapeDtypeStruct(params.shape, F32)
    return pl.pallas_call(
        adam_kernel,
        out_shape=[shape] * 3 + [jax.ShapeDtypeStruct((8, LANES), F32)],
        in_specs=[whole()] * 8,
        out_specs=[whole()] * 4,
        compiler_params=pltpu.CompilerParams(vmem_limit_bytes=24 * MIB),
        cost_estimate=pl.CostEstimate(
            flops=20 * params.size, bytes_accessed=8 * params.size, transcendentals=params.size
        ),
        name="adam",
    )(params, first, second, acc, *got)


def swap(value, axis, s):
    if s == 0:
        return value
    return lax.ppermute(value, axis, [(i, i ^ s) for i in range(lax.axis_size(axis))])


def on_device(
    cell_table,
    sample_index,
    region,
    targets,
    trunk_weight,
    expert_params,
    first_moment,
    second_moment,
):
    rows = sample_index.shape[0]
    width = cell_table.shape[1]
    experts = lax.axis_size("expert")
    replicas = lax.axis_size("dp")
    capacity = 2 * rows // experts
    me = lax.axis_index("expert").astype(jnp.int32).reshape(1)
    mine = lax.axis_index("dp").astype(jnp.int32).reshape(1)

    up, down = expert_params[0, 0].astype(BF16), expert_params[0, 1].astype(BF16)
    near_up, near_down = swap(up, "dp", 1), swap(down, "dp", 2)
    *blocks, place = pack(me, mine, sample_index, region[:, 0], cell_table, targets, experts, capacity)
    ups, downs = pair(up, near_up, place), pair(down, near_down, place)
    weights = [ups, swap(ups, "dp", 2), downs, swap(downs, "dp", 1)]
    if in_turns(experts):
        batches, later = ((0, 4), (1, 5), (2,), (6, 3), (7,)), ()
    else:
        batches, later = (range(experts // 2), range(experts // 2, experts)), ()
    order = [s for batch in batches for s in batch]
    arrived = {s: swap(blocks[s], "expert", s) for s in order if s not in later}
    prior, losses = None, []
    for k, batch in enumerate(batches):
        last = k == len(batches) - 1
        relays = [blocks[s] for s in later] if k == 0 else []
        outs = expert_call(
            [arrived[s] for s in batch], trunk_weight, weights, prior, losses, mine, order, last, relays
        )
        if not last:
            prior = outs[:2]
            losses.append(outs[2])
            for s, block in zip(later, outs[3:]):
                arrived[s] = swap(block, "expert", s)
    acc, *parts, losses = outs

    def send(ahead):
        up, down = messages(send_kernel, [acc], ahead, (2, *acc.shape[2:]), "send")
        return swap(up, "dp", 1), swap(down, "dp", 2)

    def pass_on(got, ahead):
        up, down = messages(pass_on_kernel, [acc, *got], ahead, acc.shape[2:], "pass_on")
        return swap(up, "dp", 2), swap(down, "dp", 1)

    if in_turns(experts):
        quarter = width // replicas
        parts = [swap(part, "dp", j) for j, part in enumerate(parts)]
        total, note = turn(dp_turn_kernel, parts + [losses], (quarter, quarter + 8), "dp_turn")
        got = send(total)
        notes = turn(
            pair_turn_kernel,
            [total, swap(note, "expert", 1), losses],
            (quarter // 2 + 8,) * 4,
            "pair_turn",
            (me,),
        )
        more_up, more_down = pass_on(got, notes[0])
        notes = [swap(note, "expert", 2 * k) for k, note in enumerate(notes)]
        total, loss = turn(z_turn_kernel, notes, (quarter // 2, experts), "z_turn")
        row_loss, found = loss_by_row(place, loss)
        parts = [swap(total, "dp", j) for j in range(replicas)]
        (parts,) = turn(stack_kernel, parts + [found], (width // 2,), "stack_parts")
        other = swap(parts, "expert", 1)
        *news, done = adam(
            expert_params, first_moment, second_moment, acc, [*got, more_up, more_down]
        )
        (trunk_grad,) = turn(
            assemble_kernel, [parts, other, done], (width,), "assemble_trunk", (me, mine)
        )
    else:
        got = send(losses)
        more_up, more_down = pass_on(got, losses)
        *news, _ = adam(
            expert_params, first_moment, second_moment, acc, [*got, more_up, more_down]
        )
        trunk_grad = lax.psum(parts[0], ("dp", "expert"))
        places = jnp.arange(experts, dtype=jnp.int32) ^ me
        losses = losses.reshape(experts, capacity)[places]
        loss = lax.all_to_all(losses, "expert", split_axis=0, concat_axis=0, tiled=True)[places]
        row_loss, _ = loss_by_row(place, loss)

    return (trunk_grad, row_loss.reshape(rows), *news)


def solution(mesh):
    placed = (
        P(("dp", "expert"), None),
        P(("dp", "expert")),
        P(("dp", "expert"), None),
        P(("dp", "expert"), None),
        P(),
        P("expert", None, None, "dp"),
        P("expert", None, None, "dp"),
        P("expert", None, None, "dp"),
    )
    return jax.shard_map(
        on_device,
        mesh=mesh,
        in_specs=placed,
        out_specs=(
            P(),
            P(("dp", "expert")),
            P("expert", None, None, "dp"),
            P("expert", None, None, "dp"),
            P("expert", None, None, "dp"),
        ),
        check_vma=False,
    )
```
